32 devices in a mesh: space: 16 (over z, y, core), dp: 2 (over x).
Axes of the slice: x: 2, y: 2, z: 4, core: 2. Of those that a mesh axis runs over, the one named last changes fastest.
Arguments:
- node_features: float32 [2, 128, 4096], P('dp', None, 'space'), may hold values from -6 to 6
- positions: float32 [2, 3, 4096], P('dp', None, 'space')
- species: int32 [2, 4096], P('dp', 'space'), may hold values from 0 to 7
- energy_cotangent: float32 [2, 4096], P('dp', 'space'), may hold values from -6 to 6
- pair_target: int32 [2, 320], P('dp', 'space'), may hold values from 0 to 3, as said below
- pair_source: int32 [2, 320], P('dp', 'space'), may hold values from 0 to 7, as said below
- pair_count: int32 [2, 16], P('dp', 'space'), may hold values from 4 to 20, as said below
- radial_weight: float32 [8, 128], replicated, may hold values from -2 to 2
- mix_weight: bfloat16 [384, 128], replicated, may hold values from -0.3125 to 0.3125
- readout_weight: float32 [128], replicated, may hold values from -0.5 to 0.5
- species_shift: float32 [8], replicated, may hold values from -4 to 4
Outputs:
- atom_energy: float32 [2, 4096], P('dp', 'space')
- feature_grad: float32 [2, 128, 4096], P('dp', None, 'space')
- radial_grad: float32 [8, 128], replicated
- mix_grad: float32 [384, 128], replicated
- readout_grad: float32 [128], replicated
- shift_grad: float32 [8], replicated
The draws below stay inside these ranges and needn't reach their ends.
Inputs may be any that keep to these rules, and one draw needn't show every extreme that they name: `pair_target`: the target cell of a slot lies in its slab. `pair_source`: A live slot's source cell lies within 2 cells of its target cell and inside the snapshot; every target cell pairs with itself; no pair appears twice in a slab. `pair_count`: counts differ from slab to slab; in every snapshot some slab uses all 20 slots.
All inputs are finite; a program needn't handle non-finite values.
Results may differ from the reference program's by a relative error of at most 0.0009.
The reference program's roundings to bfloat16 on the way (of `scaled`, `factor`, `invariants`, `grad_pre` and `grad_msg`) count: a program that leaves them out, or rounds other values in their place, can miss the bound.
Values sent between devices are 32-bit elements; how exact they have to be, the bound alone decides.
No kernel may reach another device: no remote copies, remote signals or barrier semaphores. Data moves between devices by JAX's collectives and lax.ppermute only.
A program may use at most 64 MiB of HBM per device.

```python
import math
import jax
import jax.numpy as jnp
from jax import lax

CH = 128
NB = 8
NSPEC = 8
CELL_ATOMS = 64
HALO_CELLS = 2
CELLS_DEV = 4
DOMAINS = 16
SNAPS = 2
MAXP = 20
PAIRS = 320
ATOMS = 4096


cell_width = 2.5


def draw_positions(key, part):
    unit = jax.random.uniform(key, (SNAPS, 3, ATOMS), jnp.float32)
    cells = (jnp.arange(ATOMS).astype(jnp.int32) // CELL_ATOMS).astype(jnp.float32)
    across = math.sqrt(4.0 * CELL_ATOMS)
    along = (cells[None, :] + unit[:, 0]) * cell_width
    return jnp.stack([along, unit[:, 1] * across, unit[:, 2] * across], axis=1)


def pair_tables(key):
    base = jax.random.fold_in(key, 7)
    key_one, key_two, key_three = jax.random.split(base, 3)
    reach = 2 * HALO_CELLS + 1
    levels = jax.random.randint(key_one, (SNAPS, DOMAINS), 10, 101)
    dense = jax.random.randint(key_two, (SNAPS,), 1, DOMAINS - 1)
    domain = jnp.arange(DOMAINS).astype(jnp.int32)
    levels = jnp.where(domain[None, :] == dense[:, None], 101, levels)
    rolls = jax.random.randint(key_three, (SNAPS, DOMAINS, CELLS_DEV, reach), 0, 100)
    offsets = jnp.arange(reach).astype(jnp.int32) - HALO_CELLS
    cells = jnp.arange(CELLS_DEV).astype(jnp.int32)
    global_cell = domain[:, None, None] * CELLS_DEV + cells[None, :, None] + offsets[None, None, :]
    inside = (global_cell >= 0) & (global_cell < DOMAINS * CELLS_DEV)
    chosen = ((rolls < levels[:, :, None, None]) | (offsets[None, None, None, :] == 0)) & inside[None]
    chosen = chosen.reshape(SNAPS, DOMAINS, MAXP).astype(jnp.int32)
    source_value = (cells[:, None] + HALO_CELLS + offsets[None, :]).reshape(MAXP)
    target_value = jnp.broadcast_to(cells[:, None], (CELLS_DEV, reach)).reshape(MAXP)
    places = jnp.where(chosen > 0, jnp.cumsum(chosen, axis=-1) - 1, MAXP)
    counts = jnp.sum(chosen, axis=-1)
    onehot = (places[..., :, None] == jnp.arange(MAXP).astype(jnp.int32)).astype(jnp.int32)
    targets = jnp.sum(onehot * target_value[:, None], axis=-2)
    sources = jnp.sum(onehot * source_value[:, None], axis=-2)
    filled = jnp.arange(MAXP).astype(jnp.int32)[None, None, :] < counts[..., None]
    targets = jnp.where(filled, targets, 0)
    sources = jnp.where(filled, sources, HALO_CELLS)
    return (targets.reshape(SNAPS, PAIRS), sources.reshape(SNAPS, PAIRS), counts)


def draw_pair_target(key, part):
    return pair_tables(key)[0]


def draw_pair_source(key, part):
    return pair_tables(key)[1]


def draw_pair_count(key, part):
    return pair_tables(key)[2]


def plant(entries, stream_key, low, high):
    longest = entries.shape.index(max(entries.shape))
    spots = []
    for shift in (0, 1):
        where = [jax.random.randint(jax.random.fold_in(stream_key, axis), (), 0, length) for axis, length in enumerate(entries.shape)]
        where[longest] = (where[longest] + shift) % entries.shape[longest]
        spots.append(tuple(where))
    return entries.at[spots[0]].set(low).at[spots[1]].set(high)


def steps_of(key, shape, shards, least, high):
    level = 1.0
    for dim, parts in shards:
        draws = jax.random.uniform(jax.random.fold_in(jax.random.fold_in(key, 6), dim), (parts,), jnp.float32, least / len(shards), high / len(shards))
        level = level * jnp.repeat(jnp.exp(draws), shape[dim] // parts).reshape((-1,) + (1,) * (len(shape) - 1 - dim))
    return level


def normal_values(key, dims, spread, limit, cuts=(), kind=jnp.bfloat16):
    gain = steps_of(key, dims, cuts, -0.22, 0.18) if cuts else 1.0
    drawn = jax.random.normal(key, dims, jnp.float32) * spread * gain
    return jnp.minimum(jnp.maximum(drawn, -limit), limit).astype(kind)


def setup_inputs(seed: int = 0) -> dict:
    key_of = jax.random.split(jax.random.key(seed), 12)
    node_features = normal_values(key_of[0], (SNAPS, CH, ATOMS), 1.0, 6.0, ((0, 2), (2, 16)), jnp.float32)
    positions = draw_positions(jax.random.fold_in(key_of[11], 71), 0)
    species = plant(jax.random.randint(key_of[2], (SNAPS, ATOMS), 0, NSPEC), jax.random.fold_in(key_of[2], 1), 0, NSPEC - 1).astype(jnp.int32)
    energy_cotangent = normal_values(key_of[3], (SNAPS, ATOMS), 1.0, 6.0, ((0, 2), (1, 16)), jnp.float32)
    pair_target = draw_pair_target(jax.random.fold_in(key_of[11], 71), 0)
    pair_source = draw_pair_source(jax.random.fold_in(key_of[11], 71), 0)
    pair_count = draw_pair_count(jax.random.fold_in(key_of[11], 71), 0)
    radial_weight = normal_values(key_of[7], (NB, CH), 0.35, 2.0, (), jnp.float32)
    mix_weight = normal_values(key_of[8], (3 * CH, CH), (3 * CH) ** -0.5, 0.3125)
    readout_weight = normal_values(key_of[9], (CH,), CH ** -0.5, 0.5, (), jnp.float32)
    species_shift = normal_values(key_of[10], (NSPEC,), 1.0, 4.0, (), jnp.float32)
    return {"node_features": node_features, "positions": positions, "species": species, "energy_cotangent": energy_cotangent, "pair_target": pair_target, "pair_source": pair_source, "pair_count": pair_count, "radial_weight": radial_weight, "mix_weight": mix_weight, "readout_weight": readout_weight, "species_shift": species_shift}


cutoff = 5.0
message_scale = 0.25

def harmonics(delta):
    delta_x = delta[0]
    delta_y = delta[1]
    delta_z = delta[2]
    square_dist = delta_x * delta_x + delta_y * delta_y + delta_z * delta_z
    root_three = math.sqrt(3.0)
    root_fifteen = math.sqrt(15.0)
    root_five = math.sqrt(5.0)
    return jnp.stack([jnp.ones_like(delta_x), root_three * delta_x, root_three * delta_y, root_three * delta_z, root_fifteen * delta_x * delta_y, root_fifteen * delta_y * delta_z, 0.5 * root_five * (3.0 * delta_z * delta_z - square_dist), root_fifteen * delta_x * delta_z, 0.5 * root_fifteen * (delta_x * delta_x - delta_y * delta_y)])

def edge_table(target_coords, source_coords, self_block):
    delta = (target_coords[:, :, None] - source_coords[:, None, :]) / cutoff
    square_dist = lax.optimization_barrier(jnp.sum(delta * delta, axis=0))
    distance = jnp.sqrt(square_dist)
    envelope = jnp.square(jnp.maximum(1.0 - square_dist, 0.0))
    envelope = envelope * (1.0 - self_block * jnp.eye(CELL_ATOMS, dtype=jnp.float32))
    orders = jnp.arange(1, NB + 1).astype(jnp.float32)
    radial = jnp.sinc(orders[:, None, None] * distance[None]) * envelope[None] * message_scale
    harmonic = harmonics(delta)
    radial_t = jnp.transpose(radial, (0, 2, 1))
    harmonic_t = jnp.transpose(harmonic, (2, 0, 1))
    factor = radial_t[:, :, None, :] * harmonic_t[None]
    return factor.reshape(NB * CELL_ATOMS, 9 * CELL_ATOMS).astype(jnp.bfloat16)

def keep_same(values):
    return values

def snapshot_step(features, coords, kinds, energy_grad, targets, sources, counts, radial_weight, mix_weight, readout_weight, species_shift):
    slot = jnp.arange(PAIRS).astype(jnp.int32)
    domain = slot // MAXP
    target_cell = domain * CELLS_DEV + targets
    source_cell = domain * CELLS_DEV + sources - HALO_CELLS
    usable = slot % MAXP < counts[domain]
    scaled = (features[:, None, :] * radial_weight.T[:, :, None]).astype(jnp.bfloat16)

    def forward_step(totals, record):
        tcell, scell, live = record

        def add(current):
            tco = lax.dynamic_slice_in_dim(coords, tcell * CELL_ATOMS, CELL_ATOMS, 1)
            sco = lax.dynamic_slice_in_dim(coords, scell * CELL_ATOMS, CELL_ATOMS, 1)
            factor = edge_table(tco, sco, (tcell == scell).astype(jnp.float32))
            block = lax.dynamic_slice_in_dim(scaled, scell * CELL_ATOMS, CELL_ATOMS, 2).reshape(CH, NB * CELL_ATOMS)
            product = jnp.dot(block, factor, preferred_element_type=jnp.float32).reshape(CH, 9, CELL_ATOMS)
            before = lax.dynamic_slice_in_dim(current, tcell * CELL_ATOMS, CELL_ATOMS, 2)
            return lax.dynamic_update_slice_in_dim(current, before + product, tcell * CELL_ATOMS, 2)
        return (lax.cond(live, add, keep_same, totals), None)
    messages, unused = lax.scan(forward_step, jnp.zeros((CH, 9, ATOMS), jnp.float32), (target_cell, source_cell, usable))
    invariants = jnp.concatenate([messages[:, 0], 0.5 * lax.optimization_barrier(jnp.sum(messages[:, 1:4] ** 2, axis=1)), 0.5 * lax.optimization_barrier(jnp.sum(messages[:, 4:9] ** 2, axis=1))], axis=0).astype(jnp.bfloat16)
    preact = lax.dot_general(mix_weight, invariants, (((0,), (0,)), ((), ())), preferred_element_type=jnp.float32)
    gating = jax.nn.sigmoid(preact)
    updated = features + preact * gating
    onehot = (kinds[None, :] == jnp.arange(NSPEC).astype(jnp.int32)[:, None]).astype(jnp.float32)
    energy = lax.optimization_barrier(jnp.sum(updated * readout_weight[:, None], axis=0)) + lax.optimization_barrier(jnp.sum(onehot * species_shift[:, None], axis=0))
    grad_out = lax.optimization_barrier(jnp.sum(updated * energy_grad[None, :], axis=1))
    grad_shift = lax.optimization_barrier(jnp.sum(onehot * energy_grad[None, :], axis=1))
    grad_pre = (energy_grad[None, :] * readout_weight[:, None] * gating * (1.0 + preact * (1.0 - gating))).astype(jnp.bfloat16)
    grad_mix = lax.dot_general(invariants, grad_pre, (((1,), (1,)), ((), ())), preferred_element_type=jnp.float32)
    grad_inv = jnp.dot(mix_weight, grad_pre, preferred_element_type=jnp.float32)
    grad_msg = jnp.concatenate([grad_inv[:CH][:, None], grad_inv[CH:2 * CH][:, None] * messages[:, 1:4], grad_inv[2 * CH:][:, None] * messages[:, 4:9]], axis=1).astype(jnp.bfloat16)

    def backward_step(totals, record):
        tcell, scell, live = record

        def add(current):
            tco = lax.dynamic_slice_in_dim(coords, tcell * CELL_ATOMS, CELL_ATOMS, 1)
            sco = lax.dynamic_slice_in_dim(coords, scell * CELL_ATOMS, CELL_ATOMS, 1)
            factor = edge_table(tco, sco, (tcell == scell).astype(jnp.float32))
            block = lax.dynamic_slice_in_dim(grad_msg, tcell * CELL_ATOMS, CELL_ATOMS, 2).reshape(CH, 9 * CELL_ATOMS)
            product = lax.dot_general(block, factor, (((1,), (1,)), ((), ())), preferred_element_type=jnp.float32)
            before = lax.dynamic_slice_in_dim(current, scell * CELL_ATOMS, CELL_ATOMS, 2)
            return lax.dynamic_update_slice_in_dim(current, before + product.reshape(CH, NB, CELL_ATOMS), scell * CELL_ATOMS, 2)
        return (lax.cond(live, add, keep_same, totals), None)
    grad_scaled, unused = lax.scan(backward_step, jnp.zeros((CH, NB, ATOMS), jnp.float32), (target_cell, source_cell, usable))
    feature_grad = readout_weight[:, None] * energy_grad[None, :] + lax.optimization_barrier(jnp.sum(grad_scaled * radial_weight.T[:, :, None], axis=1))
    grad_radial = lax.optimization_barrier(jnp.sum(grad_scaled * features[:, None, :], axis=2)).T
    return (energy, feature_grad, grad_radial, grad_mix, grad_out, grad_shift)

def reference(node_features, positions, species, energy_cotangent, pair_target, pair_source, pair_count, radial_weight, mix_weight, readout_weight, species_shift):
    energies = []
    feature_grads = []
    radial_sum = jnp.zeros((NB, CH), jnp.float32)
    mix_sum = jnp.zeros((3 * CH, CH), jnp.float32)
    out_sum = jnp.zeros((CH,), jnp.float32)
    shift_sum = jnp.zeros((NSPEC,), jnp.float32)
    for snapshot in range(SNAPS):
        results = snapshot_step(node_features[snapshot], positions[snapshot], species[snapshot], energy_cotangent[snapshot], pair_target[snapshot], pair_source[snapshot], pair_count[snapshot], radial_weight, mix_weight, readout_weight, species_shift)
        energies.append(results[0])
        feature_grads.append(results[1])
        radial_sum = radial_sum + results[2]
        mix_sum = mix_sum + results[3]
        out_sum = out_sum + results[4]
        shift_sum = shift_sum + results[5]
    scale = 1.0 / math.sqrt(ATOMS * SNAPS)
    return (jnp.stack(energies), jnp.stack(feature_grads), radial_sum * scale, mix_sum * scale, out_sum * scale, shift_sum * scale)
```

```python
import functools
import math

import jax
import jax.numpy as jnp
from jax import lax
from jax.experimental import pallas as pl
from jax.experimental.pallas import tpu as pltpu
from jax.sharding import PartitionSpec as P

CH = 128
NB = 8
NY = 9
NSPEC = 8
CELL_ATOMS = 64
HALO_CELLS = 2
GROUP = 2 * CELL_ATOMS
REACH = 3
ROWS = 16

cutoff = 5.0
message_scale = 0.25

COS_COEFFS = (
    0.9999999998846169,
    -4.934802185771876,
    4.058711815779763,
    -1.3352602773967561,
    0.23532080049888648,
    -0.025785772074137014,
    0.0019043022864480008,
    -8.868331860867329e-05,
)
SINC_COEFFS = (
    0.9999999992502204,
    -1.6449339933418936,
    0.8117412468909989,
    -0.1907447263221115,
    0.02612742969685046,
    -0.0023157632409761065,
    0.00012580778956459784,
)

MIX_ROWS = 3 * CH
RADIAL_AT = MIX_ROWS
READOUT_AT = RADIAL_AT + NB
SHIFT_AT = READOUT_AT + 1
PACKED_ROWS = READOUT_AT + 8


def polynomial(coeffs, x):
    total = coeffs[-1] * x + coeffs[-2]
    for c in coeffs[-3::-1]:
        total = total * x + c
    return total


def factor_rows(factor_ref, block, row, source, target, keep):
    dx = (target[0] - source[0]) * (1.0 / cutoff)
    dy = (target[1] - source[1]) * (1.0 / cutoff)
    dz = (target[2] - source[2]) * (1.0 / cutoff)
    xx, yy, zz = dx * dx, dy * dy, dz * dz
    square = xx + yy + zz
    inside = jnp.minimum(square, 1.0)
    gap = 1.0 - inside
    base = (gap * gap) * keep * polynomial(SINC_COEFFS, inside)
    twice_cos = polynomial([2.0 * c for c in COS_COEFFS], inside)
    raw = [base, twice_cos * base]
    for _ in range(NB - 2):
        raw.append(twice_cos * raw[-1] - raw[-2])
    radial = [value if b == 0 else value * (1.0 / (b + 1)) for b, value in enumerate(raw)]
    root_three = math.sqrt(3.0)
    root_fifteen = math.sqrt(15.0)
    root_five = math.sqrt(5.0)
    wide_x = root_fifteen * dx
    harmonic = [
        None,
        root_three * dx,
        root_three * dy,
        root_three * dz,
        wide_x * dy,
        (root_fifteen * dy) * dz,
        (0.5 * root_five) * (3.0 * zz - square),
        wide_x * dz,
        (0.5 * root_fifteen) * (xx - yy),
    ]
    for b in range(NB):
        rows = pl.ds(pl.multiple_of(b * GROUP + row, ROWS), ROWS)
        for y in range(NY):
            value = radial[b] if y == 0 else radial[b] * harmonic[y]
            factor_ref[block, rows, y * GROUP : (y + 1) * GROUP] = value.astype(jnp.bfloat16)


def column_to_row(column, size):
    wide = jnp.broadcast_to(column, (size, GROUP))
    at = lax.broadcasted_iota(jnp.int32, (size, GROUP), 0)
    lane = lax.broadcasted_iota(jnp.int32, (size, GROUP), 1)
    return jnp.sum(jnp.where(at == lane, wide, 0.0), axis=0, keepdims=True)


def step_kernel(
    scale,
    pairs,
    count_ref,
    pair_target_ref,
    pair_source_ref,
    shift_ref,
    before_ref,
    low_ref,
    high_ref,
    after_ref,
    species_ref,
    energy_grad_ref,
    radial_ref,
    mix_ref,
    readout_ref,
    energy_ref,
    own_grad_ref,
    back_ref,
    ahead_ref,
    packed_ref,
    factor_ref,
    scaled_ref,
    place_ref,
    grad_scaled_ref,
    live_ref,
):
    groups = (before_ref, low_ref, high_ref, after_ref)
    cells = 4 + 2 * HALO_CELLS

    for k in range(4 * cells + 1):
        live_ref[k] = 0.0
    count = count_ref[0, 0]
    for slot in range(pairs):
        at = pair_target_ref[0, slot] * cells + pair_source_ref[0, slot]
        live_ref[jnp.where(slot < count, at, 4 * cells)] = message_scale

    weight = radial_ref[...]
    weight_t = weight.T
    for g, ref in enumerate(groups):
        features = ref[:CH, :]
        for b in range(NB):
            scaled_ref[g, :, b * GROUP : (b + 1) * GROUP] = (
                features * weight_t[:, b : b + 1]
            ).astype(jnp.bfloat16)
        place = ref[CH : CH + 8, :].T
        for axis in range(3):
            place_ref[g, axis] = jnp.broadcast_to(place[:, axis : axis + 1], (GROUP, GROUP))

    lane = lax.broadcasted_iota(jnp.int32, (1, GROUP), 1)
    row_at = lax.broadcasted_iota(jnp.int32, (ROWS, GROUP), 0)
    lane_at = lax.broadcasted_iota(jnp.int32, (ROWS, GROUP), 1)
    messages = []
    for t in range(2):
        target_ref = groups[t + 1]
        target = [target_ref[CH + axis : CH + axis + 1, :] for axis in range(3)]
        total = None
        for d in range(REACH):
            g = t + d
            block = t * REACH + d
            for half in range(2):
                scell = 2 * g + half
                keep_half = jnp.where(
                    lane < CELL_ATOMS,
                    live_ref[(2 * t) * cells + scell],
                    live_ref[(2 * t + 1) * cells + scell],
                )

                def fill(step, carry, g=g, d=d, half=half, block=block, keep_half=keep_half, target=target):
                    row = pl.multiple_of(half * CELL_ATOMS + step * ROWS, ROWS)
                    source = [place_ref[g, axis, pl.ds(row, ROWS), :] for axis in range(3)]
                    keep = jnp.broadcast_to(keep_half, (ROWS, GROUP))
                    if d == 1:
                        keep = jnp.where(row_at + row == lane_at, 0.0, keep)
                    factor_rows(factor_ref, block, row, source, target, keep)
                    return carry

                lax.fori_loop(0, CELL_ATOMS // ROWS, fill, 0)
            product = jnp.dot(
                scaled_ref[g], factor_ref[block], preferred_element_type=jnp.float32
            )
            total = product if total is None else total + product
        messages.append(total)

    readout = jnp.broadcast_to(readout_ref[...], (8, CH)).T[:, :1]
    mix = mix_ref[...]
    mix_t = mix.astype(jnp.float32).T.astype(jnp.bfloat16)
    grad_messages = []
    grad_mix = None
    grad_out = None
    for t in range(2):
        at = slice(t * GROUP, (t + 1) * GROUP)
        part = [messages[t][:, y * GROUP : (y + 1) * GROUP] for y in range(NY)]
        invariants = jnp.concatenate(
            [
                part[0],
                0.5 * (part[1] * part[1] + part[2] * part[2] + part[3] * part[3]),
                0.5
                * (
                    part[4] * part[4]
                    + part[5] * part[5]
                    + part[6] * part[6]
                    + part[7] * part[7]
                    + part[8] * part[8]
                ),
            ],
            axis=0,
        ).astype(jnp.bfloat16)
        preact = jnp.dot(mix_t, invariants, preferred_element_type=jnp.float32)
        gating = jax.nn.sigmoid(preact)
        updated = groups[t + 1][:CH, :] + preact * gating
        energy_grad = energy_grad_ref[:, at]
        kinds = species_ref[:, at]
        shifts = jnp.zeros((1, GROUP), jnp.float32)
        for n in range(NSPEC):
            shifts = jnp.where(kinds == n, shift_ref[n], shifts)
        energy_ref[:, at] = jnp.sum(updated * readout, axis=0, keepdims=True) + shifts
        out = updated * energy_grad
        grad_out = out if grad_out is None else grad_out + out
        spread = readout * energy_grad
        own_grad_ref[0, :, at] = spread
        grad_pre = (spread * gating * (1.0 + preact * (1.0 - gating))).astype(jnp.bfloat16)
        mixed = lax.dot_general(
            invariants, grad_pre, (((1,), (1,)), ((), ())), preferred_element_type=jnp.float32
        )
        grad_mix = mixed if grad_mix is None else grad_mix + mixed
        grad_inv = jnp.dot(mix, grad_pre, preferred_element_type=jnp.float32)
        grad_messages.append(
            jnp.concatenate(
                [grad_inv[:CH]]
                + [grad_inv[CH : 2 * CH] * part[y] for y in range(1, 4)]
                + [grad_inv[2 * CH :] * part[y] for y in range(4, NY)],
                axis=1,
            ).astype(jnp.bfloat16)
        )
    packed_ref[:MIX_ROWS, :] = grad_mix * scale
    readout_row = column_to_row(jnp.sum(grad_out, axis=1, keepdims=True), CH) * scale
    kinds = species_ref[...]
    here = lax.broadcasted_iota(jnp.int32, (NSPEC, 2 * GROUP), 0) == kinds
    by_kind = jnp.sum(jnp.where(here, energy_grad_ref[...], 0.0), axis=1, keepdims=True)
    shift_row = column_to_row(by_kind, NSPEC) * scale
    packed_ref[READOUT_AT:, :] = jnp.concatenate(
        [readout_row, shift_row, jnp.zeros((6, CH), jnp.float32)], axis=0
    )

    grad_radial = [None] * NB
    for g, ref in enumerate(groups):
        total = None
        for t in range(2):
            d = g - t
            if 0 <= d < REACH:
                product = lax.dot_general(
                    factor_ref[t * REACH + d],
                    grad_messages[t],
                    (((1,), (1,)), ((), ())),
                    preferred_element_type=jnp.float32,
                )
                total = product if total is None else total + product
        features_t = ref[:CH, :].T
        grad_t = None
        for b in range(NB):
            slab = total[b * GROUP : (b + 1) * GROUP]
            term = slab * weight[b : b + 1, :]
            grad_t = term if grad_t is None else grad_t + term
            share = jnp.sum(slab * features_t, axis=0, keepdims=True)
            grad_radial[b] = share if grad_radial[b] is None else grad_radial[b] + share
        grad = grad_t.T
        if g == 0:
            back_ref[...] = grad
        elif g == 3:
            ahead_ref[...] = grad
        else:
            at = slice((g - 1) * GROUP, g * GROUP)
            own_grad_ref[0, :, at] = own_grad_ref[0, :, at] + grad
    packed_ref[RADIAL_AT:READOUT_AT, :] = jnp.concatenate(grad_radial, axis=0) * scale


def finish_kernel(
    own_ref, from_before_ref, from_after_ref, mine_ref, other_ref, grad_ref, radial_ref, mix_ref, readout_ref, shift_ref
):
    grad_ref[0, :, :GROUP] = own_ref[0, :, :GROUP] + from_before_ref[...]
    grad_ref[0, :, GROUP:] = own_ref[0, :, GROUP:] + from_after_ref[...]
    mix_ref[...] = mine_ref[:MIX_ROWS, :] + other_ref[:MIX_ROWS, :]
    radial_ref[...] = mine_ref[RADIAL_AT:READOUT_AT, :] + other_ref[RADIAL_AT:READOUT_AT, :]
    rest = mine_ref[READOUT_AT:, :] + other_ref[READOUT_AT:, :]
    readout_ref[...] = rest[:1]
    shift_ref[...] = rest[1:2, :NSPEC]


def body(
    node_features,
    positions,
    species,
    energy_cotangent,
    pair_target,
    pair_source,
    pair_count,
    radial_weight,
    mix_weight,
    readout_weight,
    species_shift,
):
    features = node_features[0]
    coords = positions[0]
    atoms_here = features.shape[1]
    space, dp = lax.axis_size("space"), lax.axis_size("dp")
    scale = 1.0 / math.sqrt(atoms_here * space * dp)
    filler = jnp.zeros((5, GROUP), jnp.float32)
    low = jnp.concatenate([features[:, :GROUP], coords[:, :GROUP], filler], axis=0)
    high = jnp.concatenate([features[:, GROUP:], coords[:, GROUP:], filler], axis=0)
    up = [(i, i + 1) for i in range(space - 1)]
    down = [(i + 1, i) for i in range(space - 1)]
    before = lax.ppermute(high, "space", up)
    after = lax.ppermute(low, "space", down)

    smem = pl.BlockSpec(memory_space=pltpu.SMEM)
    vmem = pl.BlockSpec(memory_space=pltpu.VMEM)
    f32 = jnp.float32
    energy, own_grad, back, ahead, packed = pl.pallas_call(
        functools.partial(step_kernel, scale, pair_target.shape[1]),
        out_shape=(
            jax.ShapeDtypeStruct((1, atoms_here), f32),
            jax.ShapeDtypeStruct((1, CH, atoms_here), f32),
            jax.ShapeDtypeStruct((CH, GROUP), f32),
            jax.ShapeDtypeStruct((CH, GROUP), f32),
            jax.ShapeDtypeStruct((PACKED_ROWS, CH), f32),
        ),
        in_specs=[smem] * 4 + [vmem] * 9,
        out_specs=(vmem,) * 5,
        scratch_shapes=[
            pltpu.VMEM((2 * REACH, NB * GROUP, NY * GROUP), jnp.bfloat16),
            pltpu.VMEM((4, CH, NB * GROUP), jnp.bfloat16),
            pltpu.VMEM((4, 3, GROUP, GROUP), f32),
            pltpu.VMEM((NB * GROUP, CH), f32),
            pltpu.SMEM((40,), f32),
        ],
        compiler_params=pltpu.CompilerParams(vmem_limit_bytes=40 * 1024 * 1024),
        name="layer_step",
    )(
        pair_count,
        pair_target,
        pair_source,
        species_shift,
        before,
        low,
        high,
        after,
        species,
        energy_cotangent,
        radial_weight,
        mix_weight,
        readout_weight.reshape(1, CH),
    )

    rounds = []
    for axis, size in (("space", space), ("dp", dp)):
        step = 1
        while step < size:
            rounds.append((axis, [(i, i ^ step) for i in range(size)]))
            step *= 2
    for axis, route in rounds[:-1]:
        packed = packed + lax.ppermute(packed, axis, route)
    axis, route = rounds[-1]
    other = lax.ppermute(packed, axis, route)
    from_after = lax.ppermute(back, "space", down)
    from_before = lax.ppermute(ahead, "space", up)
    feature_grad, radial_grad, mix_grad, readout_grad, shift_grad = pl.pallas_call(
        finish_kernel,
        out_shape=(
            jax.ShapeDtypeStruct((1, CH, atoms_here), f32),
            jax.ShapeDtypeStruct((NB, CH), f32),
            jax.ShapeDtypeStruct((MIX_ROWS, CH), f32),
            jax.ShapeDtypeStruct((1, CH), f32),
            jax.ShapeDtypeStruct((1, NSPEC), f32),
        ),
        in_specs=[vmem] * 5,
        out_specs=(vmem,) * 5,
        name="finish",
    )(own_grad, from_before, from_after, packed, other)
    return (
        energy,
        feature_grad,
        radial_grad,
        mix_grad,
        readout_grad.reshape(CH),
        shift_grad.reshape(NSPEC),
    )


def solution(mesh):
    return jax.shard_map(
        body,
        mesh=mesh,
        in_specs=(
            P("dp", None, "space"),
            P("dp", None, "space"),
            P("dp", "space"),
            P("dp", "space"),
            P("dp", "space"),
            P("dp", "space"),
            P("dp", "space"),
            P(),
            P(),
            P(),
            P(),
        ),
        out_specs=(P("dp", "space"), P("dp", None, "space"), P(), P(), P(), P()),
        check_vma=False,
    )
```

```python
import functools
import math

import jax
import jax.numpy as jnp
from jax import lax
from jax.experimental import pallas as pl
from jax.experimental.pallas import tpu as pltpu
from jax.sharding import PartitionSpec as P

CH = 128
NB = 8
NY = 9
NSPEC = 8
CELL_ATOMS = 64
HALO_CELLS = 2
GROUP = 2 * CELL_ATOMS
REACH = 3
ROWS = 16

cutoff = 5.0
message_scale = 0.25

COS_COEFFS = (
    0.9999999998846169,
    -4.934802185771876,
    4.058711815779763,
    -1.3352602773967561,
    0.23532080049888648,
    -0.025785772074137014,
    0.0019043022864480008,
    -8.868331860867329e-05,
)
SINC_COEFFS = (
    0.9999999992502204,
    -1.6449339933418936,
    0.8117412468909989,
    -0.1907447263221115,
    0.02612742969685046,
    -0.0023157632409761065,
    0.00012580778956459784,
)

MIX_ROWS = 3 * CH
RADIAL_AT = MIX_ROWS
READOUT_AT = RADIAL_AT + NB
SHIFT_AT = READOUT_AT + 1
PACKED_ROWS = READOUT_AT + 8
SLAB_ROWS = CH + 8


def polynomial(coeffs, x):
    total = coeffs[-1] * x + coeffs[-2]
    for c in coeffs[-3::-1]:
        total = total * x + c
    return total


def factor_rows(factor_ref, block, row, source, target, keep):
    dx = (target[0] - source[0]) * (1.0 / cutoff)
    dy = (target[1] - source[1]) * (1.0 / cutoff)
    dz = (target[2] - source[2]) * (1.0 / cutoff)
    xx, yy, zz = dx * dx, dy * dy, dz * dz
    square = xx + yy + zz
    inside = jnp.minimum(square, 1.0)
    gap = 1.0 - inside
    base = (gap * gap) * keep * polynomial(SINC_COEFFS, inside)
    twice_cos = polynomial([2.0 * c for c in COS_COEFFS], inside)
    raw = [base, twice_cos * base]
    for _ in range(NB - 2):
        raw.append(twice_cos * raw[-1] - raw[-2])
    radial = [value if b == 0 else value * (1.0 / (b + 1)) for b, value in enumerate(raw)]
    root_three = math.sqrt(3.0)
    root_fifteen = math.sqrt(15.0)
    root_five = math.sqrt(5.0)
    wide_x = root_fifteen * dx
    harmonic = [
        None,
        root_three * dx,
        root_three * dy,
        root_three * dz,
        wide_x * dy,
        (root_fifteen * dy) * dz,
        (0.5 * root_five) * (3.0 * zz - square),
        wide_x * dz,
        (0.5 * root_fifteen) * (xx - yy),
    ]
    for b in range(NB):
        rows = pl.ds(pl.multiple_of(b * GROUP + row, ROWS), ROWS)
        for y in range(NY):
            value = radial[b] if y == 0 else radial[b] * harmonic[y]
            factor_ref[block, rows, y * GROUP : (y + 1) * GROUP] = value.astype(jnp.bfloat16)


def column_to_row(column, size):
    wide = jnp.broadcast_to(column, (size, GROUP))
    at = lax.broadcasted_iota(jnp.int32, (size, GROUP), 0)
    lane = lax.broadcasted_iota(jnp.int32, (size, GROUP), 1)
    return jnp.sum(jnp.where(at == lane, wide, 0.0), axis=0, keepdims=True)


def split_kernel(features_ref, place_ref, low_ref, high_ref):
    for half, ref in enumerate((low_ref, high_ref)):
        at = slice(half * GROUP, (half + 1) * GROUP)
        ref[:CH, :] = features_ref[0, :, at]
        ref[CH:, :] = jnp.concatenate(
            [place_ref[axis, :, at] for axis in range(3)] + [jnp.zeros((5, GROUP), jnp.float32)],
            axis=0,
        )


def step_kernel(
    scale,
    pairs,
    count_ref,
    pair_target_ref,
    pair_source_ref,
    shift_ref,
    before_ref,
    low_ref,
    high_ref,
    after_ref,
    species_ref,
    energy_grad_ref,
    radial_ref,
    mix_ref,
    readout_ref,
    energy_ref,
    own_grad_ref,
    back_ref,
    ahead_ref,
    packed_ref,
    factor_ref,
    scaled_ref,
    place_ref,
    grad_scaled_ref,
    live_ref,
):
    groups = (before_ref, low_ref, high_ref, after_ref)
    cells = 4 + 2 * HALO_CELLS

    for k in range(4 * cells + 1):
        live_ref[k] = 0.0
    count = count_ref[0, 0]
    for slot in range(pairs):
        at = pair_target_ref[0, slot] * cells + pair_source_ref[0, slot]
        live_ref[jnp.where(slot < count, at, 4 * cells)] = message_scale

    weight = radial_ref[...]
    weight_t = weight.T
    for g, ref in enumerate(groups):
        features = ref[:CH, :]
        for b in range(NB):
            scaled_ref[g, :, b * GROUP : (b + 1) * GROUP] = (
                features * weight_t[:, b : b + 1]
            ).astype(jnp.bfloat16)
        place = ref[CH : CH + 8, :].T
        for axis in range(3):
            place_ref[g, axis] = jnp.broadcast_to(place[:, axis : axis + 1], (GROUP, GROUP))

    lane = lax.broadcasted_iota(jnp.int32, (1, GROUP), 1)
    row_at = lax.broadcasted_iota(jnp.int32, (ROWS, GROUP), 0)
    lane_at = lax.broadcasted_iota(jnp.int32, (ROWS, GROUP), 1)
    messages = []
    for t in range(2):
        target_ref = groups[t + 1]
        target = [target_ref[CH + axis : CH + axis + 1, :] for axis in range(3)]
        total = None
        for d in range(REACH):
            g = t + d
            block = t * REACH + d
            for half in range(2):
                scell = 2 * g + half
                keep_half = jnp.where(
                    lane < CELL_ATOMS,
                    live_ref[(2 * t) * cells + scell],
                    live_ref[(2 * t + 1) * cells + scell],
                )

                def fill(step, carry, g=g, d=d, half=half, block=block, keep_half=keep_half, target=target):
                    row = pl.multiple_of(half * CELL_ATOMS + step * ROWS, ROWS)
                    source = [place_ref[g, axis, pl.ds(row, ROWS), :] for axis in range(3)]
                    keep = jnp.broadcast_to(keep_half, (ROWS, GROUP))
                    if d == 1:
                        keep = jnp.where(row_at + row == lane_at, 0.0, keep)
                    factor_rows(factor_ref, block, row, source, target, keep)
                    return carry

                lax.fori_loop(0, CELL_ATOMS // ROWS, fill, 0)
            product = jnp.dot(
                scaled_ref[g], factor_ref[block], preferred_element_type=jnp.float32
            )
            total = product if total is None else total + product
        messages.append(total)

    readout = jnp.broadcast_to(readout_ref[...], (8, CH)).T[:, :1]
    mix = mix_ref[...]
    mix_t = mix.astype(jnp.float32).T.astype(jnp.bfloat16)
    grad_messages = []
    grad_mix = None
    grad_out = None
    for t in range(2):
        at = slice(t * GROUP, (t + 1) * GROUP)
        part = [messages[t][:, y * GROUP : (y + 1) * GROUP] for y in range(NY)]
        invariants = jnp.concatenate(
            [
                part[0],
                0.5 * (part[1] * part[1] + part[2] * part[2] + part[3] * part[3]),
                0.5
                * (
                    part[4] * part[4]
                    + part[5] * part[5]
                    + part[6] * part[6]
                    + part[7] * part[7]
                    + part[8] * part[8]
                ),
            ],
            axis=0,
        ).astype(jnp.bfloat16)
        preact = jnp.dot(mix_t, invariants, preferred_element_type=jnp.float32)
        gating = jax.nn.sigmoid(preact)
        updated = groups[t + 1][:CH, :] + preact * gating
        energy_grad = energy_grad_ref[:, at]
        kinds = species_ref[:, at]
        shifts = jnp.zeros((1, GROUP), jnp.float32)
        for n in range(NSPEC):
            shifts = jnp.where(kinds == n, shift_ref[n], shifts)
        energy_ref[:, at] = jnp.sum(updated * readout, axis=0, keepdims=True) + shifts
        out = updated * energy_grad
        grad_out = out if grad_out is None else grad_out + out
        spread = readout * energy_grad
        own_grad_ref[0, :, at] = spread
        grad_pre = (spread * gating * (1.0 + preact * (1.0 - gating))).astype(jnp.bfloat16)
        mixed = lax.dot_general(
            invariants, grad_pre, (((1,), (1,)), ((), ())), preferred_element_type=jnp.float32
        )
        grad_mix = mixed if grad_mix is None else grad_mix + mixed
        grad_inv = jnp.dot(mix, grad_pre, preferred_element_type=jnp.float32)
        grad_messages.append(
            jnp.concatenate(
                [grad_inv[:CH]]
                + [grad_inv[CH : 2 * CH] * part[y] for y in range(1, 4)]
                + [grad_inv[2 * CH :] * part[y] for y in range(4, NY)],
                axis=1,
            ).astype(jnp.bfloat16)
        )
    packed_ref[:MIX_ROWS, :] = grad_mix * scale
    readout_row = column_to_row(jnp.sum(grad_out, axis=1, keepdims=True), CH) * scale
    kinds = species_ref[...]
    here = lax.broadcasted_iota(jnp.int32, (NSPEC, 2 * GROUP), 0) == kinds
    by_kind = jnp.sum(jnp.where(here, energy_grad_ref[...], 0.0), axis=1, keepdims=True)
    shift_row = column_to_row(by_kind, NSPEC) * scale
    packed_ref[READOUT_AT:, :] = jnp.concatenate(
        [readout_row, shift_row, jnp.zeros((6, CH), jnp.float32)], axis=0
    )

    grad_radial = [None] * NB
    for g, ref in enumerate(groups):
        total = None
        for t in range(2):
            d = g - t
            if 0 <= d < REACH:
                product = lax.dot_general(
                    factor_ref[t * REACH + d],
                    grad_messages[t],
                    (((1,), (1,)), ((), ())),
                    preferred_element_type=jnp.float32,
                )
                total = product if total is None else total + product
        features_t = ref[:CH, :].T
        grad_t = None
        for b in range(NB):
            slab = total[b * GROUP : (b + 1) * GROUP]
            term = slab * weight[b : b + 1, :]
            grad_t = term if grad_t is None else grad_t + term
            share = jnp.sum(slab * features_t, axis=0, keepdims=True)
            grad_radial[b] = share if grad_radial[b] is None else grad_radial[b] + share
        grad = grad_t.T
        if g == 0:
            back_ref[...] = grad
        elif g == 3:
            ahead_ref[...] = grad
        else:
            at = slice((g - 1) * GROUP, g * GROUP)
            own_grad_ref[0, :, at] = own_grad_ref[0, :, at] + grad
    packed_ref[RADIAL_AT:READOUT_AT, :] = jnp.concatenate(grad_radial, axis=0) * scale


def finish_kernel(
    own_ref, from_before_ref, from_after_ref, packed_ref, grad_ref, radial_ref, mix_ref, readout_ref, shift_ref
):
    grad_ref[0, :, :GROUP] = own_ref[0, :, :GROUP] + from_before_ref[...]
    grad_ref[0, :, GROUP:] = own_ref[0, :, GROUP:] + from_after_ref[...]
    mix_ref[...] = packed_ref[:MIX_ROWS, :]
    radial_ref[...] = packed_ref[RADIAL_AT:READOUT_AT, :]
    readout_ref[...] = packed_ref[READOUT_AT : READOUT_AT + 1, :]
    shift_ref[...] = packed_ref[SHIFT_AT : SHIFT_AT + 1, :NSPEC]


def body(
    node_features,
    positions,
    species,
    energy_cotangent,
    pair_target,
    pair_source,
    pair_count,
    radial_weight,
    mix_weight,
    readout_weight,
    species_shift,
):
    atoms_here = node_features.shape[2]
    space, dp = lax.axis_size("space"), lax.axis_size("dp")
    scale = 1.0 / math.sqrt(atoms_here * space * dp)
    up = [(i, i + 1) for i in range(space - 1)]
    down = [(i + 1, i) for i in range(space - 1)]
    smem = pl.BlockSpec(memory_space=pltpu.SMEM)
    vmem = pl.BlockSpec(memory_space=pltpu.VMEM)
    f32 = jnp.float32
    slab = jax.ShapeDtypeStruct((SLAB_ROWS, GROUP), f32)
    low, high = pl.pallas_call(
        split_kernel,
        out_shape=(slab, slab),
        in_specs=[vmem] * 2,
        out_specs=(vmem,) * 2,
        name="split",
    )(node_features, jnp.transpose(positions, (1, 0, 2)))
    before = lax.ppermute(high, "space", up)
    after = lax.ppermute(low, "space", down)
    energy, own_grad, back, ahead, packed = pl.pallas_call(
        functools.partial(step_kernel, scale, pair_target.shape[1]),
        out_shape=(
            jax.ShapeDtypeStruct((1, atoms_here), f32),
            jax.ShapeDtypeStruct((1, CH, atoms_here), f32),
            jax.ShapeDtypeStruct((CH, GROUP), f32),
            jax.ShapeDtypeStruct((CH, GROUP), f32),
            jax.ShapeDtypeStruct((PACKED_ROWS, CH), f32),
        ),
        in_specs=[smem] * 4 + [vmem] * 9,
        out_specs=(vmem,) * 5,
        scratch_shapes=[
            pltpu.VMEM((2 * REACH, NB * GROUP, NY * GROUP), jnp.bfloat16),
            pltpu.VMEM((4, CH, NB * GROUP), jnp.bfloat16),
            pltpu.VMEM((4, 3, GROUP, GROUP), f32),
            pltpu.VMEM((NB * GROUP, CH), f32),
            pltpu.SMEM((40,), f32),
        ],
        compiler_params=pltpu.CompilerParams(vmem_limit_bytes=40 * 1024 * 1024),
        name="layer_step",
    )(
        pair_count,
        pair_target,
        pair_source,
        species_shift,
        before,
        low,
        high,
        after,
        species,
        energy_cotangent,
        radial_weight,
        mix_weight,
        readout_weight.reshape(1, CH),
    )

    everyone = ("space", "dp")
    parts = space * dp
    share = -(-PACKED_ROWS // (8 * parts)) * 8
    filled = jnp.pad(packed, ((0, share * parts - PACKED_ROWS), (0, 0)))
    pieces = lax.all_to_all(filled, everyone, 0, 0, tiled=True)
    summed = jnp.sum(pieces.reshape(parts, share, CH), axis=0)
    copies = jnp.broadcast_to(summed[None], (parts, share, CH)).reshape(parts * share, CH)
    packed = lax.all_to_all(copies, everyone, 0, 0, tiled=True)[:PACKED_ROWS]
    from_after = lax.ppermute(back, "space", down)
    from_before = lax.ppermute(ahead, "space", up)
    feature_grad, radial_grad, mix_grad, readout_grad, shift_grad = pl.pallas_call(
        finish_kernel,
        out_shape=(
            jax.ShapeDtypeStruct((1, CH, atoms_here), f32),
            jax.ShapeDtypeStruct((NB, CH), f32),
            jax.ShapeDtypeStruct((MIX_ROWS, CH), f32),
            jax.ShapeDtypeStruct((1, CH), f32),
            jax.ShapeDtypeStruct((1, NSPEC), f32),
        ),
        in_specs=[vmem] * 4,
        out_specs=(vmem,) * 5,
        name="finish",
    )(own_grad, from_before, from_after, packed)
    return (
        energy,
        feature_grad,
        radial_grad,
        mix_grad,
        readout_grad.reshape(CH),
        shift_grad.reshape(NSPEC),
    )


def solution(mesh):
    return jax.shard_map(
        body,
        mesh=mesh,
        in_specs=(
            P("dp", None, "space"),
            P("dp", None, "space"),
            P("dp", "space"),
            P("dp", "space"),
            P("dp", "space"),
            P("dp", "space"),
            P("dp", "space"),
            P(),
            P(),
            P(),
            P(),
        ),
        out_specs=(P("dp", "space"), P("dp", None, "space"), P(), P(), P(), P()),
        check_vma=False,
    )
```

```python
import functools
import math

import jax
import jax.numpy as jnp
from jax import lax
from jax.experimental import pallas as pl
from jax.experimental.pallas import tpu as pltpu
from jax.sharding import PartitionSpec as P

CH = 128
NB = 8
NY = 9
NSPEC = 8
CELL_ATOMS = 64
HALO_CELLS = 2
GROUP = 2 * CELL_ATOMS
REACH = 3
ROWS = 16

cutoff = 5.0
message_scale = 0.25

COS_COEFFS = (
    0.9999999998846169,
    -4.934802185771876,
    4.058711815779763,
    -1.3352602773967561,
    0.23532080049888648,
    -0.025785772074137014,
    0.0019043022864480008,
    -8.868331860867329e-05,
)
SINC_COEFFS = (
    0.9999999992502204,
    -1.6449339933418936,
    0.8117412468909989,
    -0.1907447263221115,
    0.02612742969685046,
    -0.0023157632409761065,
    0.00012580778956459784,
)

MIX_ROWS = 3 * CH
HALF_MIX = MIX_ROWS // 2
HALF_ROWS = HALF_MIX + 8
SLAB_ROWS = CH + 8


def polynomial(coeffs, x):
    total = coeffs[-1] * x + coeffs[-2]
    for c in coeffs[-3::-1]:
        total = total * x + c
    return total


def factor_rows(factor_ref, block, row, source, target, keep):
    dx = (target[0] - source[0]) * (1.0 / cutoff)
    dy = (target[1] - source[1]) * (1.0 / cutoff)
    dz = (target[2] - source[2]) * (1.0 / cutoff)
    xx, yy, zz = dx * dx, dy * dy, dz * dz
    square = xx + yy + zz
    inside = jnp.minimum(square, 1.0)
    gap = 1.0 - inside
    base = (gap * gap) * keep * polynomial(SINC_COEFFS, inside)
    twice_cos = polynomial([2.0 * c for c in COS_COEFFS], inside)
    raw = [base, twice_cos * base]
    for _ in range(NB - 2):
        raw.append(twice_cos * raw[-1] - raw[-2])
    radial = [value if b == 0 else value * (1.0 / (b + 1)) for b, value in enumerate(raw)]
    root_three = math.sqrt(3.0)
    root_fifteen = math.sqrt(15.0)
    root_five = math.sqrt(5.0)
    wide_x = root_fifteen * dx
    harmonic = [
        None,
        root_three * dx,
        root_three * dy,
        root_three * dz,
        wide_x * dy,
        (root_fifteen * dy) * dz,
        (0.5 * root_five) * (3.0 * zz - square),
        wide_x * dz,
        (0.5 * root_fifteen) * (xx - yy),
    ]
    for b in range(NB):
        rows = slice(b * GROUP + row, b * GROUP + row + ROWS)
        for y in range(NY):
            value = radial[b] if y == 0 else radial[b] * harmonic[y]
            factor_ref[block, rows, y * GROUP : (y + 1) * GROUP] = value.astype(jnp.bfloat16)


def column_to_row(column, size):
    wide = jnp.broadcast_to(column, (size, GROUP))
    at = lax.broadcasted_iota(jnp.int32, (size, GROUP), 0)
    lane = lax.broadcasted_iota(jnp.int32, (size, GROUP), 1)
    return jnp.sum(jnp.where(at == lane, wide, 0.0), axis=0, keepdims=True)


def split_kernel(features_ref, place_ref, low_ref, high_ref):
    for half, ref in enumerate((low_ref, high_ref)):
        at = slice(half * GROUP, (half + 1) * GROUP)
        ref[:CH, :] = features_ref[0, :, at]
        ref[CH:, :] = jnp.concatenate(
            [place_ref[axis, :, at] for axis in range(3)] + [jnp.zeros((5, GROUP), jnp.float32)],
            axis=0,
        )


def step_kernel(
    scale,
    pairs,
    count_ref,
    pair_target_ref,
    pair_source_ref,
    shift_ref,
    before_ref,
    low_ref,
    high_ref,
    after_ref,
    species_ref,
    energy_grad_ref,
    radial_ref,
    mix_ref,
    readout_ref,
    energy_ref,
    own_grad_ref,
    back_ref,
    ahead_ref,
    kept_ref,
    sent_ref,
    factor_ref,
    scaled_ref,
    place_ref,
    grad_scaled_ref,
    live_ref,
):
    groups = (before_ref, low_ref, high_ref, after_ref)
    cells = 4 + 2 * HALO_CELLS

    for k in range(4 * cells + 1):
        live_ref[k] = 0.0
    count = count_ref[0, 0]
    for slot in range(pairs):
        at = pair_target_ref[0, slot] * cells + pair_source_ref[0, slot]
        live_ref[jnp.where(slot < count, at, 4 * cells)] = message_scale

    weight = radial_ref[...]
    weight_t = weight.T
    for g, ref in enumerate(groups):
        features = ref[:CH, :]
        for b in range(NB):
            scaled_ref[g, :, b * GROUP : (b + 1) * GROUP] = (
                features * weight_t[:, b : b + 1]
            ).astype(jnp.bfloat16)
        place = ref[CH : CH + 8, :].T
        for axis in range(3):
            place_ref[g, axis] = jnp.broadcast_to(place[:, axis : axis + 1], (GROUP, GROUP))

    lane = lax.broadcasted_iota(jnp.int32, (1, GROUP), 1)
    row_at = lax.broadcasted_iota(jnp.int32, (ROWS, GROUP), 0)
    lane_at = lax.broadcasted_iota(jnp.int32, (ROWS, GROUP), 1)
    def fill(block):
        t, d = block // REACH, block % REACH
        g = t + d
        target_ref = groups[t + 1]
        target = [target_ref[CH + axis : CH + axis + 1, :] for axis in range(3)]
        for half in range(2):
            scell = 2 * g + half
            keep_half = jnp.where(
                lane < CELL_ATOMS,
                live_ref[(2 * t) * cells + scell],
                live_ref[(2 * t + 1) * cells + scell],
            )
            for row in range(half * CELL_ATOMS, (half + 1) * CELL_ATOMS, ROWS):
                source = [place_ref[g, axis, row : row + ROWS, :] for axis in range(3)]
                keep = jnp.broadcast_to(keep_half, (ROWS, GROUP))
                if d == 1:
                    keep = jnp.where(row_at + row == lane_at, 0.0, keep)
                factor_rows(factor_ref, block, row, source, target, keep)

    blocks = 2 * REACH
    messages = [None, None]
    fill(0)
    for block in range(blocks):
        t, d = block // REACH, block % REACH
        product = jnp.dot(
            scaled_ref[t + d], factor_ref[block], preferred_element_type=jnp.float32
        )
        messages[t] = product if d == 0 else messages[t] + product
        if block + 1 < blocks:
            fill(block + 1)

    readout = jnp.broadcast_to(readout_ref[...], (8, CH)).T[:, :1]
    mix = mix_ref[...]
    mix_t = mix.astype(jnp.float32).T.astype(jnp.bfloat16)
    grad_messages = []
    grad_mix = None
    grad_out = None
    for t in range(2):
        at = slice(t * GROUP, (t + 1) * GROUP)
        part = [messages[t][:, y * GROUP : (y + 1) * GROUP] for y in range(NY)]
        invariants = jnp.concatenate(
            [
                part[0],
                0.5 * (part[1] * part[1] + part[2] * part[2] + part[3] * part[3]),
                0.5
                * (
                    part[4] * part[4]
                    + part[5] * part[5]
                    + part[6] * part[6]
                    + part[7] * part[7]
                    + part[8] * part[8]
                ),
            ],
            axis=0,
        ).astype(jnp.bfloat16)
        preact = jnp.dot(mix_t, invariants, preferred_element_type=jnp.float32)
        gating = jax.nn.sigmoid(preact)
        updated = groups[t + 1][:CH, :] + preact * gating
        energy_grad = energy_grad_ref[:, at]
        kinds = species_ref[:, at]
        shifts = jnp.zeros((1, GROUP), jnp.float32)
        for n in range(NSPEC):
            shifts = jnp.where(kinds == n, shift_ref[n], shifts)
        energy_ref[:, at] = jnp.sum(updated * readout, axis=0, keepdims=True) + shifts
        out = updated * energy_grad
        grad_out = out if grad_out is None else grad_out + out
        spread = readout * energy_grad
        own_grad_ref[0, :, at] = spread
        grad_pre = (spread * gating * (1.0 + preact * (1.0 - gating))).astype(jnp.bfloat16)
        mixed = lax.dot_general(
            invariants, grad_pre, (((1,), (1,)), ((), ())), preferred_element_type=jnp.float32
        )
        grad_mix = mixed if grad_mix is None else grad_mix + mixed
        grad_inv = jnp.dot(mix, grad_pre, preferred_element_type=jnp.float32)
        grad_messages.append(
            jnp.concatenate(
                [grad_inv[:CH]]
                + [grad_inv[CH : 2 * CH] * part[y] for y in range(1, 4)]
                + [grad_inv[2 * CH :] * part[y] for y in range(4, NY)],
                axis=1,
            ).astype(jnp.bfloat16)
        )
    core = lax.axis_index("space") % 2
    grad_mix = grad_mix * scale
    readout_row = column_to_row(jnp.sum(grad_out, axis=1, keepdims=True), CH) * scale
    kinds = species_ref[...]
    here = lax.broadcasted_iota(jnp.int32, (NSPEC, 2 * GROUP), 0) == kinds
    by_kind = jnp.sum(jnp.where(here, energy_grad_ref[...], 0.0), axis=1, keepdims=True)
    shift_row = column_to_row(by_kind, NSPEC) * scale
    rest = jnp.concatenate([readout_row, shift_row, jnp.zeros((6, CH), jnp.float32)], axis=0)

    grad_radial = [None] * NB
    for g, ref in enumerate(groups):
        total = None
        for t in range(2):
            d = g - t
            if 0 <= d < REACH:
                product = lax.dot_general(
                    factor_ref[t * REACH + d],
                    grad_messages[t],
                    (((1,), (1,)), ((), ())),
                    preferred_element_type=jnp.float32,
                )
                total = product if total is None else total + product
        features_t = ref[:CH, :].T
        grad_t = None
        for b in range(NB):
            slab = total[b * GROUP : (b + 1) * GROUP]
            term = slab * weight[b : b + 1, :]
            grad_t = term if grad_t is None else grad_t + term
            share = jnp.sum(slab * features_t, axis=0, keepdims=True)
            grad_radial[b] = share if grad_radial[b] is None else grad_radial[b] + share
        grad = grad_t.T
        if g == 0:
            back_ref[...] = grad
        elif g == 3:
            ahead_ref[...] = grad
        else:
            at = slice((g - 1) * GROUP, g * GROUP)
            own_grad_ref[0, :, at] = own_grad_ref[0, :, at] + grad
    first = (grad_mix[:HALF_MIX], jnp.concatenate(grad_radial, axis=0) * scale)
    second = (grad_mix[HALF_MIX:], rest)
    for at, one, two in zip((slice(HALF_MIX), slice(HALF_MIX, HALF_ROWS)), first, second):
        kept_ref[at, :] = jnp.where(core == 0, one, two)
        sent_ref[at, :] = jnp.where(core == 0, two, one)


def finish_kernel(mine_ref, other_ref, radial_ref, mix_ref, readout_ref, shift_ref):
    core = lax.axis_index("space") % 2
    mine = mine_ref[...]
    other = other_ref[...]
    first = jnp.where(core == 0, mine, other)
    second = jnp.where(core == 0, other, mine)
    mix_ref[:HALF_MIX, :] = first[:HALF_MIX]
    mix_ref[HALF_MIX:, :] = second[:HALF_MIX]
    radial_ref[...] = first[HALF_MIX:]
    readout_ref[...] = second[HALF_MIX : HALF_MIX + 1]
    shift_ref[...] = second[HALF_MIX + 1 : HALF_MIX + 2, :NSPEC]


def exchange_routes(space, dp):
    steps = [(0, 1 << k) for k in range(dp.bit_length() - 1)]
    steps += [(1 << k, 0) for k in range(1, space.bit_length() - 1)]
    routes = []
    for turn in range(len(steps)):
        route = []
        for s in range(space):
            across, along = steps[(turn + (s % 2) * (len(steps) // 2)) % len(steps)]
            for d in range(dp):
                route.append((s * dp + d, (s ^ across) * dp + (d ^ along)))
        routes.append(route)
    return routes


def body(
    node_features,
    positions,
    species,
    energy_cotangent,
    pair_target,
    pair_source,
    pair_count,
    radial_weight,
    mix_weight,
    readout_weight,
    species_shift,
):
    atoms_here = node_features.shape[2]
    space, dp = lax.axis_size("space"), lax.axis_size("dp")
    scale = 1.0 / math.sqrt(atoms_here * space * dp)
    up = [(i, i + 1) for i in range(space - 1)]
    down = [(i + 1, i) for i in range(space - 1)]
    smem = pl.BlockSpec(memory_space=pltpu.SMEM)
    vmem = pl.BlockSpec(memory_space=pltpu.VMEM)
    f32 = jnp.float32
    slab = jax.ShapeDtypeStruct((SLAB_ROWS, GROUP), f32)
    low, high = pl.pallas_call(
        split_kernel,
        out_shape=(slab, slab),
        in_specs=[vmem] * 2,
        out_specs=(vmem,) * 2,
        name="split",
    )(node_features, jnp.transpose(positions, (1, 0, 2)))
    before = lax.ppermute(high, "space", up)
    after = lax.ppermute(low, "space", down)
    energy, own_grad, back, ahead, kept, sent = pl.pallas_call(
        functools.partial(step_kernel, scale, pair_target.shape[1]),
        out_shape=(
            jax.ShapeDtypeStruct((1, atoms_here), f32),
            jax.ShapeDtypeStruct((1, CH, atoms_here), f32),
            jax.ShapeDtypeStruct((CH, GROUP), f32),
            jax.ShapeDtypeStruct((CH, GROUP), f32),
            jax.ShapeDtypeStruct((HALF_ROWS, CH), f32),
            jax.ShapeDtypeStruct((HALF_ROWS, CH), f32),
        ),
        in_specs=[smem] * 4 + [vmem] * 9,
        out_specs=(vmem,) * 6,
        scratch_shapes=[
            pltpu.VMEM((2 * REACH, NB * GROUP, NY * GROUP), jnp.bfloat16),
            pltpu.VMEM((4, CH, NB * GROUP), jnp.bfloat16),
            pltpu.VMEM((4, 3, GROUP, GROUP), f32),
            pltpu.VMEM((NB * GROUP, CH), f32),
            pltpu.SMEM((40,), f32),
        ],
        compiler_params=pltpu.CompilerParams(vmem_limit_bytes=40 * 1024 * 1024),
        name="layer_step",
    )(
        pair_count,
        pair_target,
        pair_source,
        species_shift,
        before,
        low,
        high,
        after,
        species,
        energy_cotangent,
        radial_weight,
        mix_weight,
        readout_weight.reshape(1, CH),
    )

    pair = [(i, i ^ 1) for i in range(space)]
    half = kept + lax.ppermute(sent, "space", pair)
    routes = exchange_routes(space, dp)
    for turn, route in enumerate(routes):
        if turn == 1:
            half, back, ahead = lax.optimization_barrier((half, back, ahead))
            from_after = lax.ppermute(back, "space", down)
            from_before = lax.ppermute(ahead, "space", up)
        if turn == len(routes) - 1:
            half, from_after, from_before = lax.optimization_barrier((half, from_after, from_before))
        half = half + lax.ppermute(half, ("space", "dp"), route)
    other = lax.ppermute(half, "space", pair)
    feature_grad = own_grad + jnp.concatenate([from_before, from_after], axis=1)[None]
    radial_grad, mix_grad, readout_grad, shift_grad = pl.pallas_call(
        finish_kernel,
        out_shape=(
            jax.ShapeDtypeStruct((NB, CH), f32),
            jax.ShapeDtypeStruct((MIX_ROWS, CH), f32),
            jax.ShapeDtypeStruct((1, CH), f32),
            jax.ShapeDtypeStruct((1, NSPEC), f32),
        ),
        in_specs=[vmem] * 2,
        out_specs=(vmem,) * 4,
        name="finish",
    )(half, other)
    return (
        energy,
        feature_grad,
        radial_grad,
        mix_grad,
        readout_grad.reshape(CH),
        shift_grad.reshape(NSPEC),
    )


def solution(mesh):
    return jax.shard_map(
        body,
        mesh=mesh,
        in_specs=(
            P("dp", None, "space"),
            P("dp", None, "space"),
            P("dp", "space"),
            P("dp", "space"),
            P("dp", "space"),
            P("dp", "space"),
            P("dp", "space"),
            P(),
            P(),
            P(),
            P(),
        ),
        out_specs=(P("dp", "space"), P("dp", None, "space"), P(), P(), P(), P()),
        check_vma=False,
    )
```

```python
import functools
import math

import jax
import jax.numpy as jnp
from jax import lax
from jax.experimental import pallas as pl
from jax.experimental.pallas import tpu as pltpu
from jax.sharding import PartitionSpec as P

CH = 128
NB = 8
NY = 9
NSPEC = 8
CELL_ATOMS = 64
HALO_CELLS = 2
GROUP = 2 * CELL_ATOMS
ROWS = 16

cutoff = 5.0
message_scale = 0.25

COS_COEFFS = (
    0.9999999998846169,
    -4.934802185771876,
    4.058711815779763,
    -1.3352602773967561,
    0.23532080049888648,
    -0.025785772074137014,
    0.0019043022864480008,
    -8.868331860867329e-05,
)
SINC_COEFFS = (
    0.9999999992502204,
    -1.6449339933418936,
    0.8117412468909989,
    -0.1907447263221115,
    0.02612742969685046,
    -0.0023157632409761065,
    0.00012580778956459784,
)

MIX_ROWS = 3 * CH
HALF_MIX = MIX_ROWS // 2
HALF_ROWS = HALF_MIX + 8
CELLS = 4 + 2 * HALO_CELLS
LOCAL = ((0, 1), (0, 2), (1, 0), (1, 1))
SLAB_ROWS = CH + 8


def polynomial(coeffs, x):
    total = coeffs[-1] * x + coeffs[-2]
    for c in coeffs[-3::-1]:
        total = total * x + c
    return total


def factor_rows(factor_ref, row, source, target, keep):
    dx = (target[0] - source[0]) * (1.0 / cutoff)
    dy = (target[1] - source[1]) * (1.0 / cutoff)
    dz = (target[2] - source[2]) * (1.0 / cutoff)
    xx, yy, zz = dx * dx, dy * dy, dz * dz
    square = xx + yy + zz
    inside = jnp.minimum(square, 1.0)
    gap = 1.0 - inside
    base = (gap * gap) * keep * polynomial(SINC_COEFFS, inside)
    twice_cos = polynomial([2.0 * c for c in COS_COEFFS], inside)
    raw = [base, twice_cos * base]
    for _ in range(NB - 2):
        raw.append(twice_cos * raw[-1] - raw[-2])
    radial = [value if b == 0 else value * (1.0 / (b + 1)) for b, value in enumerate(raw)]
    root_three = math.sqrt(3.0)
    root_fifteen = math.sqrt(15.0)
    root_five = math.sqrt(5.0)
    wide_x = root_fifteen * dx
    harmonic = [
        None,
        root_three * dx,
        root_three * dy,
        root_three * dz,
        wide_x * dy,
        (root_fifteen * dy) * dz,
        (0.5 * root_five) * (3.0 * zz - square),
        wide_x * dz,
        (0.5 * root_fifteen) * (xx - yy),
    ]
    for b in range(NB):
        rows = slice(b * GROUP + row, b * GROUP + row + ROWS)
        for y in range(NY):
            value = radial[b] if y == 0 else radial[b] * harmonic[y]
            factor_ref[rows, y * GROUP : (y + 1) * GROUP] = value.astype(jnp.bfloat16)


def column_to_row(column, size):
    wide = jnp.broadcast_to(column, (size, GROUP))
    at = lax.broadcasted_iota(jnp.int32, (size, GROUP), 0)
    lane = lax.broadcasted_iota(jnp.int32, (size, GROUP), 1)
    return jnp.sum(jnp.where(at == lane, wide, 0.0), axis=0, keepdims=True)


def split_kernel(features_ref, place_in_ref, pair_ref, cross_ref, place_ref, sems):
    core = lax.axis_index("space") % 2
    place_copy = pltpu.make_async_copy(place_in_ref, place_ref, sems.at[2])
    place_copy.start()
    copies = []
    for k, (ref, side) in enumerate(((pair_ref, 1 - core), (cross_ref, core))):
        at = pl.ds(pl.multiple_of(side * GROUP, GROUP), GROUP)
        copy = pltpu.make_async_copy(features_ref.at[0, :, at], ref.at[pl.ds(0, CH)], sems.at[k])
        copy.start()
        copies.append(copy)
    place_copy.wait()
    low, high = slice(GROUP), slice(GROUP, 2 * GROUP)
    filler = jnp.zeros((5, GROUP), jnp.float32)
    for ref, one, two in ((pair_ref, high, low), (cross_ref, low, high)):
        rows = [
            jnp.where(core == 0, place_ref[axis, :, one], place_ref[axis, :, two]) for axis in range(3)
        ]
        ref[CH:, :] = jnp.concatenate(rows + [filler], axis=0)
    for copy in copies:
        copy.wait()


def live_flags(count, pair_target, pair_source):
    size = (4 * CELLS, pair_target.shape[1])
    at = lax.broadcasted_iota(jnp.int32, size, 0)
    slot = lax.broadcasted_iota(jnp.int32, size, 1)
    hit = (pair_target * CELLS + pair_source == at) & (slot < count)
    return jnp.max(jnp.where(hit, message_scale, 0.0), axis=1, keepdims=True)


def keep_rows(flags, t, d):
    lane = lax.broadcasted_iota(jnp.int32, (1, GROUP), 1)
    rows = []
    for scell in (2 * (t + d), 2 * (t + d) + 1):
        one, two = [(2 * t + k) * CELLS + scell for k in range(2)]
        rows.append(jnp.where(lane < CELL_ATOMS, flags[one : one + 1], flags[two : two + 1]))
    return rows


def set_source(scaled_ref, place_ref, slab, weight_t):
    features = slab[:CH]
    for b in range(NB):
        scaled_ref[:, b * GROUP : (b + 1) * GROUP] = (features * weight_t[:, b : b + 1]).astype(
            jnp.bfloat16
        )
    place = slab[CH:].T
    for axis in range(3):
        place_ref[axis] = jnp.broadcast_to(place[:, axis : axis + 1], (GROUP, GROUP))


def fill_block(factor_ref, place_ref, keeps, target, d):
    row_at = lax.broadcasted_iota(jnp.int32, (ROWS, GROUP), 0)
    lane_at = lax.broadcasted_iota(jnp.int32, (ROWS, GROUP), 1)
    for half in range(2):
        for row in range(half * CELL_ATOMS, (half + 1) * CELL_ATOMS, ROWS):
            source = [place_ref[axis, row : row + ROWS, :] for axis in range(3)]
            keep = jnp.broadcast_to(keeps[half], (ROWS, GROUP))
            if d == 1:
                keep = jnp.where(row_at + row == lane_at, 0.0, keep)
            factor_rows(factor_ref, row, source, target, keep)


def local_kernel(
    count_in_ref,
    pair_target_in_ref,
    pair_source_in_ref,
    species_in_ref,
    shift_in_ref,
    energy_grad_in_ref,
    radial_in_ref,
    mix_in_ref,
    readout_in_ref,
    pair_ref,
    cross_ref,
    factor_ref,
    messages_ref,
    keep_ref,
    shifts_ref,
    by_kind_ref,
    energy_grad_ref,
    radial_ref,
    mix_ref,
    readout_ref,
    count_ref,
    pair_target_ref,
    pair_source_ref,
    species_ref,
    shift_ref,
    scaled_ref,
    place_ref,
    sems,
):
    moves = (
        (radial_in_ref, radial_ref),
        (count_in_ref, count_ref),
        (pair_target_in_ref, pair_target_ref),
        (pair_source_in_ref, pair_source_ref),
        (species_in_ref, species_ref),
        (shift_in_ref, shift_ref),
        (energy_grad_in_ref, energy_grad_ref),
        (mix_in_ref, mix_ref),
        (readout_in_ref, readout_ref),
    )
    copies = [pltpu.make_async_copy(src, dst, sems.at[k]) for k, (src, dst) in enumerate(moves)]
    for copy in copies:
        copy.start()
    even = lax.axis_index("space") % 2 == 0
    slabs = (
        jnp.where(even, cross_ref[...], pair_ref[...]),
        jnp.where(even, pair_ref[...], cross_ref[...]),
    )
    targets = [[slab[CH + axis : CH + axis + 1] for axis in range(3)] for slab in slabs]
    for copy in copies:
        copy.wait()
    flags = live_flags(count_ref[...], pair_target_ref[...], pair_source_ref[...])
    weight_t = radial_ref[...].T
    for g in range(2):
        set_source(scaled_ref.at[g], place_ref.at[g], slabs[g], weight_t)

    def fill(block):
        t, d = LOCAL[block]
        fill_block(factor_ref.at[block], place_ref.at[t + d - 1], keep_rows(flags, t, d), targets[t], d)

    totals = [None, None]
    fill(0)
    for block, (t, d) in enumerate(LOCAL):
        product = jnp.dot(
            scaled_ref[t + d - 1], factor_ref[block], preferred_element_type=jnp.float32
        )
        totals[t] = product if totals[t] is None else totals[t] + product
        if block + 1 < len(LOCAL):
            fill(block + 1)
    for t in range(2):
        messages_ref[t] = totals[t]

    keep_ref[...] = jnp.concatenate(
        keep_rows(flags, 0, 0) + keep_rows(flags, 1, 2) + [jnp.zeros((4, GROUP), jnp.float32)], axis=0
    )
    kinds = species_ref[...]
    shifts = jnp.zeros((1, 2 * GROUP), jnp.float32)
    for n in range(NSPEC):
        shifts = jnp.where(kinds == n, shift_ref[:, n : n + 1], shifts)
    shifts_ref[...] = shifts
    here = lax.broadcasted_iota(jnp.int32, (NSPEC, 2 * GROUP), 0) == kinds
    by_kind = jnp.sum(jnp.where(here, energy_grad_ref[...], 0.0), axis=1, keepdims=True)
    by_kind_ref[...] = column_to_row(by_kind, NSPEC)


def step_kernel(
    scale,
    pair_ref,
    cross_ref,
    from_pair_ref,
    from_cross_ref,
    local_ref,
    messages_ref,
    keep_ref,
    shifts_ref,
    by_kind_ref,
    energy_grad_ref,
    radial_ref,
    mix_ref,
    readout_ref,
    energy_ref,
    own_grad_ref,
    kept_ref,
    sent_ref,
    to_cross_ref,
    halo_ref,
    scaled_ref,
    place_ref,
):
    even = lax.axis_index("space") % 2 == 0
    weight = radial_ref[...]
    weight_t = weight.T
    slabs = (
        jnp.where(even, from_cross_ref[...], from_pair_ref[...]),
        jnp.where(even, cross_ref[...], pair_ref[...]),
        jnp.where(even, pair_ref[...], cross_ref[...]),
        jnp.where(even, from_pair_ref[...], from_cross_ref[...]),
    )
    targets = [[slab[CH + axis : CH + axis + 1] for axis in range(3)] for slab in slabs[1:3]]

    def add_halo(t):
        d = 2 * t
        set_source(scaled_ref.at[t], place_ref.at[t], slabs[t + d], weight_t)
        keeps = [keep_ref[2 * t + half : 2 * t + half + 1, :] for half in range(2)]
        fill_block(halo_ref.at[t], place_ref.at[t], keeps, targets[t], d)
        return messages_ref[t] + jnp.dot(
            scaled_ref[t], halo_ref[t], preferred_element_type=jnp.float32
        )

    readout = jnp.broadcast_to(readout_ref[...], (8, CH)).T[:, :1]
    mix = mix_ref[...]
    mix_t = mix.astype(jnp.float32).T.astype(jnp.bfloat16)

    def node_stage(t, messages):
        at = slice(t * GROUP, (t + 1) * GROUP)
        part = [messages[:, y * GROUP : (y + 1) * GROUP] for y in range(NY)]
        invariants = jnp.concatenate(
            [
                part[0],
                0.5 * (part[1] * part[1] + part[2] * part[2] + part[3] * part[3]),
                0.5
                * (
                    part[4] * part[4]
                    + part[5] * part[5]
                    + part[6] * part[6]
                    + part[7] * part[7]
                    + part[8] * part[8]
                ),
            ],
            axis=0,
        ).astype(jnp.bfloat16)
        preact = jnp.dot(mix_t, invariants, preferred_element_type=jnp.float32)
        gating = jax.nn.sigmoid(preact)
        updated = slabs[t + 1][:CH] + preact * gating
        energy_grad = energy_grad_ref[:, at]
        energy_ref[:, at] = jnp.sum(updated * readout, axis=0, keepdims=True) + shifts_ref[:, at]
        spread = readout * energy_grad
        own_grad_ref[0, :, at] = spread
        grad_pre = (spread * gating * (1.0 + preact * (1.0 - gating))).astype(jnp.bfloat16)
        grad_mix = lax.dot_general(
            invariants, grad_pre, (((1,), (1,)), ((), ())), preferred_element_type=jnp.float32
        )
        grad_inv = jnp.dot(mix, grad_pre, preferred_element_type=jnp.float32)
        grad_messages = jnp.concatenate(
            [grad_inv[:CH]]
            + [grad_inv[CH : 2 * CH] * part[y] for y in range(1, 4)]
            + [grad_inv[2 * CH :] * part[y] for y in range(4, NY)],
            axis=1,
        ).astype(jnp.bfloat16)
        return updated * energy_grad, grad_mix, grad_messages

    def back(factor, grad_messages):
        return lax.dot_general(
            factor, grad_messages, (((1,), (1,)), ((), ())), preferred_element_type=jnp.float32
        )

    first = add_halo(0)
    out_low, mix_low, grad_low = node_stage(0, first)
    second = add_halo(1)
    from_low = [back(halo_ref[0], grad_low), back(local_ref[0], grad_low), back(local_ref[1], grad_low)]
    out_high, mix_high, grad_high = node_stage(1, second)
    from_high = [back(local_ref[2], grad_high), back(local_ref[3], grad_high), back(halo_ref[1], grad_high)]

    grad_mix = (mix_low + mix_high) * scale
    readout_row = column_to_row(jnp.sum(out_low + out_high, axis=1, keepdims=True), CH) * scale
    shift_row = by_kind_ref[...] * scale
    rest = jnp.concatenate([readout_row, shift_row, jnp.zeros((6, CH), jnp.float32)], axis=0)

    grad_radial = [None] * NB
    grads = []
    totals = (from_low[0], from_low[1] + from_high[0], from_low[2] + from_high[1], from_high[2])
    for slab, total in zip(slabs, totals):
        features_t = slab[:CH].T
        grad_t = None
        for b in range(NB):
            piece = total[b * GROUP : (b + 1) * GROUP]
            term = piece * weight[b : b + 1, :]
            grad_t = term if grad_t is None else grad_t + term
            share = jnp.sum(piece * features_t, axis=0, keepdims=True)
            grad_radial[b] = share if grad_radial[b] is None else grad_radial[b] + share
        grads.append(grad_t.T)
    for t in range(2):
        at = slice(t * GROUP, (t + 1) * GROUP)
        own_grad_ref[0, :, at] = own_grad_ref[0, :, at] + grads[t + 1]
    sent_ref[HALF_ROWS:, :] = jnp.where(even, grads[3], grads[0])
    to_cross_ref[...] = jnp.where(even, grads[0], grads[3])
    one_half = (grad_mix[:HALF_MIX], jnp.concatenate(grad_radial, axis=0) * scale)
    other_half = (grad_mix[HALF_MIX:], rest)
    for at, one, two in zip((slice(HALF_MIX), slice(HALF_MIX, HALF_ROWS)), one_half, other_half):
        kept_ref[at, :] = jnp.where(even, one, two)
        sent_ref[at, :] = jnp.where(even, two, one)


def fold_kernel(own_ref, from_pair_ref, from_cross_ref, grad_ref):
    even = lax.axis_index("space") % 2 == 0
    pair = from_pair_ref[HALF_ROWS:, :]
    cross = from_cross_ref[...]
    grad_ref[0, :, :GROUP] = own_ref[0, :, :GROUP] + jnp.where(even, cross, pair)
    grad_ref[0, :, GROUP:] = own_ref[0, :, GROUP:] + jnp.where(even, pair, cross)


def finish_kernel(mine_ref, other_ref, radial_ref, mix_ref, readout_ref, shift_ref):
    even = lax.axis_index("space") % 2 == 0
    mine = mine_ref[...]
    other = other_ref[...]
    first = jnp.where(even, mine, other)
    second = jnp.where(even, other, mine)
    mix_ref[:HALF_MIX, :] = first[:HALF_MIX]
    mix_ref[HALF_MIX:, :] = second[:HALF_MIX]
    radial_ref[...] = first[HALF_MIX:]
    readout_ref[...] = second[HALF_MIX : HALF_MIX + 1]
    shift_ref[...] = second[HALF_MIX + 1 : HALF_MIX + 2, :NSPEC]


def exchange_routes(space, dp):
    steps = [(0, 1 << k) for k in range(dp.bit_length() - 1)]
    steps += [(1 << k, 0) for k in range(1, space.bit_length() - 1)]
    routes = []
    for turn in range(len(steps)):
        route = []
        for s in range(space):
            across, along = steps[(turn + (s % 2) * (len(steps) // 2)) % len(steps)]
            for d in range(dp):
                route.append((s * dp + d, (s ^ across) * dp + (d ^ along)))
        routes.append(route)
    return routes


def body(
    node_features,
    positions,
    species,
    energy_cotangent,
    pair_target,
    pair_source,
    pair_count,
    radial_weight,
    mix_weight,
    readout_weight,
    species_shift,
):
    atoms_here = node_features.shape[2]
    space, dp = lax.axis_size("space"), lax.axis_size("dp")
    scale = 1.0 / math.sqrt(atoms_here * space * dp)
    pair = [(i, i ^ 1) for i in range(space)]
    cross = [(i, ((i + 1) ^ 1) - 1) for i in range(1, space - 1)]

    vmem = pl.BlockSpec(memory_space=pltpu.VMEM)
    hbm = pl.BlockSpec(memory_space=pltpu.HBM)
    f32, bf16, i32 = jnp.float32, jnp.bfloat16, jnp.int32
    small = pltpu.CompilerParams(vmem_limit_bytes=4 * 1024 * 1024)
    pairs = pair_target.shape[1]
    slab = jax.ShapeDtypeStruct((SLAB_ROWS, GROUP), f32)
    to_pair, to_cross = pl.pallas_call(
        split_kernel,
        out_shape=(slab, slab),
        in_specs=[hbm] * 2,
        out_specs=(vmem,) * 2,
        scratch_shapes=[pltpu.VMEM((3, 1, atoms_here), f32), pltpu.SemaphoreType.DMA((3,))],
        compiler_params=small,
        name="split",
    )(node_features, jnp.transpose(positions, (1, 0, 2)))
    from_cross = lax.ppermute(to_cross, "space", cross)
    from_pair = lax.ppermute(to_pair, "space", pair)

    local_arrays = pl.pallas_call(
        local_kernel,
        out_shape=(
            jax.ShapeDtypeStruct((len(LOCAL), NB * GROUP, NY * GROUP), bf16),
            jax.ShapeDtypeStruct((2, CH, NY * GROUP), f32),
            jax.ShapeDtypeStruct((8, GROUP), f32),
            jax.ShapeDtypeStruct((1, atoms_here), f32),
            jax.ShapeDtypeStruct((1, CH), f32),
            jax.ShapeDtypeStruct((1, atoms_here), f32),
            jax.ShapeDtypeStruct((NB, CH), f32),
            jax.ShapeDtypeStruct((MIX_ROWS, CH), bf16),
            jax.ShapeDtypeStruct((1, CH), f32),
        ),
        in_specs=[hbm] * 9 + [vmem] * 2,
        out_specs=(vmem,) * 9,
        scratch_shapes=[
            pltpu.VMEM((1, 1), i32),
            pltpu.VMEM((1, pairs), i32),
            pltpu.VMEM((1, pairs), i32),
            pltpu.VMEM((1, atoms_here), i32),
            pltpu.VMEM((1, NSPEC), f32),
            pltpu.VMEM((2, CH, NB * GROUP), bf16),
            pltpu.VMEM((2, 3, GROUP, GROUP), f32),
            pltpu.SemaphoreType.DMA((9,)),
        ],
        compiler_params=pltpu.CompilerParams(vmem_limit_bytes=16 * 1024 * 1024),
        cost_estimate=pl.CostEstimate(
            flops=2 * len(LOCAL) * CH * NB * NY * GROUP * GROUP,
            bytes_accessed=14_000_000,
            transcendentals=0,
        ),
        name="local_pairs",
    )(
        pair_count,
        pair_target,
        pair_source,
        species,
        species_shift.reshape(1, NSPEC),
        energy_cotangent,
        radial_weight,
        mix_weight,
        readout_weight.reshape(1, CH),
        to_pair,
        to_cross,
    )

    energy, own_grad, kept, sent, halo_grad = pl.pallas_call(
        functools.partial(step_kernel, scale),
        out_shape=(
            jax.ShapeDtypeStruct((1, atoms_here), f32),
            jax.ShapeDtypeStruct((1, CH, atoms_here), f32),
            jax.ShapeDtypeStruct((HALF_ROWS, CH), f32),
            jax.ShapeDtypeStruct((HALF_ROWS + CH, CH), f32),
            jax.ShapeDtypeStruct((CH, GROUP), f32),
        ),
        in_specs=[vmem] * 13,
        out_specs=(vmem,) * 5,
        scratch_shapes=[
            pltpu.VMEM((2, NB * GROUP, NY * GROUP), bf16),
            pltpu.VMEM((2, CH, NB * GROUP), bf16),
            pltpu.VMEM((2, 3, GROUP, GROUP), f32),
        ],
        compiler_params=pltpu.CompilerParams(vmem_limit_bytes=24 * 1024 * 1024),
        name="layer_step",
    )(to_pair, to_cross, from_pair, from_cross, *local_arrays)

    received = lax.ppermute(sent, "space", pair)
    half = kept + received[:HALF_ROWS]
    for turn, route in enumerate(exchange_routes(space, dp)):
        if turn == 0:
            half, halo_grad = lax.optimization_barrier((half, halo_grad))
            halo_grad = lax.ppermute(halo_grad, "space", cross)
        if turn == 1:
            half, halo_grad = lax.optimization_barrier((half, halo_grad))
        half = half + lax.ppermute(half, ("space", "dp"), route)
    other = lax.ppermute(half, "space", pair)
    feature_grad = pl.pallas_call(
        fold_kernel,
        out_shape=jax.ShapeDtypeStruct((1, CH, atoms_here), f32),
        in_specs=[vmem] * 3,
        out_specs=vmem,
        compiler_params=small,
        name="fold",
    )(own_grad, received, halo_grad)
    radial_grad, mix_grad, readout_grad, shift_grad = pl.pallas_call(
        finish_kernel,
        out_shape=(
            jax.ShapeDtypeStruct((NB, CH), f32),
            jax.ShapeDtypeStruct((MIX_ROWS, CH), f32),
            jax.ShapeDtypeStruct((1, CH), f32),
            jax.ShapeDtypeStruct((1, NSPEC), f32),
        ),
        in_specs=[vmem] * 2,
        out_specs=(vmem,) * 4,
        compiler_params=small,
        name="finish",
    )(half, other)
    return (
        energy,
        feature_grad,
        radial_grad,
        mix_grad,
        readout_grad.reshape(CH),
        shift_grad.reshape(NSPEC),
    )


def solution(mesh):
    return jax.shard_map(
        body,
        mesh=mesh,
        in_specs=(
            P("dp", None, "space"),
            P("dp", None, "space"),
            P("dp", "space"),
            P("dp", "space"),
            P("dp", "space"),
            P("dp", "space"),
            P("dp", "space"),
            P(),
            P(),
            P(),
            P(),
        ),
        out_specs=(P("dp", "space"), P("dp", None, "space"), P(), P(), P(), P()),
        check_vma=False,
    )
```

```python
import functools
import math

import jax
import jax.numpy as jnp
from jax import lax
from jax.experimental import pallas as pl
from jax.experimental.pallas import tpu as pltpu
from jax.sharding import PartitionSpec as P

CH = 128
NB = 8
NY = 9
NSPEC = 8
CELL_ATOMS = 64
HALO_CELLS = 2
GROUP = 2 * CELL_ATOMS
ROWS = 16

cutoff = 5.0
message_scale = 0.25

COS_COEFFS = (
    0.9999999998846169,
    -4.934802185771876,
    4.058711815779763,
    -1.3352602773967561,
    0.23532080049888648,
    -0.025785772074137014,
    0.0019043022864480008,
    -8.868331860867329e-05,
)
SINC_COEFFS = (
    0.9999999992502204,
    -1.6449339933418936,
    0.8117412468909989,
    -0.1907447263221115,
    0.02612742969685046,
    -0.0023157632409761065,
    0.00012580778956459784,
)

MIX_ROWS = 3 * CH
HALF = MIX_ROWS // 2
QUARTER = MIX_ROWS // 4
REST = 16
CELLS = 4 + 2 * HALO_CELLS
LOCAL = ((0, 1), (0, 2), (1, 0), (1, 1))
SMALL = 8
SLAB_ROWS = CH + 8


def polynomial(coeffs, x):
    total = coeffs[-1] * x + coeffs[-2]
    for c in coeffs[-3::-1]:
        total = total * x + c
    return total


def factor_rows(factor_ref, row, source, target, keep):
    dx = (target[0] - source[0]) * (1.0 / cutoff)
    dy = (target[1] - source[1]) * (1.0 / cutoff)
    dz = (target[2] - source[2]) * (1.0 / cutoff)
    xx, yy, zz = dx * dx, dy * dy, dz * dz
    square = xx + yy + zz
    inside = jnp.minimum(square, 1.0)
    gap = 1.0 - inside
    base = (gap * gap) * keep * polynomial(SINC_COEFFS, inside)
    twice_cos = polynomial([2.0 * c for c in COS_COEFFS], inside)
    raw = [base, twice_cos * base]
    for _ in range(NB - 2):
        raw.append(twice_cos * raw[-1] - raw[-2])
    radial = [value if b == 0 else value * (1.0 / (b + 1)) for b, value in enumerate(raw)]
    root_three = math.sqrt(3.0)
    root_fifteen = math.sqrt(15.0)
    root_five = math.sqrt(5.0)
    wide_x = root_fifteen * dx
    harmonic = [
        None,
        root_three * dx,
        root_three * dy,
        root_three * dz,
        wide_x * dy,
        (root_fifteen * dy) * dz,
        (0.5 * root_five) * (3.0 * zz - square),
        wide_x * dz,
        (0.5 * root_fifteen) * (xx - yy),
    ]
    for b in range(NB):
        rows = slice(b * GROUP + row, b * GROUP + row + ROWS)
        for y in range(NY):
            value = radial[b] if y == 0 else radial[b] * harmonic[y]
            factor_ref[rows, y * GROUP : (y + 1) * GROUP] = value.astype(jnp.bfloat16)


def column_to_row(column, size):
    wide = jnp.broadcast_to(column, (size, GROUP))
    at = lax.broadcasted_iota(jnp.int32, (size, GROUP), 0)
    lane = lax.broadcasted_iota(jnp.int32, (size, GROUP), 1)
    return jnp.sum(jnp.where(at == lane, wide, 0.0), axis=0, keepdims=True)


def split_kernel(*refs):
    features_ref, place_in_ref, *inputs = refs[:SMALL + 2]
    pair_ref, cross_ref, *outputs = refs[SMALL + 2 : 2 * SMALL + 4]
    place_ref, sems = refs[2 * SMALL + 4 :]
    core = lax.axis_index("space") % 2
    place_copy = pltpu.make_async_copy(place_in_ref, place_ref, sems.at[2])
    place_copy.start()
    copies = []
    for k, (ref, side) in enumerate(((pair_ref, 1 - core), (cross_ref, core))):
        at = pl.ds(pl.multiple_of(side * GROUP, GROUP), GROUP)
        copies.append(
            pltpu.make_async_copy(features_ref.at[0, :, at], ref.at[pl.ds(0, CH)], sems.at[k])
        )
    for k, (src, dst) in enumerate(zip(inputs, outputs)):
        copies.append(pltpu.make_async_copy(src, dst, sems.at[3 + k]))
    for copy in copies:
        copy.start()
    place_copy.wait()
    low, high = slice(GROUP), slice(GROUP, 2 * GROUP)
    filler = jnp.zeros((5, GROUP), jnp.float32)
    for ref, one, two in ((pair_ref, high, low), (cross_ref, low, high)):
        rows = [
            jnp.where(core == 0, place_ref[axis, :, one], place_ref[axis, :, two]) for axis in range(3)
        ]
        ref[CH:, :] = jnp.concatenate(rows + [filler], axis=0)
    for copy in copies:
        copy.wait()


def live_flags(count, pair_target, pair_source):
    size = (4 * CELLS, pair_target.shape[1])
    at = lax.broadcasted_iota(jnp.int32, size, 0)
    slot = lax.broadcasted_iota(jnp.int32, size, 1)
    hit = (pair_target * CELLS + pair_source == at) & (slot < count)
    return jnp.max(jnp.where(hit, message_scale, 0.0), axis=1, keepdims=True)


def keep_rows(flags, t, d):
    lane = lax.broadcasted_iota(jnp.int32, (1, GROUP), 1)
    rows = []
    for scell in (2 * (t + d), 2 * (t + d) + 1):
        one, two = [(2 * t + k) * CELLS + scell for k in range(2)]
        rows.append(jnp.where(lane < CELL_ATOMS, flags[one : one + 1], flags[two : two + 1]))
    return rows


def set_source(scaled_ref, place_ref, slab, weight_t):
    features = slab[:CH]
    for b in range(NB):
        scaled_ref[:, b * GROUP : (b + 1) * GROUP] = (features * weight_t[:, b : b + 1]).astype(
            jnp.bfloat16
        )
    place = slab[CH:].T
    for axis in range(3):
        place_ref[axis] = jnp.broadcast_to(place[:, axis : axis + 1], (GROUP, GROUP))


def fill_block(factor_ref, place_ref, keeps, target, d):
    row_at = lax.broadcasted_iota(jnp.int32, (ROWS, GROUP), 0)
    lane_at = lax.broadcasted_iota(jnp.int32, (ROWS, GROUP), 1)
    for half in range(2):
        for row in range(half * CELL_ATOMS, (half + 1) * CELL_ATOMS, ROWS):
            source = [place_ref[axis, row : row + ROWS, :] for axis in range(3)]
            keep = jnp.broadcast_to(keeps[half], (ROWS, GROUP))
            if d == 1:
                keep = jnp.where(row_at + row == lane_at, 0.0, keep)
            factor_rows(factor_ref, row, source, target, keep)


def local_kernel(
    count_ref,
    pair_target_ref,
    pair_source_ref,
    radial_ref,
    pair_ref,
    cross_ref,
    factor_ref,
    messages_ref,
    keep_ref,
    scaled_ref,
    place_ref,
):
    even = lax.axis_index("space") % 2 == 0
    slabs = (
        jnp.where(even, cross_ref[...], pair_ref[...]),
        jnp.where(even, pair_ref[...], cross_ref[...]),
    )
    targets = [[slab[CH + axis : CH + axis + 1] for axis in range(3)] for slab in slabs]
    flags = live_flags(count_ref[0, 0], pair_target_ref[...], pair_source_ref[...])
    weight_t = radial_ref[...].T
    for g in range(2):
        set_source(scaled_ref.at[g], place_ref.at[g], slabs[g], weight_t)

    def fill(block):
        t, d = LOCAL[block]
        fill_block(factor_ref.at[block], place_ref.at[t + d - 1], keep_rows(flags, t, d), targets[t], d)

    totals = [None, None]
    fill(0)
    for block, (t, d) in enumerate(LOCAL):
        product = jnp.dot(
            scaled_ref[t + d - 1], factor_ref[block], preferred_element_type=jnp.float32
        )
        totals[t] = product if totals[t] is None else totals[t] + product
        if block + 1 < len(LOCAL):
            fill(block + 1)
    for t in range(2):
        messages_ref[t] = totals[t]
    keep_ref[...] = jnp.concatenate(
        keep_rows(flags, 0, 0) + keep_rows(flags, 1, 2) + [jnp.zeros((4, GROUP), jnp.float32)], axis=0
    )


def node_kernel(
    scale,
    pair_ref,
    cross_ref,
    from_pair_ref,
    from_cross_ref,
    messages_ref,
    keep_ref,
    species_ref,
    shift_ref,
    energy_grad_ref,
    radial_ref,
    mix_ref,
    readout_ref,
    energy_ref,
    spread_ref,
    kept_ref,
    sent_ref,
    rest_ref,
    grad_messages_ref,
    halo_ref,
    scaled_ref,
    place_ref,
):
    even = lax.axis_index("space") % 2 == 0
    weight_t = radial_ref[...].T
    slabs = (
        jnp.where(even, from_cross_ref[...], from_pair_ref[...]),
        jnp.where(even, cross_ref[...], pair_ref[...]),
        jnp.where(even, pair_ref[...], cross_ref[...]),
        jnp.where(even, from_pair_ref[...], from_cross_ref[...]),
    )
    targets = [[slab[CH + axis : CH + axis + 1] for axis in range(3)] for slab in slabs[1:3]]

    def fill(t):
        d = 2 * t
        set_source(scaled_ref.at[t], place_ref.at[t], slabs[t + d], weight_t)
        keeps = [keep_ref[2 * t + half : 2 * t + half + 1, :] for half in range(2)]
        fill_block(halo_ref.at[t], place_ref.at[t], keeps, targets[t], d)

    def add_halo(t):
        return messages_ref[t] + jnp.dot(
            scaled_ref[t], halo_ref[t], preferred_element_type=jnp.float32
        )

    readout = jnp.broadcast_to(readout_ref[...], (8, CH)).T[:, :1]
    mix = mix_ref[...]
    mix_t = mix.astype(jnp.float32).T.astype(jnp.bfloat16)

    def node_stage(t, messages):
        at = slice(t * GROUP, (t + 1) * GROUP)
        part = [messages[:, y * GROUP : (y + 1) * GROUP] for y in range(NY)]
        invariants = jnp.concatenate(
            [
                part[0],
                0.5 * (part[1] * part[1] + part[2] * part[2] + part[3] * part[3]),
                0.5
                * (
                    part[4] * part[4]
                    + part[5] * part[5]
                    + part[6] * part[6]
                    + part[7] * part[7]
                    + part[8] * part[8]
                ),
            ],
            axis=0,
        ).astype(jnp.bfloat16)
        preact = jnp.dot(mix_t, invariants, preferred_element_type=jnp.float32)
        gating = jax.nn.sigmoid(preact)
        updated = slabs[t + 1][:CH] + preact * gating
        energy_grad = energy_grad_ref[:, at]
        kinds = species_ref[:, at]
        shifts = jnp.zeros((1, GROUP), jnp.float32)
        for n in range(NSPEC):
            shifts = jnp.where(kinds == n, shift_ref[:, n : n + 1], shifts)
        energy_ref[:, at] = jnp.sum(updated * readout, axis=0, keepdims=True) + shifts
        spread = readout * energy_grad
        spread_ref[:, at] = spread
        grad_pre = (spread * gating * (1.0 + preact * (1.0 - gating))).astype(jnp.bfloat16)
        grad_mix = lax.dot_general(
            invariants, grad_pre, (((1,), (1,)), ((), ())), preferred_element_type=jnp.float32
        )
        grad_inv = jnp.dot(mix, grad_pre, preferred_element_type=jnp.float32)
        grad_messages_ref[t] = jnp.concatenate(
            [grad_inv[:CH]]
            + [grad_inv[CH : 2 * CH] * part[y] for y in range(1, 4)]
            + [grad_inv[2 * CH :] * part[y] for y in range(4, NY)],
            axis=1,
        ).astype(jnp.bfloat16)
        return updated * energy_grad, grad_mix

    fill(0)
    first = add_halo(0)
    fill(1)
    out_low, mix_low = node_stage(0, first)
    out_high, mix_high = node_stage(1, add_halo(1))

    grad_mix = (mix_low + mix_high) * scale
    kept_ref[...] = jnp.where(even, grad_mix[:HALF], grad_mix[HALF:])
    sent_ref[...] = jnp.where(even, grad_mix[HALF:], grad_mix[:HALF])
    readout_row = column_to_row(jnp.sum(out_low + out_high, axis=1, keepdims=True), CH)
    here = lax.broadcasted_iota(jnp.int32, (NSPEC, 2 * GROUP), 0) == species_ref[...]
    by_kind = jnp.sum(jnp.where(here, energy_grad_ref[...], 0.0), axis=1, keepdims=True)
    rest_ref[...] = jnp.concatenate(
        [readout_row, column_to_row(by_kind, NSPEC), jnp.zeros((6, CH), jnp.float32)], axis=0
    )


def back(factor, grad_messages):
    return lax.dot_general(
        factor, grad_messages, (((1,), (1,)), ((), ())), preferred_element_type=jnp.float32
    )


def source_grads(total, features, weight):
    features_t = features.T
    grad_t = None
    radial = []
    for b in range(NB):
        piece = total[b * GROUP : (b + 1) * GROUP]
        term = piece * weight[b : b + 1, :]
        grad_t = term if grad_t is None else grad_t + term
        radial.append(jnp.sum(piece * features_t, axis=0, keepdims=True))
    return grad_t.T, jnp.concatenate(radial, axis=0)


def halo_back_kernel(
    halo_ref, grad_messages_ref, from_pair_ref, from_cross_ref, radial_ref, to_pair_ref, to_cross_ref, share_ref
):
    even = lax.axis_index("space") % 2 == 0
    weight = radial_ref[...]
    before = jnp.where(even, from_cross_ref[:CH, :], from_pair_ref[:CH, :])
    after = jnp.where(even, from_pair_ref[:CH, :], from_cross_ref[:CH, :])
    grad_before, share_before = source_grads(back(halo_ref[0], grad_messages_ref[0]), before, weight)
    grad_after, share_after = source_grads(back(halo_ref[1], grad_messages_ref[1]), after, weight)
    to_pair_ref[...] = jnp.where(even, grad_after, grad_before)
    to_cross_ref[...] = jnp.where(even, grad_before, grad_after)
    share_ref[...] = share_before + share_after


def own_back_kernel(
    scale,
    local_ref,
    grad_messages_ref,
    pair_ref,
    cross_ref,
    radial_ref,
    share_ref,
    rest_ref,
    spread_ref,
    own_grad_ref,
    joined_ref,
):
    even = lax.axis_index("space") % 2 == 0
    weight = radial_ref[...]
    low = jnp.where(even, cross_ref[:CH, :], pair_ref[:CH, :])
    high = jnp.where(even, pair_ref[:CH, :], cross_ref[:CH, :])
    share = share_ref[...]
    for g, features in enumerate((low, high)):
        total = back(local_ref[g], grad_messages_ref[0]) + back(local_ref[2 + g], grad_messages_ref[1])
        grad, part = source_grads(total, features, weight)
        at = slice(g * GROUP, (g + 1) * GROUP)
        own_grad_ref[:, at] = spread_ref[:, at] + grad
        share = share + part
    joined_ref[:NB, :] = share * scale
    joined_ref[NB:, :] = rest_ref[...] * scale


def quarter_kernel(kept_ref, received_ref, keep_ref, send_ref):
    first = lax.axis_index("dp") % 2 == 0
    low = kept_ref[:QUARTER, :] + received_ref[:QUARTER, :]
    high = kept_ref[QUARTER:, :] + received_ref[QUARTER:, :]
    keep_ref[...] = jnp.where(first, low, high)
    send_ref[...] = jnp.where(first, high, low)


def join_kernel(kept_ref, received_ref, rest_ref, out_ref):
    out_ref[:QUARTER, :] = kept_ref[...] + received_ref[...]
    out_ref[QUARTER:, :] = rest_ref[...]


def gather_kernel(mine_ref, other_ref, out_ref):
    first = lax.axis_index("dp") % 2 == 0
    mine, other = mine_ref[:QUARTER, :], other_ref[:QUARTER, :]
    out_ref[:QUARTER, :] = jnp.where(first, mine, other)
    out_ref[QUARTER:HALF, :] = jnp.where(first, other, mine)
    out_ref[HALF:, :] = mine_ref[QUARTER:, :] + other_ref[QUARTER:, :]


def fold_kernel(own_ref, from_pair_ref, from_cross_ref, energy_in_ref, grad_ref, energy_ref):
    even = lax.axis_index("space") % 2 == 0
    pair = from_pair_ref[...]
    cross = from_cross_ref[...]
    grad_ref[0, :, :GROUP] = own_ref[:, :GROUP] + jnp.where(even, cross, pair)
    grad_ref[0, :, GROUP:] = own_ref[:, GROUP:] + jnp.where(even, pair, cross)
    energy_ref[...] = energy_in_ref[...]


def finish_kernel(mine_ref, other_ref, radial_ref, mix_ref, readout_ref, shift_ref):
    even = lax.axis_index("space") % 2 == 0
    mine, other = mine_ref[:HALF, :], other_ref[:HALF, :]
    mix_ref[:HALF, :] = jnp.where(even, mine, other)
    mix_ref[HALF:, :] = jnp.where(even, other, mine)
    rest = mine_ref[HALF:, :] + other_ref[HALF:, :]
    radial_ref[...] = rest[:NB]
    readout_ref[...] = rest[NB : NB + 1]
    shift_ref[...] = rest[NB + 1 : NB + 2, :NSPEC]


def exchange_routes(space, dp):
    steps = [(1 << k, 0) for k in range(1, space.bit_length() - 1)]
    steps += [(0, 1 << k) for k in range(1, dp.bit_length() - 1)]
    routes = []
    for turn in range(len(steps)):
        route = []
        for s in range(space):
            across, along = steps[(turn + s % 2) % len(steps)]
            for d in range(dp):
                route.append((s * dp + d, (s ^ across) * dp + (d ^ along)))
        routes.append(route)
    return routes


def call(kernel, name, inputs, outputs, mib=4, scratch=(), flops=0):
    vmem = pl.BlockSpec(memory_space=pltpu.VMEM)
    shapes = tuple(jax.ShapeDtypeStruct(shape, kind) for shape, kind in outputs)
    moved = sum(math.prod(v.shape) * v.dtype.itemsize for v in (*inputs, *shapes))
    return pl.pallas_call(
        kernel,
        out_shape=shapes,
        in_specs=[vmem] * len(inputs),
        out_specs=(vmem,) * len(shapes),
        scratch_shapes=scratch,
        compiler_params=pltpu.CompilerParams(vmem_limit_bytes=mib * 1024 * 1024),
        cost_estimate=pl.CostEstimate(flops=flops, bytes_accessed=moved, transcendentals=0),
        name=name,
    )(*inputs)


def in_hbm(value):
    return pltpu.with_memory_space_constraint(value, pltpu.HBM)


def body(
    node_features,
    positions,
    species,
    energy_cotangent,
    pair_target,
    pair_source,
    pair_count,
    radial_weight,
    mix_weight,
    readout_weight,
    species_shift,
):
    atoms_here = node_features.shape[2]
    space, dp = lax.axis_size("space"), lax.axis_size("dp")
    scale = 1.0 / math.sqrt(atoms_here * space * dp)
    pair = [(i, i ^ 1) for i in range(space)]
    cross = [(i, ((i + 1) ^ 1) - 1) for i in range(1, space - 1)]

    across = [(i, i ^ 1) for i in range(dp)]
    hbm = pl.BlockSpec(memory_space=pltpu.HBM)
    smem = pl.BlockSpec(memory_space=pltpu.SMEM)
    vmem = pl.BlockSpec(memory_space=pltpu.VMEM)
    f32, bf16 = jnp.float32, jnp.bfloat16
    slab = jax.ShapeDtypeStruct((SLAB_ROWS, GROUP), f32)
    small = (
        pair_target,
        pair_source,
        species,
        species_shift.reshape(1, NSPEC),
        energy_cotangent,
        radial_weight,
        mix_weight,
        readout_weight.reshape(1, CH),
    )
    to_pair, to_cross, *small = pl.pallas_call(
        split_kernel,
        out_shape=(slab, slab) + tuple(jax.ShapeDtypeStruct(v.shape, v.dtype) for v in small),
        in_specs=[hbm] * (SMALL + 2),
        out_specs=(vmem,) * (SMALL + 2),
        scratch_shapes=[
            pltpu.VMEM((3, 1, atoms_here), f32),
            pltpu.SemaphoreType.DMA((SMALL + 3,)),
        ],
        compiler_params=pltpu.CompilerParams(vmem_limit_bytes=4 * 1024 * 1024),
        name="split",
    )(
        in_hbm(node_features),
        in_hbm(jnp.transpose(positions, (1, 0, 2))),
        *[in_hbm(v) for v in small],
    )
    targets, sources, species, shift, energy_grad, radial, mix, readout = small
    from_cross = lax.ppermute(to_cross, "space", cross)
    from_pair = lax.ppermute(to_pair, "space", pair)

    block_flops = 2 * CH * NB * NY * GROUP * GROUP
    local_factor, messages, keep = pl.pallas_call(
        local_kernel,
        out_shape=(
            jax.ShapeDtypeStruct((len(LOCAL), NB * GROUP, NY * GROUP), bf16),
            jax.ShapeDtypeStruct((2, CH, NY * GROUP), f32),
            jax.ShapeDtypeStruct((8, GROUP), f32),
        ),
        in_specs=[smem] + [vmem] * 5,
        out_specs=(vmem,) * 3,
        scratch_shapes=[
            pltpu.VMEM((2, CH, NB * GROUP), bf16),
            pltpu.VMEM((2, 3, GROUP, GROUP), f32),
        ],
        compiler_params=pltpu.CompilerParams(vmem_limit_bytes=16 * 1024 * 1024),
        cost_estimate=pl.CostEstimate(
            flops=len(LOCAL) * block_flops, bytes_accessed=14_000_000, transcendentals=0
        ),
        name="local_pairs",
    )(pair_count, targets, sources, radial, to_pair, to_cross)

    energy, spread, kept, sent, rest, grad_messages, halo_factor = call(
        functools.partial(node_kernel, scale),
        "node_stage",
        (
            to_pair,
            to_cross,
            from_pair,
            from_cross,
            messages,
            keep,
            species,
            shift,
            energy_grad,
            radial,
            mix,
            readout,
        ),
        (
            ((1, atoms_here), f32),
            ((CH, atoms_here), f32),
            ((HALF, CH), f32),
            ((HALF, CH), f32),
            ((8, CH), f32),
            ((2, CH, NY * GROUP), bf16),
            ((2, NB * GROUP, NY * GROUP), bf16),
        ),
        16,
        [pltpu.VMEM((2, CH, NB * GROUP), bf16), pltpu.VMEM((2, 3, GROUP, GROUP), f32)],
        2 * block_flops,
    )

    received = lax.ppermute(sent, "space", pair)
    pair_grad, cross_grad, share = call(
        halo_back_kernel,
        "halo_back",
        (halo_factor, grad_messages, from_pair, from_cross, radial),
        (((CH, GROUP), f32), ((CH, GROUP), f32), ((NB, CH), f32)),
        12,
        (),
        2 * block_flops,
    )
    received, share = lax.optimization_barrier((received, share))
    quarter, sent = call(
        quarter_kernel,
        "quarter",
        (kept, received),
        (((QUARTER, CH), f32), ((QUARTER, CH), f32)),
    )
    sent, grad_messages = lax.optimization_barrier((sent, grad_messages))
    received = lax.ppermute(sent, "dp", across)
    own_grad, joined = call(
        functools.partial(own_back_kernel, scale),
        "own_back",
        (local_factor, grad_messages, to_pair, to_cross, radial, share, rest, spread),
        (((CH, atoms_here), f32), ((REST, CH), f32)),
        12,
        (),
        4 * block_flops,
    )
    (value,) = call(
        join_kernel, "join", (quarter, received, joined), (((QUARTER + REST, CH), f32),)
    )
    for turn, route in enumerate(exchange_routes(space, dp)):
        if turn == 0:
            value, cross_grad = lax.optimization_barrier((value, cross_grad))
            cross_grad = lax.ppermute(cross_grad, "space", cross)
        if turn == 1:
            value, cross_grad, pair_grad = lax.optimization_barrier((value, cross_grad, pair_grad))
            pair_grad = lax.ppermute(pair_grad, "space", pair)
        if turn == 2:
            value, pair_grad = lax.optimization_barrier((value, pair_grad))
        value = value + lax.ppermute(value, ("space", "dp"), route)
    (value,) = call(
        gather_kernel,
        "gather",
        (value, lax.ppermute(value, "dp", across)),
        (((HALF + REST, CH), f32),),
    )
    feature_grad, energy = call(
        fold_kernel,
        "fold",
        (own_grad, pair_grad, cross_grad, energy),
        (((1, CH, atoms_here), f32), ((1, atoms_here), f32)),
    )
    radial_grad, mix_grad, readout_grad, shift_grad = call(
        finish_kernel,
        "finish",
        (value, lax.ppermute(value, "space", pair)),
        (((NB, CH), f32), ((MIX_ROWS, CH), f32), ((1, CH), f32), ((1, NSPEC), f32)),
    )
    return (
        energy,
        feature_grad,
        radial_grad,
        mix_grad,
        readout_grad.reshape(CH),
        shift_grad.reshape(NSPEC),
    )


def solution(mesh):
    return jax.shard_map(
        body,
        mesh=mesh,
        in_specs=(
            P("dp", None, "space"),
            P("dp", None, "space"),
            P("dp", "space"),
            P("dp", "space"),
            P("dp", "space"),
            P("dp", "space"),
            P("dp", "space"),
            P(),
            P(),
            P(),
            P(),
        ),
        out_specs=(P("dp", "space"), P("dp", None, "space"), P(), P(), P(), P()),
        check_vma=False,
    )
```

```python
import functools
import math

import jax
import jax.numpy as jnp
from jax import lax
from jax.experimental import pallas as pl
from jax.experimental.pallas import tpu as pltpu
from jax.sharding import PartitionSpec as P

CH = 128
NB = 8
NY = 9
NSPEC = 8
CELL_ATOMS = 64
HALO_CELLS = 2
GROUP = 2 * CELL_ATOMS
ROWS = 16

cutoff = 5.0
message_scale = 0.25

COS_COEFFS = (
    0.9999999998846169,
    -4.934802185771876,
    4.058711815779763,
    -1.3352602773967561,
    0.23532080049888648,
    -0.025785772074137014,
    0.0019043022864480008,
    -8.868331860867329e-05,
)
SINC_COEFFS = (
    0.9999999992502204,
    -1.6449339933418936,
    0.8117412468909989,
    -0.1907447263221115,
    0.02612742969685046,
    -0.0023157632409761065,
    0.00012580778956459784,
)

MIX_ROWS = 3 * CH
HALF = MIX_ROWS // 2
QUARTER = MIX_ROWS // 4
REST = 16
CELLS = 4 + 2 * HALO_CELLS
LOCAL = ((0, 1), (0, 2), (1, 0), (1, 1))
SMALL = 8
SLAB_ROWS = CH + 8


def polynomial(coeffs, x):
    total = coeffs[-1] * x + coeffs[-2]
    for c in coeffs[-3::-1]:
        total = total * x + c
    return total


def factor_rows(factor_ref, row, source, target, keep):
    dx = (target[0] - source[0]) * (1.0 / cutoff)
    dy = (target[1] - source[1]) * (1.0 / cutoff)
    dz = (target[2] - source[2]) * (1.0 / cutoff)
    xx, yy, zz = dx * dx, dy * dy, dz * dz
    square = xx + yy + zz
    inside = jnp.minimum(square, 1.0)
    gap = 1.0 - inside
    base = (gap * gap) * keep * polynomial(SINC_COEFFS, inside)
    twice_cos = polynomial([2.0 * c for c in COS_COEFFS], inside)
    raw = [base, twice_cos * base]
    for _ in range(NB - 2):
        raw.append(twice_cos * raw[-1] - raw[-2])
    radial = [value if b == 0 else value * (1.0 / (b + 1)) for b, value in enumerate(raw)]
    root_three = math.sqrt(3.0)
    root_fifteen = math.sqrt(15.0)
    root_five = math.sqrt(5.0)
    wide_x = root_fifteen * dx
    harmonic = [
        None,
        root_three * dx,
        root_three * dy,
        root_three * dz,
        wide_x * dy,
        (root_fifteen * dy) * dz,
        (0.5 * root_five) * (3.0 * zz - square),
        wide_x * dz,
        (0.5 * root_fifteen) * (xx - yy),
    ]
    for b in range(NB):
        rows = slice(b * GROUP + row, b * GROUP + row + ROWS)
        for y in range(NY):
            value = radial[b] if y == 0 else radial[b] * harmonic[y]
            factor_ref[rows, y * GROUP : (y + 1) * GROUP] = value.astype(jnp.bfloat16)


def column_to_row(column, size):
    wide = jnp.broadcast_to(column, (size, GROUP))
    at = lax.broadcasted_iota(jnp.int32, (size, GROUP), 0)
    lane = lax.broadcasted_iota(jnp.int32, (size, GROUP), 1)
    return jnp.sum(jnp.where(at == lane, wide, 0.0), axis=0, keepdims=True)


def split_kernel(*refs):
    features_ref, place_in_ref, *inputs = refs[:SMALL + 2]
    pair_ref, cross_ref, *outputs = refs[SMALL + 2 : 2 * SMALL + 4]
    place_ref, sems = refs[2 * SMALL + 4 :]
    core = lax.axis_index("space") % 2
    place_copy = pltpu.make_async_copy(place_in_ref, place_ref, sems.at[2])
    place_copy.start()
    copies = []
    for k, (ref, side) in enumerate(((pair_ref, 1 - core), (cross_ref, core))):
        at = pl.ds(pl.multiple_of(side * GROUP, GROUP), GROUP)
        copies.append(
            pltpu.make_async_copy(features_ref.at[0, :, at], ref.at[pl.ds(0, CH)], sems.at[k])
        )
    for k, (src, dst) in enumerate(zip(inputs, outputs)):
        copies.append(pltpu.make_async_copy(src, dst, sems.at[3 + k]))
    for copy in copies:
        copy.start()
    place_copy.wait()
    low, high = slice(GROUP), slice(GROUP, 2 * GROUP)
    filler = jnp.zeros((5, GROUP), jnp.float32)
    for ref, one, two in ((pair_ref, high, low), (cross_ref, low, high)):
        rows = [
            jnp.where(core == 0, place_ref[axis, :, one], place_ref[axis, :, two]) for axis in range(3)
        ]
        ref[CH:, :] = jnp.concatenate(rows + [filler], axis=0)
    for copy in copies:
        copy.wait()


def live_flags(count, pair_target, pair_source):
    size = (4 * CELLS, pair_target.shape[1])
    at = lax.broadcasted_iota(jnp.int32, size, 0)
    slot = lax.broadcasted_iota(jnp.int32, size, 1)
    hit = (pair_target * CELLS + pair_source == at) & (slot < count)
    return jnp.max(jnp.where(hit, message_scale, 0.0), axis=1, keepdims=True)


def keep_rows(flags, t, d):
    lane = lax.broadcasted_iota(jnp.int32, (1, GROUP), 1)
    rows = []
    for scell in (2 * (t + d), 2 * (t + d) + 1):
        one, two = [(2 * t + k) * CELLS + scell for k in range(2)]
        rows.append(jnp.where(lane < CELL_ATOMS, flags[one : one + 1], flags[two : two + 1]))
    return rows


def set_source(scaled_ref, place_ref, slab, weight_t):
    features = slab[:CH]
    for b in range(NB):
        scaled_ref[:, b * GROUP : (b + 1) * GROUP] = (features * weight_t[:, b : b + 1]).astype(
            jnp.bfloat16
        )
    place = slab[CH:].T
    for axis in range(3):
        place_ref[axis] = jnp.broadcast_to(place[:, axis : axis + 1], (GROUP, GROUP))


def fill_block(factor_ref, place_ref, keeps, target, d):
    row_at = lax.broadcasted_iota(jnp.int32, (ROWS, GROUP), 0)
    lane_at = lax.broadcasted_iota(jnp.int32, (ROWS, GROUP), 1)
    for half in range(2):
        for row in range(half * CELL_ATOMS, (half + 1) * CELL_ATOMS, ROWS):
            source = [place_ref[axis, row : row + ROWS, :] for axis in range(3)]
            keep = jnp.broadcast_to(keeps[half], (ROWS, GROUP))
            if d == 1:
                keep = jnp.where(row_at + row == lane_at, 0.0, keep)
            factor_rows(factor_ref, row, source, target, keep)


def local_kernel(
    count_ref,
    pair_target_ref,
    pair_source_ref,
    radial_ref,
    pair_ref,
    cross_ref,
    factor_ref,
    messages_ref,
    keep_ref,
    scaled_ref,
    place_ref,
):
    even = lax.axis_index("space") % 2 == 0
    slabs = (
        jnp.where(even, cross_ref[...], pair_ref[...]),
        jnp.where(even, pair_ref[...], cross_ref[...]),
    )
    targets = [[slab[CH + axis : CH + axis + 1] for axis in range(3)] for slab in slabs]
    flags = live_flags(count_ref[0, 0], pair_target_ref[...], pair_source_ref[...])
    weight_t = radial_ref[...].T
    for g in range(2):
        set_source(scaled_ref.at[g], place_ref.at[g], slabs[g], weight_t)

    def fill(block):
        t, d = LOCAL[block]
        fill_block(factor_ref.at[block], place_ref.at[t + d - 1], keep_rows(flags, t, d), targets[t], d)

    totals = [None, None]
    fill(0)
    for block, (t, d) in enumerate(LOCAL):
        product = jnp.dot(
            scaled_ref[t + d - 1], factor_ref[block], preferred_element_type=jnp.float32
        )
        totals[t] = product if totals[t] is None else totals[t] + product
        if block + 1 < len(LOCAL):
            fill(block + 1)
    for t in range(2):
        messages_ref[t] = totals[t]
    keep_ref[...] = jnp.concatenate(
        keep_rows(flags, 0, 0) + keep_rows(flags, 1, 2) + [jnp.zeros((4, GROUP), jnp.float32)], axis=0
    )


def node_kernel(
    scale,
    pair_ref,
    cross_ref,
    from_pair_ref,
    from_cross_ref,
    messages_ref,
    keep_ref,
    species_ref,
    shift_ref,
    energy_grad_ref,
    radial_ref,
    mix_ref,
    readout_ref,
    energy_ref,
    spread_ref,
    kept_ref,
    sent_ref,
    rest_ref,
    grad_messages_ref,
    halo_ref,
    scaled_ref,
    place_ref,
):
    even = lax.axis_index("space") % 2 == 0
    weight_t = radial_ref[...].T
    slabs = (
        jnp.where(even, from_cross_ref[...], from_pair_ref[...]),
        jnp.where(even, cross_ref[...], pair_ref[...]),
        jnp.where(even, pair_ref[...], cross_ref[...]),
        jnp.where(even, from_pair_ref[...], from_cross_ref[...]),
    )
    targets = [[slab[CH + axis : CH + axis + 1] for axis in range(3)] for slab in slabs[1:3]]

    def fill(t):
        d = 2 * t
        set_source(scaled_ref.at[t], place_ref.at[t], slabs[t + d], weight_t)
        keeps = [keep_ref[2 * t + half : 2 * t + half + 1, :] for half in range(2)]
        fill_block(halo_ref.at[t], place_ref.at[t], keeps, targets[t], d)

    def add_halo(t):
        return messages_ref[t] + jnp.dot(
            scaled_ref[t], halo_ref[t], preferred_element_type=jnp.float32
        )

    readout = jnp.broadcast_to(readout_ref[...], (8, CH)).T[:, :1]
    mix = mix_ref[...]
    mix_t = mix.astype(jnp.float32).T.astype(jnp.bfloat16)

    def node_stage(t, messages):
        at = slice(t * GROUP, (t + 1) * GROUP)
        part = [messages[:, y * GROUP : (y + 1) * GROUP] for y in range(NY)]
        invariants = jnp.concatenate(
            [
                part[0],
                0.5 * (part[1] * part[1] + part[2] * part[2] + part[3] * part[3]),
                0.5
                * (
                    part[4] * part[4]
                    + part[5] * part[5]
                    + part[6] * part[6]
                    + part[7] * part[7]
                    + part[8] * part[8]
                ),
            ],
            axis=0,
        ).astype(jnp.bfloat16)
        preact = jnp.dot(mix_t, invariants, preferred_element_type=jnp.float32)
        gating = jax.nn.sigmoid(preact)
        updated = slabs[t + 1][:CH] + preact * gating
        energy_grad = energy_grad_ref[:, at]
        kinds = species_ref[:, at]
        shifts = jnp.zeros((1, GROUP), jnp.float32)
        for n in range(NSPEC):
            shifts = jnp.where(kinds == n, shift_ref[:, n : n + 1], shifts)
        energy_ref[:, at] = jnp.sum(updated * readout, axis=0, keepdims=True) + shifts
        spread = readout * energy_grad
        spread_ref[:, at] = spread
        grad_pre = (spread * gating * (1.0 + preact * (1.0 - gating))).astype(jnp.bfloat16)
        grad_mix = lax.dot_general(
            invariants, grad_pre, (((1,), (1,)), ((), ())), preferred_element_type=jnp.float32
        )
        grad_inv = jnp.dot(mix, grad_pre, preferred_element_type=jnp.float32)
        grad_messages_ref[t] = jnp.concatenate(
            [grad_inv[:CH]]
            + [grad_inv[CH : 2 * CH] * part[y] for y in range(1, 4)]
            + [grad_inv[2 * CH :] * part[y] for y in range(4, NY)],
            axis=1,
        ).astype(jnp.bfloat16)
        return updated * energy_grad, grad_mix

    fill(0)
    first = add_halo(0)
    fill(1)
    out_low, mix_low = node_stage(0, first)
    out_high, mix_high = node_stage(1, add_halo(1))

    grad_mix = (mix_low + mix_high) * scale
    kept_ref[...] = jnp.where(even, grad_mix[:HALF], grad_mix[HALF:])
    sent_ref[...] = jnp.where(even, grad_mix[HALF:], grad_mix[:HALF])
    readout_row = column_to_row(jnp.sum(out_low + out_high, axis=1, keepdims=True), CH)
    here = lax.broadcasted_iota(jnp.int32, (NSPEC, 2 * GROUP), 0) == species_ref[...]
    by_kind = jnp.sum(jnp.where(here, energy_grad_ref[...], 0.0), axis=1, keepdims=True)
    rest_ref[...] = jnp.concatenate(
        [readout_row, column_to_row(by_kind, NSPEC), jnp.zeros((6, CH), jnp.float32)], axis=0
    )


def back(factor, grad_messages):
    return lax.dot_general(
        factor, grad_messages, (((1,), (1,)), ((), ())), preferred_element_type=jnp.float32
    )


def source_grads(total, features, weight):
    features_t = features.T
    grad_t = None
    radial = []
    for b in range(NB):
        piece = total[b * GROUP : (b + 1) * GROUP]
        term = piece * weight[b : b + 1, :]
        grad_t = term if grad_t is None else grad_t + term
        radial.append(jnp.sum(piece * features_t, axis=0, keepdims=True))
    return grad_t.T, jnp.concatenate(radial, axis=0)


def halo_back_kernel(
    halo_ref, grad_messages_ref, from_pair_ref, from_cross_ref, radial_ref, to_pair_ref, to_cross_ref, share_ref
):
    even = lax.axis_index("space") % 2 == 0
    weight = radial_ref[...]
    before = jnp.where(even, from_cross_ref[:CH, :], from_pair_ref[:CH, :])
    after = jnp.where(even, from_pair_ref[:CH, :], from_cross_ref[:CH, :])
    grad_before, share_before = source_grads(back(halo_ref[0], grad_messages_ref[0]), before, weight)
    grad_after, share_after = source_grads(back(halo_ref[1], grad_messages_ref[1]), after, weight)
    to_pair_ref[...] = jnp.where(even, grad_after, grad_before)
    to_cross_ref[...] = jnp.where(even, grad_before, grad_after)
    share_ref[...] = share_before + share_after


def own_back_kernel(
    scale,
    local_ref,
    grad_messages_ref,
    pair_ref,
    cross_ref,
    radial_ref,
    share_ref,
    rest_ref,
    spread_ref,
    own_grad_ref,
    joined_ref,
):
    even = lax.axis_index("space") % 2 == 0
    weight = radial_ref[...]
    low = jnp.where(even, cross_ref[:CH, :], pair_ref[:CH, :])
    high = jnp.where(even, pair_ref[:CH, :], cross_ref[:CH, :])
    share = share_ref[...]
    for g, features in enumerate((low, high)):
        total = back(local_ref[g], grad_messages_ref[0]) + back(local_ref[2 + g], grad_messages_ref[1])
        grad, part = source_grads(total, features, weight)
        at = slice(g * GROUP, (g + 1) * GROUP)
        own_grad_ref[:, at] = spread_ref[:, at] + grad
        share = share + part
    joined_ref[:NB, :] = share * scale
    joined_ref[NB:, :] = rest_ref[...] * scale


def quarter_kernel(kept_ref, received_ref, keep_ref, send_ref):
    first = lax.axis_index("dp") % 2 == 0
    low = kept_ref[:QUARTER, :] + received_ref[:QUARTER, :]
    high = kept_ref[QUARTER:, :] + received_ref[QUARTER:, :]
    keep_ref[...] = jnp.where(first, low, high)
    send_ref[...] = jnp.where(first, high, low)


def join_kernel(kept_ref, received_ref, rest_ref, out_ref):
    out_ref[:QUARTER, :] = kept_ref[...] + received_ref[...]
    out_ref[QUARTER:, :] = rest_ref[...]


def gather_kernel(mine_ref, other_ref, out_ref):
    first = lax.axis_index("dp") % 2 == 0
    mine, other = mine_ref[:QUARTER, :], other_ref[:QUARTER, :]
    out_ref[:QUARTER, :] = jnp.where(first, mine, other)
    out_ref[QUARTER:HALF, :] = jnp.where(first, other, mine)
    out_ref[HALF:, :] = mine_ref[QUARTER:, :] + other_ref[QUARTER:, :]


def fold_kernel(own_ref, pair_low_ref, pair_high_ref, from_cross_ref, energy_in_ref, grad_ref, energy_ref):
    even = lax.axis_index("space") % 2 == 0
    pair = jnp.concatenate([pair_low_ref[...], pair_high_ref[...]], axis=0)
    cross = from_cross_ref[...]
    grad_ref[0, :, :GROUP] = own_ref[:, :GROUP] + jnp.where(even, cross, pair)
    grad_ref[0, :, GROUP:] = own_ref[:, GROUP:] + jnp.where(even, pair, cross)
    energy_ref[...] = energy_in_ref[...]


def finish_kernel(mine_ref, other_ref, radial_ref, mix_ref, readout_ref, shift_ref):
    even = lax.axis_index("space") % 2 == 0
    mine, other = mine_ref[:HALF, :], other_ref[:HALF, :]
    mix_ref[:HALF, :] = jnp.where(even, mine, other)
    mix_ref[HALF:, :] = jnp.where(even, other, mine)
    rest = mine_ref[HALF:, :] + other_ref[HALF:, :]
    radial_ref[...] = rest[:NB]
    readout_ref[...] = rest[NB : NB + 1]
    shift_ref[...] = rest[NB + 1 : NB + 2, :NSPEC]


def exchange_routes(space, dp):
    steps = [(1 << k, 0) for k in range(1, space.bit_length() - 1)]
    steps += [(0, 1 << k) for k in range(1, dp.bit_length() - 1)]
    rounds = []
    for turn in range(0, len(steps), 2):
        kinds = ((0,), (1,), (0, 1)) if turn + 1 < len(steps) else ((0,),)
        routes = []
        for kind in kinds:
            route = []
            for s in range(space):
                across = along = 0
                for k in kind:
                    step = steps[(turn + k + 1 - s % 2) % len(steps)]
                    across, along = across ^ step[0], along ^ step[1]
                for d in range(dp):
                    route.append((s * dp + d, (s ^ across) * dp + (d ^ along)))
            routes.append(route)
        rounds.append(routes)
    return rounds


def call(kernel, name, inputs, outputs, mib=4, scratch=(), flops=0):
    vmem = pl.BlockSpec(memory_space=pltpu.VMEM)
    shapes = tuple(jax.ShapeDtypeStruct(shape, kind) for shape, kind in outputs)
    moved = sum(math.prod(v.shape) * v.dtype.itemsize for v in (*inputs, *shapes))
    return pl.pallas_call(
        kernel,
        out_shape=shapes,
        in_specs=[vmem] * len(inputs),
        out_specs=(vmem,) * len(shapes),
        scratch_shapes=scratch,
        compiler_params=pltpu.CompilerParams(vmem_limit_bytes=mib * 1024 * 1024),
        cost_estimate=pl.CostEstimate(flops=flops, bytes_accessed=moved, transcendentals=0),
        name=name,
    )(*inputs)


def in_hbm(value):
    return pltpu.with_memory_space_constraint(value, pltpu.HBM)


def body(
    node_features,
    positions,
    species,
    energy_cotangent,
    pair_target,
    pair_source,
    pair_count,
    radial_weight,
    mix_weight,
    readout_weight,
    species_shift,
):
    atoms_here = node_features.shape[2]
    space, dp = lax.axis_size("space"), lax.axis_size("dp")
    scale = 1.0 / math.sqrt(atoms_here * space * dp)
    pair = [(i, i ^ 1) for i in range(space)]
    cross = [(i, ((i + 1) ^ 1) - 1) for i in range(1, space - 1)]

    across = [(i, i ^ 1) for i in range(dp)]
    hbm = pl.BlockSpec(memory_space=pltpu.HBM)
    smem = pl.BlockSpec(memory_space=pltpu.SMEM)
    vmem = pl.BlockSpec(memory_space=pltpu.VMEM)
    f32, bf16 = jnp.float32, jnp.bfloat16
    slab = jax.ShapeDtypeStruct((SLAB_ROWS, GROUP), f32)
    small = (
        pair_target,
        pair_source,
        species,
        species_shift.reshape(1, NSPEC),
        energy_cotangent,
        radial_weight,
        mix_weight,
        readout_weight.reshape(1, CH),
    )
    to_pair, to_cross, *small = pl.pallas_call(
        split_kernel,
        out_shape=(slab, slab) + tuple(jax.ShapeDtypeStruct(v.shape, v.dtype) for v in small),
        in_specs=[hbm] * (SMALL + 2),
        out_specs=(vmem,) * (SMALL + 2),
        scratch_shapes=[
            pltpu.VMEM((3, 1, atoms_here), f32),
            pltpu.SemaphoreType.DMA((SMALL + 3,)),
        ],
        compiler_params=pltpu.CompilerParams(vmem_limit_bytes=4 * 1024 * 1024),
        name="split",
    )(
        in_hbm(node_features),
        in_hbm(jnp.transpose(positions, (1, 0, 2))),
        *[in_hbm(v) for v in small],
    )
    targets, sources, species, shift, energy_grad, radial, mix, readout = small
    from_cross = lax.ppermute(to_cross, "space", cross)
    from_pair = lax.ppermute(to_pair, "space", pair)

    block_flops = 2 * CH * NB * NY * GROUP * GROUP
    local_factor, messages, keep = pl.pallas_call(
        local_kernel,
        out_shape=(
            jax.ShapeDtypeStruct((len(LOCAL), NB * GROUP, NY * GROUP), bf16),
            jax.ShapeDtypeStruct((2, CH, NY * GROUP), f32),
            jax.ShapeDtypeStruct((8, GROUP), f32),
        ),
        in_specs=[smem] + [vmem] * 5,
        out_specs=(vmem,) * 3,
        scratch_shapes=[
            pltpu.VMEM((2, CH, NB * GROUP), bf16),
            pltpu.VMEM((2, 3, GROUP, GROUP), f32),
        ],
        compiler_params=pltpu.CompilerParams(vmem_limit_bytes=16 * 1024 * 1024),
        cost_estimate=pl.CostEstimate(
            flops=len(LOCAL) * block_flops, bytes_accessed=14_000_000, transcendentals=0
        ),
        name="local_pairs",
    )(pair_count, targets, sources, radial, to_pair, to_cross)

    energy, spread, kept, sent, rest, grad_messages, halo_factor = call(
        functools.partial(node_kernel, scale),
        "node_stage",
        (
            to_pair,
            to_cross,
            from_pair,
            from_cross,
            messages,
            keep,
            species,
            shift,
            energy_grad,
            radial,
            mix,
            readout,
        ),
        (
            ((1, atoms_here), f32),
            ((CH, atoms_here), f32),
            ((HALF, CH), f32),
            ((HALF, CH), f32),
            ((8, CH), f32),
            ((2, CH, NY * GROUP), bf16),
            ((2, NB * GROUP, NY * GROUP), bf16),
        ),
        16,
        [pltpu.VMEM((2, CH, NB * GROUP), bf16), pltpu.VMEM((2, 3, GROUP, GROUP), f32)],
        2 * block_flops,
    )

    received = lax.ppermute(sent, "space", pair)
    pair_grad, cross_grad, share = call(
        halo_back_kernel,
        "halo_back",
        (halo_factor, grad_messages, from_pair, from_cross, radial),
        (((CH, GROUP), f32), ((CH, GROUP), f32), ((NB, CH), f32)),
        12,
        (),
        2 * block_flops,
    )
    received, share = lax.optimization_barrier((received, share))
    quarter, sent = call(
        quarter_kernel,
        "quarter",
        (kept, received),
        (((QUARTER, CH), f32), ((QUARTER, CH), f32)),
    )
    sent, grad_messages = lax.optimization_barrier((sent, grad_messages))
    received = lax.ppermute(sent, "dp", across)
    own_grad, joined = call(
        functools.partial(own_back_kernel, scale),
        "own_back",
        (local_factor, grad_messages, to_pair, to_cross, radial, share, rest, spread),
        (((CH, atoms_here), f32), ((REST, CH), f32)),
        12,
        (),
        4 * block_flops,
    )
    (value,) = call(
        join_kernel, "join", (quarter, received, joined), (((QUARTER + REST, CH), f32),)
    )
    everyone = ("space", "dp")
    rounds = exchange_routes(space, dp)
    for turn, routes in enumerate(rounds):
        if turn == len(rounds) - 1:
            value = jnp.pad(value, ((0, CH + 8 - value.shape[0]), (0, 0)))
            value, cross_grad = lax.optimization_barrier((value, cross_grad))
            cross_grad = lax.ppermute(cross_grad, "space", cross)
        arrived = [lax.ppermute(value, everyone, route) for route in routes]
        value = value + arrived[0]
        if len(arrived) == 3:
            value = value + (arrived[1] + arrived[2])
    value = value[: QUARTER + REST]
    value, cross_grad, pair_grad = lax.optimization_barrier((value, cross_grad, pair_grad))
    halves = [lax.ppermute(pair_grad[k : k + CH // 2], "space", pair) for k in (0, CH // 2)]
    other = lax.ppermute(value, "dp", across)
    other, pair_low, pair_high = lax.optimization_barrier((other, *halves))
    (value,) = call(
        gather_kernel,
        "gather",
        (value, other),
        (((HALF + REST, CH), f32),),
    )
    feature_grad, energy = call(
        fold_kernel,
        "fold",
        (own_grad, pair_low, pair_high, cross_grad, energy),
        (((1, CH, atoms_here), f32), ((1, atoms_here), f32)),
    )
    radial_grad, mix_grad, readout_grad, shift_grad = call(
        finish_kernel,
        "finish",
        (value, lax.ppermute(value, "space", pair)),
        (((NB, CH), f32), ((MIX_ROWS, CH), f32), ((1, CH), f32), ((1, NSPEC), f32)),
    )
    return (
        energy,
        feature_grad,
        radial_grad,
        mix_grad,
        readout_grad.reshape(CH),
        shift_grad.reshape(NSPEC),
    )


def solution(mesh):
    return jax.shard_map(
        body,
        mesh=mesh,
        in_specs=(
            P("dp", None, "space"),
            P("dp", None, "space"),
            P("dp", "space"),
            P("dp", "space"),
            P("dp", "space"),
            P("dp", "space"),
            P("dp", "space"),
            P(),
            P(),
            P(),
            P(),
        ),
        out_specs=(P("dp", "space"), P("dp", None, "space"), P(), P(), P(), P()),
        check_vma=False,
    )
```

```python
import functools
import math

import jax
import jax.numpy as jnp
from jax import lax
from jax.experimental import pallas as pl
from jax.experimental.pallas import tpu as pltpu
from jax.sharding import PartitionSpec as P

CH = 128
NB = 8
NY = 9
NSPEC = 8
CELL_ATOMS = 64
HALO_CELLS = 2
GROUP = 2 * CELL_ATOMS
ROWS = 16

cutoff = 5.0
message_scale = 0.25

COS_COEFFS = (
    0.9999999998846169,
    -4.934802185771876,
    4.058711815779763,
    -1.3352602773967561,
    0.23532080049888648,
    -0.025785772074137014,
    0.0019043022864480008,
    -8.868331860867329e-05,
)
SINC_COEFFS = (
    0.9999999992502204,
    -1.6449339933418936,
    0.8117412468909989,
    -0.1907447263221115,
    0.02612742969685046,
    -0.0023157632409761065,
    0.00012580778956459784,
)

MIX_ROWS = 3 * CH
HALF = MIX_ROWS // 2
QUARTER = MIX_ROWS // 4
REST = 16
CELLS = 4 + 2 * HALO_CELLS
LOCAL = ((0, 1), (0, 2), (1, 0), (1, 1))
SMALL = 8
SLAB_ROWS = CH + 8


def polynomial(coeffs, x):
    total = coeffs[-1] * x + coeffs[-2]
    for c in coeffs[-3::-1]:
        total = total * x + c
    return total


def factor_rows(factor_ref, row, source, target, keep):
    dx = (target[0] - source[0]) * (1.0 / cutoff)
    dy = (target[1] - source[1]) * (1.0 / cutoff)
    dz = (target[2] - source[2]) * (1.0 / cutoff)
    xx, yy, zz = dx * dx, dy * dy, dz * dz
    square = xx + yy + zz
    inside = jnp.minimum(square, 1.0)
    gap = 1.0 - inside
    base = (gap * gap) * keep * polynomial(SINC_COEFFS, inside)
    twice_cos = polynomial([2.0 * c for c in COS_COEFFS], inside)
    raw = [base, twice_cos * base]
    for _ in range(NB - 2):
        raw.append(twice_cos * raw[-1] - raw[-2])
    radial = [value if b == 0 else value * (1.0 / (b + 1)) for b, value in enumerate(raw)]
    root_three = math.sqrt(3.0)
    root_fifteen = math.sqrt(15.0)
    root_five = math.sqrt(5.0)
    wide_x = root_fifteen * dx
    harmonic = [
        None,
        root_three * dx,
        root_three * dy,
        root_three * dz,
        wide_x * dy,
        (root_fifteen * dy) * dz,
        (0.5 * root_five) * (3.0 * zz - square),
        wide_x * dz,
        (0.5 * root_fifteen) * (xx - yy),
    ]
    for b in range(NB):
        rows = slice(b * GROUP + row, b * GROUP + row + ROWS)
        for y in range(NY):
            value = radial[b] if y == 0 else radial[b] * harmonic[y]
            factor_ref[rows, y * GROUP : (y + 1) * GROUP] = value.astype(jnp.bfloat16)


def column_to_row(column, size):
    wide = jnp.broadcast_to(column, (size, GROUP))
    at = lax.broadcasted_iota(jnp.int32, (size, GROUP), 0)
    lane = lax.broadcasted_iota(jnp.int32, (size, GROUP), 1)
    return jnp.sum(jnp.where(at == lane, wide, 0.0), axis=0, keepdims=True)


def split_kernel(*refs):
    features_ref, place_in_ref, *inputs = refs[: SMALL + 2]
    own_ref, *outputs = refs[SMALL + 2 : 2 * SMALL + 3]
    place_ref, sems = refs[2 * SMALL + 3 :]
    core = lax.axis_index("space") % 2
    place_copy = pltpu.make_async_copy(place_in_ref, place_ref, sems.at[2])
    place_copy.start()
    copies = []
    for k, side in enumerate((1 - core, core)):
        at = pl.ds(pl.multiple_of(side * GROUP, GROUP), GROUP)
        copies.append(
            pltpu.make_async_copy(
                features_ref.at[0, :, at], own_ref.at[pl.ds(k * SLAB_ROWS, CH)], sems.at[k]
            )
        )
    for k, (src, dst) in enumerate(zip(inputs, outputs)):
        copies.append(pltpu.make_async_copy(src, dst, sems.at[3 + k]))
    for copy in copies:
        copy.start()
    place_copy.wait()
    low, high = slice(GROUP), slice(GROUP, 2 * GROUP)
    filler = jnp.zeros((5, GROUP), jnp.float32)
    for k, (one, two) in enumerate(((high, low), (low, high))):
        rows = [
            jnp.where(core == 0, place_ref[axis, :, one], place_ref[axis, :, two]) for axis in range(3)
        ]
        at = slice(k * SLAB_ROWS + CH, (k + 1) * SLAB_ROWS)
        own_ref[at, :] = jnp.concatenate(rows + [filler], axis=0)
    for copy in copies:
        copy.wait()


def live_flags(count, pair_target, pair_source):
    size = (4 * CELLS, pair_target.shape[1])
    at = lax.broadcasted_iota(jnp.int32, size, 0)
    slot = lax.broadcasted_iota(jnp.int32, size, 1)
    hit = (pair_target * CELLS + pair_source == at) & (slot < count)
    return jnp.max(jnp.where(hit, message_scale, 0.0), axis=1, keepdims=True)


def keep_rows(flags, t, d):
    lane = lax.broadcasted_iota(jnp.int32, (1, GROUP), 1)
    rows = []
    for scell in (2 * (t + d), 2 * (t + d) + 1):
        one, two = [(2 * t + k) * CELLS + scell for k in range(2)]
        rows.append(jnp.where(lane < CELL_ATOMS, flags[one : one + 1], flags[two : two + 1]))
    return rows


def set_source(scaled_ref, place_ref, slab, weight_t):
    features = slab[:CH]
    for b in range(NB):
        scaled_ref[:, b * GROUP : (b + 1) * GROUP] = (features * weight_t[:, b : b + 1]).astype(
            jnp.bfloat16
        )
    place = slab[CH:].T
    for axis in range(3):
        place_ref[axis] = jnp.broadcast_to(place[:, axis : axis + 1], (GROUP, GROUP))


def fill_block(factor_ref, place_ref, keeps, target, d):
    row_at = lax.broadcasted_iota(jnp.int32, (ROWS, GROUP), 0)
    lane_at = lax.broadcasted_iota(jnp.int32, (ROWS, GROUP), 1)
    for half in range(2):
        for row in range(half * CELL_ATOMS, (half + 1) * CELL_ATOMS, ROWS):
            source = [place_ref[axis, row : row + ROWS, :] for axis in range(3)]
            keep = jnp.broadcast_to(keeps[half], (ROWS, GROUP))
            if d == 1:
                keep = jnp.where(row_at + row == lane_at, 0.0, keep)
            factor_rows(factor_ref, row, source, target, keep)


def local_kernel(
    count_ref,
    pair_target_ref,
    pair_source_ref,
    radial_ref,
    own_ref,
    factor_ref,
    messages_ref,
    keep_ref,
    scaled_ref,
    place_ref,
):
    even = lax.axis_index("space") % 2 == 0
    near, far = own_ref[:SLAB_ROWS, :], own_ref[SLAB_ROWS:, :]
    slabs = (jnp.where(even, far, near), jnp.where(even, near, far))
    targets = [[slab[CH + axis : CH + axis + 1] for axis in range(3)] for slab in slabs]
    flags = live_flags(count_ref[0, 0], pair_target_ref[...], pair_source_ref[...])
    weight_t = radial_ref[...].T
    for g in range(2):
        set_source(scaled_ref.at[g], place_ref.at[g], slabs[g], weight_t)

    def fill(block):
        t, d = LOCAL[block]
        fill_block(factor_ref.at[block], place_ref.at[t + d - 1], keep_rows(flags, t, d), targets[t], d)

    totals = [None, None]
    fill(0)
    for block, (t, d) in enumerate(LOCAL):
        product = jnp.dot(
            scaled_ref[t + d - 1], factor_ref[block], preferred_element_type=jnp.float32
        )
        totals[t] = product if totals[t] is None else totals[t] + product
        if block + 1 < len(LOCAL):
            fill(block + 1)
    for t in range(2):
        messages_ref[t] = totals[t]
    keep_ref[...] = jnp.concatenate(
        keep_rows(flags, 0, 0) + keep_rows(flags, 1, 2) + [jnp.zeros((4, GROUP), jnp.float32)], axis=0
    )


def node_kernel(
    scale,
    own_ref,
    from_pair_ref,
    from_cross_ref,
    messages_ref,
    keep_ref,
    species_ref,
    shift_ref,
    energy_grad_ref,
    radial_ref,
    mix_ref,
    readout_ref,
    energy_ref,
    spread_ref,
    kept_ref,
    sent_ref,
    rest_ref,
    grad_messages_ref,
    halo_ref,
    scaled_ref,
    place_ref,
):
    even = lax.axis_index("space") % 2 == 0
    weight_t = radial_ref[...].T
    near, far = own_ref[:SLAB_ROWS, :], own_ref[SLAB_ROWS:, :]
    from_pair, from_cross = from_pair_ref[:SLAB_ROWS, :], from_cross_ref[...]
    slabs = (
        jnp.where(even, from_cross, from_pair),
        jnp.where(even, far, near),
        jnp.where(even, near, far),
        jnp.where(even, from_pair, from_cross),
    )
    targets = [[slab[CH + axis : CH + axis + 1] for axis in range(3)] for slab in slabs[1:3]]

    def fill(t):
        d = 2 * t
        set_source(scaled_ref.at[t], place_ref.at[t], slabs[t + d], weight_t)
        keeps = [keep_ref[2 * t + half : 2 * t + half + 1, :] for half in range(2)]
        fill_block(halo_ref.at[t], place_ref.at[t], keeps, targets[t], d)

    def add_halo(t):
        return messages_ref[t] + jnp.dot(
            scaled_ref[t], halo_ref[t], preferred_element_type=jnp.float32
        )

    readout = jnp.broadcast_to(readout_ref[...], (8, CH)).T[:, :1]
    mix = mix_ref[...]
    mix_t = mix.astype(jnp.float32).T.astype(jnp.bfloat16)

    def node_stage(t, messages):
        at = slice(t * GROUP, (t + 1) * GROUP)
        part = [messages[:, y * GROUP : (y + 1) * GROUP] for y in range(NY)]
        invariants = jnp.concatenate(
            [
                part[0],
                0.5 * (part[1] * part[1] + part[2] * part[2] + part[3] * part[3]),
                0.5
                * (
                    part[4] * part[4]
                    + part[5] * part[5]
                    + part[6] * part[6]
                    + part[7] * part[7]
                    + part[8] * part[8]
                ),
            ],
            axis=0,
        ).astype(jnp.bfloat16)
        preact = jnp.dot(mix_t, invariants, preferred_element_type=jnp.float32)
        gating = jax.nn.sigmoid(preact)
        updated = slabs[t + 1][:CH] + preact * gating
        energy_grad = energy_grad_ref[:, at]
        kinds = species_ref[:, at]
        shifts = jnp.zeros((1, GROUP), jnp.float32)
        for n in range(NSPEC):
            shifts = jnp.where(kinds == n, shift_ref[:, n : n + 1], shifts)
        energy_ref[:, at] = jnp.sum(updated * readout, axis=0, keepdims=True) + shifts
        spread = readout * energy_grad
        spread_ref[:, at] = spread
        grad_pre = (spread * gating * (1.0 + preact * (1.0 - gating))).astype(jnp.bfloat16)
        grad_mix = lax.dot_general(
            invariants, grad_pre, (((1,), (1,)), ((), ())), preferred_element_type=jnp.float32
        )
        grad_inv = jnp.dot(mix, grad_pre, preferred_element_type=jnp.float32)
        grad_messages_ref[t] = jnp.concatenate(
            [grad_inv[:CH]]
            + [grad_inv[CH : 2 * CH] * part[y] for y in range(1, 4)]
            + [grad_inv[2 * CH :] * part[y] for y in range(4, NY)],
            axis=1,
        ).astype(jnp.bfloat16)
        return updated * energy_grad, grad_mix

    fill(0)
    first = add_halo(0)
    fill(1)
    out_low, mix_low = node_stage(0, first)
    out_high, mix_high = node_stage(1, add_halo(1))

    grad_mix = (mix_low + mix_high) * scale
    kept_ref[...] = jnp.where(even, grad_mix[:HALF], grad_mix[HALF:])
    sent_ref[...] = jnp.where(even, grad_mix[HALF:], grad_mix[:HALF])
    readout_row = column_to_row(jnp.sum(out_low + out_high, axis=1, keepdims=True), CH)
    here = lax.broadcasted_iota(jnp.int32, (NSPEC, 2 * GROUP), 0) == species_ref[...]
    by_kind = jnp.sum(jnp.where(here, energy_grad_ref[...], 0.0), axis=1, keepdims=True)
    rest_ref[...] = jnp.concatenate(
        [readout_row, column_to_row(by_kind, NSPEC), jnp.zeros((6, CH), jnp.float32)], axis=0
    )


def back(factor, grad_messages):
    return lax.dot_general(
        factor, grad_messages, (((1,), (1,)), ((), ())), preferred_element_type=jnp.float32
    )


def source_grads(total, features, weight):
    features_t = features.T
    grad_t = None
    radial = []
    for b in range(NB):
        piece = total[b * GROUP : (b + 1) * GROUP]
        term = piece * weight[b : b + 1, :]
        grad_t = term if grad_t is None else grad_t + term
        radial.append(jnp.sum(piece * features_t, axis=0, keepdims=True))
    return grad_t.T, jnp.concatenate(radial, axis=0)


def halo_back_kernel(
    halo_ref, grad_messages_ref, from_pair_ref, from_cross_ref, radial_ref, sent_ref, share_ref
):
    even = lax.axis_index("space") % 2 == 0
    weight = radial_ref[...]
    before = jnp.where(even, from_cross_ref[:CH, :], from_pair_ref[:CH, :])
    after = jnp.where(even, from_pair_ref[:CH, :], from_cross_ref[:CH, :])
    grad_before, share_before = source_grads(back(halo_ref[0], grad_messages_ref[0]), before, weight)
    grad_after, share_after = source_grads(back(halo_ref[1], grad_messages_ref[1]), after, weight)
    sent_ref[:CH, :] = jnp.where(even, grad_after, grad_before)
    sent_ref[CH:, :] = jnp.where(even, grad_before, grad_after)
    share_ref[...] = share_before + share_after


def own_back_kernel(
    scale,
    local_ref,
    grad_messages_ref,
    own_ref,
    radial_ref,
    share_ref,
    rest_ref,
    spread_ref,
    own_grad_ref,
    joined_ref,
):
    even = lax.axis_index("space") % 2 == 0
    weight = radial_ref[...]
    near, far = own_ref[:CH, :], own_ref[SLAB_ROWS : SLAB_ROWS + CH, :]
    low, high = jnp.where(even, far, near), jnp.where(even, near, far)
    share = share_ref[...]
    for g, features in enumerate((low, high)):
        total = back(local_ref[g], grad_messages_ref[0]) + back(local_ref[2 + g], grad_messages_ref[1])
        grad, part = source_grads(total, features, weight)
        at = slice(g * GROUP, (g + 1) * GROUP)
        own_grad_ref[:, at] = spread_ref[:, at] + grad
        share = share + part
    joined_ref[:NB, :] = share * scale
    joined_ref[NB:, :] = rest_ref[...] * scale


def quarter_kernel(kept_ref, received_ref, keep_ref, send_ref):
    first = lax.axis_index("dp") % 2 == 0
    low = kept_ref[:QUARTER, :] + received_ref[:QUARTER, :]
    high = kept_ref[QUARTER:, :] + received_ref[QUARTER:, :]
    keep_ref[...] = jnp.where(first, low, high)
    send_ref[...] = jnp.where(first, high, low)


def join_kernel(kept_ref, received_ref, rest_ref, out_ref):
    out_ref[:QUARTER, :] = kept_ref[...] + received_ref[...]
    out_ref[QUARTER:, :] = rest_ref[...]


def gather_kernel(mine_ref, along_ref, other_ref, both_ref, out_ref):
    first = lax.axis_index("dp") % 2 == 0
    at, rest = slice(QUARTER), slice(QUARTER, QUARTER + REST)
    mine = mine_ref[at, :] + along_ref[at, :]
    other = other_ref[at, :] + both_ref[at, :]
    out_ref[:QUARTER, :] = jnp.where(first, mine, other)
    out_ref[QUARTER:HALF, :] = jnp.where(first, other, mine)
    out_ref[HALF:, :] = (mine_ref[rest, :] + along_ref[rest, :]) + (other_ref[rest, :] + both_ref[rest, :])


def fold_kernel(own_ref, from_pair_ref, from_cross_ref, energy_in_ref, grad_ref, energy_ref):
    even = lax.axis_index("space") % 2 == 0
    pair = from_pair_ref[:CH, :]
    cross = from_cross_ref[...]
    grad_ref[0, :, :GROUP] = own_ref[:, :GROUP] + jnp.where(even, cross, pair)
    grad_ref[0, :, GROUP:] = own_ref[:, GROUP:] + jnp.where(even, pair, cross)
    energy_ref[...] = energy_in_ref[...]


def finish_kernel(mine_ref, other_ref, radial_ref, mix_ref, readout_ref, shift_ref):
    even = lax.axis_index("space") % 2 == 0
    mine, other = mine_ref[:HALF, :], other_ref[:HALF, :]
    mix_ref[:HALF, :] = jnp.where(even, mine, other)
    mix_ref[HALF:, :] = jnp.where(even, other, mine)
    rest = mine_ref[HALF:, :] + other_ref[HALF:, :]
    radial_ref[...] = rest[:NB]
    readout_ref[...] = rest[NB : NB + 1]
    shift_ref[...] = rest[NB + 1 : NB + 2, :NSPEC]


def exchange_routes(space, dp):
    steps = [(1 << k, 0) for k in range(1, space.bit_length() - 1)]
    steps += [(0, 1 << k) for k in range(1, dp.bit_length() - 1)]
    orders = [[steps[(k + 1 - core) % len(steps)] for k in range(len(steps))] for core in range(2)]
    places = list(range(len(steps)))
    groups = [places[k : k + 2] for k in range(0, len(steps) - 1, 2)] + [places[-1:]]
    if len(groups[-2:]) == 2 and groups[-2][-1] == groups[-1][0]:
        groups[-2:] = [groups[-2][:1], groups[-1]]
    rounds = []
    for group in groups:
        last = group is groups[-1]
        kinds = [group[:1]] if len(group) == 1 and not last else [group[:1], group[1:], group]
        routes = []
        for n, kind in enumerate(kinds):
            route = []
            for s in range(space):
                across = along = 0
                for k in kind:
                    step = orders[s % 2][k]
                    across, along = across ^ step[0], along ^ step[1]
                if last and n:
                    along ^= 1
                for d in range(dp):
                    route.append((s * dp + d, (s ^ across) * dp + (d ^ along)))
            routes.append(route)
        rounds.append(routes)
    return rounds


def call(kernel, name, inputs, outputs, mib=4, scratch=(), flops=0):
    vmem = pl.BlockSpec(memory_space=pltpu.VMEM)
    shapes = tuple(jax.ShapeDtypeStruct(shape, kind) for shape, kind in outputs)
    moved = sum(math.prod(v.shape) * v.dtype.itemsize for v in (*inputs, *shapes))
    return pl.pallas_call(
        kernel,
        out_shape=shapes,
        in_specs=[vmem] * len(inputs),
        out_specs=(vmem,) * len(shapes),
        scratch_shapes=scratch,
        compiler_params=pltpu.CompilerParams(vmem_limit_bytes=mib * 1024 * 1024),
        cost_estimate=pl.CostEstimate(flops=flops, bytes_accessed=moved, transcendentals=0),
        name=name,
    )(*inputs)


def in_hbm(value):
    return pltpu.with_memory_space_constraint(value, pltpu.HBM)


def body(
    node_features,
    positions,
    species,
    energy_cotangent,
    pair_target,
    pair_source,
    pair_count,
    radial_weight,
    mix_weight,
    readout_weight,
    species_shift,
):
    atoms_here = node_features.shape[2]
    space, dp = lax.axis_size("space"), lax.axis_size("dp")
    scale = 1.0 / math.sqrt(atoms_here * space * dp)
    pair = [(i, i ^ 1) for i in range(space)]
    onward = [(i, i + 2) for i in range(0, space - 2, 2)] + [(i, i - 2) for i in range(3, space, 2)]

    across = [(i, i ^ 1) for i in range(dp)]
    hbm = pl.BlockSpec(memory_space=pltpu.HBM)
    smem = pl.BlockSpec(memory_space=pltpu.SMEM)
    vmem = pl.BlockSpec(memory_space=pltpu.VMEM)
    f32, bf16 = jnp.float32, jnp.bfloat16
    small = (
        pair_target,
        pair_source,
        species,
        species_shift.reshape(1, NSPEC),
        energy_cotangent,
        radial_weight,
        mix_weight,
        readout_weight.reshape(1, CH),
    )
    own, *small = pl.pallas_call(
        split_kernel,
        out_shape=(jax.ShapeDtypeStruct((2 * SLAB_ROWS, GROUP), f32),)
        + tuple(jax.ShapeDtypeStruct(v.shape, v.dtype) for v in small),
        in_specs=[hbm] * (SMALL + 2),
        out_specs=(vmem,) * (SMALL + 1),
        scratch_shapes=[
            pltpu.VMEM((3, 1, atoms_here), f32),
            pltpu.SemaphoreType.DMA((SMALL + 3,)),
        ],
        compiler_params=pltpu.CompilerParams(vmem_limit_bytes=4 * 1024 * 1024),
        name="split",
    )(
        in_hbm(node_features),
        in_hbm(jnp.transpose(positions, (1, 0, 2))),
        *[in_hbm(v) for v in small],
    )
    targets, sources, species, shift, energy_grad, radial, mix, readout = small
    from_pair = lax.ppermute(own, "space", pair)
    from_cross = lax.ppermute(from_pair[SLAB_ROWS:], "space", onward)

    block_flops = 2 * CH * NB * NY * GROUP * GROUP
    local_factor, messages, keep = pl.pallas_call(
        local_kernel,
        out_shape=(
            jax.ShapeDtypeStruct((len(LOCAL), NB * GROUP, NY * GROUP), bf16),
            jax.ShapeDtypeStruct((2, CH, NY * GROUP), f32),
            jax.ShapeDtypeStruct((8, GROUP), f32),
        ),
        in_specs=[smem] + [vmem] * 4,
        out_specs=(vmem,) * 3,
        scratch_shapes=[
            pltpu.VMEM((2, CH, NB * GROUP), bf16),
            pltpu.VMEM((2, 3, GROUP, GROUP), f32),
        ],
        compiler_params=pltpu.CompilerParams(vmem_limit_bytes=16 * 1024 * 1024),
        cost_estimate=pl.CostEstimate(
            flops=len(LOCAL) * block_flops, bytes_accessed=14_000_000, transcendentals=0
        ),
        name="local_pairs",
    )(pair_count, targets, sources, radial, own)

    energy, spread, kept, sent, rest, grad_messages, halo_factor = call(
        functools.partial(node_kernel, scale),
        "node_stage",
        (
            own,
            from_pair,
            from_cross,
            messages,
            keep,
            species,
            shift,
            energy_grad,
            radial,
            mix,
            readout,
        ),
        (
            ((1, atoms_here), f32),
            ((CH, atoms_here), f32),
            ((HALF, CH), f32),
            ((HALF, CH), f32),
            ((8, CH), f32),
            ((2, CH, NY * GROUP), bf16),
            ((2, NB * GROUP, NY * GROUP), bf16),
        ),
        16,
        [pltpu.VMEM((2, CH, NB * GROUP), bf16), pltpu.VMEM((2, 3, GROUP, GROUP), f32)],
        2 * block_flops,
    )

    received = lax.ppermute(sent, "space", pair)
    halo_grad, share = call(
        halo_back_kernel,
        "halo_back",
        (halo_factor, grad_messages, from_pair, from_cross, radial),
        (((2 * CH, GROUP), f32), ((NB, CH), f32)),
        12,
        (),
        2 * block_flops,
    )
    received, share = lax.optimization_barrier((received, share))
    quarter, sent = call(
        quarter_kernel,
        "quarter",
        (kept, received),
        (((QUARTER, CH), f32), ((QUARTER, CH), f32)),
    )
    sent, grad_messages, halo_grad = lax.optimization_barrier((sent, grad_messages, halo_grad))
    received = lax.ppermute(sent, "dp", across)
    from_pair = lax.ppermute(halo_grad, "space", pair)
    own_grad, joined = call(
        functools.partial(own_back_kernel, scale),
        "own_back",
        (local_factor, grad_messages, own, radial, share, rest, spread),
        (((CH, atoms_here), f32), ((REST, CH), f32)),
        12,
        (),
        4 * block_flops,
    )
    (value,) = call(
        join_kernel, "join", (quarter, received, joined), (((QUARTER + REST, CH), f32),)
    )
    value, from_pair = lax.optimization_barrier((value, from_pair))
    *rounds, last = exchange_routes(space, dp)
    everyone = ("space", "dp")
    for routes in rounds:
        arrived = [lax.ppermute(value, everyone, route) for route in routes]
        value = value + arrived[0]
        if len(arrived) == 3:
            value = value + (arrived[1] + arrived[2])
    value = jnp.pad(value, ((0, CH + 8 - value.shape[0]), (0, 0)))
    value, onward_grad = lax.optimization_barrier((value, from_pair[CH:]))
    arrived = [lax.ppermute(value, everyone, route) for route in last]
    from_cross = lax.ppermute(onward_grad, "space", onward)
    value, from_cross, *arrived = lax.optimization_barrier((value, from_cross, *arrived))
    (value,) = call(
        gather_kernel,
        "gather",
        (value, *arrived),
        (((HALF + REST, CH), f32),),
    )
    feature_grad, energy = call(
        fold_kernel,
        "fold",
        (own_grad, from_pair, from_cross, energy),
        (((1, CH, atoms_here), f32), ((1, atoms_here), f32)),
    )
    radial_grad, mix_grad, readout_grad, shift_grad = call(
        finish_kernel,
        "finish",
        (value, lax.ppermute(value, "space", pair)),
        (((NB, CH), f32), ((MIX_ROWS, CH), f32), ((1, CH), f32), ((1, NSPEC), f32)),
    )
    return (
        energy,
        feature_grad,
        radial_grad,
        mix_grad,
        readout_grad.reshape(CH),
        shift_grad.reshape(NSPEC),
    )


def solution(mesh):
    return jax.shard_map(
        body,
        mesh=mesh,
        in_specs=(
            P("dp", None, "space"),
            P("dp", None, "space"),
            P("dp", "space"),
            P("dp", "space"),
            P("dp", "space"),
            P("dp", "space"),
            P("dp", "space"),
            P(),
            P(),
            P(),
            P(),
        ),
        out_specs=(P("dp", "space"), P("dp", None, "space"), P(), P(), P(), P()),
        check_vma=False,
    )
```

```python
import functools
import math

import jax
import jax.numpy as jnp
from jax import lax
from jax.experimental import pallas as pl
from jax.experimental.pallas import tpu as pltpu
from jax.sharding import PartitionSpec as P

CH = 128
NB = 8
NY = 9
NSPEC = 8
CELL_ATOMS = 64
HALO_CELLS = 2
GROUP = 2 * CELL_ATOMS
ROWS = 16

cutoff = 5.0
message_scale = 0.25

COS_COEFFS = (
    0.9999999998846169,
    -4.934802185771876,
    4.058711815779763,
    -1.3352602773967561,
    0.23532080049888648,
    -0.025785772074137014,
    0.0019043022864480008,
    -8.868331860867329e-05,
)
SINC_COEFFS = (
    0.9999999992502204,
    -1.6449339933418936,
    0.8117412468909989,
    -0.1907447263221115,
    0.02612742969685046,
    -0.0023157632409761065,
    0.00012580778956459784,
)

MIX_ROWS = 3 * CH
HALF = MIX_ROWS // 2
QUARTER = MIX_ROWS // 4
REST = 16
CELLS = 4 + 2 * HALO_CELLS
LOCAL = ((0, 1), (0, 2), (1, 0), (1, 1))
SMALL = 8
SLAB_ROWS = CH + 8


def polynomial(coeffs, x):
    total = coeffs[-1] * x + coeffs[-2]
    for c in coeffs[-3::-1]:
        total = total * x + c
    return total


def factor_rows(factor_ref, row, source, target, keep):
    dx = (target[0] - source[0]) * (1.0 / cutoff)
    dy = (target[1] - source[1]) * (1.0 / cutoff)
    dz = (target[2] - source[2]) * (1.0 / cutoff)
    xx, yy, zz = dx * dx, dy * dy, dz * dz
    square = xx + yy + zz
    inside = jnp.minimum(square, 1.0)
    gap = 1.0 - inside
    base = (gap * gap) * keep * polynomial(SINC_COEFFS, inside)
    twice_cos = polynomial([2.0 * c for c in COS_COEFFS], inside)
    raw = [base, twice_cos * base]
    for _ in range(NB - 2):
        raw.append(twice_cos * raw[-1] - raw[-2])
    radial = [value if b == 0 else value * (1.0 / (b + 1)) for b, value in enumerate(raw)]
    root_three = math.sqrt(3.0)
    root_fifteen = math.sqrt(15.0)
    root_five = math.sqrt(5.0)
    wide_x = root_fifteen * dx
    harmonic = [
        None,
        root_three * dx,
        root_three * dy,
        root_three * dz,
        wide_x * dy,
        (root_fifteen * dy) * dz,
        (0.5 * root_five) * (3.0 * zz - square),
        wide_x * dz,
        (0.5 * root_fifteen) * (xx - yy),
    ]
    for b in range(NB):
        rows = slice(b * GROUP + row, b * GROUP + row + ROWS)
        for y in range(NY):
            value = radial[b] if y == 0 else radial[b] * harmonic[y]
            factor_ref[rows, y * GROUP : (y + 1) * GROUP] = value.astype(jnp.bfloat16)


def column_to_row(column, size):
    wide = jnp.broadcast_to(column, (size, GROUP))
    at = lax.broadcasted_iota(jnp.int32, (size, GROUP), 0)
    lane = lax.broadcasted_iota(jnp.int32, (size, GROUP), 1)
    return jnp.sum(jnp.where(at == lane, wide, 0.0), axis=0, keepdims=True)


def split_kernel(*refs):
    features_ref, place_in_ref, *inputs = refs[: SMALL + 2]
    near_ref, far_ref, *outputs = refs[SMALL + 2 : 2 * SMALL + 4]
    place_ref, sems = refs[2 * SMALL + 4 :]
    core = lax.axis_index("space") % 2
    place_copy = pltpu.make_async_copy(place_in_ref, place_ref, sems.at[2])
    place_copy.start()
    copies = []
    for k, (ref, side) in enumerate(((near_ref, 1 - core), (far_ref, core))):
        at = pl.ds(pl.multiple_of(side * GROUP, GROUP), GROUP)
        copies.append(
            pltpu.make_async_copy(features_ref.at[0, :, at], ref.at[pl.ds(0, CH)], sems.at[k])
        )
    for k, (src, dst) in enumerate(zip(inputs, outputs)):
        copies.append(pltpu.make_async_copy(src, dst, sems.at[3 + k]))
    for copy in copies:
        copy.start()
    place_copy.wait()
    low, high = slice(GROUP), slice(GROUP, 2 * GROUP)
    filler = jnp.zeros((5, GROUP), jnp.float32)
    for ref, one, two in ((near_ref, high, low), (far_ref, low, high)):
        rows = [
            jnp.where(core == 0, place_ref[axis, :, one], place_ref[axis, :, two]) for axis in range(3)
        ]
        ref[CH:, :] = jnp.concatenate(rows + [filler], axis=0)
    for copy in copies:
        copy.wait()


def live_flags(count, pair_target, pair_source):
    size = (4 * CELLS, pair_target.shape[1])
    at = lax.broadcasted_iota(jnp.int32, size, 0)
    slot = lax.broadcasted_iota(jnp.int32, size, 1)
    hit = (pair_target * CELLS + pair_source == at) & (slot < count)
    return jnp.max(jnp.where(hit, message_scale, 0.0), axis=1, keepdims=True)


def keep_rows(flags, t, d):
    lane = lax.broadcasted_iota(jnp.int32, (1, GROUP), 1)
    rows = []
    for scell in (2 * (t + d), 2 * (t + d) + 1):
        one, two = [(2 * t + k) * CELLS + scell for k in range(2)]
        rows.append(jnp.where(lane < CELL_ATOMS, flags[one : one + 1], flags[two : two + 1]))
    return rows


def set_source(scaled_ref, place_ref, slab, weight_t):
    features = slab[:CH]
    for b in range(NB):
        scaled_ref[:, b * GROUP : (b + 1) * GROUP] = (features * weight_t[:, b : b + 1]).astype(
            jnp.bfloat16
        )
    place = slab[CH:].T
    for axis in range(3):
        place_ref[axis] = jnp.broadcast_to(place[:, axis : axis + 1], (GROUP, GROUP))


def fill_block(factor_ref, place_ref, keeps, target, d):
    row_at = lax.broadcasted_iota(jnp.int32, (ROWS, GROUP), 0)
    lane_at = lax.broadcasted_iota(jnp.int32, (ROWS, GROUP), 1)
    for half in range(2):
        for row in range(half * CELL_ATOMS, (half + 1) * CELL_ATOMS, ROWS):
            source = [place_ref[axis, row : row + ROWS, :] for axis in range(3)]
            keep = jnp.broadcast_to(keeps[half], (ROWS, GROUP))
            if d == 1:
                keep = jnp.where(row_at + row == lane_at, 0.0, keep)
            factor_rows(factor_ref, row, source, target, keep)


def local_kernel(
    count_ref,
    pair_target_ref,
    pair_source_ref,
    radial_ref,
    near_ref,
    far_ref,
    factor_ref,
    messages_ref,
    keep_ref,
    scaled_ref,
    place_ref,
):
    even = lax.axis_index("space") % 2 == 0
    near, far = near_ref[...], far_ref[...]
    slabs = (jnp.where(even, far, near), jnp.where(even, near, far))
    targets = [[slab[CH + axis : CH + axis + 1] for axis in range(3)] for slab in slabs]
    flags = live_flags(count_ref[0, 0], pair_target_ref[...], pair_source_ref[...])
    weight_t = radial_ref[...].T
    for g in range(2):
        set_source(scaled_ref.at[g], place_ref.at[g], slabs[g], weight_t)

    def fill(block):
        t, d = LOCAL[block]
        fill_block(factor_ref.at[block], place_ref.at[t + d - 1], keep_rows(flags, t, d), targets[t], d)

    totals = [None, None]
    fill(0)
    for block, (t, d) in enumerate(LOCAL):
        product = jnp.dot(
            scaled_ref[t + d - 1], factor_ref[block], preferred_element_type=jnp.float32
        )
        totals[t] = product if totals[t] is None else totals[t] + product
        if block + 1 < len(LOCAL):
            fill(block + 1)
    for t in range(2):
        messages_ref[t] = totals[t]
    keep_ref[...] = jnp.concatenate(
        keep_rows(flags, 0, 0) + keep_rows(flags, 1, 2) + [jnp.zeros((4, GROUP), jnp.float32)], axis=0
    )


def node_kernel(
    scale,
    near_ref,
    far_ref,
    from_pair_ref,
    from_cross_ref,
    messages_ref,
    keep_ref,
    species_ref,
    shift_ref,
    energy_grad_ref,
    radial_ref,
    mix_ref,
    readout_ref,
    energy_ref,
    spread_ref,
    kept_ref,
    sent_ref,
    rest_ref,
    grad_messages_ref,
    halo_ref,
    scaled_ref,
    place_ref,
):
    even = lax.axis_index("space") % 2 == 0
    weight_t = radial_ref[...].T
    near, far = near_ref[...], far_ref[...]
    from_pair, from_cross = from_pair_ref[...], from_cross_ref[...]
    slabs = (
        jnp.where(even, from_cross, from_pair),
        jnp.where(even, far, near),
        jnp.where(even, near, far),
        jnp.where(even, from_pair, from_cross),
    )
    targets = [[slab[CH + axis : CH + axis + 1] for axis in range(3)] for slab in slabs[1:3]]

    def fill(t):
        d = 2 * t
        set_source(scaled_ref.at[t], place_ref.at[t], slabs[t + d], weight_t)
        keeps = [keep_ref[2 * t + half : 2 * t + half + 1, :] for half in range(2)]
        fill_block(halo_ref.at[t], place_ref.at[t], keeps, targets[t], d)

    def add_halo(t):
        return messages_ref[t] + jnp.dot(
            scaled_ref[t], halo_ref[t], preferred_element_type=jnp.float32
        )

    readout = jnp.broadcast_to(readout_ref[...], (8, CH)).T[:, :1]
    mix = mix_ref[...]
    mix_t = mix.astype(jnp.float32).T.astype(jnp.bfloat16)

    def node_stage(t, messages):
        at = slice(t * GROUP, (t + 1) * GROUP)
        part = [messages[:, y * GROUP : (y + 1) * GROUP] for y in range(NY)]
        invariants = jnp.concatenate(
            [
                part[0],
                0.5 * (part[1] * part[1] + part[2] * part[2] + part[3] * part[3]),
                0.5
                * (
                    part[4] * part[4]
                    + part[5] * part[5]
                    + part[6] * part[6]
                    + part[7] * part[7]
                    + part[8] * part[8]
                ),
            ],
            axis=0,
        ).astype(jnp.bfloat16)
        preact = jnp.dot(mix_t, invariants, preferred_element_type=jnp.float32)
        gating = jax.nn.sigmoid(preact)
        updated = slabs[t + 1][:CH] + preact * gating
        energy_grad = energy_grad_ref[:, at]
        kinds = species_ref[:, at]
        shifts = jnp.zeros((1, GROUP), jnp.float32)
        for n in range(NSPEC):
            shifts = jnp.where(kinds == n, shift_ref[:, n : n + 1], shifts)
        energy_ref[:, at] = jnp.sum(updated * readout, axis=0, keepdims=True) + shifts
        spread = readout * energy_grad
        spread_ref[:, at] = spread
        grad_pre = (spread * gating * (1.0 + preact * (1.0 - gating))).astype(jnp.bfloat16)
        grad_mix = lax.dot_general(
            invariants, grad_pre, (((1,), (1,)), ((), ())), preferred_element_type=jnp.float32
        )
        grad_inv = jnp.dot(mix, grad_pre, preferred_element_type=jnp.float32)
        grad_messages_ref[t] = jnp.concatenate(
            [grad_inv[:CH]]
            + [grad_inv[CH : 2 * CH] * part[y] for y in range(1, 4)]
            + [grad_inv[2 * CH :] * part[y] for y in range(4, NY)],
            axis=1,
        ).astype(jnp.bfloat16)
        return updated * energy_grad, grad_mix

    fill(0)
    first = add_halo(0)
    fill(1)
    out_low, mix_low = node_stage(0, first)
    out_high, mix_high = node_stage(1, add_halo(1))

    grad_mix = (mix_low + mix_high) * scale
    kept_ref[...] = jnp.where(even, grad_mix[:HALF], grad_mix[HALF:])
    sent_ref[...] = jnp.where(even, grad_mix[HALF:], grad_mix[:HALF])
    readout_row = column_to_row(jnp.sum(out_low + out_high, axis=1, keepdims=True), CH)
    here = lax.broadcasted_iota(jnp.int32, (NSPEC, 2 * GROUP), 0) == species_ref[...]
    by_kind = jnp.sum(jnp.where(here, energy_grad_ref[...], 0.0), axis=1, keepdims=True)
    rest_ref[...] = jnp.concatenate(
        [readout_row, column_to_row(by_kind, NSPEC), jnp.zeros((6, CH), jnp.float32)], axis=0
    )


def back(factor, grad_messages):
    return lax.dot_general(
        factor, grad_messages, (((1,), (1,)), ((), ())), preferred_element_type=jnp.float32
    )


def source_grads(total, features, weight):
    features_t = features.T
    grad_t = None
    radial = []
    for b in range(NB):
        piece = total[b * GROUP : (b + 1) * GROUP]
        term = piece * weight[b : b + 1, :]
        grad_t = term if grad_t is None else grad_t + term
        radial.append(jnp.sum(piece * features_t, axis=0, keepdims=True))
    return grad_t.T, jnp.concatenate(radial, axis=0)


def halo_back_kernel(
    halo_ref, grad_messages_ref, from_pair_ref, from_cross_ref, radial_ref, sent_ref, share_ref
):
    even = lax.axis_index("space") % 2 == 0
    weight = radial_ref[...]
    before = jnp.where(even, from_cross_ref[:CH, :], from_pair_ref[:CH, :])
    after = jnp.where(even, from_pair_ref[:CH, :], from_cross_ref[:CH, :])
    grad_before, share_before = source_grads(back(halo_ref[0], grad_messages_ref[0]), before, weight)
    grad_after, share_after = source_grads(back(halo_ref[1], grad_messages_ref[1]), after, weight)
    sent_ref[:CH, :] = jnp.where(even, grad_after, grad_before)
    sent_ref[CH:, :] = jnp.where(even, grad_before, grad_after)
    share_ref[...] = share_before + share_after


def own_back_kernel(
    scale,
    local_ref,
    grad_messages_ref,
    near_ref,
    far_ref,
    radial_ref,
    share_ref,
    rest_ref,
    spread_ref,
    own_grad_ref,
    joined_ref,
):
    even = lax.axis_index("space") % 2 == 0
    weight = radial_ref[...]
    near, far = near_ref[:CH, :], far_ref[:CH, :]
    low, high = jnp.where(even, far, near), jnp.where(even, near, far)
    share = share_ref[...]
    for g, features in enumerate((low, high)):
        total = back(local_ref[g], grad_messages_ref[0]) + back(local_ref[2 + g], grad_messages_ref[1])
        grad, part = source_grads(total, features, weight)
        at = slice(g * GROUP, (g + 1) * GROUP)
        own_grad_ref[:, at] = spread_ref[:, at] + grad
        share = share + part
    joined_ref[:NB, :] = share * scale
    joined_ref[NB:, :] = rest_ref[...] * scale


def quarter_kernel(kept_ref, received_ref, keep_ref, send_ref):
    first = lax.axis_index("dp") % 2 == 0
    low = kept_ref[:QUARTER, :] + received_ref[:QUARTER, :]
    high = kept_ref[QUARTER:, :] + received_ref[QUARTER:, :]
    keep_ref[...] = jnp.where(first, low, high)
    send_ref[...] = jnp.where(first, high, low)


def join_kernel(kept_ref, received_ref, rest_ref, out_ref):
    out_ref[:QUARTER, :] = kept_ref[...] + received_ref[...]
    out_ref[QUARTER:, :] = rest_ref[...]


def gather_kernel(mine_ref, along_ref, other_ref, both_ref, out_ref):
    first = lax.axis_index("dp") % 2 == 0
    at, rest = slice(QUARTER), slice(QUARTER, QUARTER + REST)
    mine = mine_ref[at, :] + along_ref[at, :]
    other = other_ref[at, :] + both_ref[at, :]
    out_ref[:QUARTER, :] = jnp.where(first, mine, other)
    out_ref[QUARTER:HALF, :] = jnp.where(first, other, mine)
    out_ref[HALF:, :] = (mine_ref[rest, :] + along_ref[rest, :]) + (other_ref[rest, :] + both_ref[rest, :])


def fold_kernel(own_ref, from_pair_ref, from_cross_ref, energy_in_ref, grad_ref, energy_ref):
    even = lax.axis_index("space") % 2 == 0
    pair = from_pair_ref[:CH, :]
    cross = from_cross_ref[...]
    grad_ref[0, :, :GROUP] = own_ref[:, :GROUP] + jnp.where(even, cross, pair)
    grad_ref[0, :, GROUP:] = own_ref[:, GROUP:] + jnp.where(even, pair, cross)
    energy_ref[...] = energy_in_ref[...]


def finish_kernel(mine_ref, other_ref, radial_ref, mix_ref, readout_ref, shift_ref):
    even = lax.axis_index("space") % 2 == 0
    mine, other = mine_ref[:HALF, :], other_ref[:HALF, :]
    mix_ref[:HALF, :] = jnp.where(even, mine, other)
    mix_ref[HALF:, :] = jnp.where(even, other, mine)
    rest = mine_ref[HALF:, :] + other_ref[HALF:, :]
    radial_ref[...] = rest[:NB]
    readout_ref[...] = rest[NB : NB + 1]
    shift_ref[...] = rest[NB + 1 : NB + 2, :NSPEC]


def exchange_routes(space, dp):
    steps = [(1 << k, 0) for k in range(1, space.bit_length() - 1)]
    steps += [(0, 1 << k) for k in range(1, dp.bit_length() - 1)]
    orders = [[steps[(k + 1 - core) % len(steps)] for k in range(len(steps))] for core in range(2)]
    places = list(range(len(steps)))
    groups = [places[k : k + 2] for k in range(0, len(steps) - 1, 2)] + [places[-1:]]
    if len(groups[-2:]) == 2 and groups[-2][-1] == groups[-1][0]:
        groups[-2:] = [groups[-2][:1], groups[-1]]
    rounds = []
    for group in groups:
        last = group is groups[-1]
        kinds = [group[:1]] if len(group) == 1 and not last else [group[:1], group[1:], group]
        routes = []
        for n, kind in enumerate(kinds):
            route = []
            for s in range(space):
                across = along = 0
                for k in kind:
                    step = orders[s % 2][k]
                    across, along = across ^ step[0], along ^ step[1]
                if last and n:
                    along ^= 1
                for d in range(dp):
                    route.append((s * dp + d, (s ^ across) * dp + (d ^ along)))
            routes.append(route)
        rounds.append(routes)
    return rounds


def call(kernel, name, inputs, outputs, mib=4, scratch=(), flops=0):
    vmem = pl.BlockSpec(memory_space=pltpu.VMEM)
    shapes = tuple(jax.ShapeDtypeStruct(shape, kind) for shape, kind in outputs)
    moved = sum(math.prod(v.shape) * v.dtype.itemsize for v in (*inputs, *shapes))
    return pl.pallas_call(
        kernel,
        out_shape=shapes,
        in_specs=[vmem] * len(inputs),
        out_specs=(vmem,) * len(shapes),
        scratch_shapes=scratch,
        compiler_params=pltpu.CompilerParams(vmem_limit_bytes=mib * 1024 * 1024),
        cost_estimate=pl.CostEstimate(flops=flops, bytes_accessed=moved, transcendentals=0),
        name=name,
    )(*inputs)


def in_hbm(value):
    return pltpu.with_memory_space_constraint(value, pltpu.HBM)


def body(
    node_features,
    positions,
    species,
    energy_cotangent,
    pair_target,
    pair_source,
    pair_count,
    radial_weight,
    mix_weight,
    readout_weight,
    species_shift,
):
    atoms_here = node_features.shape[2]
    space, dp = lax.axis_size("space"), lax.axis_size("dp")
    scale = 1.0 / math.sqrt(atoms_here * space * dp)
    pair = [(i, i ^ 1) for i in range(space)]
    cross = [(i, ((i + 1) ^ 1) - 1) for i in range(1, space - 1)]
    onward = [(i, i + 2) for i in range(0, space - 2, 2)] + [(i, i - 2) for i in range(3, space, 2)]

    across = [(i, i ^ 1) for i in range(dp)]
    hbm = pl.BlockSpec(memory_space=pltpu.HBM)
    smem = pl.BlockSpec(memory_space=pltpu.SMEM)
    vmem = pl.BlockSpec(memory_space=pltpu.VMEM)
    f32, bf16 = jnp.float32, jnp.bfloat16
    small = (
        pair_target,
        pair_source,
        species,
        species_shift.reshape(1, NSPEC),
        energy_cotangent,
        radial_weight,
        mix_weight,
        readout_weight.reshape(1, CH),
    )
    near, far, *small = pl.pallas_call(
        split_kernel,
        out_shape=(jax.ShapeDtypeStruct((SLAB_ROWS, GROUP), f32),) * 2
        + tuple(jax.ShapeDtypeStruct(v.shape, v.dtype) for v in small),
        in_specs=[hbm] * (SMALL + 2),
        out_specs=(vmem,) * (SMALL + 2),
        scratch_shapes=[
            pltpu.VMEM((3, 1, atoms_here), f32),
            pltpu.SemaphoreType.DMA((SMALL + 3,)),
        ],
        compiler_params=pltpu.CompilerParams(vmem_limit_bytes=4 * 1024 * 1024),
        name="split",
    )(
        in_hbm(node_features),
        in_hbm(jnp.transpose(positions, (1, 0, 2))),
        *[in_hbm(v) for v in small],
    )
    targets, sources, species, shift, energy_grad, radial, mix, readout = small
    from_cross = lax.ppermute(far, "space", cross)
    from_pair = lax.ppermute(near, "space", pair)

    block_flops = 2 * CH * NB * NY * GROUP * GROUP
    local_factor, messages, keep = pl.pallas_call(
        local_kernel,
        out_shape=(
            jax.ShapeDtypeStruct((len(LOCAL), NB * GROUP, NY * GROUP), bf16),
            jax.ShapeDtypeStruct((2, CH, NY * GROUP), f32),
            jax.ShapeDtypeStruct((8, GROUP), f32),
        ),
        in_specs=[smem] + [vmem] * 5,
        out_specs=(vmem,) * 3,
        scratch_shapes=[
            pltpu.VMEM((2, CH, NB * GROUP), bf16),
            pltpu.VMEM((2, 3, GROUP, GROUP), f32),
        ],
        compiler_params=pltpu.CompilerParams(vmem_limit_bytes=16 * 1024 * 1024),
        cost_estimate=pl.CostEstimate(
            flops=len(LOCAL) * block_flops, bytes_accessed=14_000_000, transcendentals=0
        ),
        name="local_pairs",
    )(pair_count, targets, sources, radial, near, far)

    energy, spread, kept, sent, rest, grad_messages, halo_factor = call(
        functools.partial(node_kernel, scale),
        "node_stage",
        (
            near,
            far,
            from_pair,
            from_cross,
            messages,
            keep,
            species,
            shift,
            energy_grad,
            radial,
            mix,
            readout,
        ),
        (
            ((1, atoms_here), f32),
            ((CH, atoms_here), f32),
            ((HALF, CH), f32),
            ((HALF, CH), f32),
            ((8, CH), f32),
            ((2, CH, NY * GROUP), bf16),
            ((2, NB * GROUP, NY * GROUP), bf16),
        ),
        16,
        [pltpu.VMEM((2, CH, NB * GROUP), bf16), pltpu.VMEM((2, 3, GROUP, GROUP), f32)],
        2 * block_flops,
    )

    received = lax.ppermute(sent, "space", pair)
    halo_grad, share = call(
        halo_back_kernel,
        "halo_back",
        (halo_factor, grad_messages, from_pair, from_cross, radial),
        (((2 * CH, GROUP), f32), ((NB, CH), f32)),
        12,
        (),
        2 * block_flops,
    )
    received, share = lax.optimization_barrier((received, share))
    quarter, sent = call(
        quarter_kernel,
        "quarter",
        (kept, received),
        (((QUARTER, CH), f32), ((QUARTER, CH), f32)),
    )
    sent, grad_messages, halo_grad = lax.optimization_barrier((sent, grad_messages, halo_grad))
    received = lax.ppermute(sent, "dp", across)
    from_pair = lax.ppermute(halo_grad, "space", pair)
    own_grad, joined = call(
        functools.partial(own_back_kernel, scale),
        "own_back",
        (local_factor, grad_messages, near, far, radial, share, rest, spread),
        (((CH, atoms_here), f32), ((REST, CH), f32)),
        12,
        (),
        4 * block_flops,
    )
    (value,) = call(
        join_kernel, "join", (quarter, received, joined), (((QUARTER + REST, CH), f32),)
    )
    value, from_pair = lax.optimization_barrier((value, from_pair))
    *rounds, last = exchange_routes(space, dp)
    everyone = ("space", "dp")
    for turn, routes in enumerate(rounds):
        arrived = [lax.ppermute(value, everyone, route) for route in routes]
        if turn == 0:
            from_cross = lax.ppermute(from_pair[CH:], "space", onward)
        value = value + arrived[0]
        if len(arrived) == 3:
            value = value + (arrived[1] + arrived[2])
    arrived = [lax.ppermute(value, everyone, route) for route in last]
    value, from_cross, *arrived = lax.optimization_barrier((value, from_cross, *arrived))
    (value,) = call(
        gather_kernel,
        "gather",
        (value, *arrived),
        (((HALF + REST, CH), f32),),
    )
    feature_grad, energy = call(
        fold_kernel,
        "fold",
        (own_grad, from_pair, from_cross, energy),
        (((1, CH, atoms_here), f32), ((1, atoms_here), f32)),
    )
    radial_grad, mix_grad, readout_grad, shift_grad = call(
        finish_kernel,
        "finish",
        (value, lax.ppermute(value, "space", pair)),
        (((NB, CH), f32), ((MIX_ROWS, CH), f32), ((1, CH), f32), ((1, NSPEC), f32)),
    )
    return (
        energy,
        feature_grad,
        radial_grad,
        mix_grad,
        readout_grad.reshape(CH),
        shift_grad.reshape(NSPEC),
    )


def solution(mesh):
    return jax.shard_map(
        body,
        mesh=mesh,
        in_specs=(
            P("dp", None, "space"),
            P("dp", None, "space"),
            P("dp", "space"),
            P("dp", "space"),
            P("dp", "space"),
            P("dp", "space"),
            P("dp", "space"),
            P(),
            P(),
            P(),
            P(),
        ),
        out_specs=(P("dp", "space"), P("dp", None, "space"), P(), P(), P(), P()),
        check_vma=False,
    )
```

```python
import functools
import math

import jax
import jax.numpy as jnp
from jax import lax
from jax.experimental import pallas as pl
from jax.experimental.pallas import tpu as pltpu
from jax.sharding import PartitionSpec as P

CH = 128
NB = 8
NY = 9
NSPEC = 8
CELL_ATOMS = 64
HALO_CELLS = 2
GROUP = 2 * CELL_ATOMS
ROWS = 16
WIDTH = 256
CHUNKS = -(-NY * GROUP // WIDTH)

cutoff = 5.0
message_scale = 0.25

COS_COEFFS = (
    0.9999999998846169,
    -4.934802185771876,
    4.058711815779763,
    -1.3352602773967561,
    0.23532080049888648,
    -0.025785772074137014,
    0.0019043022864480008,
    -8.868331860867329e-05,
)
SINC_COEFFS = (
    0.9999999992502204,
    -1.6449339933418936,
    0.8117412468909989,
    -0.1907447263221115,
    0.02612742969685046,
    -0.0023157632409761065,
    0.00012580778956459784,
)

MIX_ROWS = 3 * CH
HALF = MIX_ROWS // 2
QUARTER = MIX_ROWS // 4
REST = 16
CELLS = 4 + 2 * HALO_CELLS
SMALL = 8
SLAB_ROWS = CH + 8


def polynomial(coeffs, x):
    total = coeffs[-1] * x + coeffs[-2]
    for c in coeffs[-3::-1]:
        total = total * x + c
    return total


def factor_rows(factor_ref, size, row, source, target, keep):
    dx = (target[0] - source[0]) * (1.0 / cutoff)
    dy = (target[1] - source[1]) * (1.0 / cutoff)
    dz = (target[2] - source[2]) * (1.0 / cutoff)
    xx, yy, zz = dx * dx, dy * dy, dz * dz
    square = xx + yy + zz
    inside = jnp.minimum(square, 1.0)
    gap = 1.0 - inside
    base = (gap * gap) * keep * polynomial(SINC_COEFFS, inside)
    twice_cos = polynomial([2.0 * c for c in COS_COEFFS], inside)
    raw = [base, twice_cos * base]
    for _ in range(NB - 2):
        raw.append(twice_cos * raw[-1] - raw[-2])
    radial = [value if b == 0 else value * (1.0 / (b + 1)) for b, value in enumerate(raw)]
    root_three = math.sqrt(3.0)
    root_fifteen = math.sqrt(15.0)
    root_five = math.sqrt(5.0)
    wide_x = root_fifteen * dx
    harmonic = [
        None,
        root_three * dx,
        root_three * dy,
        root_three * dz,
        wide_x * dy,
        (root_fifteen * dy) * dz,
        (0.5 * root_five) * (3.0 * zz - square),
        wide_x * dz,
        (0.5 * root_fifteen) * (xx - yy),
    ]
    for b in range(NB):
        rows = slice(b * size + row, b * size + row + ROWS)
        for y in range(NY):
            value = radial[b] if y == 0 else radial[b] * harmonic[y]
            factor_ref[rows, y * GROUP : (y + 1) * GROUP] = value.astype(jnp.bfloat16)


def column_to_row(column, size):
    wide = jnp.broadcast_to(column, (size, GROUP))
    at = lax.broadcasted_iota(jnp.int32, (size, GROUP), 0)
    lane = lax.broadcasted_iota(jnp.int32, (size, GROUP), 1)
    return jnp.sum(jnp.where(at == lane, wide, 0.0), axis=0, keepdims=True)


def split_kernel(*refs):
    features_ref, place_in_ref, *inputs = refs[: SMALL + 2]
    near_ref, far_ref, *outputs = refs[SMALL + 2 : 2 * SMALL + 4]
    place_ref, sems = refs[2 * SMALL + 4 :]
    core = lax.axis_index("space") % 2
    place_copy = pltpu.make_async_copy(place_in_ref, place_ref, sems.at[2])
    place_copy.start()
    copies = []
    for k, (ref, side) in enumerate(((near_ref, 1 - core), (far_ref, core))):
        at = pl.ds(pl.multiple_of(side * GROUP, GROUP), GROUP)
        copies.append(
            pltpu.make_async_copy(features_ref.at[0, :, at], ref.at[pl.ds(0, CH)], sems.at[k])
        )
    for k, (src, dst) in enumerate(zip(inputs, outputs)):
        copies.append(pltpu.make_async_copy(src, dst, sems.at[3 + k]))
    for copy in copies:
        copy.start()
    place_copy.wait()
    low, high = slice(GROUP), slice(GROUP, 2 * GROUP)
    filler = jnp.zeros((5, GROUP), jnp.float32)
    for ref, one, two in ((near_ref, high, low), (far_ref, low, high)):
        rows = [
            jnp.where(core == 0, place_ref[axis, :, one], place_ref[axis, :, two]) for axis in range(3)
        ]
        ref[CH:, :] = jnp.concatenate(rows + [filler], axis=0)
    for copy in copies:
        copy.wait()


def live_flags(count, pair_target, pair_source):
    size = (4 * CELLS, pair_target.shape[1])
    at = lax.broadcasted_iota(jnp.int32, size, 0)
    slot = lax.broadcasted_iota(jnp.int32, size, 1)
    hit = (pair_target * CELLS + pair_source == at) & (slot < count)
    return jnp.max(jnp.where(hit, message_scale, 0.0), axis=1, keepdims=True)


def keep_row(flags, t, low, high):
    lane = lax.broadcasted_iota(jnp.int32, (1, GROUP), 1)
    one, two = (2 * t) * CELLS + low, (2 * t + 1) * CELLS + high
    return jnp.where(lane < CELL_ATOMS, flags[one : one + 1], flags[two : two + 1])


def set_group(scaled_ref, features, weight_t):
    for b in range(NB):
        scaled_ref[:, b * GROUP : (b + 1) * GROUP] = (features * weight_t[:, b : b + 1]).astype(
            jnp.bfloat16
        )


def set_cell(scaled_ref, features, half, weight_t):
    first = lax.broadcasted_iota(jnp.int32, (CH, GROUP), 1) < CELL_ATOMS
    turned = pltpu.roll(features, CELL_ATOMS, 1)
    twice = jnp.where(first, features, turned) if half == 0 else jnp.where(first, turned, features)
    for k in range(NB // 2):
        weights = jnp.where(first, weight_t[:, 2 * k : 2 * k + 1], weight_t[:, 2 * k + 1 : 2 * k + 2])
        scaled_ref[:, k * GROUP : (k + 1) * GROUP] = (twice * weights).astype(jnp.bfloat16)


def set_place(place_ref, slab):
    place = slab[CH:].T
    for axis in range(3):
        place_ref[axis] = jnp.broadcast_to(place[:, axis : axis + 1], (GROUP, GROUP))


def fill_steps(factor_ref, size, source_of, keeps, target, diagonal=False):
    def step(row):
        keep = jnp.broadcast_to(keeps[row // CELL_ATOMS], (ROWS, GROUP))
        if diagonal:
            row_at = lax.broadcasted_iota(jnp.int32, (ROWS, GROUP), 0)
            lane_at = lax.broadcasted_iota(jnp.int32, (ROWS, GROUP), 1)
            keep = jnp.where(row_at + row == lane_at, 0.0, keep)
        factor_rows(factor_ref, size, row, source_of(row), target, keep)

    return [functools.partial(step, row) for row in range(0, size, ROWS)]


def rows_of(place_ref, start):
    return lambda row: [place_ref[axis, start + row : start + row + ROWS, :] for axis in range(3)]


def merged_rows(low_ref, low_start, high_ref, high_start):
    low, high = rows_of(low_ref, low_start), rows_of(high_ref, high_start)

    def rows(row):
        first = lax.broadcasted_iota(jnp.int32, (ROWS, GROUP), 1) < CELL_ATOMS
        return [jnp.where(first, one, two) for one, two in zip(low(row), high(row))]

    return rows


def product_steps(scaled_ref, factor_ref, totals, merged=False):
    def step(k):
        width = min(WIDTH, NY * GROUP - k * WIDTH)
        product = jnp.dot(
            scaled_ref[...],
            factor_ref[:, k * WIDTH : k * WIDTH + width],
            preferred_element_type=jnp.float32,
        )
        if merged:
            lane = lax.broadcasted_iota(jnp.int32, (CH, width), 1) % GROUP
            product = jnp.where(lane < CELL_ATOMS, product[:CH], product[CH:])
        totals[k] = product if totals[k] is None else totals[k] + product

    return [functools.partial(step, k) for k in range(CHUNKS)]


def interleave(one, two):
    done = 0
    for k, step in enumerate(one):
        step()
        upto = (k + 1) * len(two) // len(one)
        for other in two[done:upto]:
            other()
        done = upto


def local_kernel(
    count_ref,
    pair_target_ref,
    pair_source_ref,
    radial_ref,
    near_ref,
    far_ref,
    group_factor_ref,
    cell_factor_ref,
    messages_ref,
    keep_ref,
    group_ref,
    cell_ref,
    place_ref,
):
    even = lax.axis_index("space") % 2 == 0
    near, far = near_ref[...], far_ref[...]
    slabs = (jnp.where(even, far, near), jnp.where(even, near, far))
    targets = [[slab[CH + axis : CH + axis + 1] for axis in range(3)] for slab in slabs]
    flags = live_flags(count_ref[0, 0], pair_target_ref[...], pair_source_ref[...])
    weight_t = radial_ref[...].T
    for g in range(2):
        set_place(place_ref.at[g], slabs[g])
        set_group(group_ref.at[g], slabs[g][:CH], weight_t)
        set_cell(cell_ref.at[g], slabs[1 - g][:CH], g, weight_t)

    def fill_group(t):
        keeps = [keep_row(flags, t, cell, cell) for cell in (2 * t + 2, 2 * t + 3)]
        return fill_steps(
            group_factor_ref.at[t], GROUP, rows_of(place_ref.at[t], 0), keeps, targets[t], True
        )

    def fill_cell(t):
        cell = 4 - t
        source_of = rows_of(place_ref.at[1 - t], t * CELL_ATOMS)
        return fill_steps(
            cell_factor_ref.at[t], CELL_ATOMS, source_of, [keep_row(flags, t, cell, cell)], targets[t]
        )

    totals = [[None] * CHUNKS for _ in range(2)]
    for step in fill_cell(0):
        step()
    interleave(product_steps(cell_ref.at[0], cell_factor_ref.at[0], totals[0]), fill_group(0))
    interleave(product_steps(group_ref.at[0], group_factor_ref.at[0], totals[0]), fill_group(1))
    interleave(product_steps(group_ref.at[1], group_factor_ref.at[1], totals[1]), fill_cell(1))
    for step in product_steps(cell_ref.at[1], cell_factor_ref.at[1], totals[1]):
        step()
    for t in range(2):
        messages_ref[t] = jnp.concatenate(totals[t], axis=1)
    rows = [
        keep_row(flags, 0, 1, 1),
        keep_row(flags, 0, 0, 5),
        keep_row(flags, 1, 6, 6),
        keep_row(flags, 1, 2, 7),
    ]
    keep_ref[...] = jnp.concatenate(rows + [jnp.zeros((4, GROUP), jnp.float32)], axis=0)


def node_kernel(
    scale,
    near_ref,
    far_ref,
    from_pair_ref,
    from_cross_ref,
    messages_ref,
    keep_ref,
    species_ref,
    shift_ref,
    energy_grad_ref,
    radial_ref,
    mix_ref,
    readout_ref,
    energy_ref,
    spread_ref,
    kept_ref,
    sent_ref,
    rest_ref,
    grad_messages_ref,
    cell_factor_ref,
    merged_factor_ref,
    cell_ref,
    merged_ref,
    place_ref,
):
    even = lax.axis_index("space") % 2 == 0
    weight_t = radial_ref[...].T
    near, far = near_ref[...], far_ref[...]
    from_pair, from_cross = from_pair_ref[...], from_cross_ref[...]
    slabs = (
        jnp.where(even, from_cross, from_pair),
        jnp.where(even, far, near),
        jnp.where(even, near, far),
        jnp.where(even, from_pair, from_cross),
    )
    targets = [[slab[CH + axis : CH + axis + 1] for axis in range(3)] for slab in slabs[1:3]]

    for g in range(4):
        set_place(place_ref.at[g], slabs[g])
    for t in range(2):
        set_cell(cell_ref.at[t], slabs[3 * t][:CH], 1 - t, weight_t)
        set_cell(merged_ref.at[t, pl.ds(0, CH)], slabs[t][:CH], 0, weight_t)
        set_cell(merged_ref.at[t, pl.ds(CH, CH)], slabs[t + 2][:CH], 1, weight_t)

    def fill_cell(t):
        source_of = rows_of(place_ref.at[3 * t], (1 - t) * CELL_ATOMS)
        keeps = [keep_ref[2 * t : 2 * t + 1, :]]
        return fill_steps(cell_factor_ref.at[t], CELL_ATOMS, source_of, keeps, targets[t])

    def fill_merged(t):
        source_of = merged_rows(place_ref.at[t], 0, place_ref.at[t + 2], CELL_ATOMS)
        keeps = [keep_ref[2 * t + 1 : 2 * t + 2, :]]
        return fill_steps(merged_factor_ref.at[t], CELL_ATOMS, source_of, keeps, targets[t])

    totals = [
        [messages_ref[t, :, k * WIDTH : min((k + 1) * WIDTH, NY * GROUP)] for k in range(CHUNKS)]
        for t in range(2)
    ]

    def add_cell(t):
        return product_steps(cell_ref.at[t], cell_factor_ref.at[t], totals[t])

    def add_merged(t):
        return product_steps(merged_ref.at[t], merged_factor_ref.at[t], totals[t], True)

    readout = jnp.broadcast_to(readout_ref[...], (8, CH)).T[:, :1]
    mix = mix_ref[...]
    mix_t = mix.astype(jnp.float32).T.astype(jnp.bfloat16)

    def node_stage(t, messages):
        at = slice(t * GROUP, (t + 1) * GROUP)
        part = [messages[:, y * GROUP : (y + 1) * GROUP] for y in range(NY)]
        invariants = jnp.concatenate(
            [
                part[0],
                0.5 * (part[1] * part[1] + part[2] * part[2] + part[3] * part[3]),
                0.5
                * (
                    part[4] * part[4]
                    + part[5] * part[5]
                    + part[6] * part[6]
                    + part[7] * part[7]
                    + part[8] * part[8]
                ),
            ],
            axis=0,
        ).astype(jnp.bfloat16)
        preact = jnp.dot(mix_t, invariants, preferred_element_type=jnp.float32)
        gating = jax.nn.sigmoid(preact)
        updated = slabs[t + 1][:CH] + preact * gating
        energy_grad = energy_grad_ref[:, at]
        kinds = species_ref[:, at]
        shifts = jnp.zeros((1, GROUP), jnp.float32)
        for n in range(NSPEC):
            shifts = jnp.where(kinds == n, shift_ref[:, n : n + 1], shifts)
        energy_ref[:, at] = jnp.sum(updated * readout, axis=0, keepdims=True) + shifts
        spread = readout * energy_grad
        spread_ref[:, at] = spread
        grad_pre = (spread * gating * (1.0 + preact * (1.0 - gating))).astype(jnp.bfloat16)
        grad_mix = lax.dot_general(
            invariants, grad_pre, (((1,), (1,)), ((), ())), preferred_element_type=jnp.float32
        )
        grad_inv = jnp.dot(mix, grad_pre, preferred_element_type=jnp.float32)
        grad_messages_ref[t] = jnp.concatenate(
            [grad_inv[:CH]]
            + [grad_inv[CH : 2 * CH] * part[y] for y in range(1, 4)]
            + [grad_inv[2 * CH :] * part[y] for y in range(4, NY)],
            axis=1,
        ).astype(jnp.bfloat16)
        return updated * energy_grad, grad_mix

    for step in fill_cell(0):
        step()
    interleave(add_cell(0), fill_merged(0))
    interleave(add_merged(0), fill_cell(1))
    interleave(add_cell(1), fill_merged(1))
    out_low, mix_low = node_stage(0, jnp.concatenate(totals[0], axis=1))
    for step in add_merged(1):
        step()
    out_high, mix_high = node_stage(1, jnp.concatenate(totals[1], axis=1))

    grad_mix = (mix_low + mix_high) * scale
    kept_ref[...] = jnp.where(even, grad_mix[:HALF], grad_mix[HALF:])
    sent_ref[...] = jnp.where(even, grad_mix[HALF:], grad_mix[:HALF])
    readout_row = column_to_row(jnp.sum(out_low + out_high, axis=1, keepdims=True), CH)
    here = lax.broadcasted_iota(jnp.int32, (NSPEC, 2 * GROUP), 0) == species_ref[...]
    by_kind = jnp.sum(jnp.where(here, energy_grad_ref[...], 0.0), axis=1, keepdims=True)
    rest_ref[...] = jnp.concatenate(
        [readout_row, column_to_row(by_kind, NSPEC), jnp.zeros((6, CH), jnp.float32)], axis=0
    )


def back(factor, grad_messages):
    return lax.dot_general(
        factor, grad_messages, (((1,), (1,)), ((), ())), preferred_element_type=jnp.float32
    )


def source_grads(total, features_t, weight):
    size = features_t.shape[0]
    grad_t = None
    radial = []
    for b in range(NB):
        piece = total[b * size : (b + 1) * size]
        term = piece * weight[b : b + 1, :]
        grad_t = term if grad_t is None else grad_t + term
        radial.append(jnp.sum(piece * features_t, axis=0, keepdims=True))
    return grad_t, jnp.concatenate(radial, axis=0)


def halo_back_kernel(
    cell_factor_ref,
    merged_factor_ref,
    grad_messages_ref,
    near_ref,
    far_ref,
    from_pair_ref,
    from_cross_ref,
    radial_ref,
    sent_ref,
    extra_ref,
    share_ref,
):
    even = lax.axis_index("space") % 2 == 0
    weight = radial_ref[...]
    near, far = near_ref[:CH, :], far_ref[:CH, :]
    from_pair, from_cross = from_pair_ref[:CH, :], from_cross_ref[:CH, :]
    features_t = [
        jnp.where(even, one, two).T
        for one, two in ((from_cross, from_pair), (far, near), (near, far), (from_pair, from_cross))
    ]
    first = lax.broadcasted_iota(jnp.int32, (CH, NY * GROUP), 1) % GROUP < CELL_ATOMS
    low, high = slice(CELL_ATOMS), slice(CELL_ATOMS, GROUP)
    share = None
    grads = {}
    for t in range(2):
        grad = grad_messages_ref[t]
        none = jnp.zeros_like(grad)
        both = jnp.concatenate([jnp.where(first, grad, none), jnp.where(first, none, grad)], axis=0)
        merged = back(merged_factor_ref[t], both)
        pieces = (
            (3 * t, 1 - t, back(cell_factor_ref[t], grad)),
            (t, 0, merged[:, :CH]),
            (t + 2, 1, merged[:, CH:]),
        )
        for g, half, total in pieces:
            grads[g, half], part = source_grads(total, features_t[g][(low, high)[half]], weight)
            share = part if share is None else share + part
    grad_before = jnp.concatenate([grads[0, 0], grads[0, 1]], axis=0).T
    grad_after = jnp.concatenate([grads[3, 0], grads[3, 1]], axis=0).T
    sent_ref[:CH, :] = jnp.where(even, grad_after, grad_before)
    sent_ref[CH:, :] = jnp.where(even, grad_before, grad_after)
    extra_ref[low, :] = grads[1, 0]
    extra_ref[high, :] = grads[2, 1]
    share_ref[...] = share


def own_back_kernel(
    scale,
    group_factor_ref,
    cell_factor_ref,
    grad_messages_ref,
    near_ref,
    far_ref,
    radial_ref,
    extra_ref,
    share_ref,
    rest_ref,
    spread_ref,
    own_grad_ref,
    joined_ref,
):
    even = lax.axis_index("space") % 2 == 0
    weight = radial_ref[...]
    near, far = near_ref[:CH, :], far_ref[:CH, :]
    share = share_ref[...]
    low, high = slice(CELL_ATOMS), slice(CELL_ATOMS, GROUP)
    for t, features in enumerate((jnp.where(even, far, near), jnp.where(even, near, far))):
        features_t = features.T
        total = back(group_factor_ref[t], grad_messages_ref[t])
        grad, part = source_grads(total, features_t, weight)
        inner, outer = (high, low) if t == 0 else (low, high)
        total = back(cell_factor_ref[1 - t], grad_messages_ref[1 - t])
        one, more = source_grads(total, features_t[inner], weight)
        two = extra_ref[outer, :]
        grad = (grad + jnp.concatenate([two, one] if t == 0 else [one, two], axis=0)).T
        at = slice(t * GROUP, (t + 1) * GROUP)
        own_grad_ref[:, at] = spread_ref[:, at] + grad
        share = share + part + more
    joined_ref[:NB, :] = share * scale
    joined_ref[NB:, :] = rest_ref[...] * scale


def quarter_kernel(kept_ref, received_ref, keep_ref, send_ref):
    first = lax.axis_index("dp") % 2 == 0
    low = kept_ref[:QUARTER, :] + received_ref[:QUARTER, :]
    high = kept_ref[QUARTER:, :] + received_ref[QUARTER:, :]
    keep_ref[...] = jnp.where(first, low, high)
    send_ref[...] = jnp.where(first, high, low)


def join_kernel(kept_ref, received_ref, rest_ref, out_ref):
    out_ref[:QUARTER, :] = kept_ref[...] + received_ref[...]
    out_ref[QUARTER:, :] = rest_ref[...]


def gather_kernel(mine_ref, along_ref, other_ref, both_ref, out_ref):
    first = lax.axis_index("dp") % 2 == 0
    at, rest = slice(QUARTER), slice(QUARTER, QUARTER + REST)
    mine = mine_ref[at, :] + along_ref[at, :]
    other = other_ref[at, :] + both_ref[at, :]
    out_ref[:QUARTER, :] = jnp.where(first, mine, other)
    out_ref[QUARTER:HALF, :] = jnp.where(first, other, mine)
    out_ref[HALF:, :] = (mine_ref[rest, :] + along_ref[rest, :]) + (other_ref[rest, :] + both_ref[rest, :])


def fold_kernel(own_ref, from_pair_ref, from_cross_ref, energy_in_ref, grad_ref, energy_ref):
    even = lax.axis_index("space") % 2 == 0
    pair = from_pair_ref[:CH, :]
    cross = from_cross_ref[...]
    grad_ref[0, :, :GROUP] = own_ref[:, :GROUP] + jnp.where(even, cross, pair)
    grad_ref[0, :, GROUP:] = own_ref[:, GROUP:] + jnp.where(even, pair, cross)
    energy_ref[...] = energy_in_ref[...]


def finish_kernel(mine_ref, other_ref, radial_ref, mix_ref, readout_ref, shift_ref):
    even = lax.axis_index("space") % 2 == 0
    mine, other = mine_ref[:HALF, :], other_ref[:HALF, :]
    mix_ref[:HALF, :] = jnp.where(even, mine, other)
    mix_ref[HALF:, :] = jnp.where(even, other, mine)
    rest = mine_ref[HALF:, :] + other_ref[HALF:, :]
    radial_ref[...] = rest[:NB]
    readout_ref[...] = rest[NB : NB + 1]
    shift_ref[...] = rest[NB + 1 : NB + 2, :NSPEC]


def exchange_routes(space, dp):
    steps = [(1 << k, 0) for k in range(1, space.bit_length() - 1)]
    steps += [(0, 1 << k) for k in range(1, dp.bit_length() - 1)]
    orders = [[steps[(k + 1 - core) % len(steps)] for k in range(len(steps))] for core in range(2)]
    places = list(range(len(steps)))
    groups = [places[k : k + 2] for k in range(0, len(steps) - 1, 2)] + [places[-1:]]
    if len(groups[-2:]) == 2 and groups[-2][-1] == groups[-1][0]:
        groups[-2:] = [groups[-2][:1], groups[-1]]
    rounds = []
    for group in groups:
        last = group is groups[-1]
        kinds = [group[:1]] if len(group) == 1 and not last else [group[:1], group[1:], group]
        routes = []
        for n, kind in enumerate(kinds):
            route = []
            for s in range(space):
                across = along = 0
                for k in kind:
                    step = orders[s % 2][k]
                    across, along = across ^ step[0], along ^ step[1]
                if last and n:
                    along ^= 1
                for d in range(dp):
                    route.append((s * dp + d, (s ^ across) * dp + (d ^ along)))
            routes.append(route)
        rounds.append(routes)
    return rounds


def call(kernel, name, inputs, outputs, mib=4, scratch=(), flops=0):
    vmem = pl.BlockSpec(memory_space=pltpu.VMEM)
    shapes = tuple(jax.ShapeDtypeStruct(shape, kind) for shape, kind in outputs)
    moved = sum(math.prod(v.shape) * v.dtype.itemsize for v in (*inputs, *shapes))
    return pl.pallas_call(
        kernel,
        out_shape=shapes,
        in_specs=[vmem] * len(inputs),
        out_specs=(vmem,) * len(shapes),
        scratch_shapes=scratch,
        compiler_params=pltpu.CompilerParams(vmem_limit_bytes=mib * 1024 * 1024),
        cost_estimate=pl.CostEstimate(flops=flops, bytes_accessed=moved, transcendentals=0),
        name=name,
    )(*inputs)


def in_hbm(value):
    return pltpu.with_memory_space_constraint(value, pltpu.HBM)


def body(
    node_features,
    positions,
    species,
    energy_cotangent,
    pair_target,
    pair_source,
    pair_count,
    radial_weight,
    mix_weight,
    readout_weight,
    species_shift,
):
    atoms_here = node_features.shape[2]
    space, dp = lax.axis_size("space"), lax.axis_size("dp")
    scale = 1.0 / math.sqrt(atoms_here * space * dp)
    pair = [(i, i ^ 1) for i in range(space)]
    cross = [(i, ((i + 1) ^ 1) - 1) for i in range(1, space - 1)]
    onward = [(i, i + 2) for i in range(0, space - 2, 2)] + [(i, i - 2) for i in range(3, space, 2)]

    across = [(i, i ^ 1) for i in range(dp)]
    hbm = pl.BlockSpec(memory_space=pltpu.HBM)
    smem = pl.BlockSpec(memory_space=pltpu.SMEM)
    vmem = pl.BlockSpec(memory_space=pltpu.VMEM)
    f32, bf16 = jnp.float32, jnp.bfloat16
    small = (
        pair_target,
        pair_source,
        species,
        species_shift.reshape(1, NSPEC),
        energy_cotangent,
        radial_weight,
        mix_weight,
        readout_weight.reshape(1, CH),
    )
    near, far, *small = pl.pallas_call(
        split_kernel,
        out_shape=(jax.ShapeDtypeStruct((SLAB_ROWS, GROUP), f32),) * 2
        + tuple(jax.ShapeDtypeStruct(v.shape, v.dtype) for v in small),
        in_specs=[hbm] * (SMALL + 2),
        out_specs=(vmem,) * (SMALL + 2),
        scratch_shapes=[
            pltpu.VMEM((3, 1, atoms_here), f32),
            pltpu.SemaphoreType.DMA((SMALL + 3,)),
        ],
        compiler_params=pltpu.CompilerParams(vmem_limit_bytes=4 * 1024 * 1024),
        name="split",
    )(
        in_hbm(node_features),
        in_hbm(jnp.transpose(positions, (1, 0, 2))),
        *[in_hbm(v) for v in small],
    )
    targets, sources, species, shift, energy_grad, radial, mix, readout = small
    from_cross = lax.ppermute(far, "space", cross)
    from_pair = lax.ppermute(near, "space", pair)

    block_flops = 2 * CH * NB * NY * GROUP * GROUP
    group_factor, cell_factor, messages, keep = pl.pallas_call(
        local_kernel,
        out_shape=(
            jax.ShapeDtypeStruct((2, NB * GROUP, NY * GROUP), bf16),
            jax.ShapeDtypeStruct((2, NB * CELL_ATOMS, NY * GROUP), bf16),
            jax.ShapeDtypeStruct((2, CH, NY * GROUP), f32),
            jax.ShapeDtypeStruct((8, GROUP), f32),
        ),
        in_specs=[smem] + [vmem] * 5,
        out_specs=(vmem,) * 4,
        scratch_shapes=[
            pltpu.VMEM((2, CH, NB * GROUP), bf16),
            pltpu.VMEM((2, CH, NB * CELL_ATOMS), bf16),
            pltpu.VMEM((2, 3, GROUP, GROUP), f32),
        ],
        compiler_params=pltpu.CompilerParams(vmem_limit_bytes=16 * 1024 * 1024),
        cost_estimate=pl.CostEstimate(
            flops=3 * block_flops, bytes_accessed=11_000_000, transcendentals=0
        ),
        name="local_pairs",
    )(pair_count, targets, sources, radial, near, far)

    energy, spread, kept, sent, rest, grad_messages, halo_factor, merged_factor = call(
        functools.partial(node_kernel, scale),
        "node_stage",
        (
            near,
            far,
            from_pair,
            from_cross,
            messages,
            keep,
            species,
            shift,
            energy_grad,
            radial,
            mix,
            readout,
        ),
        (
            ((1, atoms_here), f32),
            ((CH, atoms_here), f32),
            ((HALF, CH), f32),
            ((HALF, CH), f32),
            ((8, CH), f32),
            ((2, CH, NY * GROUP), bf16),
            ((2, NB * CELL_ATOMS, NY * GROUP), bf16),
            ((2, NB * CELL_ATOMS, NY * GROUP), bf16),
        ),
        16,
        [
            pltpu.VMEM((2, CH, NB * CELL_ATOMS), bf16),
            pltpu.VMEM((2, 2 * CH, NB * CELL_ATOMS), bf16),
            pltpu.VMEM((4, 3, GROUP, GROUP), f32),
        ],
        2 * block_flops,
    )

    received = lax.ppermute(sent, "space", pair)
    halo_grad, extra, share = call(
        halo_back_kernel,
        "halo_back",
        (
            halo_factor,
            merged_factor,
            grad_messages,
            near,
            far,
            from_pair,
            from_cross,
            radial,
        ),
        (((2 * CH, GROUP), f32), ((GROUP, CH), f32), ((NB, CH), f32)),
        12,
        (),
        2 * block_flops,
    )
    received, share = lax.optimization_barrier((received, share))
    quarter, sent = call(
        quarter_kernel,
        "quarter",
        (kept, received),
        (((QUARTER, CH), f32), ((QUARTER, CH), f32)),
    )
    sent, grad_messages, halo_grad = lax.optimization_barrier((sent, grad_messages, halo_grad))
    received = lax.ppermute(sent, "dp", across)
    from_pair = lax.ppermute(halo_grad, "space", pair)
    own_grad, joined = call(
        functools.partial(own_back_kernel, scale),
        "own_back",
        (
            group_factor,
            cell_factor,
            grad_messages,
            near,
            far,
            radial,
            extra,
            share,
            rest,
            spread,
        ),
        (((CH, atoms_here), f32), ((REST, CH), f32)),
        12,
        (),
        3 * block_flops,
    )
    (value,) = call(
        join_kernel, "join", (quarter, received, joined), (((QUARTER + REST, CH), f32),)
    )
    value, from_pair = lax.optimization_barrier((value, from_pair))
    *rounds, last = exchange_routes(space, dp)
    everyone = ("space", "dp")
    for turn, routes in enumerate(rounds):
        arrived = [lax.ppermute(value, everyone, route) for route in routes]
        if turn == 0:
            from_cross = lax.ppermute(from_pair[CH:], "space", onward)
        value = value + arrived[0]
        if len(arrived) == 3:
            value = value + (arrived[1] + arrived[2])
    arrived = [lax.ppermute(value, everyone, route) for route in last]
    value, from_cross, *arrived = lax.optimization_barrier((value, from_cross, *arrived))
    (value,) = call(
        gather_kernel,
        "gather",
        (value, *arrived),
        (((HALF + REST, CH), f32),),
    )
    feature_grad, energy = call(
        fold_kernel,
        "fold",
        (own_grad, from_pair, from_cross, energy),
        (((1, CH, atoms_here), f32), ((1, atoms_here), f32)),
    )
    radial_grad, mix_grad, readout_grad, shift_grad = call(
        finish_kernel,
        "finish",
        (value, lax.ppermute(value, "space", pair)),
        (((NB, CH), f32), ((MIX_ROWS, CH), f32), ((1, CH), f32), ((1, NSPEC), f32)),
    )
    return (
        energy,
        feature_grad,
        radial_grad,
        mix_grad,
        readout_grad.reshape(CH),
        shift_grad.reshape(NSPEC),
    )


def solution(mesh):
    return jax.shard_map(
        body,
        mesh=mesh,
        in_specs=(
            P("dp", None, "space"),
            P("dp", None, "space"),
            P("dp", "space"),
            P("dp", "space"),
            P("dp", "space"),
            P("dp", "space"),
            P("dp", "space"),
            P(),
            P(),
            P(),
            P(),
        ),
        out_specs=(P("dp", "space"), P("dp", None, "space"), P(), P(), P(), P()),
        check_vma=False,
    )
```

```python
import functools
import math

import jax
import jax.numpy as jnp
from jax import lax
from jax.experimental import pallas as pl
from jax.experimental.pallas import tpu as pltpu
from jax.sharding import PartitionSpec as P

CH = 128
NB = 8
NY = 9
NSPEC = 8
CELL_ATOMS = 64
HALO_CELLS = 2
GROUP = 2 * CELL_ATOMS
ROWS = 16
WIDTH = 256
CHUNKS = -(-NY * GROUP // WIDTH)

cutoff = 5.0
message_scale = 0.25

COS_COEFFS = (
    0.9999999998846169,
    -4.934802185771876,
    4.058711815779763,
    -1.3352602773967561,
    0.23532080049888648,
    -0.025785772074137014,
    0.0019043022864480008,
    -8.868331860867329e-05,
)
SINC_COEFFS = (
    0.9999999992502204,
    -1.6449339933418936,
    0.8117412468909989,
    -0.1907447263221115,
    0.02612742969685046,
    -0.0023157632409761065,
    0.00012580778956459784,
)

MIX_ROWS = 3 * CH
HALF = MIX_ROWS // 2
QUARTER = MIX_ROWS // 4
REST = 16
CELLS = 4 + 2 * HALO_CELLS
SMALL = 8
SLAB_ROWS = CH + 8


def polynomial(coeffs, x):
    total = coeffs[-1] * x + coeffs[-2]
    for c in coeffs[-3::-1]:
        total = total * x + c
    return total


def factor_rows(factor_ref, size, row, source, target, keep):
    dx = (target[0] - source[0]) * (1.0 / cutoff)
    dy = (target[1] - source[1]) * (1.0 / cutoff)
    dz = (target[2] - source[2]) * (1.0 / cutoff)
    xx, yy, zz = dx * dx, dy * dy, dz * dz
    square = xx + yy + zz
    inside = jnp.minimum(square, 1.0)
    gap = 1.0 - inside
    base = (gap * gap) * keep * polynomial(SINC_COEFFS, inside)
    twice_cos = polynomial([2.0 * c for c in COS_COEFFS], inside)
    raw = [base, twice_cos * base]
    for _ in range(NB - 2):
        raw.append(twice_cos * raw[-1] - raw[-2])
    radial = [value if b == 0 else value * (1.0 / (b + 1)) for b, value in enumerate(raw)]
    root_three = math.sqrt(3.0)
    root_fifteen = math.sqrt(15.0)
    root_five = math.sqrt(5.0)
    wide_x = root_fifteen * dx
    harmonic = [
        None,
        root_three * dx,
        root_three * dy,
        root_three * dz,
        wide_x * dy,
        (root_fifteen * dy) * dz,
        (0.5 * root_five) * (3.0 * zz - square),
        wide_x * dz,
        (0.5 * root_fifteen) * (xx - yy),
    ]
    for b in range(NB):
        rows = slice(b * size + row, b * size + row + ROWS)
        for y in range(NY):
            value = radial[b] if y == 0 else radial[b] * harmonic[y]
            factor_ref[rows, y * GROUP : (y + 1) * GROUP] = value.astype(jnp.bfloat16)


def column_to_row(column, size):
    wide = jnp.broadcast_to(column, (size, GROUP))
    at = lax.broadcasted_iota(jnp.int32, (size, GROUP), 0)
    lane = lax.broadcasted_iota(jnp.int32, (size, GROUP), 1)
    return jnp.sum(jnp.where(at == lane, wide, 0.0), axis=0, keepdims=True)


def split_kernel(*refs):
    features_ref, place_in_ref, *inputs = refs[: SMALL + 2]
    near_ref, far_ref, *outputs = refs[SMALL + 2 : 2 * SMALL + 4]
    place_ref, sems = refs[2 * SMALL + 4 :]
    core = lax.axis_index("space") % 2
    place_copy = pltpu.make_async_copy(place_in_ref, place_ref, sems.at[2])
    place_copy.start()
    copies = []
    for k, (ref, side) in enumerate(((near_ref, 1 - core), (far_ref, core))):
        at = pl.ds(pl.multiple_of(side * GROUP, GROUP), GROUP)
        copies.append(
            pltpu.make_async_copy(features_ref.at[0, :, at], ref.at[pl.ds(0, CH)], sems.at[k])
        )
    for k, (src, dst) in enumerate(zip(inputs, outputs)):
        copies.append(pltpu.make_async_copy(src, dst, sems.at[3 + k]))
    for copy in copies:
        copy.start()
    place_copy.wait()
    low, high = slice(GROUP), slice(GROUP, 2 * GROUP)
    filler = jnp.zeros((5, GROUP), jnp.float32)
    for ref, one, two in ((near_ref, high, low), (far_ref, low, high)):
        rows = [
            jnp.where(core == 0, place_ref[axis, :, one], place_ref[axis, :, two]) for axis in range(3)
        ]
        ref[CH:, :] = jnp.concatenate(rows + [filler], axis=0)
    for copy in copies:
        copy.wait()


def live_flags(count, pair_target, pair_source):
    size = (4 * CELLS, pair_target.shape[1])
    at = lax.broadcasted_iota(jnp.int32, size, 0)
    slot = lax.broadcasted_iota(jnp.int32, size, 1)
    hit = (pair_target * CELLS + pair_source == at) & (slot < count)
    return jnp.max(jnp.where(hit, message_scale, 0.0), axis=1, keepdims=True)


def keep_row(flags, t, low, high):
    lane = lax.broadcasted_iota(jnp.int32, (1, GROUP), 1)
    one, two = (2 * t) * CELLS + low, (2 * t + 1) * CELLS + high
    return jnp.where(lane < CELL_ATOMS, flags[one : one + 1], flags[two : two + 1])


def set_group(scaled_ref, features, weight_t):
    for b in range(NB):
        scaled_ref[:, b * GROUP : (b + 1) * GROUP] = (features * weight_t[:, b : b + 1]).astype(
            jnp.bfloat16
        )


def set_cell(scaled_ref, features, half, weight_t):
    first = lax.broadcasted_iota(jnp.int32, (CH, GROUP), 1) < CELL_ATOMS
    turned = pltpu.roll(features, CELL_ATOMS, 1)
    twice = jnp.where(first, features, turned) if half == 0 else jnp.where(first, turned, features)
    for k in range(NB // 2):
        weights = jnp.where(first, weight_t[:, 2 * k : 2 * k + 1], weight_t[:, 2 * k + 1 : 2 * k + 2])
        scaled_ref[:, k * GROUP : (k + 1) * GROUP] = (twice * weights).astype(jnp.bfloat16)


def set_place(place_ref, slab):
    place = slab[CH:].T
    for axis in range(3):
        place_ref[axis] = jnp.broadcast_to(place[:, axis : axis + 1], (GROUP, GROUP))


def fill_steps(factor_ref, size, source_of, keeps, target, diagonal=False):
    def step(row):
        keep = jnp.broadcast_to(keeps[row // CELL_ATOMS], (ROWS, GROUP))
        if diagonal:
            row_at = lax.broadcasted_iota(jnp.int32, (ROWS, GROUP), 0)
            lane_at = lax.broadcasted_iota(jnp.int32, (ROWS, GROUP), 1)
            keep = jnp.where(row_at + row == lane_at, 0.0, keep)
        factor_rows(factor_ref, size, row, source_of(row), target, keep)

    return [functools.partial(step, row) for row in range(0, size, ROWS)]


def rows_of(place_ref, start):
    return lambda row: [place_ref[axis, start + row : start + row + ROWS, :] for axis in range(3)]


def merged_rows(low_ref, low_start, high_ref, high_start):
    low, high = rows_of(low_ref, low_start), rows_of(high_ref, high_start)

    def rows(row):
        first = lax.broadcasted_iota(jnp.int32, (ROWS, GROUP), 1) < CELL_ATOMS
        return [jnp.where(first, one, two) for one, two in zip(low(row), high(row))]

    return rows


def product_steps(scaled_ref, factor_ref, totals, merged=False):
    def step(k):
        width = min(WIDTH, NY * GROUP - k * WIDTH)
        product = jnp.dot(
            scaled_ref[...],
            factor_ref[:, k * WIDTH : k * WIDTH + width],
            preferred_element_type=jnp.float32,
        )
        if merged:
            lane = lax.broadcasted_iota(jnp.int32, (CH, width), 1) % GROUP
            product = jnp.where(lane < CELL_ATOMS, product[:CH], product[CH:])
        totals[k] = product if totals[k] is None else totals[k] + product

    return [functools.partial(step, k) for k in range(CHUNKS)]


def interleave(one, two):
    done = 0
    for k, step in enumerate(one):
        step()
        upto = (k + 1) * len(two) // len(one)
        for other in two[done:upto]:
            other()
        done = upto


def local_kernel(
    count_ref,
    pair_target_ref,
    pair_source_ref,
    radial_ref,
    near_ref,
    far_ref,
    group_factor_ref,
    cell_factor_ref,
    messages_ref,
    keep_ref,
    place_ref,
    group_ref,
    cell_ref,
):
    even = lax.axis_index("space") % 2 == 0
    near, far = near_ref[...], far_ref[...]
    slabs = (jnp.where(even, far, near), jnp.where(even, near, far))
    targets = [[slab[CH + axis : CH + axis + 1] for axis in range(3)] for slab in slabs]
    flags = live_flags(count_ref[0, 0], pair_target_ref[...], pair_source_ref[...])
    weight_t = radial_ref[...].T
    for g in range(2):
        set_place(place_ref.at[g], slabs[g])
        set_group(group_ref.at[g], slabs[g][:CH], weight_t)
        set_cell(cell_ref.at[g], slabs[1 - g][:CH], g, weight_t)

    def fill_group(t):
        keeps = [keep_row(flags, t, cell, cell) for cell in (2 * t + 2, 2 * t + 3)]
        return fill_steps(
            group_factor_ref.at[t], GROUP, rows_of(place_ref.at[t], 0), keeps, targets[t], True
        )

    def fill_cell(t):
        cell = 4 - t
        source_of = rows_of(place_ref.at[1 - t], t * CELL_ATOMS)
        return fill_steps(
            cell_factor_ref.at[t], CELL_ATOMS, source_of, [keep_row(flags, t, cell, cell)], targets[t]
        )

    totals = [[None] * CHUNKS for _ in range(2)]
    for step in fill_cell(0):
        step()
    interleave(product_steps(cell_ref.at[0], cell_factor_ref.at[0], totals[0]), fill_group(0))
    interleave(product_steps(group_ref.at[0], group_factor_ref.at[0], totals[0]), fill_group(1))
    interleave(product_steps(group_ref.at[1], group_factor_ref.at[1], totals[1]), fill_cell(1))
    for step in product_steps(cell_ref.at[1], cell_factor_ref.at[1], totals[1]):
        step()
    for t in range(2):
        messages_ref[t] = jnp.concatenate(totals[t], axis=1)
    rows = [
        keep_row(flags, 0, 1, 1),
        keep_row(flags, 0, 0, 5),
        keep_row(flags, 1, 6, 6),
        keep_row(flags, 1, 2, 7),
    ]
    keep_ref[...] = jnp.concatenate(rows + [jnp.zeros((4, GROUP), jnp.float32)], axis=0)


def node_kernel(
    scale,
    near_ref,
    far_ref,
    from_pair_ref,
    from_cross_ref,
    messages_ref,
    keep_ref,
    own_place_ref,
    species_ref,
    shift_ref,
    energy_grad_ref,
    radial_ref,
    mix_ref,
    readout_ref,
    energy_ref,
    spread_ref,
    kept_ref,
    sent_ref,
    rest_ref,
    grad_messages_ref,
    cell_factor_ref,
    merged_factor_ref,
    cell_ref,
    merged_ref,
    place_ref,
):
    even = lax.axis_index("space") % 2 == 0
    weight_t = radial_ref[...].T
    near, far = near_ref[...], far_ref[...]
    from_pair, from_cross = from_pair_ref[...], from_cross_ref[...]
    slabs = (
        jnp.where(even, from_cross, from_pair),
        jnp.where(even, far, near),
        jnp.where(even, near, far),
        jnp.where(even, from_pair, from_cross),
    )
    targets = [[slab[CH + axis : CH + axis + 1] for axis in range(3)] for slab in slabs[1:3]]

    for t in range(2):
        set_place(place_ref.at[t], slabs[3 * t])
        set_cell(cell_ref.at[t], slabs[3 * t][:CH], 1 - t, weight_t)
        set_cell(merged_ref.at[t, pl.ds(0, CH)], slabs[t][:CH], 0, weight_t)
        set_cell(merged_ref.at[t, pl.ds(CH, CH)], slabs[t + 2][:CH], 1, weight_t)

    def fill_cell(t):
        source_of = rows_of(place_ref.at[t], (1 - t) * CELL_ATOMS)
        keeps = [keep_ref[2 * t : 2 * t + 1, :]]
        return fill_steps(cell_factor_ref.at[t], CELL_ATOMS, source_of, keeps, targets[t])

    def fill_merged(t):
        places = (place_ref.at[0], own_place_ref.at[0], own_place_ref.at[1], place_ref.at[1])
        source_of = merged_rows(places[t], 0, places[t + 2], CELL_ATOMS)
        keeps = [keep_ref[2 * t + 1 : 2 * t + 2, :]]
        return fill_steps(merged_factor_ref.at[t], CELL_ATOMS, source_of, keeps, targets[t])

    totals = [
        [messages_ref[t, :, k * WIDTH : min((k + 1) * WIDTH, NY * GROUP)] for k in range(CHUNKS)]
        for t in range(2)
    ]

    def add_cell(t):
        return product_steps(cell_ref.at[t], cell_factor_ref.at[t], totals[t])

    def add_merged(t):
        return product_steps(merged_ref.at[t], merged_factor_ref.at[t], totals[t], True)

    readout = jnp.broadcast_to(readout_ref[...], (8, CH)).T[:, :1]
    mix = mix_ref[...]
    mix_t = mix.astype(jnp.float32).T.astype(jnp.bfloat16)

    for step in fill_cell(0):
        step()
    interleave(add_cell(0), fill_merged(0))
    interleave(add_merged(0), fill_cell(1))
    interleave(add_cell(1), fill_merged(1))
    for step in add_merged(1):
        step()

    sides = [jnp.concatenate(total, axis=1) for total in totals]
    part = [
        jnp.concatenate([side[:, y * GROUP : (y + 1) * GROUP] for side in sides], axis=1)
        for y in range(NY)
    ]
    invariants = jnp.concatenate(
        [
            part[0],
            0.5 * (part[1] * part[1] + part[2] * part[2] + part[3] * part[3]),
            0.5
            * (
                part[4] * part[4]
                + part[5] * part[5]
                + part[6] * part[6]
                + part[7] * part[7]
                + part[8] * part[8]
            ),
        ],
        axis=0,
    ).astype(jnp.bfloat16)
    preact = jnp.dot(mix_t, invariants, preferred_element_type=jnp.float32)
    gating = jax.nn.sigmoid(preact)
    energy_grad = energy_grad_ref[...]
    spread = readout * energy_grad
    grad_pre = (spread * gating * (1.0 + preact * (1.0 - gating))).astype(jnp.bfloat16)
    grad_inv = jnp.dot(mix, grad_pre, preferred_element_type=jnp.float32)
    grad_mix = scale * lax.dot_general(
        invariants, grad_pre, (((1,), (1,)), ((), ())), preferred_element_type=jnp.float32
    )
    kept_ref[...] = jnp.where(even, grad_mix[:HALF], grad_mix[HALF:])
    sent_ref[...] = jnp.where(even, grad_mix[HALF:], grad_mix[:HALF])
    for y in range(NY):
        order = 0 if y == 0 else 1 if y < 4 else 2
        grad = grad_inv[order * CH : (order + 1) * CH]
        grad = (grad if y == 0 else grad * part[y]).astype(jnp.bfloat16)
        for t in range(2):
            grad_messages_ref[t, :, y * GROUP : (y + 1) * GROUP] = grad[:, t * GROUP : (t + 1) * GROUP]

    updated = jnp.concatenate([slabs[1][:CH], slabs[2][:CH]], axis=1) + preact * gating
    kinds = species_ref[...]
    shifts = jnp.zeros((1, 2 * GROUP), jnp.float32)
    for n in range(NSPEC):
        shifts = jnp.where(kinds == n, shift_ref[:, n : n + 1], shifts)
    energy_ref[...] = jnp.sum(updated * readout, axis=0, keepdims=True) + shifts
    spread_ref[...] = spread
    grad_out = jnp.sum(updated * energy_grad, axis=1, keepdims=True)
    readout_row = column_to_row(grad_out, CH)
    here = lax.broadcasted_iota(jnp.int32, (NSPEC, 2 * GROUP), 0) == kinds
    by_kind = jnp.sum(jnp.where(here, energy_grad, 0.0), axis=1, keepdims=True)
    rest_ref[...] = jnp.concatenate(
        [readout_row, column_to_row(by_kind, NSPEC), jnp.zeros((6, CH), jnp.float32)], axis=0
    )


def back(factor, grad_messages):
    return lax.dot_general(
        factor, grad_messages, (((1,), (1,)), ((), ())), preferred_element_type=jnp.float32
    )


def source_grads(total, features_t, weight):
    size = features_t.shape[0]
    grad_t = None
    radial = []
    for b in range(NB):
        piece = total[b * size : (b + 1) * size]
        term = piece * weight[b : b + 1, :]
        grad_t = term if grad_t is None else grad_t + term
        radial.append(jnp.sum(piece * features_t, axis=0, keepdims=True))
    return grad_t, jnp.concatenate(radial, axis=0)


def halo_back_kernel(
    cell_factor_ref,
    merged_factor_ref,
    grad_messages_ref,
    near_ref,
    far_ref,
    from_pair_ref,
    from_cross_ref,
    radial_ref,
    sent_ref,
    extra_ref,
    share_ref,
):
    even = lax.axis_index("space") % 2 == 0
    weight = radial_ref[...]
    near, far = near_ref[:CH, :], far_ref[:CH, :]
    from_pair, from_cross = from_pair_ref[:CH, :], from_cross_ref[:CH, :]
    features_t = [
        jnp.where(even, one, two).T
        for one, two in ((from_cross, from_pair), (far, near), (near, far), (from_pair, from_cross))
    ]
    first = lax.broadcasted_iota(jnp.int32, (CH, NY * GROUP), 1) % GROUP < CELL_ATOMS
    low, high = slice(CELL_ATOMS), slice(CELL_ATOMS, GROUP)
    share = None
    grads = {}
    for t in range(2):
        grad = grad_messages_ref[t]
        none = jnp.zeros_like(grad)
        both = jnp.concatenate([jnp.where(first, grad, none), jnp.where(first, none, grad)], axis=0)
        merged = back(merged_factor_ref[t], both)
        pieces = (
            (3 * t, 1 - t, back(cell_factor_ref[t], grad)),
            (t, 0, merged[:, :CH]),
            (t + 2, 1, merged[:, CH:]),
        )
        for g, half, total in pieces:
            grads[g, half], part = source_grads(total, features_t[g][(low, high)[half]], weight)
            share = part if share is None else share + part
    grad_before = jnp.concatenate([grads[0, 0], grads[0, 1]], axis=0).T
    grad_after = jnp.concatenate([grads[3, 0], grads[3, 1]], axis=0).T
    sent_ref[:CH, :] = jnp.where(even, grad_after, grad_before)
    sent_ref[CH:, :] = jnp.where(even, grad_before, grad_after)
    extra_ref[low, :] = grads[1, 0]
    extra_ref[high, :] = grads[2, 1]
    share_ref[...] = share


def own_back_kernel(
    scale,
    group_factor_ref,
    cell_factor_ref,
    grad_messages_ref,
    near_ref,
    far_ref,
    radial_ref,
    extra_ref,
    share_ref,
    rest_ref,
    spread_ref,
    own_grad_ref,
    joined_ref,
):
    even = lax.axis_index("space") % 2 == 0
    weight = radial_ref[...]
    near, far = near_ref[:CH, :], far_ref[:CH, :]
    share = share_ref[...]
    low, high = slice(CELL_ATOMS), slice(CELL_ATOMS, GROUP)
    for t, features in enumerate((jnp.where(even, far, near), jnp.where(even, near, far))):
        features_t = features.T
        total = back(group_factor_ref[t], grad_messages_ref[t])
        grad, part = source_grads(total, features_t, weight)
        inner, outer = (high, low) if t == 0 else (low, high)
        total = back(cell_factor_ref[1 - t], grad_messages_ref[1 - t])
        one, more = source_grads(total, features_t[inner], weight)
        two = extra_ref[outer, :]
        grad = (grad + jnp.concatenate([two, one] if t == 0 else [one, two], axis=0)).T
        at = slice(t * GROUP, (t + 1) * GROUP)
        own_grad_ref[:, at] = spread_ref[:, at] + grad
        share = share + part + more
    joined_ref[:NB, :] = share * scale
    joined_ref[NB:, :] = rest_ref[...] * scale


def quarter_kernel(kept_ref, received_ref, keep_ref, send_ref):
    first = lax.axis_index("dp") % 2 == 0
    low = kept_ref[:QUARTER, :] + received_ref[:QUARTER, :]
    high = kept_ref[QUARTER:, :] + received_ref[QUARTER:, :]
    keep_ref[...] = jnp.where(first, low, high)
    send_ref[...] = jnp.where(first, high, low)


def join_kernel(kept_ref, received_ref, rest_ref, out_ref):
    out_ref[:QUARTER, :] = kept_ref[...] + received_ref[...]
    out_ref[QUARTER:, :] = rest_ref[...]


def gather_kernel(mine_ref, along_ref, other_ref, both_ref, out_ref):
    first = lax.axis_index("dp") % 2 == 0
    at, rest = slice(QUARTER), slice(QUARTER, QUARTER + REST)
    mine = mine_ref[at, :] + along_ref[at, :]
    other = other_ref[at, :] + both_ref[at, :]
    out_ref[:QUARTER, :] = jnp.where(first, mine, other)
    out_ref[QUARTER:HALF, :] = jnp.where(first, other, mine)
    out_ref[HALF:, :] = (mine_ref[rest, :] + along_ref[rest, :]) + (other_ref[rest, :] + both_ref[rest, :])


def fold_kernel(own_ref, from_pair_ref, from_cross_ref, energy_in_ref, grad_ref, energy_ref):
    even = lax.axis_index("space") % 2 == 0
    pair = from_pair_ref[:CH, :]
    cross = from_cross_ref[...]
    grad_ref[0, :, :GROUP] = own_ref[:, :GROUP] + jnp.where(even, cross, pair)
    grad_ref[0, :, GROUP:] = own_ref[:, GROUP:] + jnp.where(even, pair, cross)
    energy_ref[...] = energy_in_ref[...]


def finish_kernel(mine_ref, other_ref, radial_ref, mix_ref, readout_ref, shift_ref):
    even = lax.axis_index("space") % 2 == 0
    mine, other = mine_ref[:HALF, :], other_ref[:HALF, :]
    mix_ref[:HALF, :] = jnp.where(even, mine, other)
    mix_ref[HALF:, :] = jnp.where(even, other, mine)
    rest = mine_ref[HALF:, :] + other_ref[HALF:, :]
    radial_ref[...] = rest[:NB]
    readout_ref[...] = rest[NB : NB + 1]
    shift_ref[...] = rest[NB + 1 : NB + 2, :NSPEC]


def exchange_routes(space, dp):
    steps = [(1 << k, 0) for k in range(1, space.bit_length() - 1)]
    steps += [(0, 1 << k) for k in range(1, dp.bit_length() - 1)]
    *steps, final = steps
    groups = [steps[k : k + 2] for k in range(0, len(steps), 2)]
    rounds = [[[one], [two], [one, two]] if len(rest) else [[one]] for one, *rest in groups for two in rest or [one]]
    rounds.append([[final], [(0, 1)], [final, (0, 1)]])

    def route(moves):
        across = along = 0
        for s, d in moves:
            across, along = across ^ s, along ^ d
        return [(s * dp + d, (s ^ across) * dp + (d ^ along)) for s in range(space) for d in range(dp)]

    return [[route(moves) for moves in kinds] for kinds in rounds]


def call(kernel, name, inputs, outputs, mib=4, scratch=(), flops=0):
    vmem = pl.BlockSpec(memory_space=pltpu.VMEM)
    shapes = tuple(jax.ShapeDtypeStruct(shape, kind) for shape, kind in outputs)
    moved = sum(math.prod(v.shape) * v.dtype.itemsize for v in (*inputs, *shapes))
    return pl.pallas_call(
        kernel,
        out_shape=shapes,
        in_specs=[vmem] * len(inputs),
        out_specs=(vmem,) * len(shapes),
        scratch_shapes=scratch,
        compiler_params=pltpu.CompilerParams(vmem_limit_bytes=mib * 1024 * 1024),
        cost_estimate=pl.CostEstimate(flops=flops, bytes_accessed=moved, transcendentals=0),
        name=name,
    )(*inputs)


def in_hbm(value):
    return pltpu.with_memory_space_constraint(value, pltpu.HBM)


def body(
    node_features,
    positions,
    species,
    energy_cotangent,
    pair_target,
    pair_source,
    pair_count,
    radial_weight,
    mix_weight,
    readout_weight,
    species_shift,
):
    atoms_here = node_features.shape[2]
    space, dp = lax.axis_size("space"), lax.axis_size("dp")
    scale = 1.0 / math.sqrt(atoms_here * space * dp)
    pair = [(i, i ^ 1) for i in range(space)]
    cross = [(i, ((i + 1) ^ 1) - 1) for i in range(1, space - 1)]
    onward = [(i, i + 2) for i in range(0, space - 2, 2)] + [(i, i - 2) for i in range(3, space, 2)]

    across = [(i, i ^ 1) for i in range(dp)]
    hbm = pl.BlockSpec(memory_space=pltpu.HBM)
    smem = pl.BlockSpec(memory_space=pltpu.SMEM)
    vmem = pl.BlockSpec(memory_space=pltpu.VMEM)
    f32, bf16 = jnp.float32, jnp.bfloat16
    small = (
        pair_target,
        pair_source,
        species,
        species_shift.reshape(1, NSPEC),
        energy_cotangent,
        radial_weight,
        mix_weight,
        readout_weight.reshape(1, CH),
    )
    near, far, *small = pl.pallas_call(
        split_kernel,
        out_shape=(jax.ShapeDtypeStruct((SLAB_ROWS, GROUP), f32),) * 2
        + tuple(jax.ShapeDtypeStruct(v.shape, v.dtype) for v in small),
        in_specs=[hbm] * (SMALL + 2),
        out_specs=(vmem,) * (SMALL + 2),
        scratch_shapes=[
            pltpu.VMEM((3, 1, atoms_here), f32),
            pltpu.SemaphoreType.DMA((SMALL + 3,)),
        ],
        compiler_params=pltpu.CompilerParams(vmem_limit_bytes=4 * 1024 * 1024),
        name="split",
    )(
        in_hbm(node_features),
        in_hbm(jnp.transpose(positions, (1, 0, 2))),
        *[in_hbm(v) for v in small],
    )
    targets, sources, species, shift, energy_grad, radial, mix, readout = small
    from_cross = lax.ppermute(far, "space", cross)
    from_pair = lax.ppermute(near, "space", pair)

    block_flops = 2 * CH * NB * NY * GROUP * GROUP
    group_factor, cell_factor, messages, keep, place = pl.pallas_call(
        local_kernel,
        out_shape=(
            jax.ShapeDtypeStruct((2, NB * GROUP, NY * GROUP), bf16),
            jax.ShapeDtypeStruct((2, NB * CELL_ATOMS, NY * GROUP), bf16),
            jax.ShapeDtypeStruct((2, CH, NY * GROUP), f32),
            jax.ShapeDtypeStruct((8, GROUP), f32),
            jax.ShapeDtypeStruct((2, 3, GROUP, GROUP), f32),
        ),
        in_specs=[smem] + [vmem] * 5,
        out_specs=(vmem,) * 5,
        scratch_shapes=[
            pltpu.VMEM((2, CH, NB * GROUP), bf16),
            pltpu.VMEM((2, CH, NB * CELL_ATOMS), bf16),
        ],
        compiler_params=pltpu.CompilerParams(vmem_limit_bytes=16 * 1024 * 1024),
        cost_estimate=pl.CostEstimate(
            flops=3 * block_flops, bytes_accessed=11_000_000, transcendentals=0
        ),
        name="local_pairs",
    )(pair_count, targets, sources, radial, near, far)

    energy, spread, kept, sent, rest, grad_messages, halo_factor, merged_factor = call(
        functools.partial(node_kernel, scale),
        "node_stage",
        (
            near,
            far,
            from_pair,
            from_cross,
            messages,
            keep,
            place,
            species,
            shift,
            energy_grad,
            radial,
            mix,
            readout,
        ),
        (
            ((1, atoms_here), f32),
            ((CH, atoms_here), f32),
            ((HALF, CH), f32),
            ((HALF, CH), f32),
            ((8, CH), f32),
            ((2, CH, NY * GROUP), bf16),
            ((2, NB * CELL_ATOMS, NY * GROUP), bf16),
            ((2, NB * CELL_ATOMS, NY * GROUP), bf16),
        ),
        16,
        [
            pltpu.VMEM((2, CH, NB * CELL_ATOMS), bf16),
            pltpu.VMEM((2, 2 * CH, NB * CELL_ATOMS), bf16),
            pltpu.VMEM((2, 3, GROUP, GROUP), f32),
        ],
        2 * block_flops,
    )

    received = lax.ppermute(sent, "space", pair)
    halo_grad, extra, share = call(
        halo_back_kernel,
        "halo_back",
        (
            halo_factor,
            merged_factor,
            grad_messages,
            near,
            far,
            from_pair,
            from_cross,
            radial,
        ),
        (((2 * CH, GROUP), f32), ((GROUP, CH), f32), ((NB, CH), f32)),
        12,
        (),
        2 * block_flops,
    )
    received, share = lax.optimization_barrier((received, share))
    quarter, sent = call(
        quarter_kernel,
        "quarter",
        (kept, received),
        (((QUARTER, CH), f32), ((QUARTER, CH), f32)),
    )
    sent, grad_messages, halo_grad = lax.optimization_barrier((sent, grad_messages, halo_grad))
    received = lax.ppermute(sent, "dp", across)
    from_pair = lax.ppermute(halo_grad, "space", pair)
    own_grad, joined = call(
        functools.partial(own_back_kernel, scale),
        "own_back",
        (
            group_factor,
            cell_factor,
            grad_messages,
            near,
            far,
            radial,
            extra,
            share,
            rest,
            spread,
        ),
        (((CH, atoms_here), f32), ((REST, CH), f32)),
        12,
        (),
        3 * block_flops,
    )
    (value,) = call(
        join_kernel, "join", (quarter, received, joined), (((QUARTER + REST, CH), f32),)
    )
    value, from_pair = lax.optimization_barrier((value, from_pair))
    *rounds, last = exchange_routes(space, dp)
    everyone = ("space", "dp")
    for turn, routes in enumerate(rounds):
        arrived = [lax.ppermute(value, everyone, route) for route in routes]
        if turn == 0:
            from_cross = lax.ppermute(from_pair[CH:], "space", onward)
        value = value + arrived[0]
        if len(arrived) == 3:
            value = value + (arrived[1] + arrived[2])
    arrived = [lax.ppermute(value, everyone, route) for route in last]
    value, from_cross, *arrived = lax.optimization_barrier((value, from_cross, *arrived))
    (value,) = call(
        gather_kernel,
        "gather",
        (value, *arrived),
        (((HALF + REST, CH), f32),),
    )
    feature_grad, energy = call(
        fold_kernel,
        "fold",
        (own_grad, from_pair, from_cross, energy),
        (((1, CH, atoms_here), f32), ((1, atoms_here), f32)),
    )
    radial_grad, mix_grad, readout_grad, shift_grad = call(
        finish_kernel,
        "finish",
        (value, lax.ppermute(value, "space", pair)),
        (((NB, CH), f32), ((MIX_ROWS, CH), f32), ((1, CH), f32), ((1, NSPEC), f32)),
    )
    return (
        energy,
        feature_grad,
        radial_grad,
        mix_grad,
        readout_grad.reshape(CH),
        shift_grad.reshape(NSPEC),
    )


def solution(mesh):
    return jax.shard_map(
        body,
        mesh=mesh,
        in_specs=(
            P("dp", None, "space"),
            P("dp", None, "space"),
            P("dp", "space"),
            P("dp", "space"),
            P("dp", "space"),
            P("dp", "space"),
            P("dp", "space"),
            P(),
            P(),
            P(),
            P(),
        ),
        out_specs=(P("dp", "space"), P("dp", None, "space"), P(), P(), P(), P()),
        check_vma=False,
    )
```

```python
import functools
import math

import jax
import jax.numpy as jnp
from jax import lax
from jax.experimental import pallas as pl
from jax.experimental.pallas import tpu as pltpu
from jax.sharding import PartitionSpec as P

CH = 128
NB = 8
NY = 9
NSPEC = 8
CELL_ATOMS = 64
HALO_CELLS = 2
GROUP = 2 * CELL_ATOMS
ROWS = 16
WIDTH = 256
CHUNKS = -(-NY * GROUP // WIDTH)

cutoff = 5.0
message_scale = 0.25

COS_COEFFS = (
    0.9999999998846169,
    -4.934802185771876,
    4.058711815779763,
    -1.3352602773967561,
    0.23532080049888648,
    -0.025785772074137014,
    0.0019043022864480008,
    -8.868331860867329e-05,
)
SINC_COEFFS = (
    0.9999999992502204,
    -1.6449339933418936,
    0.8117412468909989,
    -0.1907447263221115,
    0.02612742969685046,
    -0.0023157632409761065,
    0.00012580778956459784,
)

MIX_ROWS = 3 * CH
HALF = MIX_ROWS // 2
QUARTER = MIX_ROWS // 4
REST = 16
CELLS = 4 + 2 * HALO_CELLS
SMALL = 8
SLAB_ROWS = CH + 8


def polynomial(coeffs, x):
    total = coeffs[-1] * x + coeffs[-2]
    for c in coeffs[-3::-1]:
        total = total * x + c
    return total


def factor_rows(factor_ref, size, row, source, target, keep):
    dx = (target[0] - source[0]) * (1.0 / cutoff)
    dy = (target[1] - source[1]) * (1.0 / cutoff)
    dz = (target[2] - source[2]) * (1.0 / cutoff)
    xx, yy, zz = dx * dx, dy * dy, dz * dz
    square = xx + yy + zz
    inside = jnp.minimum(square, 1.0)
    gap = 1.0 - inside
    base = (gap * gap) * keep * polynomial(SINC_COEFFS, inside)
    twice_cos = polynomial([2.0 * c for c in COS_COEFFS], inside)
    raw = [base, twice_cos * base]
    for _ in range(NB - 2):
        raw.append(twice_cos * raw[-1] - raw[-2])
    radial = [value if b == 0 else value * (1.0 / (b + 1)) for b, value in enumerate(raw)]
    root_three = math.sqrt(3.0)
    root_fifteen = math.sqrt(15.0)
    root_five = math.sqrt(5.0)
    wide_x = root_fifteen * dx
    harmonic = [
        None,
        root_three * dx,
        root_three * dy,
        root_three * dz,
        wide_x * dy,
        (root_fifteen * dy) * dz,
        (0.5 * root_five) * (3.0 * zz - square),
        wide_x * dz,
        (0.5 * root_fifteen) * (xx - yy),
    ]
    for b in range(NB):
        rows = slice(b * size + row, b * size + row + ROWS)
        for y in range(NY):
            value = radial[b] if y == 0 else radial[b] * harmonic[y]
            factor_ref[rows, y * GROUP : (y + 1) * GROUP] = value.astype(jnp.bfloat16)


def column_to_row(column, size):
    wide = jnp.broadcast_to(column, (size, GROUP))
    at = lax.broadcasted_iota(jnp.int32, (size, GROUP), 0)
    lane = lax.broadcasted_iota(jnp.int32, (size, GROUP), 1)
    return jnp.sum(jnp.where(at == lane, wide, 0.0), axis=0, keepdims=True)


def split_kernel(*refs):
    features_ref, place_in_ref, *inputs = refs[: SMALL + 2]
    near_ref, far_ref, *outputs = refs[SMALL + 2 : 2 * SMALL + 4]
    place_ref, sems = refs[2 * SMALL + 4 :]
    core = lax.axis_index("space") % 2
    place_copy = pltpu.make_async_copy(place_in_ref, place_ref, sems.at[2])
    place_copy.start()
    copies = []
    for k, (ref, side) in enumerate(((near_ref, 1 - core), (far_ref, core))):
        at = pl.ds(pl.multiple_of(side * GROUP, GROUP), GROUP)
        copies.append(
            pltpu.make_async_copy(features_ref.at[0, :, at], ref.at[pl.ds(0, CH)], sems.at[k])
        )
    for k, (src, dst) in enumerate(zip(inputs, outputs)):
        copies.append(pltpu.make_async_copy(src, dst, sems.at[3 + k]))
    for copy in copies:
        copy.start()
    place_copy.wait()
    low, high = slice(GROUP), slice(GROUP, 2 * GROUP)
    filler = jnp.zeros((5, GROUP), jnp.float32)
    for ref, one, two in ((near_ref, high, low), (far_ref, low, high)):
        rows = [
            jnp.where(core == 0, place_ref[axis, :, one], place_ref[axis, :, two]) for axis in range(3)
        ]
        ref[CH:, :] = jnp.concatenate(rows + [filler], axis=0)
    for copy in copies:
        copy.wait()


def live_flags(count, pair_target, pair_source):
    size = (4 * CELLS, pair_target.shape[1])
    at = lax.broadcasted_iota(jnp.int32, size, 0)
    slot = lax.broadcasted_iota(jnp.int32, size, 1)
    hit = (pair_target * CELLS + pair_source == at) & (slot < count)
    return jnp.max(jnp.where(hit, message_scale, 0.0), axis=1, keepdims=True)


def keep_row(flags, t, low, high):
    lane = lax.broadcasted_iota(jnp.int32, (1, GROUP), 1)
    one, two = (2 * t) * CELLS + low, (2 * t + 1) * CELLS + high
    return jnp.where(lane < CELL_ATOMS, flags[one : one + 1], flags[two : two + 1])


def set_group(scaled_ref, features, weight_t):
    for b in range(NB):
        scaled_ref[:, b * GROUP : (b + 1) * GROUP] = (features * weight_t[:, b : b + 1]).astype(
            jnp.bfloat16
        )


def set_cell(scaled_ref, features, half, weight_t):
    first = lax.broadcasted_iota(jnp.int32, (CH, GROUP), 1) < CELL_ATOMS
    turned = pltpu.roll(features, CELL_ATOMS, 1)
    twice = jnp.where(first, features, turned) if half == 0 else jnp.where(first, turned, features)
    for k in range(NB // 2):
        weights = jnp.where(first, weight_t[:, 2 * k : 2 * k + 1], weight_t[:, 2 * k + 1 : 2 * k + 2])
        scaled_ref[:, k * GROUP : (k + 1) * GROUP] = (twice * weights).astype(jnp.bfloat16)


def set_place(place_ref, slab):
    place = slab[CH:].T
    for axis in range(3):
        place_ref[axis] = jnp.broadcast_to(place[:, axis : axis + 1], (GROUP, GROUP))


def fill_steps(factor_ref, size, source_of, keeps, target, diagonal=False):
    def step(row):
        keep = jnp.broadcast_to(keeps[row // CELL_ATOMS], (ROWS, GROUP))
        if diagonal:
            row_at = lax.broadcasted_iota(jnp.int32, (ROWS, GROUP), 0)
            lane_at = lax.broadcasted_iota(jnp.int32, (ROWS, GROUP), 1)
            keep = jnp.where(row_at + row == lane_at, 0.0, keep)
        factor_rows(factor_ref, size, row, source_of(row), target, keep)

    return [functools.partial(step, row) for row in range(0, size, ROWS)]


def rows_of(place_ref, start):
    return lambda row: [place_ref[axis, start + row : start + row + ROWS, :] for axis in range(3)]


def merged_rows(low_ref, low_start, high_ref, high_start):
    low, high = rows_of(low_ref, low_start), rows_of(high_ref, high_start)

    def rows(row):
        first = lax.broadcasted_iota(jnp.int32, (ROWS, GROUP), 1) < CELL_ATOMS
        return [jnp.where(first, one, two) for one, two in zip(low(row), high(row))]

    return rows


def product_steps(scaled_ref, factor_ref, totals, merged=False):
    def step(k):
        width = min(WIDTH, NY * GROUP - k * WIDTH)
        product = jnp.dot(
            scaled_ref[...],
            factor_ref[:, k * WIDTH : k * WIDTH + width],
            preferred_element_type=jnp.float32,
        )
        if merged:
            lane = lax.broadcasted_iota(jnp.int32, (CH, width), 1) % GROUP
            product = jnp.where(lane < CELL_ATOMS, product[:CH], product[CH:])
        totals[k] = product if totals[k] is None else totals[k] + product

    return [functools.partial(step, k) for k in range(CHUNKS)]


def interleave(one, two):
    done = 0
    for k, step in enumerate(one):
        step()
        upto = (k + 1) * len(two) // len(one)
        for other in two[done:upto]:
            other()
        done = upto


def local_kernel(
    count_ref,
    pair_target_ref,
    pair_source_ref,
    radial_ref,
    near_ref,
    far_ref,
    group_factor_ref,
    cell_factor_ref,
    messages_ref,
    keep_ref,
    place_ref,
    group_ref,
    cell_ref,
):
    even = lax.axis_index("space") % 2 == 0
    near, far = near_ref[...], far_ref[...]
    slabs = (jnp.where(even, far, near), jnp.where(even, near, far))
    targets = [[slab[CH + axis : CH + axis + 1] for axis in range(3)] for slab in slabs]
    flags = live_flags(count_ref[0, 0], pair_target_ref[...], pair_source_ref[...])
    weight_t = radial_ref[...].T
    for g in range(2):
        set_place(place_ref.at[g], slabs[g])
        set_group(group_ref.at[g], slabs[g][:CH], weight_t)
        set_cell(cell_ref.at[g], slabs[1 - g][:CH], g, weight_t)

    def fill_group(t):
        keeps = [keep_row(flags, t, cell, cell) for cell in (2 * t + 2, 2 * t + 3)]
        return fill_steps(
            group_factor_ref.at[t], GROUP, rows_of(place_ref.at[t], 0), keeps, targets[t], True
        )

    def fill_cell(t):
        cell = 4 - t
        source_of = rows_of(place_ref.at[1 - t], t * CELL_ATOMS)
        return fill_steps(
            cell_factor_ref.at[t], CELL_ATOMS, source_of, [keep_row(flags, t, cell, cell)], targets[t]
        )

    totals = [[None] * CHUNKS for _ in range(2)]
    for step in fill_cell(0):
        step()
    interleave(product_steps(cell_ref.at[0], cell_factor_ref.at[0], totals[0]), fill_group(0))
    interleave(product_steps(group_ref.at[0], group_factor_ref.at[0], totals[0]), fill_group(1))
    interleave(product_steps(group_ref.at[1], group_factor_ref.at[1], totals[1]), fill_cell(1))
    for step in product_steps(cell_ref.at[1], cell_factor_ref.at[1], totals[1]):
        step()
    for t in range(2):
        messages_ref[t] = jnp.concatenate(totals[t], axis=1)
    rows = [
        keep_row(flags, 0, 1, 1),
        keep_row(flags, 0, 0, 5),
        keep_row(flags, 1, 6, 6),
        keep_row(flags, 1, 2, 7),
    ]
    keep_ref[...] = jnp.concatenate(rows + [jnp.zeros((4, GROUP), jnp.float32)], axis=0)


def node_kernel(
    scale,
    near_ref,
    far_ref,
    from_pair_ref,
    from_cross_ref,
    messages_ref,
    keep_ref,
    own_place_ref,
    species_ref,
    shift_ref,
    energy_grad_ref,
    radial_ref,
    mix_ref,
    readout_ref,
    energy_ref,
    spread_ref,
    kept_ref,
    sent_ref,
    rest_ref,
    grad_messages_ref,
    cell_factor_ref,
    merged_factor_ref,
    cell_ref,
    merged_ref,
    place_ref,
):
    even = lax.axis_index("space") % 2 == 0
    weight_t = radial_ref[...].T
    near, far = near_ref[...], far_ref[...]
    from_pair, from_cross = from_pair_ref[...], from_cross_ref[...]
    slabs = (
        jnp.where(even, from_cross, from_pair),
        jnp.where(even, far, near),
        jnp.where(even, near, far),
        jnp.where(even, from_pair, from_cross),
    )
    targets = [[slab[CH + axis : CH + axis + 1] for axis in range(3)] for slab in slabs[1:3]]

    for t in range(2):
        set_place(place_ref.at[t], slabs[3 * t])
        set_cell(cell_ref.at[t], slabs[3 * t][:CH], 1 - t, weight_t)
        set_cell(merged_ref.at[t, pl.ds(0, CH)], slabs[t][:CH], 0, weight_t)
        set_cell(merged_ref.at[t, pl.ds(CH, CH)], slabs[t + 2][:CH], 1, weight_t)

    def fill_cell(t):
        source_of = rows_of(place_ref.at[t], (1 - t) * CELL_ATOMS)
        keeps = [keep_ref[2 * t : 2 * t + 1, :]]
        return fill_steps(cell_factor_ref.at[t], CELL_ATOMS, source_of, keeps, targets[t])

    def fill_merged(t):
        places = (place_ref.at[0], own_place_ref.at[0], own_place_ref.at[1], place_ref.at[1])
        source_of = merged_rows(places[t], 0, places[t + 2], CELL_ATOMS)
        keeps = [keep_ref[2 * t + 1 : 2 * t + 2, :]]
        return fill_steps(merged_factor_ref.at[t], CELL_ATOMS, source_of, keeps, targets[t])

    totals = [
        [messages_ref[t, :, k * WIDTH : min((k + 1) * WIDTH, NY * GROUP)] for k in range(CHUNKS)]
        for t in range(2)
    ]

    def add_cell(t):
        return product_steps(cell_ref.at[t], cell_factor_ref.at[t], totals[t])

    def add_merged(t):
        return product_steps(merged_ref.at[t], merged_factor_ref.at[t], totals[t], True)

    readout = jnp.broadcast_to(readout_ref[...], (8, CH)).T[:, :1]
    mix = mix_ref[...]
    mix_t = mix.astype(jnp.float32).T.astype(jnp.bfloat16)

    for step in fill_cell(0):
        step()
    interleave(add_cell(0), fill_merged(0))
    interleave(add_merged(0), fill_cell(1))
    interleave(add_cell(1), fill_merged(1))
    for step in add_merged(1):
        step()

    sides = [jnp.concatenate(total, axis=1) for total in totals]
    part = [
        jnp.concatenate([side[:, y * GROUP : (y + 1) * GROUP] for side in sides], axis=1)
        for y in range(NY)
    ]
    invariants = jnp.concatenate(
        [
            part[0],
            0.5 * (part[1] * part[1] + part[2] * part[2] + part[3] * part[3]),
            0.5
            * (
                part[4] * part[4]
                + part[5] * part[5]
                + part[6] * part[6]
                + part[7] * part[7]
                + part[8] * part[8]
            ),
        ],
        axis=0,
    ).astype(jnp.bfloat16)
    preact = jnp.dot(mix_t, invariants, preferred_element_type=jnp.float32)
    gating = jax.nn.sigmoid(preact)
    energy_grad = energy_grad_ref[...]
    spread = readout * energy_grad
    grad_pre = (spread * gating * (1.0 + preact * (1.0 - gating))).astype(jnp.bfloat16)
    grad_inv = jnp.dot(mix, grad_pre, preferred_element_type=jnp.float32)
    grad_mix = scale * lax.dot_general(
        invariants, grad_pre, (((1,), (1,)), ((), ())), preferred_element_type=jnp.float32
    )
    kept_ref[...] = jnp.where(even, grad_mix[:HALF], grad_mix[HALF:])
    sent_ref[...] = jnp.where(even, grad_mix[HALF:], grad_mix[:HALF])
    for y in range(NY):
        order = 0 if y == 0 else 1 if y < 4 else 2
        grad = grad_inv[order * CH : (order + 1) * CH]
        grad = (grad if y == 0 else grad * part[y]).astype(jnp.bfloat16)
        for t in range(2):
            grad_messages_ref[t, :, y * GROUP : (y + 1) * GROUP] = grad[:, t * GROUP : (t + 1) * GROUP]

    updated = jnp.concatenate([slabs[1][:CH], slabs[2][:CH]], axis=1) + preact * gating
    kinds = species_ref[...]
    shifts = jnp.zeros((1, 2 * GROUP), jnp.float32)
    for n in range(NSPEC):
        shifts = jnp.where(kinds == n, shift_ref[:, n : n + 1], shifts)
    energy_ref[...] = jnp.sum(updated * readout, axis=0, keepdims=True) + shifts
    spread_ref[...] = spread
    grad_out = jnp.sum(updated * energy_grad, axis=1, keepdims=True)
    readout_row = column_to_row(grad_out, CH)
    here = lax.broadcasted_iota(jnp.int32, (NSPEC, 2 * GROUP), 0) == kinds
    by_kind = jnp.sum(jnp.where(here, energy_grad, 0.0), axis=1, keepdims=True)
    rest_ref[...] = jnp.concatenate(
        [readout_row, column_to_row(by_kind, NSPEC), jnp.zeros((6, CH), jnp.float32)], axis=0
    )


def back(factor, grad_messages):
    return lax.dot_general(
        factor, grad_messages, (((1,), (1,)), ((), ())), preferred_element_type=jnp.float32
    )


def source_grads(total, features_t, weight):
    size = features_t.shape[0]
    grad_t = None
    radial = []
    for b in range(NB):
        piece = total[b * size : (b + 1) * size]
        term = piece * weight[b : b + 1, :]
        grad_t = term if grad_t is None else grad_t + term
        radial.append(jnp.sum(piece * features_t, axis=0, keepdims=True))
    return grad_t, jnp.concatenate(radial, axis=0)


def halo_back_kernel(
    cell_factor_ref,
    merged_factor_ref,
    grad_messages_ref,
    near_ref,
    far_ref,
    from_pair_ref,
    from_cross_ref,
    radial_ref,
    sent_ref,
    extra_ref,
    share_ref,
):
    even = lax.axis_index("space") % 2 == 0
    weight = radial_ref[...]
    near, far = near_ref[:CH, :], far_ref[:CH, :]
    from_pair, from_cross = from_pair_ref[:CH, :], from_cross_ref[:CH, :]
    features_t = [
        jnp.where(even, one, two).T
        for one, two in ((from_cross, from_pair), (far, near), (near, far), (from_pair, from_cross))
    ]
    first = lax.broadcasted_iota(jnp.int32, (CH, NY * GROUP), 1) % GROUP < CELL_ATOMS
    low, high = slice(CELL_ATOMS), slice(CELL_ATOMS, GROUP)
    share = None
    grads = {}
    for t in range(2):
        grad = grad_messages_ref[t]
        none = jnp.zeros_like(grad)
        both = jnp.concatenate([jnp.where(first, grad, none), jnp.where(first, none, grad)], axis=0)
        merged = back(merged_factor_ref[t], both)
        pieces = (
            (3 * t, 1 - t, back(cell_factor_ref[t], grad)),
            (t, 0, merged[:, :CH]),
            (t + 2, 1, merged[:, CH:]),
        )
        for g, half, total in pieces:
            grads[g, half], part = source_grads(total, features_t[g][(low, high)[half]], weight)
            share = part if share is None else share + part
    grad_before = jnp.concatenate([grads[0, 0], grads[0, 1]], axis=0).T
    grad_after = jnp.concatenate([grads[3, 0], grads[3, 1]], axis=0).T
    sent_ref[:CH, :] = jnp.where(even, grad_after, grad_before)
    sent_ref[CH:, :] = jnp.where(even, grad_before, grad_after)
    extra_ref[low, :] = grads[1, 0]
    extra_ref[high, :] = grads[2, 1]
    share_ref[...] = share


def own_back_kernel(
    scale,
    group_factor_ref,
    cell_factor_ref,
    grad_messages_ref,
    near_ref,
    far_ref,
    radial_ref,
    extra_ref,
    share_ref,
    rest_ref,
    spread_ref,
    own_grad_ref,
    joined_ref,
):
    even = lax.axis_index("space") % 2 == 0
    weight = radial_ref[...]
    near, far = near_ref[:CH, :], far_ref[:CH, :]
    share = share_ref[...]
    low, high = slice(CELL_ATOMS), slice(CELL_ATOMS, GROUP)
    for t, features in enumerate((jnp.where(even, far, near), jnp.where(even, near, far))):
        features_t = features.T
        total = back(group_factor_ref[t], grad_messages_ref[t])
        grad, part = source_grads(total, features_t, weight)
        inner, outer = (high, low) if t == 0 else (low, high)
        total = back(cell_factor_ref[1 - t], grad_messages_ref[1 - t])
        one, more = source_grads(total, features_t[inner], weight)
        two = extra_ref[outer, :]
        grad = (grad + jnp.concatenate([two, one] if t == 0 else [one, two], axis=0)).T
        at = slice(t * GROUP, (t + 1) * GROUP)
        own_grad_ref[:, at] = spread_ref[:, at] + grad
        share = share + part + more
    joined_ref[:NB, :] = share * scale
    joined_ref[NB:, :] = rest_ref[...] * scale


def quarter_kernel(kept_ref, received_ref, keep_ref, send_ref):
    first = first_of_pair()
    low = kept_ref[:QUARTER, :] + received_ref[:QUARTER, :]
    high = kept_ref[QUARTER:, :] + received_ref[QUARTER:, :]
    keep_ref[...] = jnp.where(first, low, high)
    send_ref[...] = jnp.where(first, high, low)


def join_kernel(kept_ref, received_ref, rest_ref, out_ref):
    out_ref[:QUARTER, :] = kept_ref[...] + received_ref[...]
    out_ref[QUARTER:, :] = rest_ref[...]


def gather_kernel(mine_ref, along_ref, other_ref, both_ref, out_ref):
    first = first_of_pair()
    at, rest = slice(QUARTER), slice(QUARTER, QUARTER + REST)
    mine = mine_ref[at, :] + along_ref[at, :]
    other = other_ref[at, :] + both_ref[at, :]
    out_ref[:QUARTER, :] = jnp.where(first, mine, other)
    out_ref[QUARTER:HALF, :] = jnp.where(first, other, mine)
    out_ref[HALF:, :] = (mine_ref[rest, :] + along_ref[rest, :]) + (other_ref[rest, :] + both_ref[rest, :])


def fold_kernel(own_ref, from_pair_ref, from_cross_ref, energy_in_ref, grad_ref, energy_ref):
    even = lax.axis_index("space") % 2 == 0
    pair = from_pair_ref[:CH, :]
    cross = from_cross_ref[...]
    grad_ref[0, :, :GROUP] = own_ref[:, :GROUP] + jnp.where(even, cross, pair)
    grad_ref[0, :, GROUP:] = own_ref[:, GROUP:] + jnp.where(even, pair, cross)
    energy_ref[...] = energy_in_ref[...]


def finish_kernel(mine_ref, other_ref, radial_ref, mix_ref, readout_ref, shift_ref):
    even = lax.axis_index("space") % 2 == 0
    mine, other = mine_ref[:HALF, :], other_ref[:HALF, :]
    mix_ref[:HALF, :] = jnp.where(even, mine, other)
    mix_ref[HALF:, :] = jnp.where(even, other, mine)
    rest = mine_ref[HALF:, :] + other_ref[HALF:, :]
    radial_ref[...] = rest[:NB]
    readout_ref[...] = rest[NB : NB + 1]
    shift_ref[...] = rest[NB + 1 : NB + 2, :NSPEC]


def first_of_pair():
    space, dp = lax.axis_index("space"), lax.axis_index("dp")
    return jnp.where(space % 2 == 0, dp, space // 2) % 2 == 0


def exchange_routes(space, dp):
    along = [(0, 1 << k) for k in range(dp.bit_length() - 1)]
    across = [(1 << k, 0) for k in range(1, space.bit_length() - 1)]
    shared = (along[0], across[0])
    orders = (across + along[1:], along[:1] + across[1:] + along[1:])
    orders = (orders[0][:-2] + orders[0][:-3:-1], orders[1])
    count = len(orders[0])

    def route(*places):
        moves = []
        for s in range(space):
            step = [shared[s % 2] if k < 0 else orders[s % 2][k] for k in places]
            for d in range(dp):
                to_s, to_d = s, d
                for one, two in step:
                    to_s, to_d = to_s ^ one, to_d ^ two
                moves.append((s * dp + d, to_s * dp + to_d))
        return moves

    rounds = []
    for k in range(0, count - 1, 2):
        if k + 1 < count - 1:
            rounds.append([route(k), route(k + 1), route(k, k + 1)])
        else:
            rounds.append([route(k)])
    last = count - 1
    rounds.append([route(last), route(-1), route(last, -1)])
    return route(-1), rounds


def call(kernel, name, inputs, outputs, mib=4, scratch=(), flops=0):
    vmem = pl.BlockSpec(memory_space=pltpu.VMEM)
    shapes = tuple(jax.ShapeDtypeStruct(shape, kind) for shape, kind in outputs)
    moved = sum(math.prod(v.shape) * v.dtype.itemsize for v in (*inputs, *shapes))
    return pl.pallas_call(
        kernel,
        out_shape=shapes,
        in_specs=[vmem] * len(inputs),
        out_specs=(vmem,) * len(shapes),
        scratch_shapes=scratch,
        compiler_params=pltpu.CompilerParams(vmem_limit_bytes=mib * 1024 * 1024),
        cost_estimate=pl.CostEstimate(flops=flops, bytes_accessed=moved, transcendentals=0),
        name=name,
    )(*inputs)


def in_hbm(value):
    return pltpu.with_memory_space_constraint(value, pltpu.HBM)


def body(
    node_features,
    positions,
    species,
    energy_cotangent,
    pair_target,
    pair_source,
    pair_count,
    radial_weight,
    mix_weight,
    readout_weight,
    species_shift,
):
    atoms_here = node_features.shape[2]
    space, dp = lax.axis_size("space"), lax.axis_size("dp")
    scale = 1.0 / math.sqrt(atoms_here * space * dp)
    pair = [(i, i ^ 1) for i in range(space)]
    cross = [(i, ((i + 1) ^ 1) - 1) for i in range(1, space - 1)]
    onward = [(i, i + 2) for i in range(0, space - 2, 2)] + [(i, i - 2) for i in range(3, space, 2)]

    hbm = pl.BlockSpec(memory_space=pltpu.HBM)
    smem = pl.BlockSpec(memory_space=pltpu.SMEM)
    vmem = pl.BlockSpec(memory_space=pltpu.VMEM)
    f32, bf16 = jnp.float32, jnp.bfloat16
    small = (
        pair_target,
        pair_source,
        species,
        species_shift.reshape(1, NSPEC),
        energy_cotangent,
        radial_weight,
        mix_weight,
        readout_weight.reshape(1, CH),
    )
    near, far, *small = pl.pallas_call(
        split_kernel,
        out_shape=(jax.ShapeDtypeStruct((SLAB_ROWS, GROUP), f32),) * 2
        + tuple(jax.ShapeDtypeStruct(v.shape, v.dtype) for v in small),
        in_specs=[hbm] * (SMALL + 2),
        out_specs=(vmem,) * (SMALL + 2),
        scratch_shapes=[
            pltpu.VMEM((3, 1, atoms_here), f32),
            pltpu.SemaphoreType.DMA((SMALL + 3,)),
        ],
        compiler_params=pltpu.CompilerParams(vmem_limit_bytes=4 * 1024 * 1024),
        name="split",
    )(
        in_hbm(node_features),
        in_hbm(jnp.transpose(positions, (1, 0, 2))),
        *[in_hbm(v) for v in small],
    )
    targets, sources, species, shift, energy_grad, radial, mix, readout = small
    from_cross = lax.ppermute(far, "space", cross)
    from_pair = lax.ppermute(near, "space", pair)

    block_flops = 2 * CH * NB * NY * GROUP * GROUP
    group_factor, cell_factor, messages, keep, place = pl.pallas_call(
        local_kernel,
        out_shape=(
            jax.ShapeDtypeStruct((2, NB * GROUP, NY * GROUP), bf16),
            jax.ShapeDtypeStruct((2, NB * CELL_ATOMS, NY * GROUP), bf16),
            jax.ShapeDtypeStruct((2, CH, NY * GROUP), f32),
            jax.ShapeDtypeStruct((8, GROUP), f32),
            jax.ShapeDtypeStruct((2, 3, GROUP, GROUP), f32),
        ),
        in_specs=[smem] + [vmem] * 5,
        out_specs=(vmem,) * 5,
        scratch_shapes=[
            pltpu.VMEM((2, CH, NB * GROUP), bf16),
            pltpu.VMEM((2, CH, NB * CELL_ATOMS), bf16),
        ],
        compiler_params=pltpu.CompilerParams(vmem_limit_bytes=16 * 1024 * 1024),
        cost_estimate=pl.CostEstimate(
            flops=3 * block_flops, bytes_accessed=11_000_000, transcendentals=0
        ),
        name="local_pairs",
    )(pair_count, targets, sources, radial, near, far)

    energy, spread, kept, sent, rest, grad_messages, halo_factor, merged_factor = call(
        functools.partial(node_kernel, scale),
        "node_stage",
        (
            near,
            far,
            from_pair,
            from_cross,
            messages,
            keep,
            place,
            species,
            shift,
            energy_grad,
            radial,
            mix,
            readout,
        ),
        (
            ((1, atoms_here), f32),
            ((CH, atoms_here), f32),
            ((HALF, CH), f32),
            ((HALF, CH), f32),
            ((8, CH), f32),
            ((2, CH, NY * GROUP), bf16),
            ((2, NB * CELL_ATOMS, NY * GROUP), bf16),
            ((2, NB * CELL_ATOMS, NY * GROUP), bf16),
        ),
        16,
        [
            pltpu.VMEM((2, CH, NB * CELL_ATOMS), bf16),
            pltpu.VMEM((2, 2 * CH, NB * CELL_ATOMS), bf16),
            pltpu.VMEM((2, 3, GROUP, GROUP), f32),
        ],
        2 * block_flops,
    )

    received = lax.ppermute(sent, "space", pair)
    halo_grad, extra, share = call(
        halo_back_kernel,
        "halo_back",
        (
            halo_factor,
            merged_factor,
            grad_messages,
            near,
            far,
            from_pair,
            from_cross,
            radial,
        ),
        (((2 * CH, GROUP), f32), ((GROUP, CH), f32), ((NB, CH), f32)),
        12,
        (),
        2 * block_flops,
    )
    received, share = lax.optimization_barrier((received, share))
    quarter, sent = call(
        quarter_kernel,
        "quarter",
        (kept, received),
        (((QUARTER, CH), f32), ((QUARTER, CH), f32)),
    )
    sharing, (*rounds, last) = exchange_routes(space, dp)
    everyone = ("space", "dp")
    sent, grad_messages, halo_grad = lax.optimization_barrier((sent, grad_messages, halo_grad))
    received = lax.ppermute(sent, everyone, sharing)
    from_pair = lax.ppermute(halo_grad, "space", pair)
    own_grad, joined = call(
        functools.partial(own_back_kernel, scale),
        "own_back",
        (
            group_factor,
            cell_factor,
            grad_messages,
            near,
            far,
            radial,
            extra,
            share,
            rest,
            spread,
        ),
        (((CH, atoms_here), f32), ((REST, CH), f32)),
        12,
        (),
        3 * block_flops,
    )
    (value,) = call(
        join_kernel, "join", (quarter, received, joined), (((QUARTER + REST, CH), f32),)
    )
    value, from_pair = lax.optimization_barrier((value, from_pair))
    for turn, routes in enumerate(rounds):
        arrived = [lax.ppermute(value, everyone, route) for route in routes]
        if turn == 0:
            from_cross = lax.ppermute(from_pair[CH:], "space", onward)
        value = value + arrived[0]
        if len(arrived) == 3:
            value = value + (arrived[1] + arrived[2])
    arrived = [lax.ppermute(value, everyone, route) for route in last]
    value, from_cross, *arrived = lax.optimization_barrier((value, from_cross, *arrived))
    (value,) = call(
        gather_kernel,
        "gather",
        (value, *arrived),
        (((HALF + REST, CH), f32),),
    )
    feature_grad, energy = call(
        fold_kernel,
        "fold",
        (own_grad, from_pair, from_cross, energy),
        (((1, CH, atoms_here), f32), ((1, atoms_here), f32)),
    )
    radial_grad, mix_grad, readout_grad, shift_grad = call(
        finish_kernel,
        "finish",
        (value, lax.ppermute(value, "space", pair)),
        (((NB, CH), f32), ((MIX_ROWS, CH), f32), ((1, CH), f32), ((1, NSPEC), f32)),
    )
    return (
        energy,
        feature_grad,
        radial_grad,
        mix_grad,
        readout_grad.reshape(CH),
        shift_grad.reshape(NSPEC),
    )


def solution(mesh):
    return jax.shard_map(
        body,
        mesh=mesh,
        in_specs=(
            P("dp", None, "space"),
            P("dp", None, "space"),
            P("dp", "space"),
            P("dp", "space"),
            P("dp", "space"),
            P("dp", "space"),
            P("dp", "space"),
            P(),
            P(),
            P(),
            P(),
        ),
        out_specs=(P("dp", "space"), P("dp", None, "space"), P(), P(), P(), P()),
        check_vma=False,
    )
```

```python
import functools
import math

import jax
import jax.numpy as jnp
from jax import lax
from jax.experimental import pallas as pl
from jax.experimental.pallas import tpu as pltpu
from jax.sharding import PartitionSpec as P

CH = 128
NB = 8
NY = 9
NSPEC = 8
CELL_ATOMS = 64
HALO_CELLS = 2
GROUP = 2 * CELL_ATOMS
ROWS = 16
WIDTH = 256
CHUNKS = -(-NY * GROUP // WIDTH)

cutoff = 5.0
message_scale = 0.25

COS_COEFFS = (
    0.9999999998846169,
    -4.934802185771876,
    4.058711815779763,
    -1.3352602773967561,
    0.23532080049888648,
    -0.025785772074137014,
    0.0019043022864480008,
    -8.868331860867329e-05,
)
SINC_COEFFS = (
    0.9999999992502204,
    -1.6449339933418936,
    0.8117412468909989,
    -0.1907447263221115,
    0.02612742969685046,
    -0.0023157632409761065,
    0.00012580778956459784,
)

MIX_ROWS = 3 * CH
HALF = MIX_ROWS // 2
QUARTER = MIX_ROWS // 4
REST = 16
CELLS = 4 + 2 * HALO_CELLS
SMALL = 8
SLAB_ROWS = CH + 8


def polynomial(coeffs, x):
    total = coeffs[-1] * x + coeffs[-2]
    for c in coeffs[-3::-1]:
        total = total * x + c
    return total


def factor_rows(factor_ref, size, row, source, target, keep):
    dx = (target[0] - source[0]) * (1.0 / cutoff)
    dy = (target[1] - source[1]) * (1.0 / cutoff)
    dz = (target[2] - source[2]) * (1.0 / cutoff)
    xx, yy, zz = dx * dx, dy * dy, dz * dz
    square = xx + yy + zz
    inside = jnp.minimum(square, 1.0)
    gap = 1.0 - inside
    base = (gap * gap) * keep * polynomial(SINC_COEFFS, inside)
    twice_cos = polynomial([2.0 * c for c in COS_COEFFS], inside)
    raw = [base, twice_cos * base]
    for _ in range(NB - 2):
        raw.append(twice_cos * raw[-1] - raw[-2])
    radial = [value if b == 0 else value * (1.0 / (b + 1)) for b, value in enumerate(raw)]
    root_three = math.sqrt(3.0)
    root_fifteen = math.sqrt(15.0)
    root_five = math.sqrt(5.0)
    wide_x = root_fifteen * dx
    harmonic = [
        None,
        root_three * dx,
        root_three * dy,
        root_three * dz,
        wide_x * dy,
        (root_fifteen * dy) * dz,
        (0.5 * root_five) * (3.0 * zz - square),
        wide_x * dz,
        (0.5 * root_fifteen) * (xx - yy),
    ]
    for b in range(NB):
        rows = slice(b * size + row, b * size + row + ROWS)
        for y in range(NY):
            value = radial[b] if y == 0 else radial[b] * harmonic[y]
            factor_ref[rows, y * GROUP : (y + 1) * GROUP] = value.astype(jnp.bfloat16)


def column_to_row(column, size):
    wide = jnp.broadcast_to(column, (size, GROUP))
    at = lax.broadcasted_iota(jnp.int32, (size, GROUP), 0)
    lane = lax.broadcasted_iota(jnp.int32, (size, GROUP), 1)
    return jnp.sum(jnp.where(at == lane, wide, 0.0), axis=0, keepdims=True)


def split_kernel(*refs):
    features_ref, place_in_ref, *inputs = refs[: SMALL + 2]
    near_ref, far_ref, *outputs = refs[SMALL + 2 : 2 * SMALL + 4]
    place_ref, sems = refs[2 * SMALL + 4 :]
    core = lax.axis_index("space") % 2
    place_copy = pltpu.make_async_copy(place_in_ref, place_ref, sems.at[2])
    place_copy.start()
    copies = []
    for k, (ref, side) in enumerate(((near_ref, 1 - core), (far_ref, core))):
        at = pl.ds(pl.multiple_of(side * GROUP, GROUP), GROUP)
        copies.append(
            pltpu.make_async_copy(features_ref.at[0, :, at], ref.at[pl.ds(0, CH)], sems.at[k])
        )
    for k, (src, dst) in enumerate(zip(inputs, outputs)):
        copies.append(pltpu.make_async_copy(src, dst, sems.at[3 + k]))
    for copy in copies:
        copy.start()
    place_copy.wait()
    low, high = slice(GROUP), slice(GROUP, 2 * GROUP)
    filler = jnp.zeros((5, GROUP), jnp.float32)
    for ref, one, two in ((near_ref, high, low), (far_ref, low, high)):
        rows = [
            jnp.where(core == 0, place_ref[axis, :, one], place_ref[axis, :, two]) for axis in range(3)
        ]
        ref[CH:, :] = jnp.concatenate(rows + [filler], axis=0)
    for copy in copies:
        copy.wait()


def live_flags(count, pair_target, pair_source):
    size = (4 * CELLS, pair_target.shape[1])
    at = lax.broadcasted_iota(jnp.int32, size, 0)
    slot = lax.broadcasted_iota(jnp.int32, size, 1)
    hit = (pair_target * CELLS + pair_source == at) & (slot < count)
    return jnp.max(jnp.where(hit, message_scale, 0.0), axis=1, keepdims=True)


def keep_row(flags, t, low, high):
    lane = lax.broadcasted_iota(jnp.int32, (1, GROUP), 1)
    one, two = (2 * t) * CELLS + low, (2 * t + 1) * CELLS + high
    return jnp.where(lane < CELL_ATOMS, flags[one : one + 1], flags[two : two + 1])


def set_group(scaled_ref, features, weight_t):
    for b in range(NB):
        scaled_ref[:, b * GROUP : (b + 1) * GROUP] = (features * weight_t[:, b : b + 1]).astype(
            jnp.bfloat16
        )


def set_cell(scaled_ref, features, half, weight_t):
    first = lax.broadcasted_iota(jnp.int32, (CH, GROUP), 1) < CELL_ATOMS
    turned = pltpu.roll(features, CELL_ATOMS, 1)
    twice = jnp.where(first, features, turned) if half == 0 else jnp.where(first, turned, features)
    for k in range(NB // 2):
        weights = jnp.where(first, weight_t[:, 2 * k : 2 * k + 1], weight_t[:, 2 * k + 1 : 2 * k + 2])
        scaled_ref[:, k * GROUP : (k + 1) * GROUP] = (twice * weights).astype(jnp.bfloat16)


def set_place(place_ref, slab):
    place = slab[CH:].T
    for axis in range(3):
        place_ref[axis] = jnp.broadcast_to(place[:, axis : axis + 1], (GROUP, GROUP))


def fill_steps(factor_ref, size, source_of, keeps, target, diagonal=False):
    def step(row):
        keep = jnp.broadcast_to(keeps[row // CELL_ATOMS], (ROWS, GROUP))
        if diagonal:
            row_at = lax.broadcasted_iota(jnp.int32, (ROWS, GROUP), 0)
            lane_at = lax.broadcasted_iota(jnp.int32, (ROWS, GROUP), 1)
            keep = jnp.where(row_at + row == lane_at, 0.0, keep)
        factor_rows(factor_ref, size, row, source_of(row), target, keep)

    return [functools.partial(step, row) for row in range(0, size, ROWS)]


def rows_of(place_ref, start):
    return lambda row: [place_ref[axis, start + row : start + row + ROWS, :] for axis in range(3)]


def merged_rows(low_ref, low_start, high_ref, high_start):
    low, high = rows_of(low_ref, low_start), rows_of(high_ref, high_start)

    def rows(row):
        first = lax.broadcasted_iota(jnp.int32, (ROWS, GROUP), 1) < CELL_ATOMS
        return [jnp.where(first, one, two) for one, two in zip(low(row), high(row))]

    return rows


def product_steps(scaled_ref, factor_ref, totals, merged=False):
    def step(k):
        width = min(WIDTH, NY * GROUP - k * WIDTH)
        product = jnp.dot(
            scaled_ref[...],
            factor_ref[:, k * WIDTH : k * WIDTH + width],
            preferred_element_type=jnp.float32,
        )
        if merged:
            lane = lax.broadcasted_iota(jnp.int32, (CH, width), 1) % GROUP
            product = jnp.where(lane < CELL_ATOMS, product[:CH], product[CH:])
        totals[k] = product if totals[k] is None else totals[k] + product

    return [functools.partial(step, k) for k in range(CHUNKS)]


def interleave(one, two):
    done = 0
    for k, step in enumerate(one):
        step()
        upto = (k + 1) * len(two) // len(one)
        for other in two[done:upto]:
            other()
        done = upto


def local_kernel(
    count_ref,
    pair_target_ref,
    pair_source_ref,
    radial_ref,
    near_ref,
    far_ref,
    group_factor_ref,
    cell_factor_ref,
    messages_ref,
    keep_ref,
    place_ref,
    group_ref,
    cell_ref,
):
    even = lax.axis_index("space") % 2 == 0
    near, far = near_ref[...], far_ref[...]
    slabs = (jnp.where(even, far, near), jnp.where(even, near, far))
    targets = [[slab[CH + axis : CH + axis + 1] for axis in range(3)] for slab in slabs]
    flags = live_flags(count_ref[0, 0], pair_target_ref[...], pair_source_ref[...])
    weight_t = radial_ref[...].T
    for g in range(2):
        set_place(place_ref.at[g], slabs[g])
        set_group(group_ref.at[g], slabs[g][:CH], weight_t)
        set_cell(cell_ref.at[g], slabs[1 - g][:CH], g, weight_t)

    def fill_group(t):
        keeps = [keep_row(flags, t, cell, cell) for cell in (2 * t + 2, 2 * t + 3)]
        return fill_steps(
            group_factor_ref.at[t], GROUP, rows_of(place_ref.at[t], 0), keeps, targets[t], True
        )

    def fill_cell(t):
        cell = 4 - t
        source_of = rows_of(place_ref.at[1 - t], t * CELL_ATOMS)
        return fill_steps(
            cell_factor_ref.at[t], CELL_ATOMS, source_of, [keep_row(flags, t, cell, cell)], targets[t]
        )

    totals = [[None] * CHUNKS for _ in range(2)]
    for step in fill_cell(0):
        step()
    interleave(product_steps(cell_ref.at[0], cell_factor_ref.at[0], totals[0]), fill_group(0))
    interleave(product_steps(group_ref.at[0], group_factor_ref.at[0], totals[0]), fill_group(1))
    interleave(product_steps(group_ref.at[1], group_factor_ref.at[1], totals[1]), fill_cell(1))
    for step in product_steps(cell_ref.at[1], cell_factor_ref.at[1], totals[1]):
        step()
    for t in range(2):
        messages_ref[t] = jnp.concatenate(totals[t], axis=1)
    rows = [
        keep_row(flags, 0, 1, 1),
        keep_row(flags, 0, 0, 5),
        keep_row(flags, 1, 6, 6),
        keep_row(flags, 1, 2, 7),
    ]
    keep_ref[...] = jnp.concatenate(rows + [jnp.zeros((4, GROUP), jnp.float32)], axis=0)


def node_kernel(
    scale,
    near_ref,
    far_ref,
    from_pair_ref,
    from_cross_ref,
    messages_ref,
    keep_ref,
    own_place_ref,
    species_ref,
    shift_ref,
    energy_grad_ref,
    radial_ref,
    mix_ref,
    readout_ref,
    energy_ref,
    spread_ref,
    kept_ref,
    sent_ref,
    rest_ref,
    grad_messages_ref,
    cell_factor_ref,
    merged_factor_ref,
    cell_ref,
    merged_ref,
    place_ref,
):
    even = lax.axis_index("space") % 2 == 0
    weight_t = radial_ref[...].T
    near, far = near_ref[...], far_ref[...]
    from_pair, from_cross = from_pair_ref[...], from_cross_ref[...]
    slabs = (
        jnp.where(even, from_cross, from_pair),
        jnp.where(even, far, near),
        jnp.where(even, near, far),
        jnp.where(even, from_pair, from_cross),
    )
    targets = [[slab[CH + axis : CH + axis + 1] for axis in range(3)] for slab in slabs[1:3]]

    for t in range(2):
        set_place(place_ref.at[t], slabs[3 * t])
        set_cell(cell_ref.at[t], slabs[3 * t][:CH], 1 - t, weight_t)
        set_cell(merged_ref.at[t, pl.ds(0, CH)], slabs[t][:CH], 0, weight_t)
        set_cell(merged_ref.at[t, pl.ds(CH, CH)], slabs[t + 2][:CH], 1, weight_t)

    def fill_cell(t):
        source_of = rows_of(place_ref.at[t], (1 - t) * CELL_ATOMS)
        keeps = [keep_ref[2 * t : 2 * t + 1, :]]
        return fill_steps(cell_factor_ref.at[t], CELL_ATOMS, source_of, keeps, targets[t])

    def fill_merged(t):
        places = (place_ref.at[0], own_place_ref.at[0], own_place_ref.at[1], place_ref.at[1])
        source_of = merged_rows(places[t], 0, places[t + 2], CELL_ATOMS)
        keeps = [keep_ref[2 * t + 1 : 2 * t + 2, :]]
        return fill_steps(merged_factor_ref.at[t], CELL_ATOMS, source_of, keeps, targets[t])

    totals = [
        [messages_ref[t, :, k * WIDTH : min((k + 1) * WIDTH, NY * GROUP)] for k in range(CHUNKS)]
        for t in range(2)
    ]

    def add_cell(t):
        return product_steps(cell_ref.at[t], cell_factor_ref.at[t], totals[t])

    def add_merged(t):
        return product_steps(merged_ref.at[t], merged_factor_ref.at[t], totals[t], True)

    readout = jnp.broadcast_to(readout_ref[...], (8, CH)).T[:, :1]
    mix = mix_ref[...]
    mix_t = mix.astype(jnp.float32).T.astype(jnp.bfloat16)

    for step in fill_cell(0):
        step()
    interleave(add_cell(0), fill_merged(0))
    interleave(add_merged(0), fill_cell(1))
    interleave(add_cell(1), fill_merged(1))
    for step in add_merged(1):
        step()

    sides = [jnp.concatenate(total, axis=1) for total in totals]
    part = [
        jnp.concatenate([side[:, y * GROUP : (y + 1) * GROUP] for side in sides], axis=1)
        for y in range(NY)
    ]
    invariants = jnp.concatenate(
        [
            part[0],
            0.5 * (part[1] * part[1] + part[2] * part[2] + part[3] * part[3]),
            0.5
            * (
                part[4] * part[4]
                + part[5] * part[5]
                + part[6] * part[6]
                + part[7] * part[7]
                + part[8] * part[8]
            ),
        ],
        axis=0,
    ).astype(jnp.bfloat16)
    preact = jnp.dot(mix_t, invariants, preferred_element_type=jnp.float32)
    gating = jax.nn.sigmoid(preact)
    energy_grad = energy_grad_ref[...]
    spread = readout * energy_grad
    grad_pre = (spread * gating * (1.0 + preact * (1.0 - gating))).astype(jnp.bfloat16)
    grad_inv = jnp.dot(mix, grad_pre, preferred_element_type=jnp.float32)
    grad_mix = scale * lax.dot_general(
        invariants, grad_pre, (((1,), (1,)), ((), ())), preferred_element_type=jnp.float32
    )
    kept_ref[...] = jnp.where(even, grad_mix[:HALF], grad_mix[HALF:])
    sent_ref[...] = jnp.where(even, grad_mix[HALF:], grad_mix[:HALF])
    for y in range(NY):
        order = 0 if y == 0 else 1 if y < 4 else 2
        grad = grad_inv[order * CH : (order + 1) * CH]
        grad = (grad if y == 0 else grad * part[y]).astype(jnp.bfloat16)
        for t in range(2):
            grad_messages_ref[t, :, y * GROUP : (y + 1) * GROUP] = grad[:, t * GROUP : (t + 1) * GROUP]

    updated = jnp.concatenate([slabs[1][:CH], slabs[2][:CH]], axis=1) + preact * gating
    kinds = species_ref[...]
    shifts = jnp.zeros((1, 2 * GROUP), jnp.float32)
    for n in range(NSPEC):
        shifts = jnp.where(kinds == n, shift_ref[:, n : n + 1], shifts)
    energy_ref[...] = jnp.sum(updated * readout, axis=0, keepdims=True) + shifts
    spread_ref[...] = spread
    grad_out = jnp.sum(updated * energy_grad, axis=1, keepdims=True)
    readout_row = column_to_row(grad_out, CH)
    here = lax.broadcasted_iota(jnp.int32, (NSPEC, 2 * GROUP), 0) == kinds
    by_kind = jnp.sum(jnp.where(here, energy_grad, 0.0), axis=1, keepdims=True)
    rest_ref[...] = jnp.concatenate(
        [readout_row, column_to_row(by_kind, NSPEC), jnp.zeros((6, CH), jnp.float32)], axis=0
    )


def back(factor, grad_messages):
    return lax.dot_general(
        factor, grad_messages, (((1,), (1,)), ((), ())), preferred_element_type=jnp.float32
    )


def source_grads(total, features_t, weight):
    size = features_t.shape[0]
    grad_t = None
    radial = []
    for b in range(NB):
        piece = total[b * size : (b + 1) * size]
        term = piece * weight[b : b + 1, :]
        grad_t = term if grad_t is None else grad_t + term
        radial.append(jnp.sum(piece * features_t, axis=0, keepdims=True))
    return grad_t, jnp.concatenate(radial, axis=0)


def halo_back_kernel(
    cell_factor_ref,
    merged_factor_ref,
    grad_messages_ref,
    near_ref,
    far_ref,
    from_pair_ref,
    from_cross_ref,
    radial_ref,
    sent_ref,
    extra_ref,
    share_ref,
):
    even = lax.axis_index("space") % 2 == 0
    weight = radial_ref[...]
    near, far = near_ref[:CH, :], far_ref[:CH, :]
    from_pair, from_cross = from_pair_ref[:CH, :], from_cross_ref[:CH, :]
    features_t = [
        jnp.where(even, one, two).T
        for one, two in ((from_cross, from_pair), (far, near), (near, far), (from_pair, from_cross))
    ]
    first = lax.broadcasted_iota(jnp.int32, (CH, NY * GROUP), 1) % GROUP < CELL_ATOMS
    low, high = slice(CELL_ATOMS), slice(CELL_ATOMS, GROUP)
    share = None
    grads = {}
    for t in range(2):
        grad = grad_messages_ref[t]
        none = jnp.zeros_like(grad)
        both = jnp.concatenate([jnp.where(first, grad, none), jnp.where(first, none, grad)], axis=0)
        merged = back(merged_factor_ref[t], both)
        pieces = (
            (3 * t, 1 - t, back(cell_factor_ref[t], grad)),
            (t, 0, merged[:, :CH]),
            (t + 2, 1, merged[:, CH:]),
        )
        for g, half, total in pieces:
            grads[g, half], part = source_grads(total, features_t[g][(low, high)[half]], weight)
            share = part if share is None else share + part
    grad_before = jnp.concatenate([grads[0, 0], grads[0, 1]], axis=0).T
    grad_after = jnp.concatenate([grads[3, 0], grads[3, 1]], axis=0).T
    sent_ref[:CH, :] = jnp.where(even, grad_after, grad_before)
    sent_ref[CH:, :] = jnp.where(even, grad_before, grad_after)
    extra_ref[low, :] = grads[1, 0]
    extra_ref[high, :] = grads[2, 1]
    share_ref[...] = share


def own_back_kernel(
    scale,
    group_factor_ref,
    cell_factor_ref,
    grad_messages_ref,
    near_ref,
    far_ref,
    radial_ref,
    extra_ref,
    share_ref,
    rest_ref,
    spread_ref,
    own_grad_ref,
    joined_ref,
):
    even = lax.axis_index("space") % 2 == 0
    weight = radial_ref[...]
    near, far = near_ref[:CH, :], far_ref[:CH, :]
    share = share_ref[...]
    low, high = slice(CELL_ATOMS), slice(CELL_ATOMS, GROUP)
    for t, features in enumerate((jnp.where(even, far, near), jnp.where(even, near, far))):
        features_t = features.T
        total = back(group_factor_ref[t], grad_messages_ref[t])
        grad, part = source_grads(total, features_t, weight)
        inner, outer = (high, low) if t == 0 else (low, high)
        total = back(cell_factor_ref[1 - t], grad_messages_ref[1 - t])
        one, more = source_grads(total, features_t[inner], weight)
        two = extra_ref[outer, :]
        grad = (grad + jnp.concatenate([two, one] if t == 0 else [one, two], axis=0)).T
        at = slice(t * GROUP, (t + 1) * GROUP)
        own_grad_ref[:, at] = spread_ref[:, at] + grad
        share = share + part + more
    joined_ref[:NB, :] = share * scale
    joined_ref[NB:, :] = rest_ref[...] * scale


def quarter_kernel(kept_ref, received_ref, keep_ref, send_ref):
    first = first_of_pair()
    low = kept_ref[:QUARTER, :] + received_ref[:QUARTER, :]
    high = kept_ref[QUARTER:, :] + received_ref[QUARTER:, :]
    keep_ref[...] = jnp.where(first, low, high)
    send_ref[...] = jnp.where(first, high, low)


def join_kernel(kept_ref, received_ref, rest_ref, out_ref):
    out_ref[:QUARTER, :] = kept_ref[...] + received_ref[...]
    out_ref[QUARTER:, :] = rest_ref[...]


def gather_kernel(mine_ref, along_ref, other_ref, both_ref, out_ref):
    first = first_of_pair()
    at, rest = slice(QUARTER), slice(QUARTER, QUARTER + REST)
    mine = mine_ref[at, :] + along_ref[at, :]
    other = other_ref[at, :] + both_ref[at, :]
    out_ref[:QUARTER, :] = jnp.where(first, mine, other)
    out_ref[QUARTER:HALF, :] = jnp.where(first, other, mine)
    out_ref[HALF:, :] = (mine_ref[rest, :] + along_ref[rest, :]) + (other_ref[rest, :] + both_ref[rest, :])


def fold_kernel(own_ref, from_pair_ref, from_cross_ref, energy_in_ref, grad_ref, energy_ref):
    even = lax.axis_index("space") % 2 == 0
    pair = from_pair_ref[:CH, :]
    cross = from_cross_ref[...]
    grad_ref[0, :, :GROUP] = own_ref[:, :GROUP] + jnp.where(even, cross, pair)
    grad_ref[0, :, GROUP:] = own_ref[:, GROUP:] + jnp.where(even, pair, cross)
    energy_ref[...] = energy_in_ref[...]


def finish_kernel(mine_ref, other_ref, radial_ref, mix_ref, readout_ref, shift_ref):
    even = lax.axis_index("space") % 2 == 0
    mine, other = mine_ref[:HALF, :], other_ref[:HALF, :]
    mix_ref[:HALF, :] = jnp.where(even, mine, other)
    mix_ref[HALF:, :] = jnp.where(even, other, mine)
    rest = mine_ref[HALF:, :] + other_ref[HALF:, :]
    radial_ref[...] = rest[:NB]
    readout_ref[...] = rest[NB : NB + 1]
    shift_ref[...] = rest[NB + 1 : NB + 2, :NSPEC]


def first_of_pair():
    space, dp = lax.axis_index("space"), lax.axis_index("dp")
    return jnp.where(space % 2 == 0, dp, space // 2) % 2 == 0


def exchange_routes(space, dp):
    along = [(0, 1 << k) for k in range(dp.bit_length() - 1)]
    across = [(1 << k, 0) for k in range(1, space.bit_length() - 1)]
    shared = (along[0], across[0])
    orders = (across + along[1:], along[:1] + across[1:] + along[1:])
    orders = (orders[0], orders[1][:-2] + orders[1][:-3:-1])
    count = len(orders[0])

    def route(*places):
        moves = []
        for s in range(space):
            step = [shared[s % 2] if k < 0 else orders[s % 2][k] for k in places]
            for d in range(dp):
                to_s, to_d = s, d
                for one, two in step:
                    to_s, to_d = to_s ^ one, to_d ^ two
                moves.append((s * dp + d, to_s * dp + to_d))
        return moves

    rounds = []
    for k in range(0, count - 1, 2):
        if k + 1 < count - 1:
            rounds.append([route(k), route(k + 1), route(k, k + 1)])
        else:
            rounds.append([route(k)])
    last = count - 1
    rounds.append([route(last), route(-1), route(last, -1)])
    return route(-1), rounds


def call(kernel, name, inputs, outputs, mib=4, scratch=(), flops=0):
    vmem = pl.BlockSpec(memory_space=pltpu.VMEM)
    shapes = tuple(jax.ShapeDtypeStruct(shape, kind) for shape, kind in outputs)
    moved = sum(math.prod(v.shape) * v.dtype.itemsize for v in (*inputs, *shapes))
    return pl.pallas_call(
        kernel,
        out_shape=shapes,
        in_specs=[vmem] * len(inputs),
        out_specs=(vmem,) * len(shapes),
        scratch_shapes=scratch,
        compiler_params=pltpu.CompilerParams(vmem_limit_bytes=mib * 1024 * 1024),
        cost_estimate=pl.CostEstimate(flops=flops, bytes_accessed=moved, transcendentals=0),
        name=name,
    )(*inputs)


def in_hbm(value):
    return pltpu.with_memory_space_constraint(value, pltpu.HBM)


def body(
    node_features,
    positions,
    species,
    energy_cotangent,
    pair_target,
    pair_source,
    pair_count,
    radial_weight,
    mix_weight,
    readout_weight,
    species_shift,
):
    atoms_here = node_features.shape[2]
    space, dp = lax.axis_size("space"), lax.axis_size("dp")
    scale = 1.0 / math.sqrt(atoms_here * space * dp)
    pair = [(i, i ^ 1) for i in range(space)]
    cross = [(i, ((i + 1) ^ 1) - 1) for i in range(1, space - 1)]
    onward = [(i, i + 2) for i in range(0, space - 2, 2)] + [(i, i - 2) for i in range(3, space, 2)]

    hbm = pl.BlockSpec(memory_space=pltpu.HBM)
    smem = pl.BlockSpec(memory_space=pltpu.SMEM)
    vmem = pl.BlockSpec(memory_space=pltpu.VMEM)
    f32, bf16 = jnp.float32, jnp.bfloat16
    small = (
        pair_target,
        pair_source,
        species,
        species_shift.reshape(1, NSPEC),
        energy_cotangent,
        radial_weight,
        mix_weight,
        readout_weight.reshape(1, CH),
    )
    near, far, *small = pl.pallas_call(
        split_kernel,
        out_shape=(jax.ShapeDtypeStruct((SLAB_ROWS, GROUP), f32),) * 2
        + tuple(jax.ShapeDtypeStruct(v.shape, v.dtype) for v in small),
        in_specs=[hbm] * (SMALL + 2),
        out_specs=(vmem,) * (SMALL + 2),
        scratch_shapes=[
            pltpu.VMEM((3, 1, atoms_here), f32),
            pltpu.SemaphoreType.DMA((SMALL + 3,)),
        ],
        compiler_params=pltpu.CompilerParams(vmem_limit_bytes=4 * 1024 * 1024),
        name="split",
    )(
        in_hbm(node_features),
        in_hbm(jnp.transpose(positions, (1, 0, 2))),
        *[in_hbm(v) for v in small],
    )
    targets, sources, species, shift, energy_grad, radial, mix, readout = small
    from_cross = lax.ppermute(far, "space", cross)
    from_pair = lax.ppermute(near, "space", pair)

    block_flops = 2 * CH * NB * NY * GROUP * GROUP
    group_factor, cell_factor, messages, keep, place = pl.pallas_call(
        local_kernel,
        out_shape=(
            jax.ShapeDtypeStruct((2, NB * GROUP, NY * GROUP), bf16),
            jax.ShapeDtypeStruct((2, NB * CELL_ATOMS, NY * GROUP), bf16),
            jax.ShapeDtypeStruct((2, CH, NY * GROUP), f32),
            jax.ShapeDtypeStruct((8, GROUP), f32),
            jax.ShapeDtypeStruct((2, 3, GROUP, GROUP), f32),
        ),
        in_specs=[smem] + [vmem] * 5,
        out_specs=(vmem,) * 5,
        scratch_shapes=[
            pltpu.VMEM((2, CH, NB * GROUP), bf16),
            pltpu.VMEM((2, CH, NB * CELL_ATOMS), bf16),
        ],
        compiler_params=pltpu.CompilerParams(vmem_limit_bytes=16 * 1024 * 1024),
        cost_estimate=pl.CostEstimate(
            flops=3 * block_flops, bytes_accessed=11_000_000, transcendentals=0
        ),
        name="local_pairs",
    )(pair_count, targets, sources, radial, near, far)

    energy, spread, kept, sent, rest, grad_messages, halo_factor, merged_factor = call(
        functools.partial(node_kernel, scale),
        "node_stage",
        (
            near,
            far,
            from_pair,
            from_cross,
            messages,
            keep,
            place,
            species,
            shift,
            energy_grad,
            radial,
            mix,
            readout,
        ),
        (
            ((1, atoms_here), f32),
            ((CH, atoms_here), f32),
            ((HALF, CH), f32),
            ((HALF, CH), f32),
            ((8, CH), f32),
            ((2, CH, NY * GROUP), bf16),
            ((2, NB * CELL_ATOMS, NY * GROUP), bf16),
            ((2, NB * CELL_ATOMS, NY * GROUP), bf16),
        ),
        16,
        [
            pltpu.VMEM((2, CH, NB * CELL_ATOMS), bf16),
            pltpu.VMEM((2, 2 * CH, NB * CELL_ATOMS), bf16),
            pltpu.VMEM((2, 3, GROUP, GROUP), f32),
        ],
        2 * block_flops,
    )

    received = lax.ppermute(sent, "space", pair)
    halo_grad, extra, share = call(
        halo_back_kernel,
        "halo_back",
        (
            halo_factor,
            merged_factor,
            grad_messages,
            near,
            far,
            from_pair,
            from_cross,
            radial,
        ),
        (((2 * CH, GROUP), f32), ((GROUP, CH), f32), ((NB, CH), f32)),
        12,
        (),
        2 * block_flops,
    )
    received, share = lax.optimization_barrier((received, share))
    quarter, sent = call(
        quarter_kernel,
        "quarter",
        (kept, received),
        (((QUARTER, CH), f32), ((QUARTER, CH), f32)),
    )
    sharing, (*rounds, last) = exchange_routes(space, dp)
    everyone = ("space", "dp")
    sent, grad_messages, halo_grad = lax.optimization_barrier((sent, grad_messages, halo_grad))
    received = lax.ppermute(sent, everyone, sharing)
    from_pair = lax.ppermute(halo_grad, "space", pair)
    own_grad, joined = call(
        functools.partial(own_back_kernel, scale),
        "own_back",
        (
            group_factor,
            cell_factor,
            grad_messages,
            near,
            far,
            radial,
            extra,
            share,
            rest,
            spread,
        ),
        (((CH, atoms_here), f32), ((REST, CH), f32)),
        12,
        (),
        3 * block_flops,
    )
    (value,) = call(
        join_kernel, "join", (quarter, received, joined), (((QUARTER + REST, CH), f32),)
    )
    value, from_pair = lax.optimization_barrier((value, from_pair))
    for turn, routes in enumerate(rounds):
        arrived = [lax.ppermute(value, everyone, route) for route in routes]
        if turn == 0:
            from_cross = lax.ppermute(from_pair[CH:], "space", onward)
        value = value + arrived[0]
        if len(arrived) == 3:
            value = value + (arrived[1] + arrived[2])
    arrived = [lax.ppermute(value, everyone, route) for route in last]
    value, from_cross, *arrived = lax.optimization_barrier((value, from_cross, *arrived))
    (value,) = call(
        gather_kernel,
        "gather",
        (value, *arrived),
        (((HALF + REST, CH), f32),),
    )
    feature_grad, energy = call(
        fold_kernel,
        "fold",
        (own_grad, from_pair, from_cross, energy),
        (((1, CH, atoms_here), f32), ((1, atoms_here), f32)),
    )
    radial_grad, mix_grad, readout_grad, shift_grad = call(
        finish_kernel,
        "finish",
        (value, lax.ppermute(value, "space", pair)),
        (((NB, CH), f32), ((MIX_ROWS, CH), f32), ((1, CH), f32), ((1, NSPEC), f32)),
    )
    return (
        energy,
        feature_grad,
        radial_grad,
        mix_grad,
        readout_grad.reshape(CH),
        shift_grad.reshape(NSPEC),
    )


def solution(mesh):
    return jax.shard_map(
        body,
        mesh=mesh,
        in_specs=(
            P("dp", None, "space"),
            P("dp", None, "space"),
            P("dp", "space"),
            P("dp", "space"),
            P("dp", "space"),
            P("dp", "space"),
            P("dp", "space"),
            P(),
            P(),
            P(),
            P(),
        ),
        out_specs=(P("dp", "space"), P("dp", None, "space"), P(), P(), P(), P()),
        check_vma=False,
    )
```

```python
import functools
import math

import jax
import jax.numpy as jnp
from jax import lax
from jax.experimental import pallas as pl
from jax.experimental.pallas import tpu as pltpu
from jax.sharding import PartitionSpec as P

CH = 128
NB = 8
NY = 9
NSPEC = 8
CELL_ATOMS = 64
HALO_CELLS = 2
GROUP = 2 * CELL_ATOMS
ROWS = 16
WIDTH = 256
CHUNKS = -(-NY * GROUP // WIDTH)

cutoff = 5.0
message_scale = 0.25

COS_COEFFS = (
    0.9999999998846169,
    -4.934802185771876,
    4.058711815779763,
    -1.3352602773967561,
    0.23532080049888648,
    -0.025785772074137014,
    0.0019043022864480008,
    -8.868331860867329e-05,
)
SINC_COEFFS = (
    0.9999999992502204,
    -1.6449339933418936,
    0.8117412468909989,
    -0.1907447263221115,
    0.02612742969685046,
    -0.0023157632409761065,
    0.00012580778956459784,
)

MIX_ROWS = 3 * CH
HALF = MIX_ROWS // 2
QUARTER = MIX_ROWS // 4
REST = 16
CELLS = 4 + 2 * HALO_CELLS
SMALL = 3
LATER = 5
SLAB_ROWS = CH + 8


def polynomial(coeffs, x):
    total = coeffs[-1] * x + coeffs[-2]
    for c in coeffs[-3::-1]:
        total = total * x + c
    return total


def factor_rows(factor_ref, size, row, source, target, keep):
    dx = (target[0] - source[0]) * (1.0 / cutoff)
    dy = (target[1] - source[1]) * (1.0 / cutoff)
    dz = (target[2] - source[2]) * (1.0 / cutoff)
    xx, yy, zz = dx * dx, dy * dy, dz * dz
    square = xx + yy + zz
    inside = jnp.minimum(square, 1.0)
    gap = 1.0 - inside
    base = (gap * gap) * keep * polynomial(SINC_COEFFS, inside)
    twice_cos = polynomial([2.0 * c for c in COS_COEFFS], inside)
    raw = [base, twice_cos * base]
    for _ in range(NB - 2):
        raw.append(twice_cos * raw[-1] - raw[-2])
    radial = [value if b == 0 else value * (1.0 / (b + 1)) for b, value in enumerate(raw)]
    root_three = math.sqrt(3.0)
    root_fifteen = math.sqrt(15.0)
    root_five = math.sqrt(5.0)
    wide_x = root_fifteen * dx
    harmonic = [
        None,
        root_three * dx,
        root_three * dy,
        root_three * dz,
        wide_x * dy,
        (root_fifteen * dy) * dz,
        (0.5 * root_five) * (3.0 * zz - square),
        wide_x * dz,
        (0.5 * root_fifteen) * (xx - yy),
    ]
    for b in range(NB):
        rows = slice(b * size + row, b * size + row + ROWS)
        for y in range(NY):
            value = radial[b] if y == 0 else radial[b] * harmonic[y]
            factor_ref[rows, y * GROUP : (y + 1) * GROUP] = value.astype(jnp.bfloat16)


def column_to_row(column, size):
    wide = jnp.broadcast_to(column, (size, GROUP))
    at = lax.broadcasted_iota(jnp.int32, (size, GROUP), 0)
    lane = lax.broadcasted_iota(jnp.int32, (size, GROUP), 1)
    return jnp.sum(jnp.where(at == lane, wide, 0.0), axis=0, keepdims=True)


def split_kernel(*refs):
    features_ref, place_in_ref, *inputs = refs[: SMALL + 2]
    near_ref, far_ref, *outputs = refs[SMALL + 2 : 2 * SMALL + 4]
    place_ref, sems = refs[2 * SMALL + 4 :]
    core = lax.axis_index("space") % 2
    place_copy = pltpu.make_async_copy(place_in_ref, place_ref, sems.at[2])
    place_copy.start()
    copies = []
    for k, (ref, side) in enumerate(((near_ref, 1 - core), (far_ref, core))):
        at = pl.ds(pl.multiple_of(side * GROUP, GROUP), GROUP)
        copies.append(
            pltpu.make_async_copy(features_ref.at[0, :, at], ref.at[pl.ds(0, CH)], sems.at[k])
        )
    for k, (src, dst) in enumerate(zip(inputs, outputs)):
        copies.append(pltpu.make_async_copy(src, dst, sems.at[3 + k]))
    for copy in copies:
        copy.start()
    place_copy.wait()
    low, high = slice(GROUP), slice(GROUP, 2 * GROUP)
    filler = jnp.zeros((5, GROUP), jnp.float32)
    for ref, one, two in ((near_ref, high, low), (far_ref, low, high)):
        rows = [
            jnp.where(core == 0, place_ref[axis, :, one], place_ref[axis, :, two]) for axis in range(3)
        ]
        ref[CH:, :] = jnp.concatenate(rows + [filler], axis=0)
    for copy in copies:
        copy.wait()


def live_flags(count, pair_target, pair_source):
    size = (4 * CELLS, pair_target.shape[1])
    at = lax.broadcasted_iota(jnp.int32, size, 0)
    slot = lax.broadcasted_iota(jnp.int32, size, 1)
    hit = (pair_target * CELLS + pair_source == at) & (slot < count)
    return jnp.max(jnp.where(hit, message_scale, 0.0), axis=1, keepdims=True)


def keep_row(flags, t, low, high):
    lane = lax.broadcasted_iota(jnp.int32, (1, GROUP), 1)
    one, two = (2 * t) * CELLS + low, (2 * t + 1) * CELLS + high
    return jnp.where(lane < CELL_ATOMS, flags[one : one + 1], flags[two : two + 1])


def set_group(scaled_ref, features, weight_t):
    for b in range(NB):
        scaled_ref[:, b * GROUP : (b + 1) * GROUP] = (features * weight_t[:, b : b + 1]).astype(
            jnp.bfloat16
        )


def set_cell(scaled_ref, features, half, weight_t):
    first = lax.broadcasted_iota(jnp.int32, (CH, GROUP), 1) < CELL_ATOMS
    turned = pltpu.roll(features, CELL_ATOMS, 1)
    twice = jnp.where(first, features, turned) if half == 0 else jnp.where(first, turned, features)
    for k in range(NB // 2):
        weights = jnp.where(first, weight_t[:, 2 * k : 2 * k + 1], weight_t[:, 2 * k + 1 : 2 * k + 2])
        scaled_ref[:, k * GROUP : (k + 1) * GROUP] = (twice * weights).astype(jnp.bfloat16)


def set_place(place_ref, slab):
    place = slab[CH:].T
    for axis in range(3):
        place_ref[axis] = jnp.broadcast_to(place[:, axis : axis + 1], (GROUP, GROUP))


def fill_steps(factor_ref, size, source_of, keeps, target, diagonal=False):
    def step(row):
        keep = jnp.broadcast_to(keeps[row // CELL_ATOMS], (ROWS, GROUP))
        if diagonal:
            row_at = lax.broadcasted_iota(jnp.int32, (ROWS, GROUP), 0)
            lane_at = lax.broadcasted_iota(jnp.int32, (ROWS, GROUP), 1)
            keep = jnp.where(row_at + row == lane_at, 0.0, keep)
        factor_rows(factor_ref, size, row, source_of(row), target, keep)

    return [functools.partial(step, row) for row in range(0, size, ROWS)]


def rows_of(place_ref, start):
    return lambda row: [place_ref[axis, start + row : start + row + ROWS, :] for axis in range(3)]


def merged_rows(low_ref, low_start, high_ref, high_start):
    low, high = rows_of(low_ref, low_start), rows_of(high_ref, high_start)

    def rows(row):
        first = lax.broadcasted_iota(jnp.int32, (ROWS, GROUP), 1) < CELL_ATOMS
        return [jnp.where(first, one, two) for one, two in zip(low(row), high(row))]

    return rows


def product_steps(scaled_ref, factor_ref, totals, merged=False):
    def step(k):
        width = min(WIDTH, NY * GROUP - k * WIDTH)
        product = jnp.dot(
            scaled_ref[...],
            factor_ref[:, k * WIDTH : k * WIDTH + width],
            preferred_element_type=jnp.float32,
        )
        if merged:
            lane = lax.broadcasted_iota(jnp.int32, (CH, width), 1) % GROUP
            product = jnp.where(lane < CELL_ATOMS, product[:CH], product[CH:])
        totals[k] = product if totals[k] is None else totals[k] + product

    return [functools.partial(step, k) for k in range(CHUNKS)]


def interleave(one, two):
    done = 0
    for k, step in enumerate(one):
        step()
        upto = (k + 1) * len(two) // len(one)
        for other in two[done:upto]:
            other()
        done = upto


def local_kernel(*refs):
    count_ref, pair_target_ref, pair_source_ref, radial_ref, near_ref, far_ref = refs[:6]
    later_in = refs[6 : 6 + LATER]
    group_factor_ref, cell_factor_ref, messages_ref, keep_ref, place_ref = refs[6 + LATER : 11 + LATER]
    later_out = refs[11 + LATER : 11 + 2 * LATER]
    group_ref, cell_ref, sems = refs[11 + 2 * LATER :]
    copies = [
        pltpu.make_async_copy(src, dst, sems.at[k]) for k, (src, dst) in enumerate(zip(later_in, later_out))
    ]
    for copy in copies:
        copy.start()
    even = lax.axis_index("space") % 2 == 0
    near, far = near_ref[...], far_ref[...]
    slabs = (jnp.where(even, far, near), jnp.where(even, near, far))
    targets = [[slab[CH + axis : CH + axis + 1] for axis in range(3)] for slab in slabs]
    flags = live_flags(count_ref[0, 0], pair_target_ref[...], pair_source_ref[...])
    weight_t = radial_ref[...].T
    for g in range(2):
        set_place(place_ref.at[g], slabs[g])
        set_group(group_ref.at[g], slabs[g][:CH], weight_t)
        set_cell(cell_ref.at[g], slabs[1 - g][:CH], g, weight_t)

    def fill_group(t):
        keeps = [keep_row(flags, t, cell, cell) for cell in (2 * t + 2, 2 * t + 3)]
        return fill_steps(
            group_factor_ref.at[t], GROUP, rows_of(place_ref.at[t], 0), keeps, targets[t], True
        )

    def fill_cell(t):
        cell = 4 - t
        source_of = rows_of(place_ref.at[1 - t], t * CELL_ATOMS)
        return fill_steps(
            cell_factor_ref.at[t], CELL_ATOMS, source_of, [keep_row(flags, t, cell, cell)], targets[t]
        )

    totals = [[None] * CHUNKS for _ in range(2)]
    for step in fill_cell(0):
        step()
    interleave(product_steps(cell_ref.at[0], cell_factor_ref.at[0], totals[0]), fill_group(0))
    interleave(product_steps(group_ref.at[0], group_factor_ref.at[0], totals[0]), fill_group(1))
    interleave(product_steps(group_ref.at[1], group_factor_ref.at[1], totals[1]), fill_cell(1))
    for step in product_steps(cell_ref.at[1], cell_factor_ref.at[1], totals[1]):
        step()
    for t in range(2):
        messages_ref[t] = jnp.concatenate(totals[t], axis=1)
    rows = [
        keep_row(flags, 0, 1, 1),
        keep_row(flags, 0, 0, 5),
        keep_row(flags, 1, 6, 6),
        keep_row(flags, 1, 2, 7),
    ]
    keep_ref[...] = jnp.concatenate(rows + [jnp.zeros((4, GROUP), jnp.float32)], axis=0)
    for copy in copies:
        copy.wait()


def node_kernel(
    scale,
    near_ref,
    far_ref,
    from_pair_ref,
    from_cross_ref,
    messages_ref,
    keep_ref,
    own_place_ref,
    energy_grad_ref,
    radial_ref,
    mix_ref,
    readout_ref,
    updated_ref,
    kept_ref,
    sent_ref,
    grad_messages_ref,
    cell_factor_ref,
    merged_factor_ref,
    cell_ref,
    merged_ref,
    place_ref,
):
    even = lax.axis_index("space") % 2 == 0
    weight_t = radial_ref[...].T
    near, far = near_ref[...], far_ref[...]
    from_pair, from_cross = from_pair_ref[...], from_cross_ref[...]
    slabs = (
        jnp.where(even, from_cross, from_pair),
        jnp.where(even, far, near),
        jnp.where(even, near, far),
        jnp.where(even, from_pair, from_cross),
    )
    targets = [[slab[CH + axis : CH + axis + 1] for axis in range(3)] for slab in slabs[1:3]]

    for t in range(2):
        set_place(place_ref.at[t], slabs[3 * t])
        set_cell(cell_ref.at[t], slabs[3 * t][:CH], 1 - t, weight_t)
        set_cell(merged_ref.at[t, pl.ds(0, CH)], slabs[t][:CH], 0, weight_t)
        set_cell(merged_ref.at[t, pl.ds(CH, CH)], slabs[t + 2][:CH], 1, weight_t)

    def fill_cell(t):
        source_of = rows_of(place_ref.at[t], (1 - t) * CELL_ATOMS)
        keeps = [keep_ref[2 * t : 2 * t + 1, :]]
        return fill_steps(cell_factor_ref.at[t], CELL_ATOMS, source_of, keeps, targets[t])

    def fill_merged(t):
        places = (place_ref.at[0], own_place_ref.at[0], own_place_ref.at[1], place_ref.at[1])
        source_of = merged_rows(places[t], 0, places[t + 2], CELL_ATOMS)
        keeps = [keep_ref[2 * t + 1 : 2 * t + 2, :]]
        return fill_steps(merged_factor_ref.at[t], CELL_ATOMS, source_of, keeps, targets[t])

    totals = [
        [messages_ref[t, :, k * WIDTH : min((k + 1) * WIDTH, NY * GROUP)] for k in range(CHUNKS)]
        for t in range(2)
    ]

    def add_cell(t):
        return product_steps(cell_ref.at[t], cell_factor_ref.at[t], totals[t])

    def add_merged(t):
        return product_steps(merged_ref.at[t], merged_factor_ref.at[t], totals[t], True)

    readout = jnp.broadcast_to(readout_ref[...], (8, CH)).T[:, :1]
    mix = mix_ref[...]
    mix_t = mix.astype(jnp.float32).T.astype(jnp.bfloat16)

    for step in fill_cell(0):
        step()
    interleave(add_cell(0), fill_merged(0))
    interleave(add_merged(0), fill_cell(1))
    interleave(add_cell(1), fill_merged(1))
    for step in add_merged(1):
        step()

    sides = [jnp.concatenate(total, axis=1) for total in totals]
    part = [
        jnp.concatenate([side[:, y * GROUP : (y + 1) * GROUP] for side in sides], axis=1)
        for y in range(NY)
    ]
    invariants = jnp.concatenate(
        [
            part[0],
            0.5 * (part[1] * part[1] + part[2] * part[2] + part[3] * part[3]),
            0.5
            * (
                part[4] * part[4]
                + part[5] * part[5]
                + part[6] * part[6]
                + part[7] * part[7]
                + part[8] * part[8]
            ),
        ],
        axis=0,
    ).astype(jnp.bfloat16)
    preact = jnp.dot(mix_t, invariants, preferred_element_type=jnp.float32)
    gating = jax.nn.sigmoid(preact)
    energy_grad = energy_grad_ref[...]
    spread = readout * energy_grad
    grad_pre = (spread * gating * (1.0 + preact * (1.0 - gating))).astype(jnp.bfloat16)
    grad_inv = jnp.dot(mix, grad_pre, preferred_element_type=jnp.float32)
    grad_mix = scale * lax.dot_general(
        invariants, grad_pre, (((1,), (1,)), ((), ())), preferred_element_type=jnp.float32
    )
    kept_ref[...] = jnp.where(even, grad_mix[:HALF], grad_mix[HALF:])
    sent_ref[...] = jnp.where(even, grad_mix[HALF:], grad_mix[:HALF])
    for y in range(NY):
        order = 0 if y == 0 else 1 if y < 4 else 2
        grad = grad_inv[order * CH : (order + 1) * CH]
        grad = (grad if y == 0 else grad * part[y]).astype(jnp.bfloat16)
        for t in range(2):
            grad_messages_ref[t, :, y * GROUP : (y + 1) * GROUP] = grad[:, t * GROUP : (t + 1) * GROUP]

    updated_ref[...] = jnp.concatenate([slabs[1][:CH], slabs[2][:CH]], axis=1) + preact * gating


def back(factor, grad_messages):
    return lax.dot_general(
        factor, grad_messages, (((1,), (1,)), ((), ())), preferred_element_type=jnp.float32
    )


def source_grads(total, features_t, weight):
    size = features_t.shape[0]
    grad_t = None
    radial = []
    for b in range(NB):
        piece = total[b * size : (b + 1) * size]
        term = piece * weight[b : b + 1, :]
        grad_t = term if grad_t is None else grad_t + term
        radial.append(jnp.sum(piece * features_t, axis=0, keepdims=True))
    return grad_t, jnp.concatenate(radial, axis=0)


def halo_back_kernel(
    cell_factor_ref,
    merged_factor_ref,
    grad_messages_ref,
    near_ref,
    far_ref,
    from_pair_ref,
    from_cross_ref,
    radial_ref,
    sent_ref,
    extra_ref,
    share_ref,
):
    even = lax.axis_index("space") % 2 == 0
    weight = radial_ref[...]
    near, far = near_ref[:CH, :], far_ref[:CH, :]
    from_pair, from_cross = from_pair_ref[:CH, :], from_cross_ref[:CH, :]
    features_t = [
        jnp.where(even, one, two).T
        for one, two in ((from_cross, from_pair), (far, near), (near, far), (from_pair, from_cross))
    ]
    first = lax.broadcasted_iota(jnp.int32, (CH, NY * GROUP), 1) % GROUP < CELL_ATOMS
    low, high = slice(CELL_ATOMS), slice(CELL_ATOMS, GROUP)
    share = None
    grads = {}
    for t in range(2):
        grad = grad_messages_ref[t]
        none = jnp.zeros_like(grad)
        both = jnp.concatenate([jnp.where(first, grad, none), jnp.where(first, none, grad)], axis=0)
        merged = back(merged_factor_ref[t], both)
        pieces = (
            (3 * t, 1 - t, back(cell_factor_ref[t], grad)),
            (t, 0, merged[:, :CH]),
            (t + 2, 1, merged[:, CH:]),
        )
        for g, half, total in pieces:
            grads[g, half], part = source_grads(total, features_t[g][(low, high)[half]], weight)
            share = part if share is None else share + part
    grad_before = jnp.concatenate([grads[0, 0], grads[0, 1]], axis=0).T
    grad_after = jnp.concatenate([grads[3, 0], grads[3, 1]], axis=0).T
    sent_ref[:CH, :] = jnp.where(even, grad_after, grad_before)
    sent_ref[CH:, :] = jnp.where(even, grad_before, grad_after)
    extra_ref[low, :] = grads[1, 0]
    extra_ref[high, :] = grads[2, 1]
    share_ref[...] = share


def own_back_kernel(
    scale,
    group_factor_ref,
    cell_factor_ref,
    grad_messages_ref,
    near_ref,
    far_ref,
    radial_ref,
    extra_ref,
    share_ref,
    updated_ref,
    species_ref,
    shift_ref,
    energy_grad_ref,
    readout_ref,
    own_grad_ref,
    joined_ref,
    energy_ref,
):
    even = lax.axis_index("space") % 2 == 0
    weight = radial_ref[...]
    near, far = near_ref[:CH, :], far_ref[:CH, :]
    share = share_ref[...]
    low, high = slice(CELL_ATOMS), slice(CELL_ATOMS, GROUP)
    readout = jnp.broadcast_to(readout_ref[...], (8, CH)).T[:, :1]
    updated, energy_grad, kinds = updated_ref[...], energy_grad_ref[...], species_ref[...]
    spread = readout * energy_grad
    shifts = jnp.zeros((1, 2 * GROUP), jnp.float32)
    for n in range(NSPEC):
        shifts = jnp.where(kinds == n, shift_ref[:, n : n + 1], shifts)
    energy_ref[...] = jnp.sum(updated * readout, axis=0, keepdims=True) + shifts
    readout_row = column_to_row(jnp.sum(updated * energy_grad, axis=1, keepdims=True), CH)
    here = lax.broadcasted_iota(jnp.int32, (NSPEC, 2 * GROUP), 0) == kinds
    by_kind = jnp.sum(jnp.where(here, energy_grad, 0.0), axis=1, keepdims=True)
    for t, features in enumerate((jnp.where(even, far, near), jnp.where(even, near, far))):
        features_t = features.T
        total = back(group_factor_ref[t], grad_messages_ref[t])
        grad, part = source_grads(total, features_t, weight)
        inner, outer = (high, low) if t == 0 else (low, high)
        total = back(cell_factor_ref[1 - t], grad_messages_ref[1 - t])
        one, more = source_grads(total, features_t[inner], weight)
        two = extra_ref[outer, :]
        grad = (grad + jnp.concatenate([two, one] if t == 0 else [one, two], axis=0)).T
        at = slice(t * GROUP, (t + 1) * GROUP)
        own_grad_ref[:, at] = spread[:, at] + grad
        share = share + part + more
    joined_ref[:NB, :] = share * scale
    rest = [readout_row, column_to_row(by_kind, NSPEC), jnp.zeros((6, CH), jnp.float32)]
    joined_ref[NB:, :] = jnp.concatenate(rest, axis=0) * scale


def quarter_kernel(kept_ref, received_ref, keep_ref, send_ref):
    first = first_of_pair()
    low = kept_ref[:QUARTER, :] + received_ref[:QUARTER, :]
    high = kept_ref[QUARTER:, :] + received_ref[QUARTER:, :]
    keep_ref[...] = jnp.where(first, low, high)
    send_ref[...] = jnp.where(first, high, low)


def join_kernel(kept_ref, received_ref, rest_ref, out_ref):
    out_ref[:QUARTER, :] = kept_ref[...] + received_ref[...]
    out_ref[QUARTER:, :] = rest_ref[...]


def gather_kernel(mine_ref, along_ref, other_ref, both_ref, out_ref):
    first = first_of_pair()
    at, rest = slice(QUARTER), slice(QUARTER, QUARTER + REST)
    mine = mine_ref[at, :] + along_ref[at, :]
    other = other_ref[at, :] + both_ref[at, :]
    out_ref[:QUARTER, :] = jnp.where(first, mine, other)
    out_ref[QUARTER:HALF, :] = jnp.where(first, other, mine)
    out_ref[HALF:, :] = (mine_ref[rest, :] + along_ref[rest, :]) + (other_ref[rest, :] + both_ref[rest, :])


def fold_kernel(own_ref, from_pair_ref, cross_one_ref, cross_two_ref, energy_in_ref, grad_ref, energy_ref):
    even = lax.axis_index("space") % 2 == 0
    pair = from_pair_ref[:CH, :]
    cross = cross_one_ref[...] + cross_two_ref[...]
    grad_ref[0, :, :GROUP] = own_ref[:, :GROUP] + jnp.where(even, cross, pair)
    grad_ref[0, :, GROUP:] = own_ref[:, GROUP:] + jnp.where(even, pair, cross)
    energy_ref[...] = energy_in_ref[...]


def finish_kernel(mine_ref, other_ref, radial_ref, mix_ref, readout_ref, shift_ref):
    even = lax.axis_index("space") % 2 == 0
    mine, other = mine_ref[:HALF, :], other_ref[:HALF, :]
    mix_ref[:HALF, :] = jnp.where(even, mine, other)
    mix_ref[HALF:, :] = jnp.where(even, other, mine)
    rest = mine_ref[HALF:, :] + other_ref[HALF:, :]
    radial_ref[...] = rest[:NB]
    readout_ref[...] = rest[NB : NB + 1]
    shift_ref[...] = rest[NB + 1 : NB + 2, :NSPEC]


def first_of_pair():
    space, dp = lax.axis_index("space"), lax.axis_index("dp")
    return jnp.where(space % 2 == 0, dp, space // 2) % 2 == 0


def exchange_routes(space, dp):
    along = [(0, 1 << k) for k in range(dp.bit_length() - 1)]
    across = [(1 << k, 0) for k in range(1, space.bit_length() - 1)]
    shared = (along[0], across[0])
    orders = (across + along[1:], along[:1] + across[1:] + along[1:])
    orders = (orders[0][:-2] + orders[0][:-3:-1], orders[1])
    count = len(orders[0])

    def route(*places):
        moves = []
        for s in range(space):
            step = [shared[s % 2] if k < 0 else orders[s % 2][k] for k in places]
            for d in range(dp):
                to_s, to_d = s, d
                for one, two in step:
                    to_s, to_d = to_s ^ one, to_d ^ two
                moves.append((s * dp + d, to_s * dp + to_d))
        return moves

    rounds = []
    for k in range(0, count - 1, 2):
        if k + 1 < count - 1:
            rounds.append([route(k), route(k + 1), route(k, k + 1)])
        else:
            rounds.append([route(k)])
    last = count - 1
    rounds.append([route(last), route(-1), route(last, -1)])
    return route(-1), rounds


def call(kernel, name, inputs, outputs, mib=4, scratch=(), flops=0):
    vmem = pl.BlockSpec(memory_space=pltpu.VMEM)
    shapes = tuple(jax.ShapeDtypeStruct(shape, kind) for shape, kind in outputs)
    moved = sum(math.prod(v.shape) * v.dtype.itemsize for v in (*inputs, *shapes))
    return pl.pallas_call(
        kernel,
        out_shape=shapes,
        in_specs=[vmem] * len(inputs),
        out_specs=(vmem,) * len(shapes),
        scratch_shapes=scratch,
        compiler_params=pltpu.CompilerParams(vmem_limit_bytes=mib * 1024 * 1024),
        cost_estimate=pl.CostEstimate(flops=flops, bytes_accessed=moved, transcendentals=0),
        name=name,
    )(*inputs)


def in_hbm(value):
    return pltpu.with_memory_space_constraint(value, pltpu.HBM)


def body(
    node_features,
    positions,
    species,
    energy_cotangent,
    pair_target,
    pair_source,
    pair_count,
    radial_weight,
    mix_weight,
    readout_weight,
    species_shift,
):
    atoms_here = node_features.shape[2]
    space, dp = lax.axis_size("space"), lax.axis_size("dp")
    scale = 1.0 / math.sqrt(atoms_here * space * dp)
    pair = [(i, i ^ 1) for i in range(space)]
    cross = [(i, ((i + 1) ^ 1) - 1) for i in range(1, space - 1)]
    onward = [[], []]
    for i in range(space):
        to = i + 2 if i % 2 == 0 else i - 2
        if 0 <= to < space:
            onward[(i // 2 + i) % 2].append((i, to))

    hbm = pl.BlockSpec(memory_space=pltpu.HBM)
    smem = pl.BlockSpec(memory_space=pltpu.SMEM)
    vmem = pl.BlockSpec(memory_space=pltpu.VMEM)
    f32, bf16 = jnp.float32, jnp.bfloat16
    small = (pair_target, pair_source, radial_weight)
    later = (
        species,
        species_shift.reshape(1, NSPEC),
        energy_cotangent,
        mix_weight,
        readout_weight.reshape(1, CH),
    )
    near, far, *small = pl.pallas_call(
        split_kernel,
        out_shape=(jax.ShapeDtypeStruct((SLAB_ROWS, GROUP), f32),) * 2
        + tuple(jax.ShapeDtypeStruct(v.shape, v.dtype) for v in small),
        in_specs=[hbm] * (SMALL + 2),
        out_specs=(vmem,) * (SMALL + 2),
        scratch_shapes=[
            pltpu.VMEM((3, 1, atoms_here), f32),
            pltpu.SemaphoreType.DMA((SMALL + 3,)),
        ],
        compiler_params=pltpu.CompilerParams(vmem_limit_bytes=4 * 1024 * 1024),
        name="split",
    )(
        in_hbm(node_features),
        in_hbm(jnp.transpose(positions, (1, 0, 2))),
        *[in_hbm(v) for v in small],
    )
    targets, sources, radial = small
    from_cross = lax.ppermute(far, "space", cross)
    from_pair = lax.ppermute(near, "space", pair)

    block_flops = 2 * CH * NB * NY * GROUP * GROUP
    group_factor, cell_factor, messages, keep, place, *later = pl.pallas_call(
        local_kernel,
        out_shape=(
            jax.ShapeDtypeStruct((2, NB * GROUP, NY * GROUP), bf16),
            jax.ShapeDtypeStruct((2, NB * CELL_ATOMS, NY * GROUP), bf16),
            jax.ShapeDtypeStruct((2, CH, NY * GROUP), f32),
            jax.ShapeDtypeStruct((8, GROUP), f32),
            jax.ShapeDtypeStruct((2, 3, GROUP, GROUP), f32),
            *[jax.ShapeDtypeStruct(v.shape, v.dtype) for v in later],
        ),
        in_specs=[smem] + [vmem] * 5 + [hbm] * LATER,
        out_specs=(vmem,) * (5 + LATER),
        scratch_shapes=[
            pltpu.VMEM((2, CH, NB * GROUP), bf16),
            pltpu.VMEM((2, CH, NB * CELL_ATOMS), bf16),
            pltpu.SemaphoreType.DMA((LATER,)),
        ],
        compiler_params=pltpu.CompilerParams(vmem_limit_bytes=16 * 1024 * 1024),
        cost_estimate=pl.CostEstimate(
            flops=3 * block_flops, bytes_accessed=11_000_000, transcendentals=0
        ),
        name="local_pairs",
    )(pair_count, targets, sources, radial, near, far, *[in_hbm(v) for v in later])
    species, shift, energy_grad, mix, readout = later

    updated, kept, sent, grad_messages, halo_factor, merged_factor = call(
        functools.partial(node_kernel, scale),
        "node_stage",
        (
            near,
            far,
            from_pair,
            from_cross,
            messages,
            keep,
            place,
            energy_grad,
            radial,
            mix,
            readout,
        ),
        (
            ((CH, atoms_here), f32),
            ((HALF, CH), f32),
            ((HALF, CH), f32),
            ((2, CH, NY * GROUP), bf16),
            ((2, NB * CELL_ATOMS, NY * GROUP), bf16),
            ((2, NB * CELL_ATOMS, NY * GROUP), bf16),
        ),
        16,
        [
            pltpu.VMEM((2, CH, NB * CELL_ATOMS), bf16),
            pltpu.VMEM((2, 2 * CH, NB * CELL_ATOMS), bf16),
            pltpu.VMEM((2, 3, GROUP, GROUP), f32),
        ],
        2 * block_flops,
    )

    received = lax.ppermute(sent, "space", pair)
    halo_grad, extra, share = call(
        halo_back_kernel,
        "halo_back",
        (
            halo_factor,
            merged_factor,
            grad_messages,
            near,
            far,
            from_pair,
            from_cross,
            radial,
        ),
        (((2 * CH, GROUP), f32), ((GROUP, CH), f32), ((NB, CH), f32)),
        12,
        (),
        2 * block_flops,
    )
    received, share = lax.optimization_barrier((received, share))
    quarter, sent = call(
        quarter_kernel,
        "quarter",
        (kept, received),
        (((QUARTER, CH), f32), ((QUARTER, CH), f32)),
    )
    sharing, (*rounds, last) = exchange_routes(space, dp)
    everyone = ("space", "dp")
    sent, grad_messages, halo_grad = lax.optimization_barrier((sent, grad_messages, halo_grad))
    received = lax.ppermute(sent, everyone, sharing)
    from_pair = lax.ppermute(halo_grad, "space", pair)
    own_grad, joined, energy = call(
        functools.partial(own_back_kernel, scale),
        "own_back",
        (
            group_factor,
            cell_factor,
            grad_messages,
            near,
            far,
            radial,
            extra,
            share,
            updated,
            species,
            shift,
            energy_grad,
            readout,
        ),
        (((CH, atoms_here), f32), ((REST, CH), f32), ((1, atoms_here), f32)),
        12,
        (),
        3 * block_flops,
    )
    (value,) = call(
        join_kernel, "join", (quarter, received, joined), (((QUARTER + REST, CH), f32),)
    )
    value, from_pair = lax.optimization_barrier((value, from_pair))
    for turn, routes in enumerate(rounds):
        arrived = [lax.ppermute(value, everyone, route) for route in routes]
        if turn == 0:
            from_cross = [lax.ppermute(from_pair[CH:], "space", route) for route in onward]
        value = value + arrived[0]
        if len(arrived) == 3:
            value = value + (arrived[1] + arrived[2])
    arrived = [lax.ppermute(value, everyone, route) for route in last]
    value, from_cross, *arrived = lax.optimization_barrier((value, from_cross, *arrived))
    (value,) = call(
        gather_kernel,
        "gather",
        (value, *arrived),
        (((HALF + REST, CH), f32),),
    )
    feature_grad, energy = call(
        fold_kernel,
        "fold",
        (own_grad, from_pair, *from_cross, energy),
        (((1, CH, atoms_here), f32), ((1, atoms_here), f32)),
    )
    radial_grad, mix_grad, readout_grad, shift_grad = call(
        finish_kernel,
        "finish",
        (value, lax.ppermute(value, "space", pair)),
        (((NB, CH), f32), ((MIX_ROWS, CH), f32), ((1, CH), f32), ((1, NSPEC), f32)),
    )
    return (
        energy,
        feature_grad,
        radial_grad,
        mix_grad,
        readout_grad.reshape(CH),
        shift_grad.reshape(NSPEC),
    )


def solution(mesh):
    return jax.shard_map(
        body,
        mesh=mesh,
        in_specs=(
            P("dp", None, "space"),
            P("dp", None, "space"),
            P("dp", "space"),
            P("dp", "space"),
            P("dp", "space"),
            P("dp", "space"),
            P("dp", "space"),
            P(),
            P(),
            P(),
            P(),
        ),
        out_specs=(P("dp", "space"), P("dp", None, "space"), P(), P(), P(), P()),
        check_vma=False,
    )
```

```python
import functools
import math

import jax
import jax.numpy as jnp
from jax import lax
from jax.experimental import pallas as pl
from jax.experimental.pallas import tpu as pltpu
from jax.sharding import PartitionSpec as P

CH = 128
NB = 8
NY = 9
NSPEC = 8
CELL_ATOMS = 64
HALO_CELLS = 2
GROUP = 2 * CELL_ATOMS
ROWS = 16
WIDTH = 256
CHUNKS = -(-NY * GROUP // WIDTH)

cutoff = 5.0
message_scale = 0.25

COS_COEFFS = (
    0.9999999998846169,
    -4.934802185771876,
    4.058711815779763,
    -1.3352602773967561,
    0.23532080049888648,
    -0.025785772074137014,
    0.0019043022864480008,
    -8.868331860867329e-05,
)
SINC_COEFFS = (
    0.9999999992502204,
    -1.6449339933418936,
    0.8117412468909989,
    -0.1907447263221115,
    0.02612742969685046,
    -0.0023157632409761065,
    0.00012580778956459784,
)

MIX_ROWS = 3 * CH
HALF = MIX_ROWS // 2
QUARTER = MIX_ROWS // 4
REST = 16
CELLS = 4 + 2 * HALO_CELLS
SMALL = 3
LATER = 5
SLAB_ROWS = CH + 8


def polynomial(coeffs, x):
    total = coeffs[-1] * x + coeffs[-2]
    for c in coeffs[-3::-1]:
        total = total * x + c
    return total


def factor_rows(factor_ref, size, row, source, target, keep):
    dx = (target[0] - source[0]) * (1.0 / cutoff)
    dy = (target[1] - source[1]) * (1.0 / cutoff)
    dz = (target[2] - source[2]) * (1.0 / cutoff)
    xx, yy, zz = dx * dx, dy * dy, dz * dz
    square = xx + yy + zz
    inside = jnp.minimum(square, 1.0)
    gap = 1.0 - inside
    base = (gap * gap) * keep * polynomial(SINC_COEFFS, inside)
    twice_cos = polynomial([2.0 * c for c in COS_COEFFS], inside)
    raw = [base, twice_cos * base]
    for _ in range(NB - 2):
        raw.append(twice_cos * raw[-1] - raw[-2])
    radial = [value if b == 0 else value * (1.0 / (b + 1)) for b, value in enumerate(raw)]
    root_three = math.sqrt(3.0)
    root_fifteen = math.sqrt(15.0)
    root_five = math.sqrt(5.0)
    wide_x = root_fifteen * dx
    harmonic = [
        None,
        root_three * dx,
        root_three * dy,
        root_three * dz,
        wide_x * dy,
        (root_fifteen * dy) * dz,
        (0.5 * root_five) * (3.0 * zz - square),
        wide_x * dz,
        (0.5 * root_fifteen) * (xx - yy),
    ]
    for b in range(NB):
        rows = slice(b * size + row, b * size + row + ROWS)
        for y in range(NY):
            value = radial[b] if y == 0 else radial[b] * harmonic[y]
            factor_ref[rows, y * GROUP : (y + 1) * GROUP] = value.astype(jnp.bfloat16)


def column_to_row(column, size):
    wide = jnp.broadcast_to(column, (size, GROUP))
    at = lax.broadcasted_iota(jnp.int32, (size, GROUP), 0)
    lane = lax.broadcasted_iota(jnp.int32, (size, GROUP), 1)
    return jnp.sum(jnp.where(at == lane, wide, 0.0), axis=0, keepdims=True)


def split_kernel(*refs):
    features_ref, place_in_ref, *inputs = refs[: SMALL + 2]
    near_ref, far_ref, *outputs = refs[SMALL + 2 : 2 * SMALL + 4]
    place_ref, sems = refs[2 * SMALL + 4 :]
    core = lax.axis_index("space") % 2
    place_copy = pltpu.make_async_copy(place_in_ref, place_ref, sems.at[2])
    place_copy.start()
    copies = []
    for k, (ref, side) in enumerate(((near_ref, 1 - core), (far_ref, core))):
        at = pl.ds(pl.multiple_of(side * GROUP, GROUP), GROUP)
        copies.append(
            pltpu.make_async_copy(features_ref.at[0, :, at], ref.at[pl.ds(0, CH)], sems.at[k])
        )
    for k, (src, dst) in enumerate(zip(inputs, outputs)):
        copies.append(pltpu.make_async_copy(src, dst, sems.at[3 + k]))
    for copy in copies:
        copy.start()
    place_copy.wait()
    low, high = slice(GROUP), slice(GROUP, 2 * GROUP)
    filler = jnp.zeros((5, GROUP), jnp.float32)
    for ref, one, two in ((near_ref, high, low), (far_ref, low, high)):
        rows = [
            jnp.where(core == 0, place_ref[axis, :, one], place_ref[axis, :, two]) for axis in range(3)
        ]
        ref[CH:, :] = jnp.concatenate(rows + [filler], axis=0)
    for copy in copies:
        copy.wait()


def live_flags(count, pair_target, pair_source):
    size = (4 * CELLS, pair_target.shape[1])
    at = lax.broadcasted_iota(jnp.int32, size, 0)
    slot = lax.broadcasted_iota(jnp.int32, size, 1)
    hit = (pair_target * CELLS + pair_source == at) & (slot < count)
    return jnp.max(jnp.where(hit, message_scale, 0.0), axis=1, keepdims=True)


def keep_row(flags, t, low, high):
    lane = lax.broadcasted_iota(jnp.int32, (1, GROUP), 1)
    one, two = (2 * t) * CELLS + low, (2 * t + 1) * CELLS + high
    return jnp.where(lane < CELL_ATOMS, flags[one : one + 1], flags[two : two + 1])


def set_group(scaled_ref, features, weight_t):
    for b in range(NB):
        scaled_ref[:, b * GROUP : (b + 1) * GROUP] = (features * weight_t[:, b : b + 1]).astype(
            jnp.bfloat16
        )


def set_cell(scaled_ref, features, half, weight_t):
    first = lax.broadcasted_iota(jnp.int32, (CH, GROUP), 1) < CELL_ATOMS
    turned = pltpu.roll(features, CELL_ATOMS, 1)
    twice = jnp.where(first, features, turned) if half == 0 else jnp.where(first, turned, features)
    for k in range(NB // 2):
        weights = jnp.where(first, weight_t[:, 2 * k : 2 * k + 1], weight_t[:, 2 * k + 1 : 2 * k + 2])
        scaled_ref[:, k * GROUP : (k + 1) * GROUP] = (twice * weights).astype(jnp.bfloat16)


def set_place(place_ref, slab):
    place = slab[CH:].T
    for axis in range(3):
        place_ref[axis] = jnp.broadcast_to(place[:, axis : axis + 1], (GROUP, GROUP))


def fill_steps(factor_ref, size, source_of, keeps, target, diagonal=False):
    def step(row):
        keep = jnp.broadcast_to(keeps[row // CELL_ATOMS], (ROWS, GROUP))
        if diagonal:
            row_at = lax.broadcasted_iota(jnp.int32, (ROWS, GROUP), 0)
            lane_at = lax.broadcasted_iota(jnp.int32, (ROWS, GROUP), 1)
            keep = jnp.where(row_at + row == lane_at, 0.0, keep)
        factor_rows(factor_ref, size, row, source_of(row), target, keep)

    return [functools.partial(step, row) for row in range(0, size, ROWS)]


def rows_of(place_ref, start):
    return lambda row: [place_ref[axis, start + row : start + row + ROWS, :] for axis in range(3)]


def merged_rows(low_ref, low_start, high_ref, high_start):
    low, high = rows_of(low_ref, low_start), rows_of(high_ref, high_start)

    def rows(row):
        first = lax.broadcasted_iota(jnp.int32, (ROWS, GROUP), 1) < CELL_ATOMS
        return [jnp.where(first, one, two) for one, two in zip(low(row), high(row))]

    return rows


def product_steps(scaled_ref, factor_ref, totals, merged=False):
    def step(k):
        width = min(WIDTH, NY * GROUP - k * WIDTH)
        product = jnp.dot(
            scaled_ref[...],
            factor_ref[:, k * WIDTH : k * WIDTH + width],
            preferred_element_type=jnp.float32,
        )
        if merged:
            lane = lax.broadcasted_iota(jnp.int32, (CH, width), 1) % GROUP
            product = jnp.where(lane < CELL_ATOMS, product[:CH], product[CH:])
        totals[k] = product if totals[k] is None else totals[k] + product

    return [functools.partial(step, k) for k in range(CHUNKS)]


def interleave(one, two):
    done = 0
    for k, step in enumerate(one):
        step()
        upto = (k + 1) * len(two) // len(one)
        for other in two[done:upto]:
            other()
        done = upto


def local_kernel(*refs):
    count_ref, pair_target_ref, pair_source_ref, radial_ref, near_ref, far_ref = refs[:6]
    later_in = refs[6 : 6 + LATER]
    group_factor_ref, cell_factor_ref, messages_ref, keep_ref, place_ref = refs[6 + LATER : 11 + LATER]
    later_out = refs[11 + LATER : 11 + 2 * LATER]
    group_ref, cell_ref, sems = refs[11 + 2 * LATER :]
    copies = [
        pltpu.make_async_copy(src, dst, sems.at[k]) for k, (src, dst) in enumerate(zip(later_in, later_out))
    ]
    for copy in copies:
        copy.start()
    even = lax.axis_index("space") % 2 == 0
    near, far = near_ref[...], far_ref[...]
    slabs = (jnp.where(even, far, near), jnp.where(even, near, far))
    targets = [[slab[CH + axis : CH + axis + 1] for axis in range(3)] for slab in slabs]
    flags = live_flags(count_ref[0, 0], pair_target_ref[...], pair_source_ref[...])
    weight_t = radial_ref[...].T
    for g in range(2):
        set_place(place_ref.at[g], slabs[g])
        set_group(group_ref.at[g], slabs[g][:CH], weight_t)
        set_cell(cell_ref.at[g], slabs[1 - g][:CH], g, weight_t)

    def fill_group(t):
        keeps = [keep_row(flags, t, cell, cell) for cell in (2 * t + 2, 2 * t + 3)]
        return fill_steps(
            group_factor_ref.at[t], GROUP, rows_of(place_ref.at[t], 0), keeps, targets[t], True
        )

    def fill_cell(t):
        cell = 4 - t
        source_of = rows_of(place_ref.at[1 - t], t * CELL_ATOMS)
        return fill_steps(
            cell_factor_ref.at[t], CELL_ATOMS, source_of, [keep_row(flags, t, cell, cell)], targets[t]
        )

    totals = [[None] * CHUNKS for _ in range(2)]
    for step in fill_cell(0):
        step()
    interleave(product_steps(cell_ref.at[0], cell_factor_ref.at[0], totals[0]), fill_group(0))
    interleave(product_steps(group_ref.at[0], group_factor_ref.at[0], totals[0]), fill_group(1))
    interleave(product_steps(group_ref.at[1], group_factor_ref.at[1], totals[1]), fill_cell(1))
    for step in product_steps(cell_ref.at[1], cell_factor_ref.at[1], totals[1]):
        step()
    for t in range(2):
        messages_ref[t] = jnp.concatenate(totals[t], axis=1)
    rows = [
        keep_row(flags, 0, 1, 1),
        keep_row(flags, 0, 0, 5),
        keep_row(flags, 1, 6, 6),
        keep_row(flags, 1, 2, 7),
    ]
    keep_ref[...] = jnp.concatenate(rows + [jnp.zeros((4, GROUP), jnp.float32)], axis=0)
    for copy in copies:
        copy.wait()


def node_kernel(
    scale,
    near_ref,
    far_ref,
    from_pair_ref,
    from_cross_ref,
    messages_ref,
    keep_ref,
    own_place_ref,
    energy_grad_ref,
    radial_ref,
    mix_ref,
    readout_ref,
    updated_ref,
    kept_ref,
    sent_ref,
    grad_messages_ref,
    cell_factor_ref,
    merged_factor_ref,
    cell_ref,
    merged_ref,
    place_ref,
):
    even = lax.axis_index("space") % 2 == 0
    weight_t = radial_ref[...].T
    near, far = near_ref[...], far_ref[...]
    from_pair, from_cross = from_pair_ref[...], from_cross_ref[...]
    slabs = (
        jnp.where(even, from_cross, from_pair),
        jnp.where(even, far, near),
        jnp.where(even, near, far),
        jnp.where(even, from_pair, from_cross),
    )
    targets = [[slab[CH + axis : CH + axis + 1] for axis in range(3)] for slab in slabs[1:3]]

    for t in range(2):
        set_place(place_ref.at[t], slabs[3 * t])
        set_cell(cell_ref.at[t], slabs[3 * t][:CH], 1 - t, weight_t)
        set_cell(merged_ref.at[t, pl.ds(0, CH)], slabs[t][:CH], 0, weight_t)
        set_cell(merged_ref.at[t, pl.ds(CH, CH)], slabs[t + 2][:CH], 1, weight_t)

    def fill_cell(t):
        source_of = rows_of(place_ref.at[t], (1 - t) * CELL_ATOMS)
        keeps = [keep_ref[2 * t : 2 * t + 1, :]]
        return fill_steps(cell_factor_ref.at[t], CELL_ATOMS, source_of, keeps, targets[t])

    def fill_merged(t):
        places = (place_ref.at[0], own_place_ref.at[0], own_place_ref.at[1], place_ref.at[1])
        source_of = merged_rows(places[t], 0, places[t + 2], CELL_ATOMS)
        keeps = [keep_ref[2 * t + 1 : 2 * t + 2, :]]
        return fill_steps(merged_factor_ref.at[t], CELL_ATOMS, source_of, keeps, targets[t])

    totals = [
        [messages_ref[t, :, k * WIDTH : min((k + 1) * WIDTH, NY * GROUP)] for k in range(CHUNKS)]
        for t in range(2)
    ]

    def add_cell(t):
        return product_steps(cell_ref.at[t], cell_factor_ref.at[t], totals[t])

    def add_merged(t):
        return product_steps(merged_ref.at[t], merged_factor_ref.at[t], totals[t], True)

    readout = jnp.broadcast_to(readout_ref[...], (8, CH)).T[:, :1]
    mix = mix_ref[...]
    mix_t = mix.astype(jnp.float32).T.astype(jnp.bfloat16)

    for step in fill_cell(0):
        step()
    interleave(add_cell(0), fill_merged(0))
    interleave(add_merged(0), fill_cell(1))
    interleave(add_cell(1), fill_merged(1))
    for step in add_merged(1):
        step()

    sides = [jnp.concatenate(total, axis=1) for total in totals]
    part = [
        jnp.concatenate([side[:, y * GROUP : (y + 1) * GROUP] for side in sides], axis=1)
        for y in range(NY)
    ]
    invariants = jnp.concatenate(
        [
            part[0],
            0.5 * (part[1] * part[1] + part[2] * part[2] + part[3] * part[3]),
            0.5
            * (
                part[4] * part[4]
                + part[5] * part[5]
                + part[6] * part[6]
                + part[7] * part[7]
                + part[8] * part[8]
            ),
        ],
        axis=0,
    ).astype(jnp.bfloat16)
    preact = jnp.dot(mix_t, invariants, preferred_element_type=jnp.float32)
    gating = jax.nn.sigmoid(preact)
    energy_grad = energy_grad_ref[...]
    spread = readout * energy_grad
    grad_pre = (spread * gating * (1.0 + preact * (1.0 - gating))).astype(jnp.bfloat16)
    grad_inv = jnp.dot(mix, grad_pre, preferred_element_type=jnp.float32)
    grad_mix = scale * lax.dot_general(
        invariants, grad_pre, (((1,), (1,)), ((), ())), preferred_element_type=jnp.float32
    )
    kept_ref[...] = jnp.where(even, grad_mix[:HALF], grad_mix[HALF:])
    sent_ref[...] = jnp.where(even, grad_mix[HALF:], grad_mix[:HALF])
    for y in range(NY):
        order = 0 if y == 0 else 1 if y < 4 else 2
        grad = grad_inv[order * CH : (order + 1) * CH]
        grad = (grad if y == 0 else grad * part[y]).astype(jnp.bfloat16)
        for t in range(2):
            grad_messages_ref[t, :, y * GROUP : (y + 1) * GROUP] = grad[:, t * GROUP : (t + 1) * GROUP]

    updated_ref[...] = jnp.concatenate([slabs[1][:CH], slabs[2][:CH]], axis=1) + preact * gating


def back(factor, grad_messages):
    return lax.dot_general(
        factor, grad_messages, (((1,), (1,)), ((), ())), preferred_element_type=jnp.float32
    )


def source_grads(total, features_t, weight):
    size = features_t.shape[0]
    grad_t = None
    radial = []
    for b in range(NB):
        piece = total[b * size : (b + 1) * size]
        term = piece * weight[b : b + 1, :]
        grad_t = term if grad_t is None else grad_t + term
        radial.append(jnp.sum(piece * features_t, axis=0, keepdims=True))
    return grad_t, jnp.concatenate(radial, axis=0)


def halo_back_kernel(
    cell_factor_ref,
    merged_factor_ref,
    grad_messages_ref,
    near_ref,
    far_ref,
    from_pair_ref,
    from_cross_ref,
    radial_ref,
    to_pair_ref,
    to_cross_ref,
    extra_ref,
    share_ref,
):
    even = lax.axis_index("space") % 2 == 0
    weight = radial_ref[...]
    near, far = near_ref[:CH, :], far_ref[:CH, :]
    from_pair, from_cross = from_pair_ref[:CH, :], from_cross_ref[:CH, :]
    features_t = [
        jnp.where(even, one, two).T
        for one, two in ((from_cross, from_pair), (far, near), (near, far), (from_pair, from_cross))
    ]
    first = lax.broadcasted_iota(jnp.int32, (CH, NY * GROUP), 1) % GROUP < CELL_ATOMS
    low, high = slice(CELL_ATOMS), slice(CELL_ATOMS, GROUP)
    share = None
    grads = {}
    for t in range(2):
        grad = grad_messages_ref[t]
        none = jnp.zeros_like(grad)
        both = jnp.concatenate([jnp.where(first, grad, none), jnp.where(first, none, grad)], axis=0)
        merged = back(merged_factor_ref[t], both)
        pieces = (
            (3 * t, 1 - t, back(cell_factor_ref[t], grad)),
            (t, 0, merged[:, :CH]),
            (t + 2, 1, merged[:, CH:]),
        )
        for g, half, total in pieces:
            grads[g, half], part = source_grads(total, features_t[g][(low, high)[half]], weight)
            share = part if share is None else share + part
    grad_before = jnp.concatenate([grads[0, 0], grads[0, 1]], axis=0).T
    grad_after = jnp.concatenate([grads[3, 0], grads[3, 1]], axis=0).T
    to_pair_ref[...] = jnp.where(even, grad_after, grad_before)
    to_cross_ref[...] = jnp.where(even, grad_before, grad_after)
    extra_ref[low, :] = grads[1, 0]
    extra_ref[high, :] = grads[2, 1]
    share_ref[...] = share


def own_back_kernel(
    scale,
    group_factor_ref,
    cell_factor_ref,
    grad_messages_ref,
    near_ref,
    far_ref,
    radial_ref,
    extra_ref,
    share_ref,
    updated_ref,
    species_ref,
    shift_ref,
    energy_grad_ref,
    readout_ref,
    own_grad_ref,
    joined_ref,
    energy_ref,
):
    even = lax.axis_index("space") % 2 == 0
    weight = radial_ref[...]
    near, far = near_ref[:CH, :], far_ref[:CH, :]
    share = share_ref[...]
    low, high = slice(CELL_ATOMS), slice(CELL_ATOMS, GROUP)
    readout = jnp.broadcast_to(readout_ref[...], (8, CH)).T[:, :1]
    updated, energy_grad, kinds = updated_ref[...], energy_grad_ref[...], species_ref[...]
    spread = readout * energy_grad
    shifts = jnp.zeros((1, 2 * GROUP), jnp.float32)
    for n in range(NSPEC):
        shifts = jnp.where(kinds == n, shift_ref[:, n : n + 1], shifts)
    energy_ref[...] = jnp.sum(updated * readout, axis=0, keepdims=True) + shifts
    readout_row = column_to_row(jnp.sum(updated * energy_grad, axis=1, keepdims=True), CH)
    here = lax.broadcasted_iota(jnp.int32, (NSPEC, 2 * GROUP), 0) == kinds
    by_kind = jnp.sum(jnp.where(here, energy_grad, 0.0), axis=1, keepdims=True)
    for t, features in enumerate((jnp.where(even, far, near), jnp.where(even, near, far))):
        features_t = features.T
        total = back(group_factor_ref[t], grad_messages_ref[t])
        grad, part = source_grads(total, features_t, weight)
        inner, outer = (high, low) if t == 0 else (low, high)
        total = back(cell_factor_ref[1 - t], grad_messages_ref[1 - t])
        one, more = source_grads(total, features_t[inner], weight)
        two = extra_ref[outer, :]
        grad = (grad + jnp.concatenate([two, one] if t == 0 else [one, two], axis=0)).T
        at = slice(t * GROUP, (t + 1) * GROUP)
        own_grad_ref[:, at] = spread[:, at] + grad
        share = share + part + more
    joined_ref[:NB, :] = share * scale
    rest = [readout_row, column_to_row(by_kind, NSPEC), jnp.zeros((6, CH), jnp.float32)]
    joined_ref[NB:, :] = jnp.concatenate(rest, axis=0) * scale


def quarter_kernel(kept_ref, received_ref, keep_ref, send_ref):
    first = first_of_pair()
    low = kept_ref[:QUARTER, :] + received_ref[:QUARTER, :]
    high = kept_ref[QUARTER:, :] + received_ref[QUARTER:, :]
    keep_ref[...] = jnp.where(first, low, high)
    send_ref[...] = jnp.where(first, high, low)


def join_kernel(kept_ref, received_ref, rest_ref, out_ref):
    out_ref[:QUARTER, :] = kept_ref[...] + received_ref[...]
    out_ref[QUARTER:, :] = rest_ref[...]


def gather_kernel(mine_ref, along_ref, other_ref, both_ref, out_ref):
    first = first_of_pair()
    at, rest = slice(QUARTER), slice(QUARTER, QUARTER + REST)
    mine = mine_ref[at, :] + along_ref[at, :]
    other = other_ref[at, :] + both_ref[at, :]
    out_ref[:QUARTER, :] = jnp.where(first, mine, other)
    out_ref[QUARTER:HALF, :] = jnp.where(first, other, mine)
    out_ref[HALF:, :] = (mine_ref[rest, :] + along_ref[rest, :]) + (other_ref[rest, :] + both_ref[rest, :])


def fold_kernel(own_ref, from_pair_ref, from_cross_ref, energy_in_ref, grad_ref, energy_ref):
    even = lax.axis_index("space") % 2 == 0
    pair = from_pair_ref[...]
    cross = from_cross_ref[...]
    grad_ref[0, :, :GROUP] = own_ref[:, :GROUP] + jnp.where(even, cross, pair)
    grad_ref[0, :, GROUP:] = own_ref[:, GROUP:] + jnp.where(even, pair, cross)
    energy_ref[...] = energy_in_ref[...]


def finish_kernel(mine_ref, other_ref, radial_ref, mix_ref, readout_ref, shift_ref):
    even = lax.axis_index("space") % 2 == 0
    mine, other = mine_ref[:HALF, :], other_ref[:HALF, :]
    mix_ref[:HALF, :] = jnp.where(even, mine, other)
    mix_ref[HALF:, :] = jnp.where(even, other, mine)
    rest = mine_ref[HALF:, :] + other_ref[HALF:, :]
    radial_ref[...] = rest[:NB]
    readout_ref[...] = rest[NB : NB + 1]
    shift_ref[...] = rest[NB + 1 : NB + 2, :NSPEC]


def first_of_pair():
    space, dp = lax.axis_index("space"), lax.axis_index("dp")
    return jnp.where(space % 2 == 0, dp, space // 2) % 2 == 0


def exchange_routes(space, dp):
    along = [(0, 1 << k) for k in range(dp.bit_length() - 1)]
    across = [(1 << k, 0) for k in range(1, space.bit_length() - 1)]
    shared = (along[0], across[0])
    orders = (across + along[1:], along[:1] + across[1:] + along[1:])
    orders = (orders[0][:-2] + orders[0][:-3:-1], orders[1])
    count = len(orders[0])

    def route(*places):
        moves = []
        for s in range(space):
            step = [shared[s % 2] if k < 0 else orders[s % 2][k] for k in places]
            for d in range(dp):
                to_s, to_d = s, d
                for one, two in step:
                    to_s, to_d = to_s ^ one, to_d ^ two
                moves.append((s * dp + d, to_s * dp + to_d))
        return moves

    rounds = []
    for k in range(0, count - 1, 2):
        if k + 1 < count - 1:
            rounds.append([route(k), route(k + 1), route(k, k + 1)])
        else:
            rounds.append([route(k)])
    last = count - 1
    rounds.append([route(last), route(-1), route(last, -1)])
    return route(-1), rounds


def call(kernel, name, inputs, outputs, mib=4, scratch=(), flops=0):
    vmem = pl.BlockSpec(memory_space=pltpu.VMEM)
    shapes = tuple(jax.ShapeDtypeStruct(shape, kind) for shape, kind in outputs)
    moved = sum(math.prod(v.shape) * v.dtype.itemsize for v in (*inputs, *shapes))
    return pl.pallas_call(
        kernel,
        out_shape=shapes,
        in_specs=[vmem] * len(inputs),
        out_specs=(vmem,) * len(shapes),
        scratch_shapes=scratch,
        compiler_params=pltpu.CompilerParams(vmem_limit_bytes=mib * 1024 * 1024),
        cost_estimate=pl.CostEstimate(flops=flops, bytes_accessed=moved, transcendentals=0),
        name=name,
    )(*inputs)


def in_hbm(value):
    return pltpu.with_memory_space_constraint(value, pltpu.HBM)


def body(
    node_features,
    positions,
    species,
    energy_cotangent,
    pair_target,
    pair_source,
    pair_count,
    radial_weight,
    mix_weight,
    readout_weight,
    species_shift,
):
    atoms_here = node_features.shape[2]
    space, dp = lax.axis_size("space"), lax.axis_size("dp")
    scale = 1.0 / math.sqrt(atoms_here * space * dp)
    pair = [(i, i ^ 1) for i in range(space)]
    cross = [(i, ((i + 1) ^ 1) - 1) for i in range(1, space - 1)]
    hbm = pl.BlockSpec(memory_space=pltpu.HBM)
    smem = pl.BlockSpec(memory_space=pltpu.SMEM)
    vmem = pl.BlockSpec(memory_space=pltpu.VMEM)
    f32, bf16 = jnp.float32, jnp.bfloat16
    small = (pair_target, pair_source, radial_weight)
    later = (
        species,
        species_shift.reshape(1, NSPEC),
        energy_cotangent,
        mix_weight,
        readout_weight.reshape(1, CH),
    )
    near, far, *small = pl.pallas_call(
        split_kernel,
        out_shape=(jax.ShapeDtypeStruct((SLAB_ROWS, GROUP), f32),) * 2
        + tuple(jax.ShapeDtypeStruct(v.shape, v.dtype) for v in small),
        in_specs=[hbm] * (SMALL + 2),
        out_specs=(vmem,) * (SMALL + 2),
        scratch_shapes=[
            pltpu.VMEM((3, 1, atoms_here), f32),
            pltpu.SemaphoreType.DMA((SMALL + 3,)),
        ],
        compiler_params=pltpu.CompilerParams(vmem_limit_bytes=4 * 1024 * 1024),
        name="split",
    )(
        in_hbm(node_features),
        in_hbm(jnp.transpose(positions, (1, 0, 2))),
        *[in_hbm(v) for v in small],
    )
    targets, sources, radial = small
    from_cross = lax.ppermute(far, "space", cross)
    from_pair = lax.ppermute(near, "space", pair)

    block_flops = 2 * CH * NB * NY * GROUP * GROUP
    group_factor, cell_factor, messages, keep, place, *later = pl.pallas_call(
        local_kernel,
        out_shape=(
            jax.ShapeDtypeStruct((2, NB * GROUP, NY * GROUP), bf16),
            jax.ShapeDtypeStruct((2, NB * CELL_ATOMS, NY * GROUP), bf16),
            jax.ShapeDtypeStruct((2, CH, NY * GROUP), f32),
            jax.ShapeDtypeStruct((8, GROUP), f32),
            jax.ShapeDtypeStruct((2, 3, GROUP, GROUP), f32),
            *[jax.ShapeDtypeStruct(v.shape, v.dtype) for v in later],
        ),
        in_specs=[smem] + [vmem] * 5 + [hbm] * LATER,
        out_specs=(vmem,) * (5 + LATER),
        scratch_shapes=[
            pltpu.VMEM((2, CH, NB * GROUP), bf16),
            pltpu.VMEM((2, CH, NB * CELL_ATOMS), bf16),
            pltpu.SemaphoreType.DMA((LATER,)),
        ],
        compiler_params=pltpu.CompilerParams(vmem_limit_bytes=16 * 1024 * 1024),
        cost_estimate=pl.CostEstimate(
            flops=3 * block_flops, bytes_accessed=11_000_000, transcendentals=0
        ),
        name="local_pairs",
    )(pair_count, targets, sources, radial, near, far, *[in_hbm(v) for v in later])
    species, shift, energy_grad, mix, readout = later

    updated, kept, sent, grad_messages, halo_factor, merged_factor = call(
        functools.partial(node_kernel, scale),
        "node_stage",
        (
            near,
            far,
            from_pair,
            from_cross,
            messages,
            keep,
            place,
            energy_grad,
            radial,
            mix,
            readout,
        ),
        (
            ((CH, atoms_here), f32),
            ((HALF, CH), f32),
            ((HALF, CH), f32),
            ((2, CH, NY * GROUP), bf16),
            ((2, NB * CELL_ATOMS, NY * GROUP), bf16),
            ((2, NB * CELL_ATOMS, NY * GROUP), bf16),
        ),
        16,
        [
            pltpu.VMEM((2, CH, NB * CELL_ATOMS), bf16),
            pltpu.VMEM((2, 2 * CH, NB * CELL_ATOMS), bf16),
            pltpu.VMEM((2, 3, GROUP, GROUP), f32),
        ],
        2 * block_flops,
    )

    received = lax.ppermute(sent, "space", pair)
    pair_grad, cross_grad, extra, share = call(
        halo_back_kernel,
        "halo_back",
        (
            halo_factor,
            merged_factor,
            grad_messages,
            near,
            far,
            from_pair,
            from_cross,
            radial,
        ),
        (((CH, GROUP), f32), ((CH, GROUP), f32), ((GROUP, CH), f32), ((NB, CH), f32)),
        12,
        (),
        2 * block_flops,
    )
    received, share = lax.optimization_barrier((received, share))
    quarter, sent = call(
        quarter_kernel,
        "quarter",
        (kept, received),
        (((QUARTER, CH), f32), ((QUARTER, CH), f32)),
    )
    sharing, (*rounds, last) = exchange_routes(space, dp)
    everyone = ("space", "dp")
    sent, grad_messages, pair_grad = lax.optimization_barrier((sent, grad_messages, pair_grad))
    received = lax.ppermute(sent, everyone, sharing)
    from_pair = lax.ppermute(pair_grad, "space", pair)
    own_grad, joined, energy = call(
        functools.partial(own_back_kernel, scale),
        "own_back",
        (
            group_factor,
            cell_factor,
            grad_messages,
            near,
            far,
            radial,
            extra,
            share,
            updated,
            species,
            shift,
            energy_grad,
            readout,
        ),
        (((CH, atoms_here), f32), ((REST, CH), f32), ((1, atoms_here), f32)),
        12,
        (),
        3 * block_flops,
    )
    (value,) = call(
        join_kernel, "join", (quarter, received, joined), (((QUARTER + REST, CH), f32),)
    )
    value, from_pair, cross_grad = lax.optimization_barrier((value, from_pair, cross_grad))
    for turn, routes in enumerate(rounds):
        arrived = [lax.ppermute(value, everyone, route) for route in routes]
        if turn == 0:
            from_cross = lax.ppermute(cross_grad, "space", cross)
        value = value + arrived[0]
        if len(arrived) == 3:
            value = value + (arrived[1] + arrived[2])
    arrived = [lax.ppermute(value, everyone, route) for route in last]
    value, from_cross, *arrived = lax.optimization_barrier((value, from_cross, *arrived))
    (value,) = call(
        gather_kernel,
        "gather",
        (value, *arrived),
        (((HALF + REST, CH), f32),),
    )
    feature_grad, energy = call(
        fold_kernel,
        "fold",
        (own_grad, from_pair, from_cross, energy),
        (((1, CH, atoms_here), f32), ((1, atoms_here), f32)),
    )
    radial_grad, mix_grad, readout_grad, shift_grad = call(
        finish_kernel,
        "finish",
        (value, lax.ppermute(value, "space", pair)),
        (((NB, CH), f32), ((MIX_ROWS, CH), f32), ((1, CH), f32), ((1, NSPEC), f32)),
    )
    return (
        energy,
        feature_grad,
        radial_grad,
        mix_grad,
        readout_grad.reshape(CH),
        shift_grad.reshape(NSPEC),
    )


def solution(mesh):
    return jax.shard_map(
        body,
        mesh=mesh,
        in_specs=(
            P("dp", None, "space"),
            P("dp", None, "space"),
            P("dp", "space"),
            P("dp", "space"),
            P("dp", "space"),
            P("dp", "space"),
            P("dp", "space"),
            P(),
            P(),
            P(),
            P(),
        ),
        out_specs=(P("dp", "space"), P("dp", None, "space"), P(), P(), P(), P()),
        check_vma=False,
    )
```

```python
import functools
import math

import jax
import jax.numpy as jnp
from jax import lax
from jax.experimental import pallas as pl
from jax.experimental.pallas import tpu as pltpu
from jax.sharding import PartitionSpec as P

CH = 128
NB = 8
NY = 9
NSPEC = 8
CELL_ATOMS = 64
HALO_CELLS = 2
GROUP = 2 * CELL_ATOMS
ROWS = 16
WIDTH = 256
CHUNKS = -(-NY * GROUP // WIDTH)

cutoff = 5.0
message_scale = 0.25

COS_COEFFS = (
    0.9999999998846169,
    -4.934802185771876,
    4.058711815779763,
    -1.3352602773967561,
    0.23532080049888648,
    -0.025785772074137014,
    0.0019043022864480008,
    -8.868331860867329e-05,
)
SINC_COEFFS = (
    0.9999999992502204,
    -1.6449339933418936,
    0.8117412468909989,
    -0.1907447263221115,
    0.02612742969685046,
    -0.0023157632409761065,
    0.00012580778956459784,
)

MIX_ROWS = 3 * CH
HALF = MIX_ROWS // 2
QUARTER = MIX_ROWS // 4
REST = 16
CELLS = 4 + 2 * HALO_CELLS
SMALL = 3
LATER = 5
SLAB_ROWS = CH + 8


def polynomial(coeffs, x):
    total = coeffs[-1] * x + coeffs[-2]
    for c in coeffs[-3::-1]:
        total = total * x + c
    return total


def factor_rows(factor_ref, size, row, source, target, keep):
    dx = (target[0] - source[0]) * (1.0 / cutoff)
    dy = (target[1] - source[1]) * (1.0 / cutoff)
    dz = (target[2] - source[2]) * (1.0 / cutoff)
    xx, yy, zz = dx * dx, dy * dy, dz * dz
    square = xx + yy + zz
    inside = jnp.minimum(square, 1.0)
    gap = 1.0 - inside
    base = (gap * gap) * keep * polynomial(SINC_COEFFS, inside)
    twice_cos = polynomial([2.0 * c for c in COS_COEFFS], inside)
    raw = [base, twice_cos * base]
    for _ in range(NB - 2):
        raw.append(twice_cos * raw[-1] - raw[-2])
    radial = [value if b == 0 else value * (1.0 / (b + 1)) for b, value in enumerate(raw)]
    root_three = math.sqrt(3.0)
    root_fifteen = math.sqrt(15.0)
    root_five = math.sqrt(5.0)
    wide_x = root_fifteen * dx
    harmonic = [
        None,
        root_three * dx,
        root_three * dy,
        root_three * dz,
        wide_x * dy,
        (root_fifteen * dy) * dz,
        (0.5 * root_five) * (3.0 * zz - square),
        wide_x * dz,
        (0.5 * root_fifteen) * (xx - yy),
    ]
    for b in range(NB):
        rows = slice(b * size + row, b * size + row + ROWS)
        for y in range(NY):
            value = radial[b] if y == 0 else radial[b] * harmonic[y]
            factor_ref[rows, y * GROUP : (y + 1) * GROUP] = value.astype(jnp.bfloat16)


def column_to_row(column, size):
    wide = jnp.broadcast_to(column, (size, GROUP))
    at = lax.broadcasted_iota(jnp.int32, (size, GROUP), 0)
    lane = lax.broadcasted_iota(jnp.int32, (size, GROUP), 1)
    return jnp.sum(jnp.where(at == lane, wide, 0.0), axis=0, keepdims=True)


def split_kernel(*refs):
    features_ref, place_in_ref, *inputs = refs[: SMALL + 2]
    near_ref, far_ref, *outputs = refs[SMALL + 2 : 2 * SMALL + 4]
    place_ref, sems = refs[2 * SMALL + 4 :]
    core = lax.axis_index("space") % 2
    place_copy = pltpu.make_async_copy(place_in_ref, place_ref, sems.at[2])
    place_copy.start()
    copies = []
    for k, (ref, side) in enumerate(((near_ref, 1 - core), (far_ref, core))):
        at = pl.ds(pl.multiple_of(side * GROUP, GROUP), GROUP)
        copies.append(
            pltpu.make_async_copy(features_ref.at[0, :, at], ref.at[pl.ds(0, CH)], sems.at[k])
        )
    for k, (src, dst) in enumerate(zip(inputs, outputs)):
        copies.append(pltpu.make_async_copy(src, dst, sems.at[3 + k]))
    for copy in copies:
        copy.start()
    place_copy.wait()
    low, high = slice(GROUP), slice(GROUP, 2 * GROUP)
    filler = jnp.zeros((5, GROUP), jnp.float32)
    for ref, one, two in ((near_ref, high, low), (far_ref, low, high)):
        rows = [
            jnp.where(core == 0, place_ref[axis, :, one], place_ref[axis, :, two]) for axis in range(3)
        ]
        ref[CH:, :] = jnp.concatenate(rows + [filler], axis=0)
    for copy in copies:
        copy.wait()


def live_flags(count, pair_target, pair_source):
    size = (4 * CELLS, pair_target.shape[1])
    at = lax.broadcasted_iota(jnp.int32, size, 0)
    slot = lax.broadcasted_iota(jnp.int32, size, 1)
    hit = (pair_target * CELLS + pair_source == at) & (slot < count)
    return jnp.max(jnp.where(hit, message_scale, 0.0), axis=1, keepdims=True)


def keep_row(flags, t, low, high):
    lane = lax.broadcasted_iota(jnp.int32, (1, GROUP), 1)
    one, two = (2 * t) * CELLS + low, (2 * t + 1) * CELLS + high
    return jnp.where(lane < CELL_ATOMS, flags[one : one + 1], flags[two : two + 1])


def set_group(scaled_ref, features, weight_t):
    for b in range(NB):
        scaled_ref[:, b * GROUP : (b + 1) * GROUP] = (features * weight_t[:, b : b + 1]).astype(
            jnp.bfloat16
        )


def set_cell(scaled_ref, features, half, weight_t):
    first = lax.broadcasted_iota(jnp.int32, (CH, GROUP), 1) < CELL_ATOMS
    turned = pltpu.roll(features, CELL_ATOMS, 1)
    twice = jnp.where(first, features, turned) if half == 0 else jnp.where(first, turned, features)
    for k in range(NB // 2):
        weights = jnp.where(first, weight_t[:, 2 * k : 2 * k + 1], weight_t[:, 2 * k + 1 : 2 * k + 2])
        scaled_ref[:, k * GROUP : (k + 1) * GROUP] = (twice * weights).astype(jnp.bfloat16)


def set_place(place_ref, slab):
    place = slab[CH:].T
    for axis in range(3):
        place_ref[axis] = jnp.broadcast_to(place[:, axis : axis + 1], (GROUP, GROUP))


def fill_steps(factor_ref, size, source_of, keeps, target, diagonal=False):
    def step(row):
        keep = jnp.broadcast_to(keeps[row // CELL_ATOMS], (ROWS, GROUP))
        if diagonal:
            row_at = lax.broadcasted_iota(jnp.int32, (ROWS, GROUP), 0)
            lane_at = lax.broadcasted_iota(jnp.int32, (ROWS, GROUP), 1)
            keep = jnp.where(row_at + row == lane_at, 0.0, keep)
        factor_rows(factor_ref, size, row, source_of(row), target, keep)

    return [functools.partial(step, row) for row in range(0, size, ROWS)]


def rows_of(place_ref, start):
    return lambda row: [place_ref[axis, start + row : start + row + ROWS, :] for axis in range(3)]


def merged_rows(low_ref, low_start, high_ref, high_start):
    low, high = rows_of(low_ref, low_start), rows_of(high_ref, high_start)

    def rows(row):
        first = lax.broadcasted_iota(jnp.int32, (ROWS, GROUP), 1) < CELL_ATOMS
        return [jnp.where(first, one, two) for one, two in zip(low(row), high(row))]

    return rows


def product_steps(scaled_ref, factor_ref, totals, merged=False):
    def step(k):
        width = min(WIDTH, NY * GROUP - k * WIDTH)
        product = jnp.dot(
            scaled_ref[...],
            factor_ref[:, k * WIDTH : k * WIDTH + width],
            preferred_element_type=jnp.float32,
        )
        if merged:
            lane = lax.broadcasted_iota(jnp.int32, (CH, width), 1) % GROUP
            product = jnp.where(lane < CELL_ATOMS, product[:CH], product[CH:])
        totals[k] = product if totals[k] is None else totals[k] + product

    return [functools.partial(step, k) for k in range(CHUNKS)]


def interleave(one, two):
    done = 0
    for k, step in enumerate(one):
        step()
        upto = (k + 1) * len(two) // len(one)
        for other in two[done:upto]:
            other()
        done = upto


def local_kernel(*refs):
    count_ref, pair_target_ref, pair_source_ref, radial_ref, near_ref, far_ref = refs[:6]
    later_in = refs[6 : 6 + LATER]
    group_factor_ref, cell_factor_ref, messages_ref, keep_ref, place_ref = refs[6 + LATER : 11 + LATER]
    later_out = refs[11 + LATER : 11 + 2 * LATER]
    group_ref, cell_ref, sems = refs[11 + 2 * LATER :]
    copies = [
        pltpu.make_async_copy(src, dst, sems.at[k]) for k, (src, dst) in enumerate(zip(later_in, later_out))
    ]
    for copy in copies:
        copy.start()
    even = lax.axis_index("space") % 2 == 0
    near, far = near_ref[...], far_ref[...]
    slabs = (jnp.where(even, far, near), jnp.where(even, near, far))
    targets = [[slab[CH + axis : CH + axis + 1] for axis in range(3)] for slab in slabs]
    flags = live_flags(count_ref[0, 0], pair_target_ref[...], pair_source_ref[...])
    weight_t = radial_ref[...].T
    for g in range(2):
        set_place(place_ref.at[g], slabs[g])
        set_group(group_ref.at[g], slabs[g][:CH], weight_t)
        set_cell(cell_ref.at[g], slabs[1 - g][:CH], g, weight_t)

    def fill_group(t):
        keeps = [keep_row(flags, t, cell, cell) for cell in (2 * t + 2, 2 * t + 3)]
        return fill_steps(
            group_factor_ref.at[t], GROUP, rows_of(place_ref.at[t], 0), keeps, targets[t], True
        )

    def fill_cell(t):
        cell = 4 - t
        source_of = rows_of(place_ref.at[1 - t], t * CELL_ATOMS)
        return fill_steps(
            cell_factor_ref.at[t], CELL_ATOMS, source_of, [keep_row(flags, t, cell, cell)], targets[t]
        )

    totals = [[None] * CHUNKS for _ in range(2)]
    for step in fill_cell(0):
        step()
    interleave(product_steps(cell_ref.at[0], cell_factor_ref.at[0], totals[0]), fill_group(0))
    interleave(product_steps(group_ref.at[0], group_factor_ref.at[0], totals[0]), fill_group(1))
    interleave(product_steps(group_ref.at[1], group_factor_ref.at[1], totals[1]), fill_cell(1))
    for step in product_steps(cell_ref.at[1], cell_factor_ref.at[1], totals[1]):
        step()
    for t in range(2):
        messages_ref[t] = jnp.concatenate(totals[t], axis=1)
    rows = [
        keep_row(flags, 0, 1, 1),
        keep_row(flags, 0, 0, 5),
        keep_row(flags, 1, 6, 6),
        keep_row(flags, 1, 2, 7),
    ]
    keep_ref[...] = jnp.concatenate(rows + [jnp.zeros((4, GROUP), jnp.float32)], axis=0)
    for copy in copies:
        copy.wait()


def node_kernel(
    scale,
    near_ref,
    far_ref,
    from_pair_ref,
    from_cross_ref,
    messages_ref,
    keep_ref,
    own_place_ref,
    energy_grad_ref,
    radial_ref,
    mix_ref,
    readout_ref,
    updated_ref,
    kept_ref,
    sent_ref,
    grad_messages_ref,
    cell_factor_ref,
    merged_factor_ref,
    cell_ref,
    merged_ref,
    place_ref,
):
    even = lax.axis_index("space") % 2 == 0
    weight_t = radial_ref[...].T
    near, far = near_ref[...], far_ref[...]
    from_pair, from_cross = from_pair_ref[...], from_cross_ref[...]
    slabs = (
        jnp.where(even, from_cross, from_pair),
        jnp.where(even, far, near),
        jnp.where(even, near, far),
        jnp.where(even, from_pair, from_cross),
    )
    targets = [[slab[CH + axis : CH + axis + 1] for axis in range(3)] for slab in slabs[1:3]]

    for t in range(2):
        set_place(place_ref.at[t], slabs[3 * t])
        set_cell(cell_ref.at[t], slabs[3 * t][:CH], 1 - t, weight_t)
        set_cell(merged_ref.at[t, pl.ds(0, CH)], slabs[t][:CH], 0, weight_t)
        set_cell(merged_ref.at[t, pl.ds(CH, CH)], slabs[t + 2][:CH], 1, weight_t)

    def fill_cell(t):
        source_of = rows_of(place_ref.at[t], (1 - t) * CELL_ATOMS)
        keeps = [keep_ref[2 * t : 2 * t + 1, :]]
        return fill_steps(cell_factor_ref.at[t], CELL_ATOMS, source_of, keeps, targets[t])

    def fill_merged(t):
        places = (place_ref.at[0], own_place_ref.at[0], own_place_ref.at[1], place_ref.at[1])
        source_of = merged_rows(places[t], 0, places[t + 2], CELL_ATOMS)
        keeps = [keep_ref[2 * t + 1 : 2 * t + 2, :]]
        return fill_steps(merged_factor_ref.at[t], CELL_ATOMS, source_of, keeps, targets[t])

    totals = [
        [messages_ref[t, :, k * WIDTH : min((k + 1) * WIDTH, NY * GROUP)] for k in range(CHUNKS)]
        for t in range(2)
    ]

    def add_cell(t):
        return product_steps(cell_ref.at[t], cell_factor_ref.at[t], totals[t])

    def add_merged(t):
        return product_steps(merged_ref.at[t], merged_factor_ref.at[t], totals[t], True)

    readout = jnp.broadcast_to(readout_ref[...], (8, CH)).T[:, :1]
    mix = mix_ref[...]
    mix_t = mix.astype(jnp.float32).T.astype(jnp.bfloat16)

    for step in fill_cell(0):
        step()
    interleave(add_cell(0), fill_merged(0))
    interleave(add_merged(0), fill_cell(1))
    interleave(add_cell(1), fill_merged(1))
    for step in add_merged(1):
        step()

    sides = [jnp.concatenate(total, axis=1) for total in totals]
    part = [
        jnp.concatenate([side[:, y * GROUP : (y + 1) * GROUP] for side in sides], axis=1)
        for y in range(NY)
    ]
    invariants = jnp.concatenate(
        [
            part[0],
            0.5 * (part[1] * part[1] + part[2] * part[2] + part[3] * part[3]),
            0.5
            * (
                part[4] * part[4]
                + part[5] * part[5]
                + part[6] * part[6]
                + part[7] * part[7]
                + part[8] * part[8]
            ),
        ],
        axis=0,
    ).astype(jnp.bfloat16)
    preact = jnp.dot(mix_t, invariants, preferred_element_type=jnp.float32)
    gating = jax.nn.sigmoid(preact)
    energy_grad = energy_grad_ref[...]
    spread = readout * energy_grad
    grad_pre = (spread * gating * (1.0 + preact * (1.0 - gating))).astype(jnp.bfloat16)
    grad_inv = jnp.dot(mix, grad_pre, preferred_element_type=jnp.float32)
    grad_mix = scale * lax.dot_general(
        invariants, grad_pre, (((1,), (1,)), ((), ())), preferred_element_type=jnp.float32
    )
    kept_ref[...] = jnp.where(even, grad_mix[:HALF], grad_mix[HALF:])
    sent_ref[...] = jnp.where(even, grad_mix[HALF:], grad_mix[:HALF])
    for y in range(NY):
        order = 0 if y == 0 else 1 if y < 4 else 2
        grad = grad_inv[order * CH : (order + 1) * CH]
        grad = (grad if y == 0 else grad * part[y]).astype(jnp.bfloat16)
        for t in range(2):
            grad_messages_ref[t, :, y * GROUP : (y + 1) * GROUP] = grad[:, t * GROUP : (t + 1) * GROUP]

    updated_ref[...] = jnp.concatenate([slabs[1][:CH], slabs[2][:CH]], axis=1) + preact * gating


def back(factor, grad_messages):
    return lax.dot_general(
        factor, grad_messages, (((1,), (1,)), ((), ())), preferred_element_type=jnp.float32
    )


def source_grads(total, features_t, weight):
    size = features_t.shape[0]
    grad_t = None
    radial = []
    for b in range(NB):
        piece = total[b * size : (b + 1) * size]
        term = piece * weight[b : b + 1, :]
        grad_t = term if grad_t is None else grad_t + term
        radial.append(jnp.sum(piece * features_t, axis=0, keepdims=True))
    return grad_t, jnp.concatenate(radial, axis=0)


def halo_back_kernel(
    cell_factor_ref,
    merged_factor_ref,
    grad_messages_ref,
    near_ref,
    far_ref,
    from_pair_ref,
    from_cross_ref,
    radial_ref,
    to_pair_ref,
    to_cross_ref,
    extra_ref,
    share_ref,
):
    even = lax.axis_index("space") % 2 == 0
    weight = radial_ref[...]
    near, far = near_ref[:CH, :], far_ref[:CH, :]
    from_pair, from_cross = from_pair_ref[:CH, :], from_cross_ref[:CH, :]
    features_t = [
        jnp.where(even, one, two).T
        for one, two in ((from_cross, from_pair), (far, near), (near, far), (from_pair, from_cross))
    ]
    first = lax.broadcasted_iota(jnp.int32, (CH, NY * GROUP), 1) % GROUP < CELL_ATOMS
    low, high = slice(CELL_ATOMS), slice(CELL_ATOMS, GROUP)
    share = None
    grads = {}
    for t in range(2):
        grad = grad_messages_ref[t]
        none = jnp.zeros_like(grad)
        both = jnp.concatenate([jnp.where(first, grad, none), jnp.where(first, none, grad)], axis=0)
        merged = back(merged_factor_ref[t], both)
        pieces = (
            (3 * t, 1 - t, back(cell_factor_ref[t], grad)),
            (t, 0, merged[:, :CH]),
            (t + 2, 1, merged[:, CH:]),
        )
        for g, half, total in pieces:
            grads[g, half], part = source_grads(total, features_t[g][(low, high)[half]], weight)
            share = part if share is None else share + part
    grad_before = jnp.concatenate([grads[0, 0], grads[0, 1]], axis=0).T
    grad_after = jnp.concatenate([grads[3, 0], grads[3, 1]], axis=0).T
    to_pair_ref[...] = jnp.where(even, grad_after, grad_before)
    to_cross_ref[...] = jnp.where(even, grad_before, grad_after)
    extra_ref[low, :] = grads[1, 0]
    extra_ref[high, :] = grads[2, 1]
    share_ref[...] = share


def own_back_kernel(
    scale,
    group_factor_ref,
    cell_factor_ref,
    grad_messages_ref,
    near_ref,
    far_ref,
    radial_ref,
    extra_ref,
    share_ref,
    updated_ref,
    species_ref,
    shift_ref,
    energy_grad_ref,
    readout_ref,
    own_grad_ref,
    joined_ref,
    energy_ref,
):
    even = lax.axis_index("space") % 2 == 0
    weight = radial_ref[...]
    near, far = near_ref[:CH, :], far_ref[:CH, :]
    share = share_ref[...]
    low, high = slice(CELL_ATOMS), slice(CELL_ATOMS, GROUP)
    readout = jnp.broadcast_to(readout_ref[...], (8, CH)).T[:, :1]
    updated, energy_grad, kinds = updated_ref[...], energy_grad_ref[...], species_ref[...]
    spread = readout * energy_grad
    shifts = jnp.zeros((1, 2 * GROUP), jnp.float32)
    for n in range(NSPEC):
        shifts = jnp.where(kinds == n, shift_ref[:, n : n + 1], shifts)
    energy_ref[...] = jnp.sum(updated * readout, axis=0, keepdims=True) + shifts
    readout_row = column_to_row(jnp.sum(updated * energy_grad, axis=1, keepdims=True), CH)
    here = lax.broadcasted_iota(jnp.int32, (NSPEC, 2 * GROUP), 0) == kinds
    by_kind = jnp.sum(jnp.where(here, energy_grad, 0.0), axis=1, keepdims=True)
    for t, features in enumerate((jnp.where(even, far, near), jnp.where(even, near, far))):
        features_t = features.T
        total = back(group_factor_ref[t], grad_messages_ref[t])
        grad, part = source_grads(total, features_t, weight)
        inner, outer = (high, low) if t == 0 else (low, high)
        total = back(cell_factor_ref[1 - t], grad_messages_ref[1 - t])
        one, more = source_grads(total, features_t[inner], weight)
        two = extra_ref[outer, :]
        grad = (grad + jnp.concatenate([two, one] if t == 0 else [one, two], axis=0)).T
        at = slice(t * GROUP, (t + 1) * GROUP)
        own_grad_ref[:, at] = spread[:, at] + grad
        share = share + part + more
    joined_ref[:NB, :] = share * scale
    rest = [readout_row, column_to_row(by_kind, NSPEC), jnp.zeros((6, CH), jnp.float32)]
    joined_ref[NB:, :] = jnp.concatenate(rest, axis=0) * scale


def quarter_kernel(kept_ref, received_ref, keep_ref, send_ref):
    first = first_of_pair()
    low = kept_ref[:QUARTER, :] + received_ref[:QUARTER, :]
    high = kept_ref[QUARTER:, :] + received_ref[QUARTER:, :]
    keep_ref[...] = jnp.where(first, low, high)
    send_ref[...] = jnp.where(first, high, low)


def join_kernel(kept_ref, received_ref, rest_ref, out_ref):
    out_ref[:QUARTER, :] = kept_ref[...] + received_ref[...]
    out_ref[QUARTER:, :] = rest_ref[...]


def gather_kernel(mine_ref, along_ref, other_ref, both_ref, out_ref):
    first = first_of_pair()
    at, rest = slice(QUARTER), slice(QUARTER, QUARTER + REST)
    mine = mine_ref[at, :] + along_ref[at, :]
    other = other_ref[at, :] + both_ref[at, :]
    out_ref[:QUARTER, :] = jnp.where(first, mine, other)
    out_ref[QUARTER:HALF, :] = jnp.where(first, other, mine)
    out_ref[HALF:, :] = (mine_ref[rest, :] + along_ref[rest, :]) + (other_ref[rest, :] + both_ref[rest, :])


def fold_kernel(own_ref, from_pair_ref, from_cross_ref, energy_in_ref, grad_ref, energy_ref):
    even = lax.axis_index("space") % 2 == 0
    pair = from_pair_ref[...]
    cross = from_cross_ref[...]
    grad_ref[0, :, :GROUP] = own_ref[:, :GROUP] + jnp.where(even, cross, pair)
    grad_ref[0, :, GROUP:] = own_ref[:, GROUP:] + jnp.where(even, pair, cross)
    energy_ref[...] = energy_in_ref[...]


def finish_kernel(mine_ref, other_ref, radial_ref, mix_ref, readout_ref, shift_ref):
    even = lax.axis_index("space") % 2 == 0
    mine, other = mine_ref[:HALF, :], other_ref[:HALF, :]
    mix_ref[:HALF, :] = jnp.where(even, mine, other)
    mix_ref[HALF:, :] = jnp.where(even, other, mine)
    rest = mine_ref[HALF:, :] + other_ref[HALF:, :]
    radial_ref[...] = rest[:NB]
    readout_ref[...] = rest[NB : NB + 1]
    shift_ref[...] = rest[NB + 1 : NB + 2, :NSPEC]


def first_of_pair():
    space, dp = lax.axis_index("space"), lax.axis_index("dp")
    return jnp.where(space % 2 == 0, dp, space // 2) % 2 == 0


def exchange_routes(space, dp):
    along = [(0, 1 << k) for k in range(dp.bit_length() - 1)]
    across = [(1 << k, 0) for k in range(1, space.bit_length() - 1)]
    shared = (along[0], across[0])
    orders = (across + along[1:], along[:1] + across[1:] + along[1:])
    orders = (orders[0], orders[1][:-2] + orders[1][:-3:-1])
    count = len(orders[0])

    def route(*places):
        moves = []
        for s in range(space):
            step = [shared[s % 2] if k < 0 else orders[s % 2][k] for k in places]
            for d in range(dp):
                to_s, to_d = s, d
                for one, two in step:
                    to_s, to_d = to_s ^ one, to_d ^ two
                moves.append((s * dp + d, to_s * dp + to_d))
        return moves

    rounds = []
    for k in range(0, count - 1, 2):
        if k + 1 < count - 1:
            rounds.append([route(k), route(k + 1), route(k, k + 1)])
        else:
            rounds.append([route(k)])
    last = count - 1
    rounds.append([route(last), route(-1), route(last, -1)])
    return route(-1), rounds


def call(kernel, name, inputs, outputs, mib=4, scratch=(), flops=0):
    vmem = pl.BlockSpec(memory_space=pltpu.VMEM)
    shapes = tuple(jax.ShapeDtypeStruct(shape, kind) for shape, kind in outputs)
    moved = sum(math.prod(v.shape) * v.dtype.itemsize for v in (*inputs, *shapes))
    return pl.pallas_call(
        kernel,
        out_shape=shapes,
        in_specs=[vmem] * len(inputs),
        out_specs=(vmem,) * len(shapes),
        scratch_shapes=scratch,
        compiler_params=pltpu.CompilerParams(vmem_limit_bytes=mib * 1024 * 1024),
        cost_estimate=pl.CostEstimate(flops=flops, bytes_accessed=moved, transcendentals=0),
        name=name,
    )(*inputs)


def in_hbm(value):
    return pltpu.with_memory_space_constraint(value, pltpu.HBM)


def body(
    node_features,
    positions,
    species,
    energy_cotangent,
    pair_target,
    pair_source,
    pair_count,
    radial_weight,
    mix_weight,
    readout_weight,
    species_shift,
):
    atoms_here = node_features.shape[2]
    space, dp = lax.axis_size("space"), lax.axis_size("dp")
    scale = 1.0 / math.sqrt(atoms_here * space * dp)
    pair = [(i, i ^ 1) for i in range(space)]
    cross = [(i, ((i + 1) ^ 1) - 1) for i in range(1, space - 1)]
    hbm = pl.BlockSpec(memory_space=pltpu.HBM)
    smem = pl.BlockSpec(memory_space=pltpu.SMEM)
    vmem = pl.BlockSpec(memory_space=pltpu.VMEM)
    f32, bf16 = jnp.float32, jnp.bfloat16
    small = (pair_target, pair_source, radial_weight)
    later = (
        species,
        species_shift.reshape(1, NSPEC),
        energy_cotangent,
        mix_weight,
        readout_weight.reshape(1, CH),
    )
    near, far, *small = pl.pallas_call(
        split_kernel,
        out_shape=(jax.ShapeDtypeStruct((SLAB_ROWS, GROUP), f32),) * 2
        + tuple(jax.ShapeDtypeStruct(v.shape, v.dtype) for v in small),
        in_specs=[hbm] * (SMALL + 2),
        out_specs=(vmem,) * (SMALL + 2),
        scratch_shapes=[
            pltpu.VMEM((3, 1, atoms_here), f32),
            pltpu.SemaphoreType.DMA((SMALL + 3,)),
        ],
        compiler_params=pltpu.CompilerParams(vmem_limit_bytes=4 * 1024 * 1024),
        name="split",
    )(
        in_hbm(node_features),
        in_hbm(jnp.transpose(positions, (1, 0, 2))),
        *[in_hbm(v) for v in small],
    )
    targets, sources, radial = small
    from_cross = lax.ppermute(far, "space", cross)
    from_pair = lax.ppermute(near, "space", pair)

    block_flops = 2 * CH * NB * NY * GROUP * GROUP
    group_factor, cell_factor, messages, keep, place, *later = pl.pallas_call(
        local_kernel,
        out_shape=(
            jax.ShapeDtypeStruct((2, NB * GROUP, NY * GROUP), bf16),
            jax.ShapeDtypeStruct((2, NB * CELL_ATOMS, NY * GROUP), bf16),
            jax.ShapeDtypeStruct((2, CH, NY * GROUP), f32),
            jax.ShapeDtypeStruct((8, GROUP), f32),
            jax.ShapeDtypeStruct((2, 3, GROUP, GROUP), f32),
            *[jax.ShapeDtypeStruct(v.shape, v.dtype) for v in later],
        ),
        in_specs=[smem] + [vmem] * 5 + [hbm] * LATER,
        out_specs=(vmem,) * (5 + LATER),
        scratch_shapes=[
            pltpu.VMEM((2, CH, NB * GROUP), bf16),
            pltpu.VMEM((2, CH, NB * CELL_ATOMS), bf16),
            pltpu.SemaphoreType.DMA((LATER,)),
        ],
        compiler_params=pltpu.CompilerParams(vmem_limit_bytes=16 * 1024 * 1024),
        cost_estimate=pl.CostEstimate(
            flops=3 * block_flops, bytes_accessed=11_000_000, transcendentals=0
        ),
        name="local_pairs",
    )(pair_count, targets, sources, radial, near, far, *[in_hbm(v) for v in later])
    species, shift, energy_grad, mix, readout = later

    updated, kept, sent, grad_messages, halo_factor, merged_factor = call(
        functools.partial(node_kernel, scale),
        "node_stage",
        (
            near,
            far,
            from_pair,
            from_cross,
            messages,
            keep,
            place,
            energy_grad,
            radial,
            mix,
            readout,
        ),
        (
            ((CH, atoms_here), f32),
            ((HALF, CH), f32),
            ((HALF, CH), f32),
            ((2, CH, NY * GROUP), bf16),
            ((2, NB * CELL_ATOMS, NY * GROUP), bf16),
            ((2, NB * CELL_ATOMS, NY * GROUP), bf16),
        ),
        16,
        [
            pltpu.VMEM((2, CH, NB * CELL_ATOMS), bf16),
            pltpu.VMEM((2, 2 * CH, NB * CELL_ATOMS), bf16),
            pltpu.VMEM((2, 3, GROUP, GROUP), f32),
        ],
        2 * block_flops,
    )

    received = lax.ppermute(sent, "space", pair)
    pair_grad, cross_grad, extra, share = call(
        halo_back_kernel,
        "halo_back",
        (
            halo_factor,
            merged_factor,
            grad_messages,
            near,
            far,
            from_pair,
            from_cross,
            radial,
        ),
        (((CH, GROUP), f32), ((CH, GROUP), f32), ((GROUP, CH), f32), ((NB, CH), f32)),
        12,
        (),
        2 * block_flops,
    )
    received, share = lax.optimization_barrier((received, share))
    quarter, sent = call(
        quarter_kernel,
        "quarter",
        (kept, received),
        (((QUARTER, CH), f32), ((QUARTER, CH), f32)),
    )
    sharing, (*rounds, last) = exchange_routes(space, dp)
    everyone = ("space", "dp")
    sent, grad_messages, pair_grad = lax.optimization_barrier((sent, grad_messages, pair_grad))
    received = lax.ppermute(sent, everyone, sharing)
    from_pair = lax.ppermute(pair_grad, "space", pair)
    own_grad, joined, energy = call(
        functools.partial(own_back_kernel, scale),
        "own_back",
        (
            group_factor,
            cell_factor,
            grad_messages,
            near,
            far,
            radial,
            extra,
            share,
            updated,
            species,
            shift,
            energy_grad,
            readout,
        ),
        (((CH, atoms_here), f32), ((REST, CH), f32), ((1, atoms_here), f32)),
        12,
        (),
        3 * block_flops,
    )
    (value,) = call(
        join_kernel, "join", (quarter, received, joined), (((QUARTER + REST, CH), f32),)
    )
    value, from_pair, cross_grad = lax.optimization_barrier((value, from_pair, cross_grad))
    for turn, routes in enumerate(rounds):
        arrived = [lax.ppermute(value, everyone, route) for route in routes]
        if turn == 0:
            from_cross = lax.ppermute(cross_grad, "space", cross)
        value = value + arrived[0]
        if len(arrived) == 3:
            value = value + (arrived[1] + arrived[2])
    arrived = [lax.ppermute(value, everyone, route) for route in last]
    value, from_cross, *arrived = lax.optimization_barrier((value, from_cross, *arrived))
    (value,) = call(
        gather_kernel,
        "gather",
        (value, *arrived),
        (((HALF + REST, CH), f32),),
    )
    feature_grad, energy = call(
        fold_kernel,
        "fold",
        (own_grad, from_pair, from_cross, energy),
        (((1, CH, atoms_here), f32), ((1, atoms_here), f32)),
    )
    radial_grad, mix_grad, readout_grad, shift_grad = call(
        finish_kernel,
        "finish",
        (value, lax.ppermute(value, "space", pair)),
        (((NB, CH), f32), ((MIX_ROWS, CH), f32), ((1, CH), f32), ((1, NSPEC), f32)),
    )
    return (
        energy,
        feature_grad,
        radial_grad,
        mix_grad,
        readout_grad.reshape(CH),
        shift_grad.reshape(NSPEC),
    )


def solution(mesh):
    return jax.shard_map(
        body,
        mesh=mesh,
        in_specs=(
            P("dp", None, "space"),
            P("dp", None, "space"),
            P("dp", "space"),
            P("dp", "space"),
            P("dp", "space"),
            P("dp", "space"),
            P("dp", "space"),
            P(),
            P(),
            P(),
            P(),
        ),
        out_specs=(P("dp", "space"), P("dp", None, "space"), P(), P(), P(), P()),
        check_vma=False,
    )
```

```python
import functools
import math

import jax
import jax.numpy as jnp
from jax import lax
from jax.experimental import pallas as pl
from jax.experimental.pallas import tpu as pltpu
from jax.sharding import PartitionSpec as P

CH = 128
NB = 8
NY = 9
NSPEC = 8
CELL_ATOMS = 64
HALO_CELLS = 2
GROUP = 2 * CELL_ATOMS
ROWS = 16
WIDTH = 256
CHUNKS = -(-NY * GROUP // WIDTH)

cutoff = 5.0
message_scale = 0.25

COS_COEFFS = (
    0.9999999889445765,
    -4.93480111664404,
    4.058694745521682,
    -1.3351580223048074,
    0.2350290226247885,
    -0.025358285754444005,
    0.0015936782135993002,
)
SINC_COEFFS = (
    0.9999999992502204,
    -1.6449339933418936,
    0.8117412468909989,
    -0.1907447263221115,
    0.02612742969685046,
    -0.0023157632409761065,
    0.00012580778956459784,
)

MIX_ROWS = 3 * CH
HALF = MIX_ROWS // 2
QUARTER = MIX_ROWS // 4
REST = 16
CELLS = 4 + 2 * HALO_CELLS
SMALL = 3
LATER = 5
SLAB_ROWS = CH + 8


def polynomial(coeffs, x):
    total = coeffs[-1] * x + coeffs[-2]
    for c in coeffs[-3::-1]:
        total = total * x + c
    return total


def factor_rows(factor_ref, size, row, source, target, keep):
    dx = (target[0] - source[0]) * (1.0 / cutoff)
    dy = (target[1] - source[1]) * (1.0 / cutoff)
    dz = (target[2] - source[2]) * (1.0 / cutoff)
    xx, yy, zz = dx * dx, dy * dy, dz * dz
    square = xx + yy + zz
    inside = jnp.minimum(square, 1.0)
    gap = 1.0 - inside
    base = (gap * gap) * keep * polynomial(SINC_COEFFS, inside)
    twice_cos = polynomial([2.0 * c for c in COS_COEFFS], inside)
    raw = [base, twice_cos * base]
    for _ in range(NB - 2):
        raw.append(twice_cos * raw[-1] - raw[-2])
    radial = [value if b == 0 else value * (1.0 / (b + 1)) for b, value in enumerate(raw)]
    root_three = math.sqrt(3.0)
    root_fifteen = math.sqrt(15.0)
    root_five = math.sqrt(5.0)
    wide_x = root_fifteen * dx
    harmonic = [
        None,
        root_three * dx,
        root_three * dy,
        root_three * dz,
        wide_x * dy,
        (root_fifteen * dy) * dz,
        (0.5 * root_five) * (3.0 * zz - square),
        wide_x * dz,
        (0.5 * root_fifteen) * (xx - yy),
    ]
    for b in range(NB):
        rows = slice(b * size + row, b * size + row + ROWS)
        for y in range(NY):
            value = radial[b] if y == 0 else radial[b] * harmonic[y]
            factor_ref[rows, y * GROUP : (y + 1) * GROUP] = value.astype(jnp.bfloat16)


def column_to_row(column, size):
    wide = jnp.broadcast_to(column, (size, GROUP))
    at = lax.broadcasted_iota(jnp.int32, (size, GROUP), 0)
    lane = lax.broadcasted_iota(jnp.int32, (size, GROUP), 1)
    return jnp.sum(jnp.where(at == lane, wide, 0.0), axis=0, keepdims=True)


def split_kernel(*refs):
    features_ref, place_in_ref, *inputs = refs[: SMALL + 2]
    near_ref, far_ref, *outputs = refs[SMALL + 2 : 2 * SMALL + 4]
    place_ref, sems = refs[2 * SMALL + 4 :]
    core = lax.axis_index("space") % 2
    place_copy = pltpu.make_async_copy(place_in_ref, place_ref, sems.at[2])
    place_copy.start()
    copies = []
    for k, (ref, side) in enumerate(((near_ref, 1 - core), (far_ref, core))):
        at = pl.ds(pl.multiple_of(side * GROUP, GROUP), GROUP)
        copies.append(
            pltpu.make_async_copy(features_ref.at[0, :, at], ref.at[pl.ds(0, CH)], sems.at[k])
        )
    for k, (src, dst) in enumerate(zip(inputs, outputs)):
        copies.append(pltpu.make_async_copy(src, dst, sems.at[3 + k]))
    for copy in copies:
        copy.start()
    place_copy.wait()
    low, high = slice(GROUP), slice(GROUP, 2 * GROUP)
    filler = jnp.zeros((5, GROUP), jnp.float32)
    for ref, one, two in ((near_ref, high, low), (far_ref, low, high)):
        rows = [
            jnp.where(core == 0, place_ref[axis, :, one], place_ref[axis, :, two]) for axis in range(3)
        ]
        ref[CH:, :] = jnp.concatenate(rows + [filler], axis=0)
    for copy in copies:
        copy.wait()


def live_flags(count, pair_target, pair_source):
    size = (4 * CELLS, pair_target.shape[1])
    at = lax.broadcasted_iota(jnp.int32, size, 0)
    slot = lax.broadcasted_iota(jnp.int32, size, 1)
    hit = (pair_target * CELLS + pair_source == at) & (slot < count)
    return jnp.max(jnp.where(hit, message_scale, 0.0), axis=1, keepdims=True)


def keep_row(flags, t, low, high):
    lane = lax.broadcasted_iota(jnp.int32, (1, GROUP), 1)
    one, two = (2 * t) * CELLS + low, (2 * t + 1) * CELLS + high
    return jnp.where(lane < CELL_ATOMS, flags[one : one + 1], flags[two : two + 1])


def set_group(scaled_ref, features, weight_tiles):
    for b, weight in enumerate(weight_tiles):
        scaled_ref[:, b * GROUP : (b + 1) * GROUP] = (features * weight).astype(jnp.bfloat16)


def set_cell(scaled_ref, features, half, paired_ref):
    first = lax.broadcasted_iota(jnp.int32, (CH, GROUP), 1) < CELL_ATOMS
    turned = pltpu.roll(features, CELL_ATOMS, 1)
    twice = jnp.where(first, features, turned) if half == 0 else jnp.where(first, turned, features)
    for k in range(NB // 2):
        scaled_ref[:, k * GROUP : (k + 1) * GROUP] = (twice * paired_ref[k]).astype(jnp.bfloat16)


def set_place(place_ref, slab):
    place = slab[CH:].T
    for axis in range(3):
        place_ref[axis] = jnp.broadcast_to(place[:, axis : axis + 1], (GROUP, GROUP))


def fill_steps(factor_ref, size, source_of, keeps, target, diagonal=False):
    def step(row):
        keep = jnp.broadcast_to(keeps[row // CELL_ATOMS], (ROWS, GROUP))
        if diagonal:
            row_at = lax.broadcasted_iota(jnp.int32, (ROWS, GROUP), 0)
            lane_at = lax.broadcasted_iota(jnp.int32, (ROWS, GROUP), 1)
            keep = jnp.where(row_at + row == lane_at, 0.0, keep)
        factor_rows(factor_ref, size, row, source_of(row), target, keep)

    return [functools.partial(step, row) for row in range(0, size, ROWS)]


def rows_of(place_ref, start):
    return lambda row: [place_ref[axis, start + row : start + row + ROWS, :] for axis in range(3)]


def merged_rows(low_ref, low_start, high_ref, high_start):
    low, high = rows_of(low_ref, low_start), rows_of(high_ref, high_start)

    def rows(row):
        first = lax.broadcasted_iota(jnp.int32, (ROWS, GROUP), 1) < CELL_ATOMS
        return [jnp.where(first, one, two) for one, two in zip(low(row), high(row))]

    return rows


def product_steps(scaled_ref, factor_ref, totals, merged=False):
    def step(k):
        width = min(WIDTH, NY * GROUP - k * WIDTH)
        product = jnp.dot(
            scaled_ref[...],
            factor_ref[:, k * WIDTH : k * WIDTH + width],
            preferred_element_type=jnp.float32,
        )
        if merged:
            lane = lax.broadcasted_iota(jnp.int32, (CH, width), 1) % GROUP
            product = jnp.where(lane < CELL_ATOMS, product[:CH], product[CH:])
        totals[k] = product if totals[k] is None else totals[k] + product

    return [functools.partial(step, k) for k in range(CHUNKS)]


def interleave(one, two):
    done = 0
    for k, step in enumerate(one):
        step()
        upto = (k + 1) * len(two) // len(one)
        for other in two[done:upto]:
            other()
        done = upto


def local_kernel(*refs):
    count_ref, pair_target_ref, pair_source_ref, radial_ref, near_ref, far_ref = refs[:6]
    later_in = refs[6 : 6 + LATER]
    outs = refs[6 + LATER : 12 + LATER]
    group_factor_ref, cell_factor_ref, messages_ref, keep_ref, place_ref, paired_ref = outs
    later_out = refs[12 + LATER : 12 + 2 * LATER]
    group_ref, cell_ref, sems = refs[12 + 2 * LATER :]
    copies = [
        pltpu.make_async_copy(src, dst, sems.at[k]) for k, (src, dst) in enumerate(zip(later_in, later_out))
    ]
    for copy in copies:
        copy.start()
    even = lax.axis_index("space") % 2 == 0
    near, far = near_ref[...], far_ref[...]
    slabs = (jnp.where(even, far, near), jnp.where(even, near, far))
    targets = [[slab[CH + axis : CH + axis + 1] for axis in range(3)] for slab in slabs]
    flags = live_flags(count_ref[0, 0], pair_target_ref[...], pair_source_ref[...])
    weight_t = radial_ref[...].T
    first = lax.broadcasted_iota(jnp.int32, (CH, GROUP), 1) < CELL_ATOMS
    weight_tiles = [jnp.broadcast_to(weight_t[:, b : b + 1], (CH, GROUP)) for b in range(NB)]
    for k in range(NB // 2):
        paired_ref[k] = jnp.where(first, weight_tiles[2 * k], weight_tiles[2 * k + 1])
    for g in range(2):
        set_place(place_ref.at[g], slabs[g])
        set_cell(cell_ref.at[g], slabs[1 - g][:CH], g, paired_ref)
        set_group(group_ref.at[g], slabs[g][:CH], weight_tiles)

    def fill_group(t):
        keeps = [keep_row(flags, t, cell, cell) for cell in (2 * t + 2, 2 * t + 3)]
        return fill_steps(
            group_factor_ref.at[t], GROUP, rows_of(place_ref.at[t], 0), keeps, targets[t], True
        )

    def fill_cell(t):
        cell = 4 - t
        source_of = rows_of(place_ref.at[1 - t], t * CELL_ATOMS)
        return fill_steps(
            cell_factor_ref.at[t], CELL_ATOMS, source_of, [keep_row(flags, t, cell, cell)], targets[t]
        )

    totals = [[None] * CHUNKS for _ in range(2)]
    for step in fill_cell(0):
        step()
    interleave(product_steps(cell_ref.at[0], cell_factor_ref.at[0], totals[0]), fill_group(0))
    interleave(product_steps(group_ref.at[0], group_factor_ref.at[0], totals[0]), fill_group(1))
    interleave(product_steps(group_ref.at[1], group_factor_ref.at[1], totals[1]), fill_cell(1))
    for step in product_steps(cell_ref.at[1], cell_factor_ref.at[1], totals[1]):
        step()
    for t in range(2):
        messages_ref[t] = jnp.concatenate(totals[t], axis=1)
    rows = [
        keep_row(flags, 0, 1, 1),
        keep_row(flags, 0, 0, 5),
        keep_row(flags, 1, 6, 6),
        keep_row(flags, 1, 2, 7),
    ]
    keep_ref[...] = jnp.concatenate(rows + [jnp.zeros((4, GROUP), jnp.float32)], axis=0)
    for copy in copies:
        copy.wait()


def node_kernel(
    scale,
    near_ref,
    far_ref,
    from_pair_ref,
    from_cross_ref,
    messages_ref,
    keep_ref,
    own_place_ref,
    paired_ref,
    energy_grad_ref,
    mix_ref,
    readout_ref,
    updated_ref,
    kept_ref,
    sent_ref,
    grad_messages_ref,
    cell_factor_ref,
    merged_factor_ref,
    cell_ref,
    merged_ref,
    place_ref,
):
    even = lax.axis_index("space") % 2 == 0
    near, far = near_ref[...], far_ref[...]
    from_pair, from_cross = from_pair_ref[...], from_cross_ref[...]
    slabs = (
        jnp.where(even, from_cross, from_pair),
        jnp.where(even, far, near),
        jnp.where(even, near, far),
        jnp.where(even, from_pair, from_cross),
    )
    targets = [[slab[CH + axis : CH + axis + 1] for axis in range(3)] for slab in slabs[1:3]]

    for t in range(2):
        set_place(place_ref.at[t], slabs[3 * t])
        set_cell(cell_ref.at[t], slabs[3 * t][:CH], 1 - t, paired_ref)
        set_cell(merged_ref.at[t, pl.ds(0, CH)], slabs[t][:CH], 0, paired_ref)
        set_cell(merged_ref.at[t, pl.ds(CH, CH)], slabs[t + 2][:CH], 1, paired_ref)

    def fill_cell(t):
        source_of = rows_of(place_ref.at[t], (1 - t) * CELL_ATOMS)
        keeps = [keep_ref[2 * t : 2 * t + 1, :]]
        return fill_steps(cell_factor_ref.at[t], CELL_ATOMS, source_of, keeps, targets[t])

    def fill_merged(t):
        places = (place_ref.at[0], own_place_ref.at[0], own_place_ref.at[1], place_ref.at[1])
        source_of = merged_rows(places[t], 0, places[t + 2], CELL_ATOMS)
        keeps = [keep_ref[2 * t + 1 : 2 * t + 2, :]]
        return fill_steps(merged_factor_ref.at[t], CELL_ATOMS, source_of, keeps, targets[t])

    totals = [
        [messages_ref[t, :, k * WIDTH : min((k + 1) * WIDTH, NY * GROUP)] for k in range(CHUNKS)]
        for t in range(2)
    ]

    def add_cell(t):
        return product_steps(cell_ref.at[t], cell_factor_ref.at[t], totals[t])

    def add_merged(t):
        return product_steps(merged_ref.at[t], merged_factor_ref.at[t], totals[t], True)

    readout = jnp.broadcast_to(readout_ref[...], (8, CH)).T[:, :1]
    mix = mix_ref[...]
    mix_t = mix.astype(jnp.float32).T.astype(jnp.bfloat16)

    for step in fill_cell(0):
        step()
    interleave(add_cell(0), fill_merged(0))
    interleave(add_merged(0), fill_cell(1))
    interleave(add_cell(1), fill_merged(1))
    for step in add_merged(1):
        step()

    sides = [jnp.concatenate(total, axis=1) for total in totals]
    part = [
        jnp.concatenate([side[:, y * GROUP : (y + 1) * GROUP] for side in sides], axis=1)
        for y in range(NY)
    ]
    invariants = jnp.concatenate(
        [
            part[0],
            0.5 * (part[1] * part[1] + part[2] * part[2] + part[3] * part[3]),
            0.5
            * (
                part[4] * part[4]
                + part[5] * part[5]
                + part[6] * part[6]
                + part[7] * part[7]
                + part[8] * part[8]
            ),
        ],
        axis=0,
    ).astype(jnp.bfloat16)
    preact = jnp.dot(mix_t, invariants, preferred_element_type=jnp.float32)
    gating = jax.nn.sigmoid(preact)
    energy_grad = energy_grad_ref[...]
    spread = readout * energy_grad
    grad_pre = (spread * gating * (1.0 + preact * (1.0 - gating))).astype(jnp.bfloat16)
    grad_inv = jnp.dot(mix, grad_pre, preferred_element_type=jnp.float32)
    grad_mix = scale * lax.dot_general(
        invariants, grad_pre, (((1,), (1,)), ((), ())), preferred_element_type=jnp.float32
    )
    kept_ref[...] = jnp.where(even, grad_mix[:HALF], grad_mix[HALF:])
    sent_ref[...] = jnp.where(even, grad_mix[HALF:], grad_mix[:HALF])
    for y in range(NY):
        order = 0 if y == 0 else 1 if y < 4 else 2
        grad = grad_inv[order * CH : (order + 1) * CH]
        grad = (grad if y == 0 else grad * part[y]).astype(jnp.bfloat16)
        for t in range(2):
            grad_messages_ref[t, :, y * GROUP : (y + 1) * GROUP] = grad[:, t * GROUP : (t + 1) * GROUP]

    updated_ref[...] = jnp.concatenate([slabs[1][:CH], slabs[2][:CH]], axis=1) + preact * gating


def back(factor, grad_messages):
    return lax.dot_general(
        factor, grad_messages, (((1,), (1,)), ((), ())), preferred_element_type=jnp.float32
    )


def source_grads(total, features_t, weight):
    size = features_t.shape[0]
    grad_t = None
    radial = []
    for b in range(NB):
        piece = total[b * size : (b + 1) * size]
        term = piece * weight[b : b + 1, :]
        grad_t = term if grad_t is None else grad_t + term
        radial.append(jnp.sum(piece * features_t, axis=0, keepdims=True))
    return grad_t, jnp.concatenate(radial, axis=0)


def halo_back_kernel(
    cell_factor_ref,
    merged_factor_ref,
    grad_messages_ref,
    near_ref,
    far_ref,
    from_pair_ref,
    from_cross_ref,
    radial_ref,
    to_pair_ref,
    to_cross_ref,
    extra_ref,
    share_ref,
):
    even = lax.axis_index("space") % 2 == 0
    weight = radial_ref[...]
    near, far = near_ref[:CH, :], far_ref[:CH, :]
    from_pair, from_cross = from_pair_ref[:CH, :], from_cross_ref[:CH, :]
    features_t = [
        jnp.where(even, one, two).T
        for one, two in ((from_cross, from_pair), (far, near), (near, far), (from_pair, from_cross))
    ]
    first = lax.broadcasted_iota(jnp.int32, (CH, NY * GROUP), 1) % GROUP < CELL_ATOMS
    low, high = slice(CELL_ATOMS), slice(CELL_ATOMS, GROUP)
    share = None
    grads = {}
    for t in range(2):
        grad = grad_messages_ref[t]
        none = jnp.zeros_like(grad)
        both = jnp.concatenate([jnp.where(first, grad, none), jnp.where(first, none, grad)], axis=0)
        merged = back(merged_factor_ref[t], both)
        pieces = (
            (3 * t, 1 - t, back(cell_factor_ref[t], grad)),
            (t, 0, merged[:, :CH]),
            (t + 2, 1, merged[:, CH:]),
        )
        for g, half, total in pieces:
            grads[g, half], part = source_grads(total, features_t[g][(low, high)[half]], weight)
            share = part if share is None else share + part
    grad_before = jnp.concatenate([grads[0, 0], grads[0, 1]], axis=0).T
    grad_after = jnp.concatenate([grads[3, 0], grads[3, 1]], axis=0).T
    to_pair_ref[...] = jnp.where(even, grad_after, grad_before)
    to_cross_ref[...] = jnp.where(even, grad_before, grad_after)
    extra_ref[low, :] = grads[1, 0]
    extra_ref[high, :] = grads[2, 1]
    share_ref[...] = share


def own_back_kernel(
    scale,
    group_factor_ref,
    cell_factor_ref,
    grad_messages_ref,
    near_ref,
    far_ref,
    radial_ref,
    extra_ref,
    share_ref,
    updated_ref,
    species_ref,
    shift_ref,
    energy_grad_ref,
    readout_ref,
    own_grad_ref,
    joined_ref,
    energy_ref,
):
    even = lax.axis_index("space") % 2 == 0
    weight = radial_ref[...]
    near, far = near_ref[:CH, :], far_ref[:CH, :]
    share = share_ref[...]
    low, high = slice(CELL_ATOMS), slice(CELL_ATOMS, GROUP)
    readout = jnp.broadcast_to(readout_ref[...], (8, CH)).T[:, :1]
    updated, energy_grad, kinds = updated_ref[...], energy_grad_ref[...], species_ref[...]
    spread = readout * energy_grad
    shifts = jnp.zeros((1, 2 * GROUP), jnp.float32)
    for n in range(NSPEC):
        shifts = jnp.where(kinds == n, shift_ref[:, n : n + 1], shifts)
    energy_ref[...] = jnp.sum(updated * readout, axis=0, keepdims=True) + shifts
    readout_row = column_to_row(jnp.sum(updated * energy_grad, axis=1, keepdims=True), CH)
    here = lax.broadcasted_iota(jnp.int32, (NSPEC, 2 * GROUP), 0) == kinds
    by_kind = jnp.sum(jnp.where(here, energy_grad, 0.0), axis=1, keepdims=True)
    for t, features in enumerate((jnp.where(even, far, near), jnp.where(even, near, far))):
        features_t = features.T
        total = back(group_factor_ref[t], grad_messages_ref[t])
        grad, part = source_grads(total, features_t, weight)
        inner, outer = (high, low) if t == 0 else (low, high)
        total = back(cell_factor_ref[1 - t], grad_messages_ref[1 - t])
        one, more = source_grads(total, features_t[inner], weight)
        two = extra_ref[outer, :]
        grad = (grad + jnp.concatenate([two, one] if t == 0 else [one, two], axis=0)).T
        at = slice(t * GROUP, (t + 1) * GROUP)
        own_grad_ref[:, at] = spread[:, at] + grad
        share = share + part + more
    joined_ref[:NB, :] = share * scale
    rest = [readout_row, column_to_row(by_kind, NSPEC), jnp.zeros((6, CH), jnp.float32)]
    joined_ref[NB:, :] = jnp.concatenate(rest, axis=0) * scale


def quarter_kernel(kept_ref, received_ref, keep_ref, send_ref):
    first = first_of_pair()
    low = kept_ref[:QUARTER, :] + received_ref[:QUARTER, :]
    high = kept_ref[QUARTER:, :] + received_ref[QUARTER:, :]
    keep_ref[...] = jnp.where(first, low, high)
    send_ref[...] = jnp.where(first, high, low)


def join_kernel(kept_ref, received_ref, rest_ref, out_ref):
    out_ref[:QUARTER, :] = kept_ref[...] + received_ref[...]
    out_ref[QUARTER:, :] = rest_ref[...]


def gather_kernel(mine_ref, along_ref, other_ref, both_ref, out_ref):
    first = first_of_pair()
    at, rest = slice(QUARTER), slice(QUARTER, QUARTER + REST)
    mine = mine_ref[at, :] + along_ref[at, :]
    other = other_ref[at, :] + both_ref[at, :]
    out_ref[:QUARTER, :] = jnp.where(first, mine, other)
    out_ref[QUARTER:HALF, :] = jnp.where(first, other, mine)
    out_ref[HALF:, :] = (mine_ref[rest, :] + along_ref[rest, :]) + (other_ref[rest, :] + both_ref[rest, :])


def fold_kernel(own_ref, from_pair_ref, from_cross_ref, energy_in_ref, grad_ref, energy_ref):
    even = lax.axis_index("space") % 2 == 0
    pair = from_pair_ref[...]
    cross = from_cross_ref[...]
    grad_ref[0, :, :GROUP] = own_ref[:, :GROUP] + jnp.where(even, cross, pair)
    grad_ref[0, :, GROUP:] = own_ref[:, GROUP:] + jnp.where(even, pair, cross)
    energy_ref[...] = energy_in_ref[...]


def finish_kernel(mine_ref, other_ref, radial_ref, mix_ref, readout_ref, shift_ref):
    even = lax.axis_index("space") % 2 == 0
    mine, other = mine_ref[:HALF, :], other_ref[:HALF, :]
    mix_ref[:HALF, :] = jnp.where(even, mine, other)
    mix_ref[HALF:, :] = jnp.where(even, other, mine)
    rest = mine_ref[HALF:, :] + other_ref[HALF:, :]
    radial_ref[...] = rest[:NB]
    readout_ref[...] = rest[NB : NB + 1]
    shift_ref[...] = rest[NB + 1 : NB + 2, :NSPEC]


def first_of_pair():
    space, dp = lax.axis_index("space"), lax.axis_index("dp")
    return jnp.where(space % 2 == 0, dp, space // 2) % 2 == 0


def exchange_routes(space, dp):
    along = [(0, 1 << k) for k in range(dp.bit_length() - 1)]
    across = [(1 << k, 0) for k in range(1, space.bit_length() - 1)]
    shared = (along[0], across[0])
    orders = (across + along[1:], along[:1] + across[1:] + along[1:])
    orders = (orders[0][:-2] + orders[0][:-3:-1], orders[1])
    count = len(orders[0])

    def route(*places):
        moves = []
        for s in range(space):
            step = [shared[s % 2] if k < 0 else orders[s % 2][k] for k in places]
            for d in range(dp):
                to_s, to_d = s, d
                for one, two in step:
                    to_s, to_d = to_s ^ one, to_d ^ two
                moves.append((s * dp + d, to_s * dp + to_d))
        return moves

    rounds = []
    for k in range(0, count - 1, 2):
        if k + 1 < count - 1:
            rounds.append([route(k), route(k + 1), route(k, k + 1)])
        else:
            rounds.append([route(k)])
    last = count - 1
    rounds.append([route(last), route(-1), route(last, -1)])
    return route(-1), rounds


def call(kernel, name, inputs, outputs, mib=4, scratch=(), flops=0):
    vmem = pl.BlockSpec(memory_space=pltpu.VMEM)
    shapes = tuple(jax.ShapeDtypeStruct(shape, kind) for shape, kind in outputs)
    moved = sum(math.prod(v.shape) * v.dtype.itemsize for v in (*inputs, *shapes))
    return pl.pallas_call(
        kernel,
        out_shape=shapes,
        in_specs=[vmem] * len(inputs),
        out_specs=(vmem,) * len(shapes),
        scratch_shapes=scratch,
        compiler_params=pltpu.CompilerParams(vmem_limit_bytes=mib * 1024 * 1024),
        cost_estimate=pl.CostEstimate(flops=flops, bytes_accessed=moved, transcendentals=0),
        name=name,
    )(*inputs)


def in_hbm(value):
    return pltpu.with_memory_space_constraint(value, pltpu.HBM)


def body(
    node_features,
    positions,
    species,
    energy_cotangent,
    pair_target,
    pair_source,
    pair_count,
    radial_weight,
    mix_weight,
    readout_weight,
    species_shift,
):
    atoms_here = node_features.shape[2]
    space, dp = lax.axis_size("space"), lax.axis_size("dp")
    scale = 1.0 / math.sqrt(atoms_here * space * dp)
    pair = [(i, i ^ 1) for i in range(space)]
    cross = [(i, ((i + 1) ^ 1) - 1) for i in range(1, space - 1)]
    hbm = pl.BlockSpec(memory_space=pltpu.HBM)
    smem = pl.BlockSpec(memory_space=pltpu.SMEM)
    vmem = pl.BlockSpec(memory_space=pltpu.VMEM)
    f32, bf16 = jnp.float32, jnp.bfloat16
    small = (pair_target, pair_source, radial_weight)
    later = (
        species,
        species_shift.reshape(1, NSPEC),
        energy_cotangent,
        mix_weight,
        readout_weight.reshape(1, CH),
    )
    near, far, *small = pl.pallas_call(
        split_kernel,
        out_shape=(jax.ShapeDtypeStruct((SLAB_ROWS, GROUP), f32),) * 2
        + tuple(jax.ShapeDtypeStruct(v.shape, v.dtype) for v in small),
        in_specs=[hbm] * (SMALL + 2),
        out_specs=(vmem,) * (SMALL + 2),
        scratch_shapes=[
            pltpu.VMEM((3, 1, atoms_here), f32),
            pltpu.SemaphoreType.DMA((SMALL + 3,)),
        ],
        compiler_params=pltpu.CompilerParams(vmem_limit_bytes=4 * 1024 * 1024),
        name="split",
    )(
        in_hbm(node_features),
        in_hbm(jnp.transpose(positions, (1, 0, 2))),
        *[in_hbm(v) for v in small],
    )
    targets, sources, radial = small
    from_cross = lax.ppermute(far, "space", cross)
    from_pair = lax.ppermute(near, "space", pair)

    block_flops = 2 * CH * NB * NY * GROUP * GROUP
    group_factor, cell_factor, messages, keep, place, paired, *later = pl.pallas_call(
        local_kernel,
        out_shape=(
            jax.ShapeDtypeStruct((2, NB * GROUP, NY * GROUP), bf16),
            jax.ShapeDtypeStruct((2, NB * CELL_ATOMS, NY * GROUP), bf16),
            jax.ShapeDtypeStruct((2, CH, NY * GROUP), f32),
            jax.ShapeDtypeStruct((8, GROUP), f32),
            jax.ShapeDtypeStruct((2, 3, GROUP, GROUP), f32),
            jax.ShapeDtypeStruct((NB // 2, CH, GROUP), f32),
            *[jax.ShapeDtypeStruct(v.shape, v.dtype) for v in later],
        ),
        in_specs=[smem] + [vmem] * 5 + [hbm] * LATER,
        out_specs=(vmem,) * (6 + LATER),
        scratch_shapes=[
            pltpu.VMEM((2, CH, NB * GROUP), bf16),
            pltpu.VMEM((2, CH, NB * CELL_ATOMS), bf16),
            pltpu.SemaphoreType.DMA((LATER,)),
        ],
        compiler_params=pltpu.CompilerParams(vmem_limit_bytes=16 * 1024 * 1024),
        cost_estimate=pl.CostEstimate(
            flops=3 * block_flops, bytes_accessed=11_000_000, transcendentals=0
        ),
        name="local_pairs",
    )(pair_count, targets, sources, radial, near, far, *[in_hbm(v) for v in later])
    species, shift, energy_grad, mix, readout = later

    updated, kept, sent, grad_messages, halo_factor, merged_factor = call(
        functools.partial(node_kernel, scale),
        "node_stage",
        (
            near,
            far,
            from_pair,
            from_cross,
            messages,
            keep,
            place,
            paired,
            energy_grad,
            mix,
            readout,
        ),
        (
            ((CH, atoms_here), f32),
            ((HALF, CH), f32),
            ((HALF, CH), f32),
            ((2, CH, NY * GROUP), bf16),
            ((2, NB * CELL_ATOMS, NY * GROUP), bf16),
            ((2, NB * CELL_ATOMS, NY * GROUP), bf16),
        ),
        16,
        [
            pltpu.VMEM((2, CH, NB * CELL_ATOMS), bf16),
            pltpu.VMEM((2, 2 * CH, NB * CELL_ATOMS), bf16),
            pltpu.VMEM((2, 3, GROUP, GROUP), f32),
        ],
        2 * block_flops,
    )

    received = lax.ppermute(sent, "space", pair)
    pair_grad, cross_grad, extra, share = call(
        halo_back_kernel,
        "halo_back",
        (
            halo_factor,
            merged_factor,
            grad_messages,
            near,
            far,
            from_pair,
            from_cross,
            radial,
        ),
        (((CH, GROUP), f32), ((CH, GROUP), f32), ((GROUP, CH), f32), ((NB, CH), f32)),
        12,
        (),
        2 * block_flops,
    )
    received, share = lax.optimization_barrier((received, share))
    quarter, sent = call(
        quarter_kernel,
        "quarter",
        (kept, received),
        (((QUARTER, CH), f32), ((QUARTER, CH), f32)),
    )
    sharing, (*rounds, last) = exchange_routes(space, dp)
    everyone = ("space", "dp")
    sent, grad_messages, pair_grad = lax.optimization_barrier((sent, grad_messages, pair_grad))
    received = lax.ppermute(sent, everyone, sharing)
    from_pair = lax.ppermute(pair_grad, "space", pair)
    own_grad, joined, energy = call(
        functools.partial(own_back_kernel, scale),
        "own_back",
        (
            group_factor,
            cell_factor,
            grad_messages,
            near,
            far,
            radial,
            extra,
            share,
            updated,
            species,
            shift,
            energy_grad,
            readout,
        ),
        (((CH, atoms_here), f32), ((REST, CH), f32), ((1, atoms_here), f32)),
        12,
        (),
        3 * block_flops,
    )
    (value,) = call(
        join_kernel, "join", (quarter, received, joined), (((QUARTER + REST, CH), f32),)
    )
    value, from_pair, cross_grad = lax.optimization_barrier((value, from_pair, cross_grad))
    for turn, routes in enumerate(rounds):
        arrived = [lax.ppermute(value, everyone, route) for route in routes]
        if turn == 0:
            from_cross = lax.ppermute(cross_grad, "space", cross)
        value = value + arrived[0]
        if len(arrived) == 3:
            value = value + (arrived[1] + arrived[2])
    arrived = [lax.ppermute(value, everyone, route) for route in last]
    value, from_cross, *arrived = lax.optimization_barrier((value, from_cross, *arrived))
    (value,) = call(
        gather_kernel,
        "gather",
        (value, *arrived),
        (((HALF + REST, CH), f32),),
    )
    feature_grad, energy = call(
        fold_kernel,
        "fold",
        (own_grad, from_pair, from_cross, energy),
        (((1, CH, atoms_here), f32), ((1, atoms_here), f32)),
    )
    radial_grad, mix_grad, readout_grad, shift_grad = call(
        finish_kernel,
        "finish",
        (value, lax.ppermute(value, "space", pair)),
        (((NB, CH), f32), ((MIX_ROWS, CH), f32), ((1, CH), f32), ((1, NSPEC), f32)),
    )
    return (
        energy,
        feature_grad,
        radial_grad,
        mix_grad,
        readout_grad.reshape(CH),
        shift_grad.reshape(NSPEC),
    )


def solution(mesh):
    return jax.shard_map(
        body,
        mesh=mesh,
        in_specs=(
            P("dp", None, "space"),
            P("dp", None, "space"),
            P("dp", "space"),
            P("dp", "space"),
            P("dp", "space"),
            P("dp", "space"),
            P("dp", "space"),
            P(),
            P(),
            P(),
            P(),
        ),
        out_specs=(P("dp", "space"), P("dp", None, "space"), P(), P(), P(), P()),
        check_vma=False,
    )
```

```python
import functools
import math

import jax
import jax.numpy as jnp
from jax import lax
from jax.experimental import pallas as pl
from jax.experimental.pallas import tpu as pltpu
from jax.sharding import PartitionSpec as P

CH = 128
NB = 8
NY = 9
NSPEC = 8
CELL_ATOMS = 64
HALO_CELLS = 2
GROUP = 2 * CELL_ATOMS
ROWS = 16
WIDTH = 256
CHUNKS = -(-NY * GROUP // WIDTH)

cutoff = 5.0
message_scale = 0.25

COS_COEFFS = (
    0.9999999889445765,
    -4.93480111664404,
    4.058694745521682,
    -1.3351580223048074,
    0.2350290226247885,
    -0.025358285754444005,
    0.0015936782135993002,
)
SINC_COEFFS = (
    0.9999999992502204,
    -1.6449339933418936,
    0.8117412468909989,
    -0.1907447263221115,
    0.02612742969685046,
    -0.0023157632409761065,
    0.00012580778956459784,
)

MIX_ROWS = 3 * CH
HALF = MIX_ROWS // 2
QUARTER = MIX_ROWS // 4
REST = 16
CELLS = 4 + 2 * HALO_CELLS
SMALL = 3
LATER = 5
SLAB_ROWS = CH + 8


def polynomial(coeffs, x):
    total = coeffs[-1] * x + coeffs[-2]
    for c in coeffs[-3::-1]:
        total = total * x + c
    return total


def factor_rows(factor_ref, size, row, source, target, keep):
    dx = (target[0] - source[0]) * (1.0 / cutoff)
    dy = (target[1] - source[1]) * (1.0 / cutoff)
    dz = (target[2] - source[2]) * (1.0 / cutoff)
    xx, yy, zz = dx * dx, dy * dy, dz * dz
    square = xx + yy + zz
    inside = jnp.minimum(square, 1.0)
    gap = 1.0 - inside
    base = (gap * gap) * keep * polynomial(SINC_COEFFS, inside)
    twice_cos = polynomial([2.0 * c for c in COS_COEFFS], inside)
    raw = [base, twice_cos * base]
    for _ in range(NB - 2):
        raw.append(twice_cos * raw[-1] - raw[-2])
    radial = [value if b == 0 else value * (1.0 / (b + 1)) for b, value in enumerate(raw)]
    root_three = math.sqrt(3.0)
    root_fifteen = math.sqrt(15.0)
    root_five = math.sqrt(5.0)
    wide_x = root_fifteen * dx
    harmonic = [
        None,
        root_three * dx,
        root_three * dy,
        root_three * dz,
        wide_x * dy,
        (root_fifteen * dy) * dz,
        (0.5 * root_five) * (3.0 * zz - square),
        wide_x * dz,
        (0.5 * root_fifteen) * (xx - yy),
    ]
    for b in range(NB):
        rows = slice(b * size + row, b * size + row + ROWS)
        for y in range(NY):
            value = radial[b] if y == 0 else radial[b] * harmonic[y]
            factor_ref[rows, y * GROUP : (y + 1) * GROUP] = value.astype(jnp.bfloat16)


def column_to_row(column, size):
    wide = jnp.broadcast_to(column, (size, GROUP))
    at = lax.broadcasted_iota(jnp.int32, (size, GROUP), 0)
    lane = lax.broadcasted_iota(jnp.int32, (size, GROUP), 1)
    return jnp.sum(jnp.where(at == lane, wide, 0.0), axis=0, keepdims=True)


def split_kernel(*refs):
    features_ref, place_in_ref, *inputs = refs[: SMALL + 2]
    near_ref, far_ref, *outputs = refs[SMALL + 2 : 2 * SMALL + 4]
    place_ref, sems = refs[2 * SMALL + 4 :]
    core = lax.axis_index("space") % 2
    place_copy = pltpu.make_async_copy(place_in_ref, place_ref, sems.at[2])
    place_copy.start()
    copies = []
    for k, (ref, side) in enumerate(((near_ref, 1 - core), (far_ref, core))):
        at = pl.ds(pl.multiple_of(side * GROUP, GROUP), GROUP)
        copies.append(
            pltpu.make_async_copy(features_ref.at[0, :, at], ref.at[pl.ds(0, CH)], sems.at[k])
        )
    for k, (src, dst) in enumerate(zip(inputs, outputs)):
        copies.append(pltpu.make_async_copy(src, dst, sems.at[3 + k]))
    for copy in copies:
        copy.start()
    place_copy.wait()
    low, high = slice(GROUP), slice(GROUP, 2 * GROUP)
    filler = jnp.zeros((5, GROUP), jnp.float32)
    for ref, one, two in ((near_ref, high, low), (far_ref, low, high)):
        rows = [
            jnp.where(core == 0, place_ref[axis, :, one], place_ref[axis, :, two]) for axis in range(3)
        ]
        ref[CH:, :] = jnp.concatenate(rows + [filler], axis=0)
    for copy in copies:
        copy.wait()


def live_flags(count, pair_target, pair_source):
    size = (4 * CELLS, pair_target.shape[1])
    at = lax.broadcasted_iota(jnp.int32, size, 0)
    slot = lax.broadcasted_iota(jnp.int32, size, 1)
    hit = (pair_target * CELLS + pair_source == at) & (slot < count)
    return jnp.max(jnp.where(hit, message_scale, 0.0), axis=1, keepdims=True)


def keep_row(flags, t, low, high):
    lane = lax.broadcasted_iota(jnp.int32, (1, GROUP), 1)
    one, two = (2 * t) * CELLS + low, (2 * t + 1) * CELLS + high
    return jnp.where(lane < CELL_ATOMS, flags[one : one + 1], flags[two : two + 1])


def set_group(scaled_ref, features, weight_t):
    for b in range(NB):
        scaled_ref[:, b * GROUP : (b + 1) * GROUP] = (features * weight_t[:, b : b + 1]).astype(
            jnp.bfloat16
        )


def set_cell(scaled_ref, features, half, weight_t):
    first = lax.broadcasted_iota(jnp.int32, (CH, GROUP), 1) < CELL_ATOMS
    turned = pltpu.roll(features, CELL_ATOMS, 1)
    twice = jnp.where(first, features, turned) if half == 0 else jnp.where(first, turned, features)
    for k in range(NB // 2):
        weights = jnp.where(first, weight_t[:, 2 * k : 2 * k + 1], weight_t[:, 2 * k + 1 : 2 * k + 2])
        scaled_ref[:, k * GROUP : (k + 1) * GROUP] = (twice * weights).astype(jnp.bfloat16)


def set_place(place_ref, slab):
    place = slab[CH:].T
    for axis in range(3):
        place_ref[axis] = jnp.broadcast_to(place[:, axis : axis + 1], (GROUP, GROUP))


def fill_steps(factor_ref, size, source_of, keeps, target, diagonal=False):
    def step(row):
        keep = jnp.broadcast_to(keeps[row // CELL_ATOMS], (ROWS, GROUP))
        if diagonal:
            row_at = lax.broadcasted_iota(jnp.int32, (ROWS, GROUP), 0)
            lane_at = lax.broadcasted_iota(jnp.int32, (ROWS, GROUP), 1)
            keep = jnp.where(row_at + row == lane_at, 0.0, keep)
        factor_rows(factor_ref, size, row, source_of(row), target, keep)

    return [functools.partial(step, row) for row in range(0, size, ROWS)]


def rows_of(place_ref, start):
    return lambda row: [place_ref[axis, start + row : start + row + ROWS, :] for axis in range(3)]


def merged_rows(low_ref, low_start, high_ref, high_start):
    low, high = rows_of(low_ref, low_start), rows_of(high_ref, high_start)

    def rows(row):
        first = lax.broadcasted_iota(jnp.int32, (ROWS, GROUP), 1) < CELL_ATOMS
        return [jnp.where(first, one, two) for one, two in zip(low(row), high(row))]

    return rows


def product_steps(scaled_ref, factor_ref, totals, merged=False):
    def step(k):
        width = min(WIDTH, NY * GROUP - k * WIDTH)
        product = jnp.dot(
            scaled_ref[...],
            factor_ref[:, k * WIDTH : k * WIDTH + width],
            preferred_element_type=jnp.float32,
        )
        if merged:
            lane = lax.broadcasted_iota(jnp.int32, (CH, width), 1) % GROUP
            product = jnp.where(lane < CELL_ATOMS, product[:CH], product[CH:])
        totals[k] = product if totals[k] is None else totals[k] + product

    return [functools.partial(step, k) for k in range(CHUNKS)]


def interleave(one, two):
    done = 0
    for k, step in enumerate(one):
        step()
        upto = (k + 1) * len(two) // len(one)
        for other in two[done:upto]:
            other()
        done = upto


def local_kernel(*refs):
    count_ref, pair_target_ref, pair_source_ref, radial_ref, near_ref, far_ref = refs[:6]
    later_in = refs[6 : 6 + LATER]
    group_factor_ref, cell_factor_ref, messages_ref, keep_ref, place_ref = refs[6 + LATER : 11 + LATER]
    later_out = refs[11 + LATER : 11 + 2 * LATER]
    group_ref, cell_ref, sems = refs[11 + 2 * LATER :]
    copies = [
        pltpu.make_async_copy(src, dst, sems.at[k]) for k, (src, dst) in enumerate(zip(later_in, later_out))
    ]
    for copy in copies:
        copy.start()
    even = lax.axis_index("space") % 2 == 0
    near, far = near_ref[...], far_ref[...]
    slabs = (jnp.where(even, far, near), jnp.where(even, near, far))
    targets = [[slab[CH + axis : CH + axis + 1] for axis in range(3)] for slab in slabs]
    flags = live_flags(count_ref[0, 0], pair_target_ref[...], pair_source_ref[...])
    weight_t = radial_ref[...].T
    for g in range(2):
        set_place(place_ref.at[g], slabs[g])
        set_group(group_ref.at[g], slabs[g][:CH], weight_t)
        set_cell(cell_ref.at[g], slabs[1 - g][:CH], g, weight_t)

    def fill_group(t):
        keeps = [keep_row(flags, t, cell, cell) for cell in (2 * t + 2, 2 * t + 3)]
        return fill_steps(
            group_factor_ref.at[t], GROUP, rows_of(place_ref.at[t], 0), keeps, targets[t], True
        )

    def fill_cell(t):
        cell = 4 - t
        source_of = rows_of(place_ref.at[1 - t], t * CELL_ATOMS)
        return fill_steps(
            cell_factor_ref.at[t], CELL_ATOMS, source_of, [keep_row(flags, t, cell, cell)], targets[t]
        )

    totals = [[None] * CHUNKS for _ in range(2)]
    for step in fill_cell(0):
        step()
    interleave(product_steps(cell_ref.at[0], cell_factor_ref.at[0], totals[0]), fill_group(0))
    interleave(product_steps(group_ref.at[0], group_factor_ref.at[0], totals[0]), fill_group(1))
    interleave(product_steps(group_ref.at[1], group_factor_ref.at[1], totals[1]), fill_cell(1))
    for step in product_steps(cell_ref.at[1], cell_factor_ref.at[1], totals[1]):
        step()
    for t in range(2):
        messages_ref[t] = jnp.concatenate(totals[t], axis=1)
    rows = [
        keep_row(flags, 0, 1, 1),
        keep_row(flags, 0, 0, 5),
        keep_row(flags, 1, 6, 6),
        keep_row(flags, 1, 2, 7),
    ]
    keep_ref[...] = jnp.concatenate(rows + [jnp.zeros((4, GROUP), jnp.float32)], axis=0)
    for copy in copies:
        copy.wait()


def node_kernel(
    scale,
    near_ref,
    far_ref,
    from_pair_ref,
    from_cross_ref,
    messages_ref,
    keep_ref,
    own_place_ref,
    energy_grad_ref,
    radial_ref,
    mix_ref,
    readout_ref,
    updated_ref,
    kept_ref,
    sent_ref,
    grad_messages_ref,
    cell_factor_ref,
    merged_factor_ref,
    cell_ref,
    merged_ref,
    place_ref,
):
    even = lax.axis_index("space") % 2 == 0
    weight_t = radial_ref[...].T
    near, far = near_ref[...], far_ref[...]
    from_pair, from_cross = from_pair_ref[...], from_cross_ref[...]
    slabs = (
        jnp.where(even, from_cross, from_pair),
        jnp.where(even, far, near),
        jnp.where(even, near, far),
        jnp.where(even, from_pair, from_cross),
    )
    targets = [[slab[CH + axis : CH + axis + 1] for axis in range(3)] for slab in slabs[1:3]]

    for t in range(2):
        set_place(place_ref.at[t], slabs[3 * t])
        set_cell(cell_ref.at[t], slabs[3 * t][:CH], 1 - t, weight_t)
        set_cell(merged_ref.at[t, pl.ds(0, CH)], slabs[t][:CH], 0, weight_t)
        set_cell(merged_ref.at[t, pl.ds(CH, CH)], slabs[t + 2][:CH], 1, weight_t)

    def fill_cell(t):
        source_of = rows_of(place_ref.at[t], (1 - t) * CELL_ATOMS)
        keeps = [keep_ref[2 * t : 2 * t + 1, :]]
        return fill_steps(cell_factor_ref.at[t], CELL_ATOMS, source_of, keeps, targets[t])

    def fill_merged(t):
        places = (place_ref.at[0], own_place_ref.at[0], own_place_ref.at[1], place_ref.at[1])
        source_of = merged_rows(places[t], 0, places[t + 2], CELL_ATOMS)
        keeps = [keep_ref[2 * t + 1 : 2 * t + 2, :]]
        return fill_steps(merged_factor_ref.at[t], CELL_ATOMS, source_of, keeps, targets[t])

    totals = [
        [messages_ref[t, :, k * WIDTH : min((k + 1) * WIDTH, NY * GROUP)] for k in range(CHUNKS)]
        for t in range(2)
    ]

    def add_cell(t):
        return product_steps(cell_ref.at[t], cell_factor_ref.at[t], totals[t])

    def add_merged(t):
        return product_steps(merged_ref.at[t], merged_factor_ref.at[t], totals[t], True)

    readout = jnp.broadcast_to(readout_ref[...], (8, CH)).T[:, :1]
    mix = mix_ref[...]
    mix_t = mix.astype(jnp.float32).T.astype(jnp.bfloat16)

    for step in fill_cell(0):
        step()
    interleave(add_cell(0), fill_merged(0))
    interleave(add_merged(0), fill_cell(1))
    interleave(add_cell(1), fill_merged(1))
    for step in add_merged(1):
        step()

    sides = [jnp.concatenate(total, axis=1) for total in totals]
    part = [
        jnp.concatenate([side[:, y * GROUP : (y + 1) * GROUP] for side in sides], axis=1)
        for y in range(NY)
    ]
    invariants = jnp.concatenate(
        [
            part[0],
            0.5 * (part[1] * part[1] + part[2] * part[2] + part[3] * part[3]),
            0.5
            * (
                part[4] * part[4]
                + part[5] * part[5]
                + part[6] * part[6]
                + part[7] * part[7]
                + part[8] * part[8]
            ),
        ],
        axis=0,
    ).astype(jnp.bfloat16)
    preact = jnp.dot(mix_t, invariants, preferred_element_type=jnp.float32)
    gating = jax.nn.sigmoid(preact)
    energy_grad = energy_grad_ref[...]
    spread = readout * energy_grad
    grad_pre = (spread * gating * (1.0 + preact * (1.0 - gating))).astype(jnp.bfloat16)
    grad_inv = jnp.dot(mix, grad_pre, preferred_element_type=jnp.float32)
    grad_mix = scale * lax.dot_general(
        invariants, grad_pre, (((1,), (1,)), ((), ())), preferred_element_type=jnp.float32
    )
    kept_ref[...] = jnp.where(even, grad_mix[:HALF], grad_mix[HALF:])
    sent_ref[...] = jnp.where(even, grad_mix[HALF:], grad_mix[:HALF])
    for y in range(NY):
        order = 0 if y == 0 else 1 if y < 4 else 2
        grad = grad_inv[order * CH : (order + 1) * CH]
        grad = (grad if y == 0 else grad * part[y]).astype(jnp.bfloat16)
        for t in range(2):
            grad_messages_ref[t, :, y * GROUP : (y + 1) * GROUP] = grad[:, t * GROUP : (t + 1) * GROUP]

    updated_ref[...] = jnp.concatenate([slabs[1][:CH], slabs[2][:CH]], axis=1) + preact * gating


def back(factor, grad_messages):
    return lax.dot_general(
        factor, grad_messages, (((1,), (1,)), ((), ())), preferred_element_type=jnp.float32
    )


def source_grads(total, features_t, weight):
    size = features_t.shape[0]
    grad_t = None
    radial = []
    for b in range(NB):
        piece = total[b * size : (b + 1) * size]
        term = piece * weight[b : b + 1, :]
        grad_t = term if grad_t is None else grad_t + term
        radial.append(jnp.sum(piece * features_t, axis=0, keepdims=True))
    return grad_t, jnp.concatenate(radial, axis=0)


def halo_back_kernel(
    cell_factor_ref,
    merged_factor_ref,
    grad_messages_ref,
    near_ref,
    far_ref,
    from_pair_ref,
    from_cross_ref,
    radial_ref,
    to_pair_ref,
    to_cross_ref,
    extra_ref,
    share_ref,
):
    even = lax.axis_index("space") % 2 == 0
    weight = radial_ref[...]
    near, far = near_ref[:CH, :], far_ref[:CH, :]
    from_pair, from_cross = from_pair_ref[:CH, :], from_cross_ref[:CH, :]
    features_t = [
        jnp.where(even, one, two).T
        for one, two in ((from_cross, from_pair), (far, near), (near, far), (from_pair, from_cross))
    ]
    first = lax.broadcasted_iota(jnp.int32, (CH, NY * GROUP), 1) % GROUP < CELL_ATOMS
    low, high = slice(CELL_ATOMS), slice(CELL_ATOMS, GROUP)
    share = None
    grads = {}
    for t in range(2):
        grad = grad_messages_ref[t]
        none = jnp.zeros_like(grad)
        both = jnp.concatenate([jnp.where(first, grad, none), jnp.where(first, none, grad)], axis=0)
        merged = back(merged_factor_ref[t], both)
        pieces = (
            (3 * t, 1 - t, back(cell_factor_ref[t], grad)),
            (t, 0, merged[:, :CH]),
            (t + 2, 1, merged[:, CH:]),
        )
        for g, half, total in pieces:
            grads[g, half], part = source_grads(total, features_t[g][(low, high)[half]], weight)
            share = part if share is None else share + part
    grad_before = jnp.concatenate([grads[0, 0], grads[0, 1]], axis=0).T
    grad_after = jnp.concatenate([grads[3, 0], grads[3, 1]], axis=0).T
    to_pair_ref[...] = jnp.where(even, grad_after, grad_before)
    to_cross_ref[...] = jnp.where(even, grad_before, grad_after)
    extra_ref[low, :] = grads[1, 0]
    extra_ref[high, :] = grads[2, 1]
    share_ref[...] = share


def own_back_kernel(
    scale,
    group_factor_ref,
    cell_factor_ref,
    grad_messages_ref,
    near_ref,
    far_ref,
    radial_ref,
    extra_ref,
    share_ref,
    updated_ref,
    species_ref,
    shift_ref,
    energy_grad_ref,
    readout_ref,
    own_grad_ref,
    joined_ref,
    energy_ref,
):
    even = lax.axis_index("space") % 2 == 0
    weight = radial_ref[...]
    near, far = near_ref[:CH, :], far_ref[:CH, :]
    share = share_ref[...]
    low, high = slice(CELL_ATOMS), slice(CELL_ATOMS, GROUP)
    readout = jnp.broadcast_to(readout_ref[...], (8, CH)).T[:, :1]
    updated, energy_grad, kinds = updated_ref[...], energy_grad_ref[...], species_ref[...]
    spread = readout * energy_grad
    shifts = jnp.zeros((1, 2 * GROUP), jnp.float32)
    for n in range(NSPEC):
        shifts = jnp.where(kinds == n, shift_ref[:, n : n + 1], shifts)
    energy_ref[...] = jnp.sum(updated * readout, axis=0, keepdims=True) + shifts
    readout_row = column_to_row(jnp.sum(updated * energy_grad, axis=1, keepdims=True), CH)
    here = lax.broadcasted_iota(jnp.int32, (NSPEC, 2 * GROUP), 0) == kinds
    by_kind = jnp.sum(jnp.where(here, energy_grad, 0.0), axis=1, keepdims=True)
    for t, features in enumerate((jnp.where(even, far, near), jnp.where(even, near, far))):
        features_t = features.T
        total = back(group_factor_ref[t], grad_messages_ref[t])
        grad, part = source_grads(total, features_t, weight)
        inner, outer = (high, low) if t == 0 else (low, high)
        total = back(cell_factor_ref[1 - t], grad_messages_ref[1 - t])
        one, more = source_grads(total, features_t[inner], weight)
        two = extra_ref[outer, :]
        grad = (grad + jnp.concatenate([two, one] if t == 0 else [one, two], axis=0)).T
        at = slice(t * GROUP, (t + 1) * GROUP)
        own_grad_ref[:, at] = spread[:, at] + grad
        share = share + part + more
    joined_ref[:NB, :] = share * scale
    rest = [readout_row, column_to_row(by_kind, NSPEC), jnp.zeros((6, CH), jnp.float32)]
    joined_ref[NB:, :] = jnp.concatenate(rest, axis=0) * scale


def quarter_kernel(kept_ref, received_ref, keep_ref, send_ref):
    first = first_of_pair()
    low = kept_ref[:QUARTER, :] + received_ref[:QUARTER, :]
    high = kept_ref[QUARTER:, :] + received_ref[QUARTER:, :]
    keep_ref[...] = jnp.where(first, low, high)
    send_ref[...] = jnp.where(first, high, low)


def join_kernel(kept_ref, received_ref, rest_ref, out_ref):
    out_ref[:QUARTER, :] = kept_ref[...] + received_ref[...]
    out_ref[QUARTER:, :] = rest_ref[...]


def gather_kernel(mine_ref, along_ref, other_ref, both_ref, out_ref):
    first = first_of_pair()
    at, rest = slice(QUARTER), slice(QUARTER, QUARTER + REST)
    mine = mine_ref[at, :] + along_ref[at, :]
    other = other_ref[at, :] + both_ref[at, :]
    out_ref[:QUARTER, :] = jnp.where(first, mine, other)
    out_ref[QUARTER:HALF, :] = jnp.where(first, other, mine)
    out_ref[HALF:, :] = (mine_ref[rest, :] + along_ref[rest, :]) + (other_ref[rest, :] + both_ref[rest, :])


def fold_kernel(own_ref, from_pair_ref, from_cross_ref, energy_in_ref, grad_ref, energy_ref):
    even = lax.axis_index("space") % 2 == 0
    pair = from_pair_ref[...]
    cross = from_cross_ref[...]
    grad_ref[0, :, :GROUP] = own_ref[:, :GROUP] + jnp.where(even, cross, pair)
    grad_ref[0, :, GROUP:] = own_ref[:, GROUP:] + jnp.where(even, pair, cross)
    energy_ref[...] = energy_in_ref[...]


def finish_kernel(mine_ref, other_ref, radial_ref, mix_ref, readout_ref, shift_ref):
    even = lax.axis_index("space") % 2 == 0
    mine, other = mine_ref[:HALF, :], other_ref[:HALF, :]
    mix_ref[:HALF, :] = jnp.where(even, mine, other)
    mix_ref[HALF:, :] = jnp.where(even, other, mine)
    rest = mine_ref[HALF:, :] + other_ref[HALF:, :]
    radial_ref[...] = rest[:NB]
    readout_ref[...] = rest[NB : NB + 1]
    shift_ref[...] = rest[NB + 1 : NB + 2, :NSPEC]


def first_of_pair():
    space, dp = lax.axis_index("space"), lax.axis_index("dp")
    return jnp.where(space % 2 == 0, dp, space // 2) % 2 == 0


def exchange_routes(space, dp):
    along = [(0, 1 << k) for k in range(dp.bit_length() - 1)]
    across = [(1 << k, 0) for k in range(1, space.bit_length() - 1)]
    shared = (along[0], across[0])
    orders = (across + along[1:], along[:1] + across[1:] + along[1:])
    orders = tuple(order[:-2] + order[:-3:-1] for order in orders)
    count = len(orders[0])

    def route(*places):
        moves = []
        for s in range(space):
            step = [shared[s % 2] if k < 0 else orders[s % 2][k] for k in places]
            for d in range(dp):
                to_s, to_d = s, d
                for one, two in step:
                    to_s, to_d = to_s ^ one, to_d ^ two
                moves.append((s * dp + d, to_s * dp + to_d))
        return moves

    rounds = []
    for k in range(0, count - 1, 2):
        if k + 1 < count - 1:
            rounds.append([route(k), route(k + 1), route(k, k + 1)])
        else:
            rounds.append([route(k)])
    last = count - 1
    rounds.append([route(last), route(-1), route(last, -1)])
    return route(-1), rounds


def call(kernel, name, inputs, outputs, mib=4, scratch=(), flops=0):
    vmem = pl.BlockSpec(memory_space=pltpu.VMEM)
    shapes = tuple(jax.ShapeDtypeStruct(shape, kind) for shape, kind in outputs)
    moved = sum(math.prod(v.shape) * v.dtype.itemsize for v in (*inputs, *shapes))
    return pl.pallas_call(
        kernel,
        out_shape=shapes,
        in_specs=[vmem] * len(inputs),
        out_specs=(vmem,) * len(shapes),
        scratch_shapes=scratch,
        compiler_params=pltpu.CompilerParams(vmem_limit_bytes=mib * 1024 * 1024),
        cost_estimate=pl.CostEstimate(flops=flops, bytes_accessed=moved, transcendentals=0),
        name=name,
    )(*inputs)


def in_hbm(value):
    return pltpu.with_memory_space_constraint(value, pltpu.HBM)


def body(
    node_features,
    positions,
    species,
    energy_cotangent,
    pair_target,
    pair_source,
    pair_count,
    radial_weight,
    mix_weight,
    readout_weight,
    species_shift,
):
    atoms_here = node_features.shape[2]
    space, dp = lax.axis_size("space"), lax.axis_size("dp")
    scale = 1.0 / math.sqrt(atoms_here * space * dp)
    pair = [(i, i ^ 1) for i in range(space)]
    cross = [(i, ((i + 1) ^ 1) - 1) for i in range(1, space - 1)]
    hbm = pl.BlockSpec(memory_space=pltpu.HBM)
    smem = pl.BlockSpec(memory_space=pltpu.SMEM)
    vmem = pl.BlockSpec(memory_space=pltpu.VMEM)
    f32, bf16 = jnp.float32, jnp.bfloat16
    small = (pair_target, pair_source, radial_weight)
    later = (
        species,
        species_shift.reshape(1, NSPEC),
        energy_cotangent,
        mix_weight,
        readout_weight.reshape(1, CH),
    )
    near, far, *small = pl.pallas_call(
        split_kernel,
        out_shape=(jax.ShapeDtypeStruct((SLAB_ROWS, GROUP), f32),) * 2
        + tuple(jax.ShapeDtypeStruct(v.shape, v.dtype) for v in small),
        in_specs=[hbm] * (SMALL + 2),
        out_specs=(vmem,) * (SMALL + 2),
        scratch_shapes=[
            pltpu.VMEM((3, 1, atoms_here), f32),
            pltpu.SemaphoreType.DMA((SMALL + 3,)),
        ],
        compiler_params=pltpu.CompilerParams(vmem_limit_bytes=4 * 1024 * 1024),
        name="split",
    )(
        in_hbm(node_features),
        in_hbm(jnp.transpose(positions, (1, 0, 2))),
        *[in_hbm(v) for v in small],
    )
    targets, sources, radial = small
    from_cross = lax.ppermute(far, "space", cross)
    from_pair = lax.ppermute(near, "space", pair)

    block_flops = 2 * CH * NB * NY * GROUP * GROUP
    group_factor, cell_factor, messages, keep, place, *later = pl.pallas_call(
        local_kernel,
        out_shape=(
            jax.ShapeDtypeStruct((2, NB * GROUP, NY * GROUP), bf16),
            jax.ShapeDtypeStruct((2, NB * CELL_ATOMS, NY * GROUP), bf16),
            jax.ShapeDtypeStruct((2, CH, NY * GROUP), f32),
            jax.ShapeDtypeStruct((8, GROUP), f32),
            jax.ShapeDtypeStruct((2, 3, GROUP, GROUP), f32),
            *[jax.ShapeDtypeStruct(v.shape, v.dtype) for v in later],
        ),
        in_specs=[smem] + [vmem] * 5 + [hbm] * LATER,
        out_specs=(vmem,) * (5 + LATER),
        scratch_shapes=[
            pltpu.VMEM((2, CH, NB * GROUP), bf16),
            pltpu.VMEM((2, CH, NB * CELL_ATOMS), bf16),
            pltpu.SemaphoreType.DMA((LATER,)),
        ],
        compiler_params=pltpu.CompilerParams(vmem_limit_bytes=16 * 1024 * 1024),
        cost_estimate=pl.CostEstimate(
            flops=3 * block_flops, bytes_accessed=11_000_000, transcendentals=0
        ),
        name="local_pairs",
    )(pair_count, targets, sources, radial, near, far, *[in_hbm(v) for v in later])
    species, shift, energy_grad, mix, readout = later

    updated, kept, sent, grad_messages, halo_factor, merged_factor = call(
        functools.partial(node_kernel, scale),
        "node_stage",
        (
            near,
            far,
            from_pair,
            from_cross,
            messages,
            keep,
            place,
            energy_grad,
            radial,
            mix,
            readout,
        ),
        (
            ((CH, atoms_here), f32),
            ((HALF, CH), f32),
            ((HALF, CH), f32),
            ((2, CH, NY * GROUP), bf16),
            ((2, NB * CELL_ATOMS, NY * GROUP), bf16),
            ((2, NB * CELL_ATOMS, NY * GROUP), bf16),
        ),
        16,
        [
            pltpu.VMEM((2, CH, NB * CELL_ATOMS), bf16),
            pltpu.VMEM((2, 2 * CH, NB * CELL_ATOMS), bf16),
            pltpu.VMEM((2, 3, GROUP, GROUP), f32),
        ],
        2 * block_flops,
    )

    received = lax.ppermute(sent, "space", pair)
    pair_grad, cross_grad, extra, share = call(
        halo_back_kernel,
        "halo_back",
        (
            halo_factor,
            merged_factor,
            grad_messages,
            near,
            far,
            from_pair,
            from_cross,
            radial,
        ),
        (((CH, GROUP), f32), ((CH, GROUP), f32), ((GROUP, CH), f32), ((NB, CH), f32)),
        12,
        (),
        2 * block_flops,
    )
    received, share = lax.optimization_barrier((received, share))
    quarter, sent = call(
        quarter_kernel,
        "quarter",
        (kept, received),
        (((QUARTER, CH), f32), ((QUARTER, CH), f32)),
    )
    sharing, (*rounds, last) = exchange_routes(space, dp)
    everyone = ("space", "dp")
    sent, grad_messages, pair_grad = lax.optimization_barrier((sent, grad_messages, pair_grad))
    received = lax.ppermute(sent, everyone, sharing)
    from_pair = lax.ppermute(pair_grad, "space", pair)
    own_grad, joined, energy = call(
        functools.partial(own_back_kernel, scale),
        "own_back",
        (
            group_factor,
            cell_factor,
            grad_messages,
            near,
            far,
            radial,
            extra,
            share,
            updated,
            species,
            shift,
            energy_grad,
            readout,
        ),
        (((CH, atoms_here), f32), ((REST, CH), f32), ((1, atoms_here), f32)),
        12,
        (),
        3 * block_flops,
    )
    (value,) = call(
        join_kernel, "join", (quarter, received, joined), (((QUARTER + REST, CH), f32),)
    )
    value, from_pair, cross_grad = lax.optimization_barrier((value, from_pair, cross_grad))
    for turn, routes in enumerate(rounds):
        arrived = [lax.ppermute(value, everyone, route) for route in routes]
        if turn == 0:
            from_cross = lax.ppermute(cross_grad, "space", cross)
        value = value + arrived[0]
        if len(arrived) == 3:
            value = value + (arrived[1] + arrived[2])
    arrived = [lax.ppermute(value, everyone, route) for route in last]
    value, from_cross, *arrived = lax.optimization_barrier((value, from_cross, *arrived))
    (value,) = call(
        gather_kernel,
        "gather",
        (value, *arrived),
        (((HALF + REST, CH), f32),),
    )
    feature_grad, energy = call(
        fold_kernel,
        "fold",
        (own_grad, from_pair, from_cross, energy),
        (((1, CH, atoms_here), f32), ((1, atoms_here), f32)),
    )
    radial_grad, mix_grad, readout_grad, shift_grad = call(
        finish_kernel,
        "finish",
        (value, lax.ppermute(value, "space", pair)),
        (((NB, CH), f32), ((MIX_ROWS, CH), f32), ((1, CH), f32), ((1, NSPEC), f32)),
    )
    return (
        energy,
        feature_grad,
        radial_grad,
        mix_grad,
        readout_grad.reshape(CH),
        shift_grad.reshape(NSPEC),
    )


def solution(mesh):
    return jax.shard_map(
        body,
        mesh=mesh,
        in_specs=(
            P("dp", None, "space"),
            P("dp", None, "space"),
            P("dp", "space"),
            P("dp", "space"),
            P("dp", "space"),
            P("dp", "space"),
            P("dp", "space"),
            P(),
            P(),
            P(),
            P(),
        ),
        out_specs=(P("dp", "space"), P("dp", None, "space"), P(), P(), P(), P()),
        check_vma=False,
    )
```

```python
import functools
import math

import jax
import jax.numpy as jnp
from jax import lax
from jax.experimental import pallas as pl
from jax.experimental.pallas import tpu as pltpu
from jax.sharding import PartitionSpec as P

CH = 128
NB = 8
NY = 9
NSPEC = 8
CELL_ATOMS = 64
HALO_CELLS = 2
GROUP = 2 * CELL_ATOMS
ROWS = 16
WIDTH = 256
CHUNKS = -(-NY * GROUP // WIDTH)

cutoff = 5.0
message_scale = 0.25

COS_COEFFS = (
    0.9999999889445765,
    -4.93480111664404,
    4.058694745521682,
    -1.3351580223048074,
    0.2350290226247885,
    -0.025358285754444005,
    0.0015936782135993002,
)
SINC_COEFFS = (
    0.9999999992502204,
    -1.6449339933418936,
    0.8117412468909989,
    -0.1907447263221115,
    0.02612742969685046,
    -0.0023157632409761065,
    0.00012580778956459784,
)

MIX_ROWS = 3 * CH
HALF = MIX_ROWS // 2
QUARTER = MIX_ROWS // 4
REST = 16
CELLS = 4 + 2 * HALO_CELLS
SMALL = 3
LATER = 5
SLAB_ROWS = CH + 8


def polynomial(coeffs, x, x2, x4):
    low = (coeffs[0] + coeffs[1] * x) + (coeffs[2] + coeffs[3] * x) * x2
    return low + ((coeffs[4] + coeffs[5] * x) + coeffs[6] * x2) * x4


def factor_rows(factor_ref, size, row, source, target, keep):
    dx = (target[0] - source[0]) * (1.0 / cutoff)
    dy = (target[1] - source[1]) * (1.0 / cutoff)
    dz = (target[2] - source[2]) * (1.0 / cutoff)
    xx, yy, zz = dx * dx, dy * dy, dz * dz
    square = xx + yy + zz
    inside = jnp.minimum(square, 1.0)
    gap = 1.0 - inside
    inside2 = inside * inside
    inside4 = inside2 * inside2
    base = (gap * gap) * keep * polynomial(SINC_COEFFS, inside, inside2, inside4)
    twice_cos = polynomial([2.0 * c for c in COS_COEFFS], inside, inside2, inside4)
    twice_cos2 = twice_cos * twice_cos - 2.0
    raw = [base, twice_cos * base]
    raw += [twice_cos2 * base + base, twice_cos2 * raw[1]]
    for b in range(4, NB):
        raw.append(twice_cos2 * raw[b - 2] - raw[b - 4])
    radial = [value if b == 0 else value * (1.0 / (b + 1)) for b, value in enumerate(raw)]
    root_three = math.sqrt(3.0)
    root_fifteen = math.sqrt(15.0)
    root_five = math.sqrt(5.0)
    wide_x = root_fifteen * dx
    harmonic = [
        None,
        root_three * dx,
        root_three * dy,
        root_three * dz,
        wide_x * dy,
        (root_fifteen * dy) * dz,
        (0.5 * root_five) * (3.0 * zz - square),
        wide_x * dz,
        (0.5 * root_fifteen) * (xx - yy),
    ]
    for b in range(NB):
        rows = slice(b * size + row, b * size + row + ROWS)
        for y in range(NY):
            value = radial[b] if y == 0 else radial[b] * harmonic[y]
            factor_ref[rows, y * GROUP : (y + 1) * GROUP] = value.astype(jnp.bfloat16)


def column_to_row(column, size):
    wide = jnp.broadcast_to(column, (size, GROUP))
    at = lax.broadcasted_iota(jnp.int32, (size, GROUP), 0)
    lane = lax.broadcasted_iota(jnp.int32, (size, GROUP), 1)
    return jnp.sum(jnp.where(at == lane, wide, 0.0), axis=0, keepdims=True)


def split_kernel(*refs):
    features_ref, place_in_ref, *inputs = refs[: SMALL + 2]
    near_ref, far_ref, *outputs = refs[SMALL + 2 : 2 * SMALL + 4]
    place_ref, sems = refs[2 * SMALL + 4 :]
    core = lax.axis_index("space") % 2
    place_copy = pltpu.make_async_copy(place_in_ref, place_ref, sems.at[2])
    place_copy.start()
    copies = []
    for k, (ref, side) in enumerate(((near_ref, 1 - core), (far_ref, core))):
        at = pl.ds(pl.multiple_of(side * GROUP, GROUP), GROUP)
        copies.append(
            pltpu.make_async_copy(features_ref.at[0, :, at], ref.at[pl.ds(0, CH)], sems.at[k])
        )
    for k, (src, dst) in enumerate(zip(inputs, outputs)):
        copies.append(pltpu.make_async_copy(src, dst, sems.at[3 + k]))
    for copy in copies:
        copy.start()
    place_copy.wait()
    low, high = slice(GROUP), slice(GROUP, 2 * GROUP)
    filler = jnp.zeros((5, GROUP), jnp.float32)
    for ref, one, two in ((near_ref, high, low), (far_ref, low, high)):
        rows = [
            jnp.where(core == 0, place_ref[axis, :, one], place_ref[axis, :, two]) for axis in range(3)
        ]
        ref[CH:, :] = jnp.concatenate(rows + [filler], axis=0)
    for copy in copies:
        copy.wait()


def live_flags(count, pair_target, pair_source):
    size = (4 * CELLS, pair_target.shape[1])
    at = lax.broadcasted_iota(jnp.int32, size, 0)
    slot = lax.broadcasted_iota(jnp.int32, size, 1)
    hit = (pair_target * CELLS + pair_source == at) & (slot < count)
    return jnp.max(jnp.where(hit, message_scale, 0.0), axis=1, keepdims=True)


def keep_row(flags, t, low, high):
    lane = lax.broadcasted_iota(jnp.int32, (1, GROUP), 1)
    one, two = (2 * t) * CELLS + low, (2 * t + 1) * CELLS + high
    return jnp.where(lane < CELL_ATOMS, flags[one : one + 1], flags[two : two + 1])


def set_group(scaled_ref, features, weight_t):
    for b in range(NB):
        scaled_ref[:, b * GROUP : (b + 1) * GROUP] = (features * weight_t[:, b : b + 1]).astype(
            jnp.bfloat16
        )


def set_cell(scaled_ref, features, half, weight_t):
    first = lax.broadcasted_iota(jnp.int32, (CH, GROUP), 1) < CELL_ATOMS
    turned = pltpu.roll(features, CELL_ATOMS, 1)
    twice = jnp.where(first, features, turned) if half == 0 else jnp.where(first, turned, features)
    for k in range(NB // 2):
        weights = jnp.where(first, weight_t[:, 2 * k : 2 * k + 1], weight_t[:, 2 * k + 1 : 2 * k + 2])
        scaled_ref[:, k * GROUP : (k + 1) * GROUP] = (twice * weights).astype(jnp.bfloat16)


def set_place(place_ref, slab):
    place = slab[CH:].T
    for axis in range(3):
        place_ref[axis] = jnp.broadcast_to(place[:, axis : axis + 1], (GROUP, GROUP))


def fill_steps(factor_ref, size, source_of, keeps, target, diagonal=False):
    def step(row):
        keep = jnp.broadcast_to(keeps[row // CELL_ATOMS], (ROWS, GROUP))
        if diagonal:
            row_at = lax.broadcasted_iota(jnp.int32, (ROWS, GROUP), 0)
            lane_at = lax.broadcasted_iota(jnp.int32, (ROWS, GROUP), 1)
            keep = jnp.where(row_at + row == lane_at, 0.0, keep)
        factor_rows(factor_ref, size, row, source_of(row), target, keep)

    return [functools.partial(step, row) for row in range(0, size, ROWS)]


def rows_of(place_ref, start):
    return lambda row: [place_ref[axis, start + row : start + row + ROWS, :] for axis in range(3)]


def merged_rows(low_ref, low_start, high_ref, high_start):
    low, high = rows_of(low_ref, low_start), rows_of(high_ref, high_start)

    def rows(row):
        first = lax.broadcasted_iota(jnp.int32, (ROWS, GROUP), 1) < CELL_ATOMS
        return [jnp.where(first, one, two) for one, two in zip(low(row), high(row))]

    return rows


def product_steps(scaled_ref, factor_ref, totals, merged=False):
    def step(k):
        width = min(WIDTH, NY * GROUP - k * WIDTH)
        product = jnp.dot(
            scaled_ref[...],
            factor_ref[:, k * WIDTH : k * WIDTH + width],
            preferred_element_type=jnp.float32,
        )
        if merged:
            lane = lax.broadcasted_iota(jnp.int32, (CH, width), 1) % GROUP
            product = jnp.where(lane < CELL_ATOMS, product[:CH], product[CH:])
        totals[k] = product if totals[k] is None else totals[k] + product

    return [functools.partial(step, k) for k in range(CHUNKS)]


def interleave(one, two):
    done = 0
    for k, step in enumerate(one):
        step()
        upto = (k + 1) * len(two) // len(one)
        for other in two[done:upto]:
            other()
        done = upto


def local_kernel(*refs):
    count_ref, pair_target_ref, pair_source_ref, radial_ref, near_ref, far_ref = refs[:6]
    later_in = refs[6 : 6 + LATER]
    group_factor_ref, cell_factor_ref, messages_ref, keep_ref, place_ref = refs[6 + LATER : 11 + LATER]
    later_out = refs[11 + LATER : 11 + 2 * LATER]
    group_ref, cell_ref, sems = refs[11 + 2 * LATER :]
    copies = [
        pltpu.make_async_copy(src, dst, sems.at[k]) for k, (src, dst) in enumerate(zip(later_in, later_out))
    ]
    for copy in copies:
        copy.start()
    even = lax.axis_index("space") % 2 == 0
    near, far = near_ref[...], far_ref[...]
    slabs = (jnp.where(even, far, near), jnp.where(even, near, far))
    targets = [[slab[CH + axis : CH + axis + 1] for axis in range(3)] for slab in slabs]
    flags = live_flags(count_ref[0, 0], pair_target_ref[...], pair_source_ref[...])
    weight_t = radial_ref[...].T
    for g in range(2):
        set_place(place_ref.at[g], slabs[g])
        set_group(group_ref.at[g], slabs[g][:CH], weight_t)
        set_cell(cell_ref.at[g], slabs[1 - g][:CH], g, weight_t)

    def fill_group(t):
        keeps = [keep_row(flags, t, cell, cell) for cell in (2 * t + 2, 2 * t + 3)]
        return fill_steps(
            group_factor_ref.at[t], GROUP, rows_of(place_ref.at[t], 0), keeps, targets[t], True
        )

    def fill_cell(t):
        cell = 4 - t
        source_of = rows_of(place_ref.at[1 - t], t * CELL_ATOMS)
        return fill_steps(
            cell_factor_ref.at[t], CELL_ATOMS, source_of, [keep_row(flags, t, cell, cell)], targets[t]
        )

    totals = [[None] * CHUNKS for _ in range(2)]
    for step in fill_cell(0):
        step()
    interleave(product_steps(cell_ref.at[0], cell_factor_ref.at[0], totals[0]), fill_group(0))
    interleave(product_steps(group_ref.at[0], group_factor_ref.at[0], totals[0]), fill_group(1))
    interleave(product_steps(group_ref.at[1], group_factor_ref.at[1], totals[1]), fill_cell(1))
    for step in product_steps(cell_ref.at[1], cell_factor_ref.at[1], totals[1]):
        step()
    for t in range(2):
        messages_ref[t] = jnp.concatenate(totals[t], axis=1)
    rows = [
        keep_row(flags, 0, 1, 1),
        keep_row(flags, 0, 0, 5),
        keep_row(flags, 1, 6, 6),
        keep_row(flags, 1, 2, 7),
    ]
    keep_ref[...] = jnp.concatenate(rows + [jnp.zeros((4, GROUP), jnp.float32)], axis=0)
    for copy in copies:
        copy.wait()


def node_kernel(
    scale,
    near_ref,
    far_ref,
    from_pair_ref,
    from_cross_ref,
    messages_ref,
    keep_ref,
    own_place_ref,
    energy_grad_ref,
    radial_ref,
    mix_ref,
    readout_ref,
    updated_ref,
    kept_ref,
    sent_ref,
    grad_messages_ref,
    cell_factor_ref,
    merged_factor_ref,
    cell_ref,
    merged_ref,
    place_ref,
):
    even = lax.axis_index("space") % 2 == 0
    weight_t = radial_ref[...].T
    near, far = near_ref[...], far_ref[...]
    from_pair, from_cross = from_pair_ref[...], from_cross_ref[...]
    slabs = (
        jnp.where(even, from_cross, from_pair),
        jnp.where(even, far, near),
        jnp.where(even, near, far),
        jnp.where(even, from_pair, from_cross),
    )
    targets = [[slab[CH + axis : CH + axis + 1] for axis in range(3)] for slab in slabs[1:3]]

    for t in range(2):
        set_place(place_ref.at[t], slabs[3 * t])
        set_cell(cell_ref.at[t], slabs[3 * t][:CH], 1 - t, weight_t)
        set_cell(merged_ref.at[t, pl.ds(0, CH)], slabs[t][:CH], 0, weight_t)
        set_cell(merged_ref.at[t, pl.ds(CH, CH)], slabs[t + 2][:CH], 1, weight_t)

    def fill_cell(t):
        source_of = rows_of(place_ref.at[t], (1 - t) * CELL_ATOMS)
        keeps = [keep_ref[2 * t : 2 * t + 1, :]]
        return fill_steps(cell_factor_ref.at[t], CELL_ATOMS, source_of, keeps, targets[t])

    def fill_merged(t):
        places = (place_ref.at[0], own_place_ref.at[0], own_place_ref.at[1], place_ref.at[1])
        source_of = merged_rows(places[t], 0, places[t + 2], CELL_ATOMS)
        keeps = [keep_ref[2 * t + 1 : 2 * t + 2, :]]
        return fill_steps(merged_factor_ref.at[t], CELL_ATOMS, source_of, keeps, targets[t])

    totals = [
        [messages_ref[t, :, k * WIDTH : min((k + 1) * WIDTH, NY * GROUP)] for k in range(CHUNKS)]
        for t in range(2)
    ]

    def add_cell(t):
        return product_steps(cell_ref.at[t], cell_factor_ref.at[t], totals[t])

    def add_merged(t):
        return product_steps(merged_ref.at[t], merged_factor_ref.at[t], totals[t], True)

    readout = jnp.broadcast_to(readout_ref[...], (8, CH)).T[:, :1]
    mix = mix_ref[...]
    mix_t = mix.astype(jnp.float32).T.astype(jnp.bfloat16)

    for step in fill_cell(0):
        step()
    interleave(add_cell(0), fill_merged(0))
    interleave(add_merged(0), fill_cell(1))
    interleave(add_cell(1), fill_merged(1))
    for step in add_merged(1):
        step()

    sides = [jnp.concatenate(total, axis=1) for total in totals]
    part = [
        jnp.concatenate([side[:, y * GROUP : (y + 1) * GROUP] for side in sides], axis=1)
        for y in range(NY)
    ]
    invariants = jnp.concatenate(
        [
            part[0],
            0.5 * (part[1] * part[1] + part[2] * part[2] + part[3] * part[3]),
            0.5
            * (
                part[4] * part[4]
                + part[5] * part[5]
                + part[6] * part[6]
                + part[7] * part[7]
                + part[8] * part[8]
            ),
        ],
        axis=0,
    ).astype(jnp.bfloat16)
    preact = jnp.dot(mix_t, invariants, preferred_element_type=jnp.float32)
    gating = jax.nn.sigmoid(preact)
    energy_grad = energy_grad_ref[...]
    spread = readout * energy_grad
    grad_pre = (spread * gating * (1.0 + preact * (1.0 - gating))).astype(jnp.bfloat16)
    grad_inv = jnp.dot(mix, grad_pre, preferred_element_type=jnp.float32)
    grad_mix = scale * lax.dot_general(
        invariants, grad_pre, (((1,), (1,)), ((), ())), preferred_element_type=jnp.float32
    )
    kept_ref[...] = jnp.where(even, grad_mix[:HALF], grad_mix[HALF:])
    sent_ref[...] = jnp.where(even, grad_mix[HALF:], grad_mix[:HALF])
    for y in range(NY):
        order = 0 if y == 0 else 1 if y < 4 else 2
        grad = grad_inv[order * CH : (order + 1) * CH]
        grad = (grad if y == 0 else grad * part[y]).astype(jnp.bfloat16)
        for t in range(2):
            grad_messages_ref[t, :, y * GROUP : (y + 1) * GROUP] = grad[:, t * GROUP : (t + 1) * GROUP]

    updated_ref[...] = jnp.concatenate([slabs[1][:CH], slabs[2][:CH]], axis=1) + preact * gating


def back(factor, grad_messages):
    return lax.dot_general(
        factor, grad_messages, (((1,), (1,)), ((), ())), preferred_element_type=jnp.float32
    )


def source_grads(total, features_t, weight):
    size = features_t.shape[0]
    grad_t = None
    radial = []
    for b in range(NB):
        piece = total[b * size : (b + 1) * size]
        term = piece * weight[b : b + 1, :]
        grad_t = term if grad_t is None else grad_t + term
        radial.append(jnp.sum(piece * features_t, axis=0, keepdims=True))
    return grad_t, jnp.concatenate(radial, axis=0)


def halo_back_kernel(
    cell_factor_ref,
    merged_factor_ref,
    grad_messages_ref,
    near_ref,
    far_ref,
    from_pair_ref,
    from_cross_ref,
    radial_ref,
    to_pair_ref,
    to_cross_ref,
    extra_ref,
    share_ref,
):
    even = lax.axis_index("space") % 2 == 0
    weight = radial_ref[...]
    near, far = near_ref[:CH, :], far_ref[:CH, :]
    from_pair, from_cross = from_pair_ref[:CH, :], from_cross_ref[:CH, :]
    features_t = [
        jnp.where(even, one, two).T
        for one, two in ((from_cross, from_pair), (far, near), (near, far), (from_pair, from_cross))
    ]
    first = lax.broadcasted_iota(jnp.int32, (CH, NY * GROUP), 1) % GROUP < CELL_ATOMS
    low, high = slice(CELL_ATOMS), slice(CELL_ATOMS, GROUP)
    share = None
    grads = {}
    for t in range(2):
        grad = grad_messages_ref[t]
        none = jnp.zeros_like(grad)
        both = jnp.concatenate([jnp.where(first, grad, none), jnp.where(first, none, grad)], axis=0)
        merged = back(merged_factor_ref[t], both)
        pieces = (
            (3 * t, 1 - t, back(cell_factor_ref[t], grad)),
            (t, 0, merged[:, :CH]),
            (t + 2, 1, merged[:, CH:]),
        )
        for g, half, total in pieces:
            grads[g, half], part = source_grads(total, features_t[g][(low, high)[half]], weight)
            share = part if share is None else share + part
    grad_before = jnp.concatenate([grads[0, 0], grads[0, 1]], axis=0).T
    grad_after = jnp.concatenate([grads[3, 0], grads[3, 1]], axis=0).T
    to_pair_ref[...] = jnp.where(even, grad_after, grad_before)
    to_cross_ref[...] = jnp.where(even, grad_before, grad_after)
    extra_ref[low, :] = grads[1, 0]
    extra_ref[high, :] = grads[2, 1]
    share_ref[...] = share


def own_back_kernel(
    scale,
    group_factor_ref,
    cell_factor_ref,
    grad_messages_ref,
    near_ref,
    far_ref,
    radial_ref,
    extra_ref,
    share_ref,
    updated_ref,
    species_ref,
    shift_ref,
    energy_grad_ref,
    readout_ref,
    own_grad_ref,
    joined_ref,
    energy_ref,
):
    even = lax.axis_index("space") % 2 == 0
    weight = radial_ref[...]
    near, far = near_ref[:CH, :], far_ref[:CH, :]
    share = share_ref[...]
    low, high = slice(CELL_ATOMS), slice(CELL_ATOMS, GROUP)
    readout = jnp.broadcast_to(readout_ref[...], (8, CH)).T[:, :1]
    updated, energy_grad, kinds = updated_ref[...], energy_grad_ref[...], species_ref[...]
    spread = readout * energy_grad
    shifts = jnp.zeros((1, 2 * GROUP), jnp.float32)
    for n in range(NSPEC):
        shifts = jnp.where(kinds == n, shift_ref[:, n : n + 1], shifts)
    energy_ref[...] = jnp.sum(updated * readout, axis=0, keepdims=True) + shifts
    readout_row = column_to_row(jnp.sum(updated * energy_grad, axis=1, keepdims=True), CH)
    here = lax.broadcasted_iota(jnp.int32, (NSPEC, 2 * GROUP), 0) == kinds
    by_kind = jnp.sum(jnp.where(here, energy_grad, 0.0), axis=1, keepdims=True)
    for t, features in enumerate((jnp.where(even, far, near), jnp.where(even, near, far))):
        features_t = features.T
        total = back(group_factor_ref[t], grad_messages_ref[t])
        grad, part = source_grads(total, features_t, weight)
        inner, outer = (high, low) if t == 0 else (low, high)
        total = back(cell_factor_ref[1 - t], grad_messages_ref[1 - t])
        one, more = source_grads(total, features_t[inner], weight)
        two = extra_ref[outer, :]
        grad = (grad + jnp.concatenate([two, one] if t == 0 else [one, two], axis=0)).T
        at = slice(t * GROUP, (t + 1) * GROUP)
        own_grad_ref[:, at] = spread[:, at] + grad
        share = share + part + more
    joined_ref[:NB, :] = share * scale
    rest = [readout_row, column_to_row(by_kind, NSPEC), jnp.zeros((6, CH), jnp.float32)]
    joined_ref[NB:, :] = jnp.concatenate(rest, axis=0) * scale


def quarter_kernel(kept_ref, received_ref, keep_ref, send_ref):
    first = first_of_pair()
    low = kept_ref[:QUARTER, :] + received_ref[:QUARTER, :]
    high = kept_ref[QUARTER:, :] + received_ref[QUARTER:, :]
    keep_ref[...] = jnp.where(first, low, high)
    send_ref[...] = jnp.where(first, high, low)


def join_kernel(kept_ref, received_ref, rest_ref, out_ref):
    out_ref[:QUARTER, :] = kept_ref[...] + received_ref[...]
    out_ref[QUARTER:, :] = rest_ref[...]


def gather_kernel(mine_ref, along_ref, other_ref, both_ref, out_ref):
    first = first_of_pair()
    at, rest = slice(QUARTER), slice(QUARTER, QUARTER + REST)
    mine = mine_ref[at, :] + along_ref[at, :]
    other = other_ref[at, :] + both_ref[at, :]
    out_ref[:QUARTER, :] = jnp.where(first, mine, other)
    out_ref[QUARTER:HALF, :] = jnp.where(first, other, mine)
    out_ref[HALF:, :] = (mine_ref[rest, :] + along_ref[rest, :]) + (other_ref[rest, :] + both_ref[rest, :])


def fold_kernel(own_ref, from_pair_ref, from_cross_ref, energy_in_ref, grad_ref, energy_ref):
    even = lax.axis_index("space") % 2 == 0
    pair = from_pair_ref[...]
    cross = from_cross_ref[...]
    grad_ref[0, :, :GROUP] = own_ref[:, :GROUP] + jnp.where(even, cross, pair)
    grad_ref[0, :, GROUP:] = own_ref[:, GROUP:] + jnp.where(even, pair, cross)
    energy_ref[...] = energy_in_ref[...]


def finish_kernel(mine_ref, other_ref, radial_ref, mix_ref, readout_ref, shift_ref):
    even = lax.axis_index("space") % 2 == 0
    mine, other = mine_ref[:HALF, :], other_ref[:HALF, :]
    mix_ref[:HALF, :] = jnp.where(even, mine, other)
    mix_ref[HALF:, :] = jnp.where(even, other, mine)
    rest = mine_ref[HALF:, :] + other_ref[HALF:, :]
    radial_ref[...] = rest[:NB]
    readout_ref[...] = rest[NB : NB + 1]
    shift_ref[...] = rest[NB + 1 : NB + 2, :NSPEC]


def first_of_pair():
    space, dp = lax.axis_index("space"), lax.axis_index("dp")
    return jnp.where(space % 2 == 0, dp, space // 2) % 2 == 0


def exchange_routes(space, dp):
    along = [(0, 1 << k) for k in range(dp.bit_length() - 1)]
    across = [(1 << k, 0) for k in range(1, space.bit_length() - 1)]
    shared = (along[0], across[0])
    orders = (across + along[1:], along[:1] + across[1:] + along[1:])
    orders = tuple(order[:-2] + order[:-3:-1] for order in orders)
    count = len(orders[0])

    def route(*places):
        moves = []
        for s in range(space):
            step = [shared[s % 2] if k < 0 else orders[s % 2][k] for k in places]
            for d in range(dp):
                to_s, to_d = s, d
                for one, two in step:
                    to_s, to_d = to_s ^ one, to_d ^ two
                moves.append((s * dp + d, to_s * dp + to_d))
        return moves

    rounds = []
    for k in range(0, count - 1, 2):
        if k + 1 < count - 1:
            rounds.append([route(k), route(k + 1), route(k, k + 1)])
        else:
            rounds.append([route(k)])
    last = count - 1
    rounds.append([route(last), route(-1), route(last, -1)])
    return route(-1), rounds


def call(kernel, name, inputs, outputs, mib=4, scratch=(), flops=0):
    vmem = pl.BlockSpec(memory_space=pltpu.VMEM)
    shapes = tuple(jax.ShapeDtypeStruct(shape, kind) for shape, kind in outputs)
    moved = sum(math.prod(v.shape) * v.dtype.itemsize for v in (*inputs, *shapes))
    return pl.pallas_call(
        kernel,
        out_shape=shapes,
        in_specs=[vmem] * len(inputs),
        out_specs=(vmem,) * len(shapes),
        scratch_shapes=scratch,
        compiler_params=pltpu.CompilerParams(vmem_limit_bytes=mib * 1024 * 1024),
        cost_estimate=pl.CostEstimate(flops=flops, bytes_accessed=moved, transcendentals=0),
        name=name,
    )(*inputs)


def in_hbm(value):
    return pltpu.with_memory_space_constraint(value, pltpu.HBM)


def body(
    node_features,
    positions,
    species,
    energy_cotangent,
    pair_target,
    pair_source,
    pair_count,
    radial_weight,
    mix_weight,
    readout_weight,
    species_shift,
):
    atoms_here = node_features.shape[2]
    space, dp = lax.axis_size("space"), lax.axis_size("dp")
    scale = 1.0 / math.sqrt(atoms_here * space * dp)
    pair = [(i, i ^ 1) for i in range(space)]
    cross = [(i, ((i + 1) ^ 1) - 1) for i in range(1, space - 1)]
    hbm = pl.BlockSpec(memory_space=pltpu.HBM)
    smem = pl.BlockSpec(memory_space=pltpu.SMEM)
    vmem = pl.BlockSpec(memory_space=pltpu.VMEM)
    f32, bf16 = jnp.float32, jnp.bfloat16
    small = (pair_target, pair_source, radial_weight)
    later = (
        species,
        species_shift.reshape(1, NSPEC),
        energy_cotangent,
        mix_weight,
        readout_weight.reshape(1, CH),
    )
    near, far, *small = pl.pallas_call(
        split_kernel,
        out_shape=(jax.ShapeDtypeStruct((SLAB_ROWS, GROUP), f32),) * 2
        + tuple(jax.ShapeDtypeStruct(v.shape, v.dtype) for v in small),
        in_specs=[hbm] * (SMALL + 2),
        out_specs=(vmem,) * (SMALL + 2),
        scratch_shapes=[
            pltpu.VMEM((3, 1, atoms_here), f32),
            pltpu.SemaphoreType.DMA((SMALL + 3,)),
        ],
        compiler_params=pltpu.CompilerParams(vmem_limit_bytes=4 * 1024 * 1024),
        name="split",
    )(
        in_hbm(node_features),
        in_hbm(jnp.transpose(positions, (1, 0, 2))),
        *[in_hbm(v) for v in small],
    )
    targets, sources, radial = small
    from_cross = lax.ppermute(far, "space", cross)
    from_pair = lax.ppermute(near, "space", pair)

    block_flops = 2 * CH * NB * NY * GROUP * GROUP
    group_factor, cell_factor, messages, keep, place, *later = pl.pallas_call(
        local_kernel,
        out_shape=(
            jax.ShapeDtypeStruct((2, NB * GROUP, NY * GROUP), bf16),
            jax.ShapeDtypeStruct((2, NB * CELL_ATOMS, NY * GROUP), bf16),
            jax.ShapeDtypeStruct((2, CH, NY * GROUP), f32),
            jax.ShapeDtypeStruct((8, GROUP), f32),
            jax.ShapeDtypeStruct((2, 3, GROUP, GROUP), f32),
            *[jax.ShapeDtypeStruct(v.shape, v.dtype) for v in later],
        ),
        in_specs=[smem] + [vmem] * 5 + [hbm] * LATER,
        out_specs=(vmem,) * (5 + LATER),
        scratch_shapes=[
            pltpu.VMEM((2, CH, NB * GROUP), bf16),
            pltpu.VMEM((2, CH, NB * CELL_ATOMS), bf16),
            pltpu.SemaphoreType.DMA((LATER,)),
        ],
        compiler_params=pltpu.CompilerParams(vmem_limit_bytes=16 * 1024 * 1024),
        cost_estimate=pl.CostEstimate(
            flops=3 * block_flops, bytes_accessed=11_000_000, transcendentals=0
        ),
        name="local_pairs",
    )(pair_count, targets, sources, radial, near, far, *[in_hbm(v) for v in later])
    species, shift, energy_grad, mix, readout = later

    updated, kept, sent, grad_messages, halo_factor, merged_factor = call(
        functools.partial(node_kernel, scale),
        "node_stage",
        (
            near,
            far,
            from_pair,
            from_cross,
            messages,
            keep,
            place,
            energy_grad,
            radial,
            mix,
            readout,
        ),
        (
            ((CH, atoms_here), f32),
            ((HALF, CH), f32),
            ((HALF, CH), f32),
            ((2, CH, NY * GROUP), bf16),
            ((2, NB * CELL_ATOMS, NY * GROUP), bf16),
            ((2, NB * CELL_ATOMS, NY * GROUP), bf16),
        ),
        16,
        [
            pltpu.VMEM((2, CH, NB * CELL_ATOMS), bf16),
            pltpu.VMEM((2, 2 * CH, NB * CELL_ATOMS), bf16),
            pltpu.VMEM((2, 3, GROUP, GROUP), f32),
        ],
        2 * block_flops,
    )

    received = lax.ppermute(sent, "space", pair)
    pair_grad, cross_grad, extra, share = call(
        halo_back_kernel,
        "halo_back",
        (
            halo_factor,
            merged_factor,
            grad_messages,
            near,
            far,
            from_pair,
            from_cross,
            radial,
        ),
        (((CH, GROUP), f32), ((CH, GROUP), f32), ((GROUP, CH), f32), ((NB, CH), f32)),
        12,
        (),
        2 * block_flops,
    )
    received, share = lax.optimization_barrier((received, share))
    quarter, sent = call(
        quarter_kernel,
        "quarter",
        (kept, received),
        (((QUARTER, CH), f32), ((QUARTER, CH), f32)),
    )
    sharing, (*rounds, last) = exchange_routes(space, dp)
    everyone = ("space", "dp")
    sent, grad_messages, pair_grad = lax.optimization_barrier((sent, grad_messages, pair_grad))
    received = lax.ppermute(sent, everyone, sharing)
    from_pair = lax.ppermute(pair_grad, "space", pair)
    own_grad, joined, energy = call(
        functools.partial(own_back_kernel, scale),
        "own_back",
        (
            group_factor,
            cell_factor,
            grad_messages,
            near,
            far,
            radial,
            extra,
            share,
            updated,
            species,
            shift,
            energy_grad,
            readout,
        ),
        (((CH, atoms_here), f32), ((REST, CH), f32), ((1, atoms_here), f32)),
        12,
        (),
        3 * block_flops,
    )
    (value,) = call(
        join_kernel, "join", (quarter, received, joined), (((QUARTER + REST, CH), f32),)
    )
    value, from_pair, cross_grad = lax.optimization_barrier((value, from_pair, cross_grad))
    for turn, routes in enumerate(rounds):
        arrived = [lax.ppermute(value, everyone, route) for route in routes]
        if turn == 0:
            from_cross = lax.ppermute(cross_grad, "space", cross)
        value = value + arrived[0]
        if len(arrived) == 3:
            value = value + (arrived[1] + arrived[2])
    arrived = [lax.ppermute(value, everyone, route) for route in last]
    value, from_cross, *arrived = lax.optimization_barrier((value, from_cross, *arrived))
    (value,) = call(
        gather_kernel,
        "gather",
        (value, *arrived),
        (((HALF + REST, CH), f32),),
    )
    feature_grad, energy = call(
        fold_kernel,
        "fold",
        (own_grad, from_pair, from_cross, energy),
        (((1, CH, atoms_here), f32), ((1, atoms_here), f32)),
    )
    radial_grad, mix_grad, readout_grad, shift_grad = call(
        finish_kernel,
        "finish",
        (value, lax.ppermute(value, "space", pair)),
        (((NB, CH), f32), ((MIX_ROWS, CH), f32), ((1, CH), f32), ((1, NSPEC), f32)),
    )
    return (
        energy,
        feature_grad,
        radial_grad,
        mix_grad,
        readout_grad.reshape(CH),
        shift_grad.reshape(NSPEC),
    )


def solution(mesh):
    return jax.shard_map(
        body,
        mesh=mesh,
        in_specs=(
            P("dp", None, "space"),
            P("dp", None, "space"),
            P("dp", "space"),
            P("dp", "space"),
            P("dp", "space"),
            P("dp", "space"),
            P("dp", "space"),
            P(),
            P(),
            P(),
            P(),
        ),
        out_specs=(P("dp", "space"), P("dp", None, "space"), P(), P(), P(), P()),
        check_vma=False,
    )
```

```python
import functools
import math

import jax
import jax.numpy as jnp
from jax import lax
from jax.experimental import pallas as pl
from jax.experimental.pallas import tpu as pltpu
from jax.sharding import PartitionSpec as P

CH = 128
NB = 8
NY = 9
NSPEC = 8
CELL_ATOMS = 64
HALO_CELLS = 2
GROUP = 2 * CELL_ATOMS
ROWS = 16
WIDTH = 256
CHUNKS = -(-NY * GROUP // WIDTH)

cutoff = 5.0
message_scale = 0.25

COS_COEFFS = (
    0.9999999889445765,
    -4.93480111664404,
    4.058694745521682,
    -1.3351580223048074,
    0.2350290226247885,
    -0.025358285754444005,
    0.0015936782135993002,
)
SINC_COEFFS = (
    0.9999999992502204,
    -1.6449339933418936,
    0.8117412468909989,
    -0.1907447263221115,
    0.02612742969685046,
    -0.0023157632409761065,
    0.00012580778956459784,
)

MIX_ROWS = 3 * CH
HALF = MIX_ROWS // 2
QUARTER = MIX_ROWS // 4
REST = 16
CELLS = 4 + 2 * HALO_CELLS
SMALL = 3
LATER = 5
SLAB_ROWS = CH + 8


def polynomial(coeffs, x, x2, x4):
    low = (coeffs[0] + coeffs[1] * x) + (coeffs[2] + coeffs[3] * x) * x2
    return low + ((coeffs[4] + coeffs[5] * x) + coeffs[6] * x2) * x4


def edge_terms(source, target, keep):
    dx = (target[0] - source[0]) * (1.0 / cutoff)
    dy = (target[1] - source[1]) * (1.0 / cutoff)
    dz = (target[2] - source[2]) * (1.0 / cutoff)
    xx, yy, zz = dx * dx, dy * dy, dz * dz
    square = xx + yy + zz
    inside = jnp.minimum(square, 1.0)
    gap = 1.0 - inside
    inside2 = inside * inside
    inside4 = inside2 * inside2
    base = (gap * gap) * keep * polynomial(SINC_COEFFS, inside, inside2, inside4)
    twice_cos = polynomial([2.0 * c for c in COS_COEFFS], inside, inside2, inside4)
    return base, twice_cos, dx, dy, dz, xx - yy, 3.0 * zz - square


def factor_rows(factor_ref, size, row, terms):
    base, twice_cos, dx, dy, dz, across, along = terms
    twice_cos2 = twice_cos * twice_cos - 2.0
    raw = [base, twice_cos * base]
    raw += [twice_cos2 * base + base, twice_cos2 * raw[1]]
    for b in range(4, NB):
        raw.append(twice_cos2 * raw[b - 2] - raw[b - 4])
    radial = [value if b == 0 else value * (1.0 / (b + 1)) for b, value in enumerate(raw)]
    root_three = math.sqrt(3.0)
    root_fifteen = math.sqrt(15.0)
    root_five = math.sqrt(5.0)
    wide_x = root_fifteen * dx
    harmonic = [
        None,
        root_three * dx,
        root_three * dy,
        root_three * dz,
        wide_x * dy,
        (root_fifteen * dy) * dz,
        (0.5 * root_five) * along,
        wide_x * dz,
        (0.5 * root_fifteen) * across,
    ]
    for b in range(NB):
        rows = slice(b * size + row, b * size + row + ROWS)
        for y in range(NY):
            value = radial[b] if y == 0 else radial[b] * harmonic[y]
            factor_ref[rows, y * GROUP : (y + 1) * GROUP] = value.astype(jnp.bfloat16)


def column_to_row(column, size):
    wide = jnp.broadcast_to(column, (size, GROUP))
    at = lax.broadcasted_iota(jnp.int32, (size, GROUP), 0)
    lane = lax.broadcasted_iota(jnp.int32, (size, GROUP), 1)
    return jnp.sum(jnp.where(at == lane, wide, 0.0), axis=0, keepdims=True)


def split_kernel(*refs):
    features_ref, place_in_ref, *inputs = refs[: SMALL + 2]
    near_ref, far_ref, *outputs = refs[SMALL + 2 : 2 * SMALL + 4]
    place_ref, sems = refs[2 * SMALL + 4 :]
    core = lax.axis_index("space") % 2
    place_copy = pltpu.make_async_copy(place_in_ref, place_ref, sems.at[2])
    place_copy.start()
    copies = []
    for k, (ref, side) in enumerate(((near_ref, 1 - core), (far_ref, core))):
        at = pl.ds(pl.multiple_of(side * GROUP, GROUP), GROUP)
        copies.append(
            pltpu.make_async_copy(features_ref.at[0, :, at], ref.at[pl.ds(0, CH)], sems.at[k])
        )
    for k, (src, dst) in enumerate(zip(inputs, outputs)):
        copies.append(pltpu.make_async_copy(src, dst, sems.at[3 + k]))
    for copy in copies:
        copy.start()
    place_copy.wait()
    low, high = slice(GROUP), slice(GROUP, 2 * GROUP)
    filler = jnp.zeros((5, GROUP), jnp.float32)
    for ref, one, two in ((near_ref, high, low), (far_ref, low, high)):
        rows = [
            jnp.where(core == 0, place_ref[axis, :, one], place_ref[axis, :, two]) for axis in range(3)
        ]
        ref[CH:, :] = jnp.concatenate(rows + [filler], axis=0)
    for copy in copies:
        copy.wait()


def live_flags(count, pair_target, pair_source):
    size = (4 * CELLS, pair_target.shape[1])
    at = lax.broadcasted_iota(jnp.int32, size, 0)
    slot = lax.broadcasted_iota(jnp.int32, size, 1)
    hit = (pair_target * CELLS + pair_source == at) & (slot < count)
    return jnp.max(jnp.where(hit, message_scale, 0.0), axis=1, keepdims=True)


def keep_row(flags, t, low, high):
    lane = lax.broadcasted_iota(jnp.int32, (1, GROUP), 1)
    one, two = (2 * t) * CELLS + low, (2 * t + 1) * CELLS + high
    return jnp.where(lane < CELL_ATOMS, flags[one : one + 1], flags[two : two + 1])


def set_group(scaled_ref, features, weight_t):
    for b in range(NB):
        scaled_ref[:, b * GROUP : (b + 1) * GROUP] = (features * weight_t[:, b : b + 1]).astype(
            jnp.bfloat16
        )


def set_cell(scaled_ref, features, half, weight_t):
    first = lax.broadcasted_iota(jnp.int32, (CH, GROUP), 1) < CELL_ATOMS
    turned = pltpu.roll(features, CELL_ATOMS, 1)
    twice = jnp.where(first, features, turned) if half == 0 else jnp.where(first, turned, features)
    for k in range(NB // 2):
        weights = jnp.where(first, weight_t[:, 2 * k : 2 * k + 1], weight_t[:, 2 * k + 1 : 2 * k + 2])
        scaled_ref[:, k * GROUP : (k + 1) * GROUP] = (twice * weights).astype(jnp.bfloat16)


def set_place(place_ref, slab):
    place = slab[CH:].T
    for axis in range(3):
        place_ref[axis] = jnp.broadcast_to(place[:, axis : axis + 1], (GROUP, GROUP))


def fill_steps(factor_ref, size, source_of, keeps, target, diagonal=False):
    def terms_of(row):
        keep = jnp.broadcast_to(keeps[row // CELL_ATOMS], (ROWS, GROUP))
        if diagonal:
            row_at = lax.broadcasted_iota(jnp.int32, (ROWS, GROUP), 0)
            lane_at = lax.broadcasted_iota(jnp.int32, (ROWS, GROUP), 1)
            keep = jnp.where(row_at + row == lane_at, 0.0, keep)
        return edge_terms(source_of(row), target, keep)

    ready = {}

    def step(row):
        for k in (row, row + ROWS):
            if k < size and k not in ready:
                ready[k] = terms_of(k)
        factor_rows(factor_ref, size, row, ready[row])

    return [functools.partial(step, row) for row in range(0, size, ROWS)]


def rows_of(place_ref, start):
    return lambda row: [place_ref[axis, start + row : start + row + ROWS, :] for axis in range(3)]


def merged_rows(low_ref, low_start, high_ref, high_start):
    low, high = rows_of(low_ref, low_start), rows_of(high_ref, high_start)

    def rows(row):
        first = lax.broadcasted_iota(jnp.int32, (ROWS, GROUP), 1) < CELL_ATOMS
        return [jnp.where(first, one, two) for one, two in zip(low(row), high(row))]

    return rows


def product_steps(scaled_ref, factor_ref, totals, merged=False):
    def step(k):
        width = min(WIDTH, NY * GROUP - k * WIDTH)
        product = jnp.dot(
            scaled_ref[...],
            factor_ref[:, k * WIDTH : k * WIDTH + width],
            preferred_element_type=jnp.float32,
        )
        if merged:
            lane = lax.broadcasted_iota(jnp.int32, (CH, width), 1) % GROUP
            product = jnp.where(lane < CELL_ATOMS, product[:CH], product[CH:])
        totals[k] = product if totals[k] is None else totals[k] + product

    return [functools.partial(step, k) for k in range(CHUNKS)]


def interleave(one, two):
    done = 0
    for k, step in enumerate(one):
        step()
        upto = (k + 1) * len(two) // len(one)
        for other in two[done:upto]:
            other()
        done = upto


def local_kernel(*refs):
    count_ref, pair_target_ref, pair_source_ref, radial_ref, near_ref, far_ref = refs[:6]
    later_in = refs[6 : 6 + LATER]
    group_factor_ref, cell_factor_ref, messages_ref, keep_ref, place_ref = refs[6 + LATER : 11 + LATER]
    later_out = refs[11 + LATER : 11 + 2 * LATER]
    group_ref, cell_ref, sems = refs[11 + 2 * LATER :]
    copies = [
        pltpu.make_async_copy(src, dst, sems.at[k]) for k, (src, dst) in enumerate(zip(later_in, later_out))
    ]
    for copy in copies:
        copy.start()
    even = lax.axis_index("space") % 2 == 0
    near, far = near_ref[...], far_ref[...]
    slabs = (jnp.where(even, far, near), jnp.where(even, near, far))
    targets = [[slab[CH + axis : CH + axis + 1] for axis in range(3)] for slab in slabs]
    flags = live_flags(count_ref[0, 0], pair_target_ref[...], pair_source_ref[...])
    weight_t = radial_ref[...].T
    for g in range(2):
        set_place(place_ref.at[g], slabs[g])
        set_group(group_ref.at[g], slabs[g][:CH], weight_t)
        set_cell(cell_ref.at[g], slabs[1 - g][:CH], g, weight_t)

    def fill_group(t):
        keeps = [keep_row(flags, t, cell, cell) for cell in (2 * t + 2, 2 * t + 3)]
        return fill_steps(
            group_factor_ref.at[t], GROUP, rows_of(place_ref.at[t], 0), keeps, targets[t], True
        )

    def fill_cell(t):
        cell = 4 - t
        source_of = rows_of(place_ref.at[1 - t], t * CELL_ATOMS)
        return fill_steps(
            cell_factor_ref.at[t], CELL_ATOMS, source_of, [keep_row(flags, t, cell, cell)], targets[t]
        )

    totals = [[None] * CHUNKS for _ in range(2)]
    for step in fill_cell(0):
        step()
    interleave(product_steps(cell_ref.at[0], cell_factor_ref.at[0], totals[0]), fill_group(0))
    interleave(product_steps(group_ref.at[0], group_factor_ref.at[0], totals[0]), fill_group(1))
    interleave(product_steps(group_ref.at[1], group_factor_ref.at[1], totals[1]), fill_cell(1))
    for step in product_steps(cell_ref.at[1], cell_factor_ref.at[1], totals[1]):
        step()
    for t in range(2):
        messages_ref[t] = jnp.concatenate(totals[t], axis=1)
    rows = [
        keep_row(flags, 0, 1, 1),
        keep_row(flags, 0, 0, 5),
        keep_row(flags, 1, 6, 6),
        keep_row(flags, 1, 2, 7),
    ]
    keep_ref[...] = jnp.concatenate(rows + [jnp.zeros((4, GROUP), jnp.float32)], axis=0)
    for copy in copies:
        copy.wait()


def node_kernel(
    scale,
    near_ref,
    far_ref,
    from_pair_ref,
    from_cross_ref,
    messages_ref,
    keep_ref,
    own_place_ref,
    energy_grad_ref,
    radial_ref,
    mix_ref,
    readout_ref,
    updated_ref,
    kept_ref,
    sent_ref,
    grad_messages_ref,
    cell_factor_ref,
    merged_factor_ref,
    cell_ref,
    merged_ref,
    place_ref,
):
    even = lax.axis_index("space") % 2 == 0
    weight_t = radial_ref[...].T
    near, far = near_ref[...], far_ref[...]
    from_pair, from_cross = from_pair_ref[...], from_cross_ref[...]
    slabs = (
        jnp.where(even, from_cross, from_pair),
        jnp.where(even, far, near),
        jnp.where(even, near, far),
        jnp.where(even, from_pair, from_cross),
    )
    targets = [[slab[CH + axis : CH + axis + 1] for axis in range(3)] for slab in slabs[1:3]]

    for t in range(2):
        set_place(place_ref.at[t], slabs[3 * t])
        set_cell(cell_ref.at[t], slabs[3 * t][:CH], 1 - t, weight_t)
        set_cell(merged_ref.at[t, pl.ds(0, CH)], slabs[t][:CH], 0, weight_t)
        set_cell(merged_ref.at[t, pl.ds(CH, CH)], slabs[t + 2][:CH], 1, weight_t)

    def fill_cell(t):
        source_of = rows_of(place_ref.at[t], (1 - t) * CELL_ATOMS)
        keeps = [keep_ref[2 * t : 2 * t + 1, :]]
        return fill_steps(cell_factor_ref.at[t], CELL_ATOMS, source_of, keeps, targets[t])

    def fill_merged(t):
        places = (place_ref.at[0], own_place_ref.at[0], own_place_ref.at[1], place_ref.at[1])
        source_of = merged_rows(places[t], 0, places[t + 2], CELL_ATOMS)
        keeps = [keep_ref[2 * t + 1 : 2 * t + 2, :]]
        return fill_steps(merged_factor_ref.at[t], CELL_ATOMS, source_of, keeps, targets[t])

    totals = [
        [messages_ref[t, :, k * WIDTH : min((k + 1) * WIDTH, NY * GROUP)] for k in range(CHUNKS)]
        for t in range(2)
    ]

    def add_cell(t):
        return product_steps(cell_ref.at[t], cell_factor_ref.at[t], totals[t])

    def add_merged(t):
        return product_steps(merged_ref.at[t], merged_factor_ref.at[t], totals[t], True)

    readout = jnp.broadcast_to(readout_ref[...], (8, CH)).T[:, :1]
    mix = mix_ref[...]
    mix_t = mix.astype(jnp.float32).T.astype(jnp.bfloat16)

    for step in fill_cell(0):
        step()
    interleave(add_cell(0), fill_merged(0))
    interleave(add_merged(0), fill_cell(1))
    interleave(add_cell(1), fill_merged(1))
    for step in add_merged(1):
        step()

    sides = [jnp.concatenate(total, axis=1) for total in totals]
    part = [
        jnp.concatenate([side[:, y * GROUP : (y + 1) * GROUP] for side in sides], axis=1)
        for y in range(NY)
    ]
    invariants = jnp.concatenate(
        [
            part[0],
            0.5 * (part[1] * part[1] + part[2] * part[2] + part[3] * part[3]),
            0.5
            * (
                part[4] * part[4]
                + part[5] * part[5]
                + part[6] * part[6]
                + part[7] * part[7]
                + part[8] * part[8]
            ),
        ],
        axis=0,
    ).astype(jnp.bfloat16)
    preact = jnp.dot(mix_t, invariants, preferred_element_type=jnp.float32)
    gating = jax.nn.sigmoid(preact)
    energy_grad = energy_grad_ref[...]
    spread = readout * energy_grad
    grad_pre = (spread * gating * (1.0 + preact * (1.0 - gating))).astype(jnp.bfloat16)
    grad_inv = jnp.dot(mix, grad_pre, preferred_element_type=jnp.float32)
    grad_mix = scale * lax.dot_general(
        invariants, grad_pre, (((1,), (1,)), ((), ())), preferred_element_type=jnp.float32
    )
    kept_ref[...] = jnp.where(even, grad_mix[:HALF], grad_mix[HALF:])
    sent_ref[...] = jnp.where(even, grad_mix[HALF:], grad_mix[:HALF])
    for y in range(NY):
        order = 0 if y == 0 else 1 if y < 4 else 2
        grad = grad_inv[order * CH : (order + 1) * CH]
        grad = (grad if y == 0 else grad * part[y]).astype(jnp.bfloat16)
        for t in range(2):
            grad_messages_ref[t, :, y * GROUP : (y + 1) * GROUP] = grad[:, t * GROUP : (t + 1) * GROUP]

    updated_ref[...] = jnp.concatenate([slabs[1][:CH], slabs[2][:CH]], axis=1) + preact * gating


def back(factor, grad_messages):
    return lax.dot_general(
        factor, grad_messages, (((1,), (1,)), ((), ())), preferred_element_type=jnp.float32
    )


def source_grads(total, features_t, weight):
    size = features_t.shape[0]
    grad_t = None
    radial = []
    for b in range(NB):
        piece = total[b * size : (b + 1) * size]
        term = piece * weight[b : b + 1, :]
        grad_t = term if grad_t is None else grad_t + term
        radial.append(jnp.sum(piece * features_t, axis=0, keepdims=True))
    return grad_t, jnp.concatenate(radial, axis=0)


def halo_back_kernel(
    cell_factor_ref,
    merged_factor_ref,
    grad_messages_ref,
    near_ref,
    far_ref,
    from_pair_ref,
    from_cross_ref,
    radial_ref,
    to_pair_ref,
    to_cross_ref,
    extra_ref,
    share_ref,
):
    even = lax.axis_index("space") % 2 == 0
    weight = radial_ref[...]
    near, far = near_ref[:CH, :], far_ref[:CH, :]
    from_pair, from_cross = from_pair_ref[:CH, :], from_cross_ref[:CH, :]
    features_t = [
        jnp.where(even, one, two).T
        for one, two in ((from_cross, from_pair), (far, near), (near, far), (from_pair, from_cross))
    ]
    first = lax.broadcasted_iota(jnp.int32, (CH, NY * GROUP), 1) % GROUP < CELL_ATOMS
    low, high = slice(CELL_ATOMS), slice(CELL_ATOMS, GROUP)
    share = None
    grads = {}
    for t in range(2):
        grad = grad_messages_ref[t]
        none = jnp.zeros_like(grad)
        both = jnp.concatenate([jnp.where(first, grad, none), jnp.where(first, none, grad)], axis=0)
        merged = back(merged_factor_ref[t], both)
        pieces = (
            (3 * t, 1 - t, back(cell_factor_ref[t], grad)),
            (t, 0, merged[:, :CH]),
            (t + 2, 1, merged[:, CH:]),
        )
        for g, half, total in pieces:
            grads[g, half], part = source_grads(total, features_t[g][(low, high)[half]], weight)
            share = part if share is None else share + part
    grad_before = jnp.concatenate([grads[0, 0], grads[0, 1]], axis=0).T
    grad_after = jnp.concatenate([grads[3, 0], grads[3, 1]], axis=0).T
    to_pair_ref[...] = jnp.where(even, grad_after, grad_before)
    to_cross_ref[...] = jnp.where(even, grad_before, grad_after)
    extra_ref[low, :] = grads[1, 0]
    extra_ref[high, :] = grads[2, 1]
    share_ref[...] = share


def own_back_kernel(
    scale,
    group_factor_ref,
    cell_factor_ref,
    grad_messages_ref,
    near_ref,
    far_ref,
    radial_ref,
    extra_ref,
    share_ref,
    updated_ref,
    species_ref,
    shift_ref,
    energy_grad_ref,
    readout_ref,
    own_grad_ref,
    joined_ref,
    energy_ref,
):
    even = lax.axis_index("space") % 2 == 0
    weight = radial_ref[...]
    near, far = near_ref[:CH, :], far_ref[:CH, :]
    share = share_ref[...]
    low, high = slice(CELL_ATOMS), slice(CELL_ATOMS, GROUP)
    readout = jnp.broadcast_to(readout_ref[...], (8, CH)).T[:, :1]
    updated, energy_grad, kinds = updated_ref[...], energy_grad_ref[...], species_ref[...]
    spread = readout * energy_grad
    shifts = jnp.zeros((1, 2 * GROUP), jnp.float32)
    for n in range(NSPEC):
        shifts = jnp.where(kinds == n, shift_ref[:, n : n + 1], shifts)
    energy_ref[...] = jnp.sum(updated * readout, axis=0, keepdims=True) + shifts
    readout_row = column_to_row(jnp.sum(updated * energy_grad, axis=1, keepdims=True), CH)
    here = lax.broadcasted_iota(jnp.int32, (NSPEC, 2 * GROUP), 0) == kinds
    by_kind = jnp.sum(jnp.where(here, energy_grad, 0.0), axis=1, keepdims=True)
    for t, features in enumerate((jnp.where(even, far, near), jnp.where(even, near, far))):
        features_t = features.T
        total = back(group_factor_ref[t], grad_messages_ref[t])
        grad, part = source_grads(total, features_t, weight)
        inner, outer = (high, low) if t == 0 else (low, high)
        total = back(cell_factor_ref[1 - t], grad_messages_ref[1 - t])
        one, more = source_grads(total, features_t[inner], weight)
        two = extra_ref[outer, :]
        grad = (grad + jnp.concatenate([two, one] if t == 0 else [one, two], axis=0)).T
        at = slice(t * GROUP, (t + 1) * GROUP)
        own_grad_ref[:, at] = spread[:, at] + grad
        share = share + part + more
    joined_ref[:NB, :] = share * scale
    rest = [readout_row, column_to_row(by_kind, NSPEC), jnp.zeros((6, CH), jnp.float32)]
    joined_ref[NB:, :] = jnp.concatenate(rest, axis=0) * scale


def quarter_kernel(kept_ref, received_ref, keep_ref, send_ref):
    first = first_of_pair()
    low = kept_ref[:QUARTER, :] + received_ref[:QUARTER, :]
    high = kept_ref[QUARTER:, :] + received_ref[QUARTER:, :]
    keep_ref[...] = jnp.where(first, low, high)
    send_ref[...] = jnp.where(first, high, low)


def join_kernel(kept_ref, received_ref, rest_ref, out_ref):
    out_ref[:QUARTER, :] = kept_ref[...] + received_ref[...]
    out_ref[QUARTER:, :] = rest_ref[...]


def gather_kernel(mine_ref, along_ref, other_ref, both_ref, out_ref):
    first = first_of_pair()
    at, rest = slice(QUARTER), slice(QUARTER, QUARTER + REST)
    mine = mine_ref[at, :] + along_ref[at, :]
    other = other_ref[at, :] + both_ref[at, :]
    out_ref[:QUARTER, :] = jnp.where(first, mine, other)
    out_ref[QUARTER:HALF, :] = jnp.where(first, other, mine)
    out_ref[HALF:, :] = (mine_ref[rest, :] + along_ref[rest, :]) + (other_ref[rest, :] + both_ref[rest, :])


def fold_kernel(own_ref, from_pair_ref, from_cross_ref, energy_in_ref, grad_ref, energy_ref):
    even = lax.axis_index("space") % 2 == 0
    pair = from_pair_ref[...]
    cross = from_cross_ref[...]
    grad_ref[0, :, :GROUP] = own_ref[:, :GROUP] + jnp.where(even, cross, pair)
    grad_ref[0, :, GROUP:] = own_ref[:, GROUP:] + jnp.where(even, pair, cross)
    energy_ref[...] = energy_in_ref[...]


def finish_kernel(mine_ref, other_ref, radial_ref, mix_ref, readout_ref, shift_ref):
    even = lax.axis_index("space") % 2 == 0
    mine, other = mine_ref[:HALF, :], other_ref[:HALF, :]
    mix_ref[:HALF, :] = jnp.where(even, mine, other)
    mix_ref[HALF:, :] = jnp.where(even, other, mine)
    rest = mine_ref[HALF:, :] + other_ref[HALF:, :]
    radial_ref[...] = rest[:NB]
    readout_ref[...] = rest[NB : NB + 1]
    shift_ref[...] = rest[NB + 1 : NB + 2, :NSPEC]


def first_of_pair():
    space, dp = lax.axis_index("space"), lax.axis_index("dp")
    return jnp.where(space % 2 == 0, dp, space // 2) % 2 == 0


def exchange_routes(space, dp):
    along = [(0, 1 << k) for k in range(dp.bit_length() - 1)]
    across = [(1 << k, 0) for k in range(1, space.bit_length() - 1)]
    shared = (along[0], across[0])
    orders = (across + along[1:], along[:1] + across[1:] + along[1:])
    orders = tuple(order[:-2] + order[:-3:-1] for order in orders)
    count = len(orders[0])

    def route(*places):
        moves = []
        for s in range(space):
            step = [shared[s % 2] if k < 0 else orders[s % 2][k] for k in places]
            for d in range(dp):
                to_s, to_d = s, d
                for one, two in step:
                    to_s, to_d = to_s ^ one, to_d ^ two
                moves.append((s * dp + d, to_s * dp + to_d))
        return moves

    rounds = []
    for k in range(0, count - 1, 2):
        if k + 1 < count - 1:
            rounds.append([route(k), route(k + 1), route(k, k + 1)])
        else:
            rounds.append([route(k)])
    last = count - 1
    rounds.append([route(last), route(-1), route(last, -1)])
    return route(-1), rounds


def call(kernel, name, inputs, outputs, mib=4, scratch=(), flops=0):
    vmem = pl.BlockSpec(memory_space=pltpu.VMEM)
    shapes = tuple(jax.ShapeDtypeStruct(shape, kind) for shape, kind in outputs)
    moved = sum(math.prod(v.shape) * v.dtype.itemsize for v in (*inputs, *shapes))
    return pl.pallas_call(
        kernel,
        out_shape=shapes,
        in_specs=[vmem] * len(inputs),
        out_specs=(vmem,) * len(shapes),
        scratch_shapes=scratch,
        compiler_params=pltpu.CompilerParams(vmem_limit_bytes=mib * 1024 * 1024),
        cost_estimate=pl.CostEstimate(flops=flops, bytes_accessed=moved, transcendentals=0),
        name=name,
    )(*inputs)


def in_hbm(value):
    return pltpu.with_memory_space_constraint(value, pltpu.HBM)


def body(
    node_features,
    positions,
    species,
    energy_cotangent,
    pair_target,
    pair_source,
    pair_count,
    radial_weight,
    mix_weight,
    readout_weight,
    species_shift,
):
    atoms_here = node_features.shape[2]
    space, dp = lax.axis_size("space"), lax.axis_size("dp")
    scale = 1.0 / math.sqrt(atoms_here * space * dp)
    pair = [(i, i ^ 1) for i in range(space)]
    cross = [(i, ((i + 1) ^ 1) - 1) for i in range(1, space - 1)]
    hbm = pl.BlockSpec(memory_space=pltpu.HBM)
    smem = pl.BlockSpec(memory_space=pltpu.SMEM)
    vmem = pl.BlockSpec(memory_space=pltpu.VMEM)
    f32, bf16 = jnp.float32, jnp.bfloat16
    small = (pair_target, pair_source, radial_weight)
    later = (
        species,
        species_shift.reshape(1, NSPEC),
        energy_cotangent,
        mix_weight,
        readout_weight.reshape(1, CH),
    )
    near, far, *small = pl.pallas_call(
        split_kernel,
        out_shape=(jax.ShapeDtypeStruct((SLAB_ROWS, GROUP), f32),) * 2
        + tuple(jax.ShapeDtypeStruct(v.shape, v.dtype) for v in small),
        in_specs=[hbm] * (SMALL + 2),
        out_specs=(vmem,) * (SMALL + 2),
        scratch_shapes=[
            pltpu.VMEM((3, 1, atoms_here), f32),
            pltpu.SemaphoreType.DMA((SMALL + 3,)),
        ],
        compiler_params=pltpu.CompilerParams(vmem_limit_bytes=4 * 1024 * 1024),
        name="split",
    )(
        in_hbm(node_features),
        in_hbm(jnp.transpose(positions, (1, 0, 2))),
        *[in_hbm(v) for v in small],
    )
    targets, sources, radial = small
    from_cross = lax.ppermute(far, "space", cross)
    from_pair = lax.ppermute(near, "space", pair)

    block_flops = 2 * CH * NB * NY * GROUP * GROUP
    group_factor, cell_factor, messages, keep, place, *later = pl.pallas_call(
        local_kernel,
        out_shape=(
            jax.ShapeDtypeStruct((2, NB * GROUP, NY * GROUP), bf16),
            jax.ShapeDtypeStruct((2, NB * CELL_ATOMS, NY * GROUP), bf16),
            jax.ShapeDtypeStruct((2, CH, NY * GROUP), f32),
            jax.ShapeDtypeStruct((8, GROUP), f32),
            jax.ShapeDtypeStruct((2, 3, GROUP, GROUP), f32),
            *[jax.ShapeDtypeStruct(v.shape, v.dtype) for v in later],
        ),
        in_specs=[smem] + [vmem] * 5 + [hbm] * LATER,
        out_specs=(vmem,) * (5 + LATER),
        scratch_shapes=[
            pltpu.VMEM((2, CH, NB * GROUP), bf16),
            pltpu.VMEM((2, CH, NB * CELL_ATOMS), bf16),
            pltpu.SemaphoreType.DMA((LATER,)),
        ],
        compiler_params=pltpu.CompilerParams(vmem_limit_bytes=16 * 1024 * 1024),
        cost_estimate=pl.CostEstimate(
            flops=3 * block_flops, bytes_accessed=11_000_000, transcendentals=0
        ),
        name="local_pairs",
    )(pair_count, targets, sources, radial, near, far, *[in_hbm(v) for v in later])
    species, shift, energy_grad, mix, readout = later

    updated, kept, sent, grad_messages, halo_factor, merged_factor = call(
        functools.partial(node_kernel, scale),
        "node_stage",
        (
            near,
            far,
            from_pair,
            from_cross,
            messages,
            keep,
            place,
            energy_grad,
            radial,
            mix,
            readout,
        ),
        (
            ((CH, atoms_here), f32),
            ((HALF, CH), f32),
            ((HALF, CH), f32),
            ((2, CH, NY * GROUP), bf16),
            ((2, NB * CELL_ATOMS, NY * GROUP), bf16),
            ((2, NB * CELL_ATOMS, NY * GROUP), bf16),
        ),
        16,
        [
            pltpu.VMEM((2, CH, NB * CELL_ATOMS), bf16),
            pltpu.VMEM((2, 2 * CH, NB * CELL_ATOMS), bf16),
            pltpu.VMEM((2, 3, GROUP, GROUP), f32),
        ],
        2 * block_flops,
    )

    received = lax.ppermute(sent, "space", pair)
    pair_grad, cross_grad, extra, share = call(
        halo_back_kernel,
        "halo_back",
        (
            halo_factor,
            merged_factor,
            grad_messages,
            near,
            far,
            from_pair,
            from_cross,
            radial,
        ),
        (((CH, GROUP), f32), ((CH, GROUP), f32), ((GROUP, CH), f32), ((NB, CH), f32)),
        12,
        (),
        2 * block_flops,
    )
    received, share = lax.optimization_barrier((received, share))
    quarter, sent = call(
        quarter_kernel,
        "quarter",
        (kept, received),
        (((QUARTER, CH), f32), ((QUARTER, CH), f32)),
    )
    sharing, (*rounds, last) = exchange_routes(space, dp)
    everyone = ("space", "dp")
    sent, grad_messages, pair_grad = lax.optimization_barrier((sent, grad_messages, pair_grad))
    received = lax.ppermute(sent, everyone, sharing)
    from_pair = lax.ppermute(pair_grad, "space", pair)
    own_grad, joined, energy = call(
        functools.partial(own_back_kernel, scale),
        "own_back",
        (
            group_factor,
            cell_factor,
            grad_messages,
            near,
            far,
            radial,
            extra,
            share,
            updated,
            species,
            shift,
            energy_grad,
            readout,
        ),
        (((CH, atoms_here), f32), ((REST, CH), f32), ((1, atoms_here), f32)),
        12,
        (),
        3 * block_flops,
    )
    (value,) = call(
        join_kernel, "join", (quarter, received, joined), (((QUARTER + REST, CH), f32),)
    )
    value, from_pair, cross_grad = lax.optimization_barrier((value, from_pair, cross_grad))
    for turn, routes in enumerate(rounds):
        arrived = [lax.ppermute(value, everyone, route) for route in routes]
        if turn == 0:
            from_cross = lax.ppermute(cross_grad, "space", cross)
        value = value + arrived[0]
        if len(arrived) == 3:
            value = value + (arrived[1] + arrived[2])
    arrived = [lax.ppermute(value, everyone, route) for route in last]
    value, from_cross, *arrived = lax.optimization_barrier((value, from_cross, *arrived))
    (value,) = call(
        gather_kernel,
        "gather",
        (value, *arrived),
        (((HALF + REST, CH), f32),),
    )
    feature_grad, energy = call(
        fold_kernel,
        "fold",
        (own_grad, from_pair, from_cross, energy),
        (((1, CH, atoms_here), f32), ((1, atoms_here), f32)),
    )
    radial_grad, mix_grad, readout_grad, shift_grad = call(
        finish_kernel,
        "finish",
        (value, lax.ppermute(value, "space", pair)),
        (((NB, CH), f32), ((MIX_ROWS, CH), f32), ((1, CH), f32), ((1, NSPEC), f32)),
    )
    return (
        energy,
        feature_grad,
        radial_grad,
        mix_grad,
        readout_grad.reshape(CH),
        shift_grad.reshape(NSPEC),
    )


def solution(mesh):
    return jax.shard_map(
        body,
        mesh=mesh,
        in_specs=(
            P("dp", None, "space"),
            P("dp", None, "space"),
            P("dp", "space"),
            P("dp", "space"),
            P("dp", "space"),
            P("dp", "space"),
            P("dp", "space"),
            P(),
            P(),
            P(),
            P(),
        ),
        out_specs=(P("dp", "space"), P("dp", None, "space"), P(), P(), P(), P()),
        check_vma=False,
    )
```
